32 devices in a mesh: boot: 2 (over x), space: 16 (over z, y, core).
Axes of the slice: x: 2, y: 2, z: 4, core: 2. Of those that a mesh axis runs over, the one named last changes fastest.
Arguments:
- background_states: bfloat16 [512, 32768], P('space'), may hold values from -6 to 6
- measurement_anomaly_matrix: bfloat16 [6144, 512], P('space'), may hold values from -6 to 6
- departure_vector: bfloat16 [6144], P('space'), may hold values from -6 to 6
- measurement_precision: float32 [6144], P('space'), may hold values from 0.25 to 4
- measurement_region_targets: int32 [6144, 2], P('space'), may hold values from 0 to 15, all different within a row; in each aligned block of 384 rows (0 to 383, 384 to 767, ...) at most 96 rows name the same one
- localization_factor_scaled: int32 [6144, 2], P('space'), may hold values from 16 to 1024
- bootstrap_multiplicity: int32 [12288], P(('boot', 'space')), parts along dimension 0, may hold values from 0 to 3
Outputs:
- analysis: bfloat16 [1024, 32768], P(('boot', 'space')), parts along dimension 0
The draws below stay inside these ranges and needn't reach their ends.
There are 2 independent parts, one for each index of `boot`. The reference program is written for one: setup_inputs(seed, part) draws one part's arguments, and reference() takes and returns one part's arrays. A program takes and returns all parts, laid end to end along the dimension named above; an argument that names none is the same for every part. Nothing has to cross between parts.
Inputs may be any that keep to these rules, and one draw needn't show every extreme that they name: `measurement_region_targets`: each row names 2 different patches. Among the rows of one device (aligned blocks of 384 rows) no patch is named more than 96 times, a bound that some block reaches.
All inputs are finite; a program needn't handle non-finite values.
Results may differ from the reference program's by a relative error of at most 0.0075.
Values may be sent and summed in bfloat16 or wider, within the bound.
No kernel may reach another device: no remote copies, remote signals or barrier semaphores. Data moves between devices by JAX's collectives and lax.ppermute only.
A program may use at most 64 MiB of HBM per device.

```python
import math
import jax
import jax.numpy as jnp
import numpy as np
from jax import lax

ENSEMBLE_SIZE = 512
REGION_LOCATIONS = 2048
O_DEV = 384
TOP = 2
NS_STEPS = 6
PATCHES = 16
STATE_LOCATIONS = 32768
OBS = 6144
CAP = 96
N_SPACE = 16


def touch_ends(values, stream_key, smallest, high):
    place = [jax.random.randint(jax.random.fold_in(stream_key, axis), (), 0, length) for axis, length in enumerate(values.shape)]
    longest = values.shape.index(max(values.shape))
    neighbour = place[:longest] + [(place[longest] + 1) % values.shape[longest]] + place[longest + 1:]
    return values.at[tuple(place)].set(smallest).at[tuple(neighbour)].set(high)


def steps_of(own_key, extent, split, low, top_value):
    level = 1.0
    for position, shards_of in split:
        steps = jax.random.uniform(jax.random.fold_in(jax.random.fold_in(own_key, 6), position), (shards_of,), jnp.float32, low / len(split), top_value / len(split))
        level = level * jnp.repeat(jnp.exp(steps), extent[position] // shards_of).reshape((-1,) + (1,) * (len(extent) - 1 - position))
    return level


def deal_out(rng, own, number, rows, count, top, limit, skew):
    ranking = jax.random.permutation(rng, count)
    packed, usual = portions_of(count, rows * top, limit, skew, True), portions_of(count, rows * top, limit, skew, False)
    places = jnp.arange(count)

    def named(lengths, rotation):
        used = int((lengths > 0).sum())
        fixed = max(1, used // 4)
        moved = fixed + (places - fixed + rotation * (used - fixed)) % max(1, count - fixed)
        return jnp.zeros((count,), jnp.int32).at[ranking[jnp.where(places < fixed, places, moved)]].set(jnp.asarray(lengths, jnp.int32))

    lengths = jnp.where(number % 4 == 0, named(packed, number // 4), named(usual, number - number // 4 - 1))
    mixed = jax.random.permutation(jax.random.fold_in(own, 3), count)
    donor, sink = mixed[0:count // 2 * 2:2], mixed[1:count // 2 * 2:2]
    room = jnp.minimum(lengths[donor] - 1, limit - lengths[sink]) // 2
    room = jnp.where((donor == ranking[0]) | (sink == ranking[0]) | (lengths[sink] == 0), 0, jnp.maximum(room, 0))
    moved = jax.random.randint(jax.random.fold_in(own, 4), (count // 2,), 0, 1 << 20) % (room + 1)
    lengths = lengths.at[donor].add(-moved).at[sink].add(moved)
    members = jnp.searchsorted(jnp.cumsum(lengths), jnp.arange(rows * top), side="right").astype(jnp.int32)
    listing = members.reshape(top, rows).T
    listing = listing[jax.random.permutation(jax.random.fold_in(own, 1), rows)]
    rotation = jax.random.randint(jax.random.fold_in(own, 2), (rows, 1), 0, top)
    return jnp.take_along_axis(listing, (jnp.arange(top)[None, :] + rotation) % top, axis=1)


def portions_of(amount, total, limit, slope, full):
    portions = [(1 << 20) // math.isqrt(rank ** slope) + 1 for rank in range(1, amount + 1)]
    largest = limit if full else min(limit, max(-(-total // amount), total * portions[0] // sum(portions)))
    least = 1 if total - largest >= amount - 1 else 0
    holding, rest = [largest] + [least] * (amount - 1), total - largest - least * (amount - 1)
    while rest > 0:
        candidates = [i for i in range(1, amount) if holding[i] < largest] or [i for i in range(1, amount) if holding[i] < limit]
        pool, left = sum([portions[i] for i in candidates]), rest
        for i in candidates:
            more = min(limit - holding[i], max(1, left * portions[i] // pool), rest)
            holding[i] = holding[i] + more
            rest = rest - more
    return np.array(holding)


def noise(rng, dims, scale, bound, pieces=(), kind=jnp.bfloat16):
    values = scale * jax.random.normal(rng, dims, jnp.float32)
    if pieces:
        values = values * steps_of(rng, dims, pieces, -0.22, 0.18)
    return jnp.clip(values, -bound, bound).astype(kind)


def setup_inputs(seed: int = 0, part: int = 0) -> dict:
    streams_of = jax.random.split(jax.random.key(seed), 8)
    part_keys = jax.random.split(jax.random.fold_in(streams_of[7], part), 8)
    background_states = noise(streams_of[0], (ENSEMBLE_SIZE, STATE_LOCATIONS), 1.0, 6.0, ((0, 16),))
    measurement_anomaly_matrix = noise(streams_of[1], (OBS, ENSEMBLE_SIZE), 1.0, 6.0, ((0, 16),))
    departure_vector = noise(streams_of[2], (OBS,), 1.0, 6.0, ((0, 16),))
    measurement_precision = jnp.clip(jnp.exp(math.log(4.0) - 2.7725887 * jax.random.uniform(streams_of[3], (OBS,), jnp.float32) ** steps_of(streams_of[3], (OBS,), ((0, 16),), -0.2, 0.2)), 0.25, 4.0)
    measurement_region_targets_keys = jax.random.split(jax.random.fold_in(streams_of[4], 1), OBS // O_DEV)
    measurement_region_targets_turns = jax.random.permutation(jax.random.fold_in(streams_of[4], 3), OBS // O_DEV)
    measurement_region_targets = jax.vmap(lambda own, number: deal_out(jax.random.fold_in(streams_of[4], 2), own, number, O_DEV, PATCHES, TOP, CAP, 2))(measurement_region_targets_keys, measurement_region_targets_turns).reshape((OBS, TOP))
    localization_factor_scaled = touch_ends(jax.random.randint(streams_of[5], (OBS, TOP), 16, 1025), jax.random.fold_in(streams_of[5], 1), 16, 1024).astype(jnp.int32)
    bootstrap_multiplicity = touch_ends(jax.random.randint(part_keys[6], (OBS,), 0, 4), jax.random.fold_in(part_keys[6], 1), 0, 3).astype(jnp.int32)
    return dict(background_states=background_states, measurement_anomaly_matrix=measurement_anomaly_matrix, departure_vector=departure_vector, measurement_precision=measurement_precision, measurement_region_targets=measurement_region_targets, localization_factor_scaled=localization_factor_scaled, bootstrap_multiplicity=bootstrap_multiplicity)


def inverse_root(shifted):
    size_k = shifted.shape[0]
    identity = jnp.eye(size_k, dtype=jnp.float32)
    frobenius = jnp.sqrt(jnp.sum(shifted * shifted))
    current = shifted / frobenius
    root = identity
    for iteration in range(NS_STEPS):
        factor = 1.5 * identity - 0.5 * jnp.dot(root, current, precision=lax.Precision.HIGHEST)
        current = jnp.dot(current, factor, precision=lax.Precision.HIGHEST)
        root = jnp.dot(factor, root, precision=lax.Precision.HIGHEST)
    return root / jnp.sqrt(frobenius)

def analyse(obs_rows, weights, innov_vals, background_submatrix):
    scaled = (weights[:, None].astype(jnp.float32) * obs_rows.astype(jnp.float32)).astype(jnp.bfloat16)
    gram_matrix = lax.dot_general(obs_rows, scaled, (((0,), (0,)), ((), ())), preferred_element_type=jnp.float32)
    drive_vec = jnp.dot(innov_vals, scaled, preferred_element_type=jnp.float32)
    member_count = obs_rows.shape[1]
    shifted = jnp.eye(member_count, dtype=jnp.float32) + gram_matrix / (member_count - 1.0)
    root = inverse_root(shifted)
    inner = jnp.dot(root, drive_vec, precision=lax.Precision.HIGHEST)
    mean_weight = jnp.dot(root, inner, precision=lax.Precision.HIGHEST) / (member_count - 1.0)
    blended = (root + mean_weight[:, None]).astype(jnp.bfloat16)
    centre = lax.optimization_barrier(jnp.mean(background_submatrix.astype(jnp.float32), axis=0))
    perturb = (background_submatrix.astype(jnp.float32) - centre[None, :]).astype(jnp.bfloat16)
    update = lax.dot_general(blended, perturb, (((0,), (0,)), ((), ())), preferred_element_type=jnp.float32)
    return (centre[None, :] + update).astype(jnp.bfloat16)

def reference(background_states, measurement_anomaly_matrix, departure_vector, measurement_precision, measurement_region_targets, localization_factor_scaled, bootstrap_multiplicity):
    weight = (localization_factor_scaled.astype(jnp.float32) / 1024.0 * (bootstrap_multiplicity.astype(jnp.float32) * measurement_precision)[:, None]).astype(jnp.bfloat16)
    targets = measurement_region_targets.reshape(-1).astype(jnp.int32)
    flat_weight = weight.reshape(-1)
    owner_row = (jnp.arange(targets.shape[0], dtype=jnp.int32) // TOP).astype(jnp.int32)
    sorted_pairs = jnp.argsort(targets, stable=True).astype(jnp.int32)
    matches = lax.optimization_barrier(jnp.sum((targets[:, None] == jnp.arange(PATCHES, dtype=jnp.int32)[None, :]).astype(jnp.int32), axis=0)).astype(jnp.int32)
    starts = (jnp.cumsum(matches) - matches).astype(jnp.int32)
    slot_limit = N_SPACE * CAP
    padded = jnp.concatenate([sorted_pairs, jnp.zeros((slot_limit,), jnp.int32)])

    def one_patch(patch_index):
        picked = lax.dynamic_slice(padded, (starts[patch_index],), (slot_limit,)).astype(jnp.int32)
        alive_mask = jnp.arange(slot_limit, dtype=jnp.int32) < matches[patch_index]
        obs_rows = measurement_anomaly_matrix[owner_row[picked]]
        weights = jnp.where(alive_mask, flat_weight[picked], jnp.zeros((), flat_weight.dtype))
        innov_vals = jnp.where(alive_mask, departure_vector[owner_row[picked]], jnp.zeros((), departure_vector.dtype))
        starting_index = (patch_index * REGION_LOCATIONS).astype(jnp.int32)
        background_submatrix = lax.dynamic_slice(background_states, (jnp.zeros((), jnp.int32), starting_index), (ENSEMBLE_SIZE, REGION_LOCATIONS))
        return analyse(obs_rows, weights, innov_vals, background_submatrix)
    result = lax.map(one_patch, jnp.arange(PATCHES, dtype=jnp.int32))
    return jnp.transpose(result, (1, 0, 2)).reshape(ENSEMBLE_SIZE, PATCHES * REGION_LOCATIONS)
```

```python
import functools

import jax
import jax.numpy as jnp
from jax import lax
from jax.experimental import pallas as pl
from jax.experimental.pallas import tpu as pltpu
from jax.sharding import PartitionSpec as P

NS_STEPS = 6
LANES = 128
VMEM_BYTES = 48 * 1024 * 1024
F32 = jnp.float32
BF16 = jnp.bfloat16


def pack_kernel(targets_ref, local_ref, mult_ref, prec_ref, dep_ref, rows_ref, slots_ref, info_ref):
    patches, cap, _ = slots_ref.shape
    count = rows_ref.shape[0]
    weight = local_ref[...].astype(F32) / 1024.0 * (mult_ref[...].astype(F32) * prec_ref[...])
    weight = weight.astype(BF16).astype(F32)
    dep = dep_ref[...].astype(F32)
    patch_id = lax.broadcasted_iota(jnp.int32, (patches, count), 0)
    first = patch_id == targets_ref[0:1, :]
    second = patch_id == targets_ref[1:2, :]
    named = jnp.logical_or(first, second)
    earlier = lax.broadcasted_iota(jnp.int32, (count, count), 0) < lax.broadcasted_iota(
        jnp.int32, (count, count), 1
    )
    rank = jnp.dot(
        named.astype(F32).astype(BF16), earlier.astype(F32).astype(BF16), preferred_element_type=F32
    )
    rank = jnp.where(named, rank, -1.0)
    by_patch = jnp.where(first, weight[0:1, :], jnp.where(second, weight[1:2, :], 0.0))
    slot_id = lax.broadcasted_iota(jnp.int32, (cap, count), 0).astype(F32)
    lane = lax.broadcasted_iota(jnp.int32, (cap, LANES), 1)
    info = jnp.zeros((cap, LANES), F32)
    rows = rows_ref[...]
    for patch in range(patches):
        pick = jnp.where(slot_id == rank[patch : patch + 1, :], 1.0, 0.0)
        slots_ref[patch] = jnp.dot(pick.astype(BF16), rows, preferred_element_type=F32).astype(BF16)
        weight_col = jnp.sum(pick * by_patch[patch : patch + 1, :], axis=1, keepdims=True)
        dep_col = jnp.sum(pick * dep, axis=1, keepdims=True)
        info = jnp.where(lane == patch, weight_col, info)
        info = jnp.where(lane == patches + patch, dep_col, info)
    info_ref[...] = info.astype(BF16)


def pack(targets, local, mult, prec, dep, rows, patches, cap):
    members = rows.shape[1]
    count = rows.shape[0]
    return pl.pallas_call(
        pack_kernel,
        out_shape=(
            jax.ShapeDtypeStruct((patches, cap, members), BF16),
            jax.ShapeDtypeStruct((cap, LANES), BF16),
        ),
        compiler_params=pltpu.CompilerParams(vmem_limit_bytes=VMEM_BYTES),
        cost_estimate=pl.CostEstimate(
            flops=2 * patches * cap * count * members,
            bytes_accessed=2 * (patches * cap + count) * members,
            transcendentals=0,
        ),
        name="pack_rows",
    )(targets.T, local.T, mult[None, :], prec[None, :], dep[None, :], rows)


def halves(value):
    high = value.astype(BF16)
    return high, (value - high.astype(F32)).astype(BF16)


def product(left_high, left_low, right_high, right_low):
    dot = functools.partial(jnp.dot, preferred_element_type=F32)
    return dot(left_high, right_high) + (dot(left_high, right_low) + dot(left_low, right_high))


def weights_kernel(rows_ref, info_ref, blended_ref, y_high, y_low, z_high, z_low, f_high, f_low):
    sources, cap, members = rows_ref.shape
    patch = lax.axis_index("space")
    lane = lax.broadcasted_iota(jnp.int32, (cap, LANES), 1)
    gram = jnp.zeros((members, members), F32)
    drive = jnp.zeros((1, members), F32)
    for source in range(sources):
        info = info_ref[source].astype(F32)
        weight_col = jnp.sum(jnp.where(lane == patch, info, 0.0), axis=1, keepdims=True)
        dep_col = jnp.sum(jnp.where(lane == sources + patch, info, 0.0), axis=1, keepdims=True)
        rows = rows_ref[source]
        scaled = (weight_col * rows.astype(F32)).astype(BF16)
        gram += lax.dot_general(rows, scaled, (((0,), (0,)), ((), ())), preferred_element_type=F32)
        drive += jnp.sum(dep_col * scaled.astype(F32), axis=0, keepdims=True)

    row_id = lax.broadcasted_iota(jnp.int32, (members, members), 0)
    col_id = lax.broadcasted_iota(jnp.int32, (members, members), 1)
    diagonal = row_id == col_id
    identity = jnp.where(diagonal, 1.0, 0.0)
    shifted = identity + gram / (members - 1.0)
    squares = jnp.sum(jnp.sum(shifted * shifted, axis=0, keepdims=True), axis=1, keepdims=True)
    frobenius = jnp.sqrt(squares)
    current = shifted / frobenius

    def put(high_ref, low_ref, value):
        high_ref[...], low_ref[...] = halves(value)

    def factor_of(zy):
        return 1.5 * identity - 0.5 * zy

    first = factor_of(current)
    put(y_high, y_low, current)
    put(f_high, f_low, first)
    put(z_high, z_low, first)
    put(y_high, y_low, product(y_high[...], y_low[...], f_high[...], f_low[...]))

    def step(_, carry):
        zy = product(z_high[...], z_low[...], y_high[...], y_low[...])
        put(f_high, f_low, factor_of(zy))
        put(y_high, y_low, product(y_high[...], y_low[...], f_high[...], f_low[...]))
        put(z_high, z_low, product(f_high[...], f_low[...], z_high[...], z_low[...]))
        return carry

    lax.fori_loop(1, NS_STEPS - 1, step, 0)
    zy = product(z_high[...], z_low[...], y_high[...], y_low[...])
    put(f_high, f_low, factor_of(zy))
    root = product(f_high[...], f_low[...], z_high[...], z_low[...]) / jnp.sqrt(frobenius)

    drive_col = jnp.sum(jnp.where(diagonal, drive, 0.0), axis=1, keepdims=True)
    inner = jnp.sum(root * drive_col, axis=0, keepdims=True)
    mean_weight = jnp.sum(root * inner, axis=1, keepdims=True) / (members - 1.0)
    blended_ref[...] = (root + mean_weight).astype(BF16)


def patch_weights(rows, info):
    sources, cap, members = rows.shape
    half = pltpu.VMEM((members, members), BF16)
    return pl.pallas_call(
        weights_kernel,
        out_shape=jax.ShapeDtypeStruct((members, members), BF16),
        scratch_shapes=[half] * 6,
        compiler_params=pltpu.CompilerParams(vmem_limit_bytes=VMEM_BYTES),
        cost_estimate=pl.CostEstimate(
            flops=2 * members * members * (sources * cap + 45 * members),
            bytes_accessed=2 * sources * cap * members,
            transcendentals=0,
        ),
        name="patch_weights",
    )(rows, info)


def local(
    background_states,
    measurement_anomaly_matrix,
    departure_vector,
    measurement_precision,
    measurement_region_targets,
    localization_factor_scaled,
    bootstrap_multiplicity,
):
    device_count = lax.axis_size("space")
    local_rows = measurement_anomaly_matrix.shape[0]
    targets_per = measurement_region_targets.shape[1]
    slot_cap = 2 * targets_per * local_rows // device_count
    slots, info = pack(
        measurement_region_targets,
        localization_factor_scaled,
        bootstrap_multiplicity,
        measurement_precision,
        departure_vector,
        measurement_anomaly_matrix,
        device_count,
        slot_cap,
    )
    info_got = lax.all_gather(info, "space", axis=0, tiled=False)
    rows_got = lax.all_to_all(slots, "space", split_axis=0, concat_axis=0, tiled=True)
    background = lax.all_to_all(
        background_states, "space", split_axis=1, concat_axis=0, tiled=True
    )
    blended = patch_weights(rows_got, info_got)
    centre = jnp.mean(background.astype(F32), axis=0)
    perturb = (background.astype(F32) - centre[None, :]).astype(BF16)
    update = lax.dot_general(
        blended, perturb, (((0,), (0,)), ((), ())), preferred_element_type=F32
    )
    analysis = (centre[None, :] + update).astype(BF16)
    return lax.all_to_all(analysis, "space", split_axis=0, concat_axis=1, tiled=True)


def solution(mesh):
    in_specs = (
        P("space", None),
        P("space", None),
        P("space"),
        P("space"),
        P("space", None),
        P("space", None),
        P(("boot", "space")),
    )
    out_specs = P(("boot", "space"), None)
    return jax.shard_map(local, mesh=mesh, in_specs=in_specs, out_specs=out_specs, check_vma=False)
```

```python
import functools

import jax
import jax.numpy as jnp
from jax import lax
from jax.experimental import pallas as pl
from jax.experimental.pallas import tpu as pltpu
from jax.sharding import PartitionSpec as P

NS_STEPS = 6
LANES = 128
TAIL = 8
VMEM_BYTES = 48 * 1024 * 1024
F32 = jnp.float32
BF16 = jnp.bfloat16


def pack_kernel(*refs):
    sources, slots_ref, fetched, info_ref, sems = refs[:6], refs[6], refs[7:13], refs[13], refs[14]
    copies = [
        pltpu.make_async_copy(source, target, sems.at[i])
        for i, (source, target) in enumerate(zip(sources, fetched))
    ]
    for copy in copies:
        copy.start()
    for copy in copies:
        copy.wait()
    targets_ref, local_ref, mult_ref, prec_ref, dep_ref, rows_ref = fetched
    patches = slots_ref.shape[0]
    cap = slots_ref.shape[1] - TAIL
    count, members = rows_ref.shape
    mult = mult_ref[...].reshape(1, count).astype(F32)
    prec = prec_ref[...].reshape(1, count)
    weight = local_ref[...].astype(F32) / 1024.0 * (mult * prec)
    weight = weight.astype(BF16).astype(F32)
    dep = dep_ref[...].astype(F32).reshape(1, count)
    patch_id = lax.broadcasted_iota(jnp.int32, (patches, count), 0)
    first = patch_id == targets_ref[0:1, :]
    second = patch_id == targets_ref[1:2, :]
    named = jnp.logical_or(first, second)
    earlier = lax.broadcasted_iota(jnp.int32, (count, count), 0) < lax.broadcasted_iota(
        jnp.int32, (count, count), 1
    )
    rank = jnp.dot(
        named.astype(F32).astype(BF16), earlier.astype(F32).astype(BF16), preferred_element_type=F32
    )
    rank = jnp.where(named, rank, -1.0)
    by_patch = jnp.where(first, weight[0:1, :], jnp.where(second, weight[1:2, :], 0.0))
    slot_id = lax.broadcasted_iota(jnp.int32, (cap, count), 0).astype(F32)
    lane = lax.broadcasted_iota(jnp.int32, (cap, LANES), 1)
    info = jnp.zeros((cap, LANES), F32)
    rows = rows_ref[...]
    filled = []
    for patch in range(patches):
        pick = jnp.where(slot_id == rank[patch : patch + 1, :], 1.0, 0.0)
        weight_col = jnp.sum(pick * by_patch[patch : patch + 1, :], axis=1, keepdims=True)
        dep_col = jnp.sum(pick * dep, axis=1, keepdims=True)
        info = jnp.where(lane == patch, weight_col, info)
        info = jnp.where(lane == patches + patch, dep_col, info)
    info_ref[...] = jnp.zeros((LANES, LANES), F32)
    info_ref[0:cap, :] = info
    info = info_ref[...].T
    tail_id = lax.broadcasted_iota(jnp.int32, (TAIL, LANES), 0)
    blank = jnp.zeros((TAIL, members - LANES), F32)
    for patch in range(patches):
        pick = jnp.where(slot_id == rank[patch : patch + 1, :], 1.0, 0.0)
        block = jnp.dot(pick.astype(BF16), rows, preferred_element_type=F32)
        tail = jnp.where(
            tail_id == 0,
            info[patch : patch + 1, :],
            jnp.where(tail_id == 1, info[patches + patch : patches + patch + 1, :], 0.0),
        )
        tail = jnp.concatenate([tail, blank], axis=1)
        slots_ref[patch] = jnp.concatenate([block, tail], axis=0).astype(BF16)


def pack(targets, local, mult, prec, dep, rows, patches, cap):
    count, members = rows.shape
    operands = (targets.T, local.T, mult, prec, dep, rows)
    return pl.pallas_call(
        pack_kernel,
        out_shape=jax.ShapeDtypeStruct((patches, cap + TAIL, members), BF16),
        in_specs=[pl.BlockSpec(memory_space=pltpu.HBM)] * len(operands),
        scratch_shapes=[pltpu.VMEM(operand.shape, operand.dtype) for operand in operands]
        + [pltpu.VMEM((LANES, LANES), F32), pltpu.SemaphoreType.DMA((len(operands),))],
        compiler_params=pltpu.CompilerParams(vmem_limit_bytes=VMEM_BYTES),
        cost_estimate=pl.CostEstimate(
            flops=2 * patches * cap * count * members,
            bytes_accessed=2 * (patches * cap + count) * members,
            transcendentals=0,
        ),
        name="pack_rows",
    )(*operands)


def halves(value):
    high = value.astype(BF16)
    return high, (value - high.astype(F32)).astype(BF16)


def product(left_high, left_low, right_high, right_low):
    dot = functools.partial(jnp.dot, preferred_element_type=F32)
    return dot(left_high, right_high) + (dot(left_high, right_low) + dot(left_low, right_high))


def weights_kernel(rows_ref, blended_ref, info_ref, y_high, y_low, z_high, z_low, f_high, f_low):
    sources, depth, members = rows_ref.shape
    cap = depth - TAIL
    for source in range(sources):
        tail = rows_ref[source].astype(F32)[cap:depth, 0:LANES]
        info_ref[source : source + 1, :] = tail[0:1, :]
        info_ref[sources + source : sources + source + 1, :] = tail[1:2, :]
    info = info_ref[...].T[0:depth, :]
    real = lax.broadcasted_iota(jnp.int32, (depth, LANES), 0) < cap
    info = jnp.where(real, info, 0.0)
    gram = jnp.zeros((members, members), F32)
    drive = jnp.zeros((1, members), F32)
    for source in range(sources):
        weight_col = info[:, source : source + 1]
        dep_col = info[:, sources + source : sources + source + 1]
        rows = rows_ref[source]
        scaled = (weight_col * rows.astype(F32)).astype(BF16)
        gram += lax.dot_general(rows, scaled, (((0,), (0,)), ((), ())), preferred_element_type=F32)
        drive += jnp.sum(dep_col * scaled.astype(F32), axis=0, keepdims=True)

    row_id = lax.broadcasted_iota(jnp.int32, (members, members), 0)
    col_id = lax.broadcasted_iota(jnp.int32, (members, members), 1)
    diagonal = row_id == col_id
    identity = jnp.where(diagonal, 1.0, 0.0)
    shifted = identity + gram / (members - 1.0)
    squares = jnp.sum(jnp.sum(shifted * shifted, axis=0, keepdims=True), axis=1, keepdims=True)
    frobenius = jnp.sqrt(squares)
    current = shifted / frobenius

    def put(high_ref, low_ref, value):
        high_ref[...], low_ref[...] = halves(value)

    def factor_of(zy):
        return 1.5 * identity - 0.5 * zy

    first = factor_of(current)
    put(y_high, y_low, current)
    put(f_high, f_low, first)
    put(z_high, z_low, first)
    put(y_high, y_low, product(y_high[...], y_low[...], f_high[...], f_low[...]))

    def step(_, carry):
        zy = product(z_high[...], z_low[...], y_high[...], y_low[...])
        put(f_high, f_low, factor_of(zy))
        put(y_high, y_low, product(y_high[...], y_low[...], f_high[...], f_low[...]))
        put(z_high, z_low, product(f_high[...], f_low[...], z_high[...], z_low[...]))
        return carry

    lax.fori_loop(1, NS_STEPS - 1, step, 0)
    zy = product(z_high[...], z_low[...], y_high[...], y_low[...])
    put(f_high, f_low, factor_of(zy))
    root = product(f_high[...], f_low[...], z_high[...], z_low[...]) / jnp.sqrt(frobenius)

    drive_col = jnp.sum(jnp.where(diagonal, drive, 0.0), axis=1, keepdims=True)
    inner = jnp.sum(root * drive_col, axis=0, keepdims=True)
    inner_col = jnp.sum(jnp.where(diagonal, inner, 0.0), axis=1, keepdims=True)
    mean_weight = jnp.sum(root * inner_col, axis=0, keepdims=True) / (members - 1.0)
    blended_ref[...] = (root + mean_weight).astype(BF16)


def patch_weights(rows):
    sources, depth, members = rows.shape
    half = pltpu.VMEM((members, members), BF16)
    return pl.pallas_call(
        weights_kernel,
        out_shape=jax.ShapeDtypeStruct((members, members), BF16),
        scratch_shapes=[pltpu.VMEM((LANES, LANES), F32)] + [half] * 6,
        compiler_params=pltpu.CompilerParams(vmem_limit_bytes=VMEM_BYTES),
        cost_estimate=pl.CostEstimate(
            flops=2 * members * members * (sources * depth + 45 * members),
            bytes_accessed=2 * sources * depth * members,
            transcendentals=0,
        ),
        name="patch_weights",
    )(rows)


def update_kernel(blended_ref, background_ref, analysis_ref):
    background = background_ref[...].astype(F32)
    centre = jnp.sum(background, axis=0, keepdims=True) / background.shape[0]
    perturb = (background - centre).astype(BF16)
    update = jnp.dot(blended_ref[...], perturb, preferred_element_type=F32)
    analysis_ref[...] = (centre + update).astype(BF16)


def update_points(blended, background):
    members, points = background.shape
    tile = min(points, 256)
    return pl.pallas_call(
        update_kernel,
        grid=(points // tile,),
        in_specs=[
            pl.BlockSpec((members, members), lambda i: (0, 0)),
            pl.BlockSpec((members, tile), lambda i: (0, i)),
        ],
        out_specs=pl.BlockSpec((members, tile), lambda i: (0, i)),
        out_shape=jax.ShapeDtypeStruct((members, points), BF16),
        compiler_params=pltpu.CompilerParams(vmem_limit_bytes=VMEM_BYTES),
        cost_estimate=pl.CostEstimate(
            flops=2 * members * members * points,
            bytes_accessed=4 * members * points + 2 * members * members,
            transcendentals=0,
        ),
        name="update_points",
    )(blended, background)


def share_columns(turn, share):
    groups = lax.axis_size("boot")
    return lax.rem(lax.axis_index("boot") + turn, groups) * share


def run_copies(copies):
    for copy in copies:
        copy.start()
    for copy in copies:
        copy.wait()


def cut_kernel(states_ref, cut_ref, sems):
    patches, _, share = cut_ref.shape
    region = states_ref.shape[1] // patches
    begin = share_columns(0, share)
    run_copies(
        [
            pltpu.make_async_copy(
                states_ref.at[:, pl.ds(pl.multiple_of(patch * region + begin, LANES), share)],
                cut_ref.at[patch],
                sems.at[patch],
            )
            for patch in range(patches)
        ]
    )


def cut_share(states, patches, share):
    own_members = states.shape[0]
    return pl.pallas_call(
        cut_kernel,
        in_specs=[pl.BlockSpec(memory_space=pltpu.HBM)],
        out_specs=pl.BlockSpec(memory_space=pl.ANY),
        out_shape=jax.ShapeDtypeStruct((patches, own_members, share), BF16),
        scratch_shapes=[pltpu.SemaphoreType.DMA((patches,))],
        cost_estimate=pl.CostEstimate(
            flops=0, bytes_accessed=4 * patches * own_members * share, transcendentals=0
        ),
        name="cut_share",
    )(states)


def place_kernel(turn, piece_ref, *refs):
    whole_ref, sems = refs[-2:]
    patches, _, share = piece_ref.shape
    region = whole_ref.shape[1] // patches
    begin = share_columns(turn, share)
    run_copies(
        [
            pltpu.make_async_copy(
                piece_ref.at[patch],
                whole_ref.at[:, pl.ds(pl.multiple_of(patch * region + begin, LANES), share)],
                sems.at[patch],
            )
            for patch in range(patches)
        ]
    )


def place_piece(turn, piece, whole, points):
    patches, own_members, share = piece.shape
    operands = (piece,) if whole is None else (piece, whole)
    return pl.pallas_call(
        functools.partial(place_kernel, turn),
        in_specs=[pl.BlockSpec(memory_space=pl.ANY)] * len(operands),
        out_specs=pl.BlockSpec(memory_space=pl.ANY),
        out_shape=jax.ShapeDtypeStruct((own_members, points), BF16),
        input_output_aliases={} if whole is None else {1: 0},
        scratch_shapes=[pltpu.SemaphoreType.DMA((patches,))],
        cost_estimate=pl.CostEstimate(
            flops=0, bytes_accessed=4 * patches * own_members * share, transcendentals=0
        ),
        name="place_piece",
    )(*operands)


def local(
    background_states,
    measurement_anomaly_matrix,
    departure_vector,
    measurement_precision,
    measurement_region_targets,
    localization_factor_scaled,
    bootstrap_multiplicity,
):
    device_count = lax.axis_size("space")
    groups = lax.axis_size("boot")
    local_rows = measurement_anomaly_matrix.shape[0]
    targets_per = measurement_region_targets.shape[1]
    slot_cap = 2 * targets_per * local_rows // device_count
    own_members, points = background_states.shape
    members = own_members * device_count
    region = points // device_count
    share = region // groups
    slots = pack(
        measurement_region_targets,
        localization_factor_scaled,
        bootstrap_multiplicity,
        measurement_precision,
        departure_vector,
        measurement_anomaly_matrix,
        device_count,
        slot_cap,
    )
    rows_got = lax.all_to_all(slots, "space", split_axis=0, concat_axis=0, tiled=True)

    own_share = cut_share(background_states, device_count, share)
    rows_got, own_share = lax.optimization_barrier((rows_got, own_share))
    own_share = lax.all_to_all(own_share, "space", split_axis=0, concat_axis=0, tiled=True)
    own_share = own_share.reshape(members, share)
    shares = [own_share]
    for turn in range(1, groups):
        shares.append(
            lax.ppermute(own_share, "boot", [(g, (g - turn) % groups) for g in range(groups)])
        )

    blended = patch_weights(rows_got)
    whole = None
    for turn, part in enumerate(shares):
        analysis = update_points(blended, part).reshape(device_count, own_members, share)
        piece = lax.all_to_all(analysis, "space", split_axis=0, concat_axis=0, tiled=True)
        whole = place_piece(turn, piece, whole, points)
    return whole


def solution(mesh):
    in_specs = (
        P("space", None),
        P("space", None),
        P("space"),
        P("space"),
        P("space", None),
        P("space", None),
        P(("boot", "space")),
    )
    out_specs = P(("boot", "space"), None)
    return jax.shard_map(local, mesh=mesh, in_specs=in_specs, out_specs=out_specs, check_vma=False)
```

```python
import functools

import jax
import jax.numpy as jnp
from jax import lax
from jax.experimental import pallas as pl
from jax.experimental.pallas import tpu as pltpu
from jax.sharding import PartitionSpec as P

NS_STEPS = 6
LANES = 128
TAIL = 8
MOST_PERMUTES = 16
VMEM_BYTES = 48 * 1024 * 1024
F32 = jnp.float32
BF16 = jnp.bfloat16


def pack_kernel(*refs):
    sources, refs = refs[:6], refs[6:]
    fetched, info_ref, rank_ref, sems = refs[-9:-3], refs[-3], refs[-2], refs[-1]
    slots_refs = refs[:-9]
    copies = [
        pltpu.make_async_copy(source, target, sems.at[i])
        for i, (source, target) in enumerate(zip(sources, fetched))
    ]
    for copy in copies:
        copy.start()
    for copy in copies:
        copy.wait()
    targets_ref, local_ref, mult_ref, prec_ref, dep_ref, rows_ref = fetched
    patches = len(slots_refs)
    cap = slots_refs[0].shape[0] - TAIL
    count, members = rows_ref.shape
    me = lax.axis_index("space")
    mult = mult_ref[...].reshape(1, count).astype(F32)
    prec = prec_ref[...].reshape(1, count)
    weight = local_ref[...].astype(F32) / 1024.0 * (mult * prec)
    weight = weight.astype(BF16).astype(F32)
    dep = dep_ref[...].astype(F32).reshape(1, count)
    patch_id = lax.broadcasted_iota(jnp.int32, (patches, count), 0)
    first = patch_id == targets_ref[0:1, :]
    second = patch_id == targets_ref[1:2, :]
    named = jnp.logical_or(first, second)
    earlier = lax.broadcasted_iota(jnp.int32, (count, count), 0) < lax.broadcasted_iota(
        jnp.int32, (count, count), 1
    )
    rank = jnp.dot(
        named.astype(F32).astype(BF16), earlier.astype(F32).astype(BF16), preferred_element_type=F32
    )
    rank = jnp.where(named, rank, -1.0)
    by_patch = jnp.where(first, weight[0:1, :], jnp.where(second, weight[1:2, :], 0.0))
    slot_id = lax.broadcasted_iota(jnp.int32, (cap, count), 0).astype(F32)
    lane = lax.broadcasted_iota(jnp.int32, (cap, LANES), 1)
    info = jnp.zeros((cap, LANES), F32)
    rows = rows_ref[...]
    for patch in range(patches):
        pick = jnp.where(slot_id == rank[patch : patch + 1, :], 1.0, 0.0)
        weight_col = jnp.sum(pick * by_patch[patch : patch + 1, :], axis=1, keepdims=True)
        dep_col = jnp.sum(pick * dep, axis=1, keepdims=True)
        info = jnp.where(lane == patch, weight_col, info)
        info = jnp.where(lane == patches + patch, dep_col, info)
    info_ref[...] = jnp.zeros((LANES, LANES), F32)
    info_ref[0:cap, :] = info
    info_ref[...] = info_ref[...].T
    rank_ref[...] = rank
    tail_id = lax.broadcasted_iota(jnp.int32, (TAIL, LANES), 0)
    blank = jnp.zeros((TAIL, members - LANES), F32)
    for turn, slots_ref in enumerate(slots_refs):
        patch = me ^ turn
        pick = jnp.where(slot_id == rank_ref[pl.ds(patch, 1), :], 1.0, 0.0)
        block = jnp.dot(pick.astype(BF16), rows, preferred_element_type=F32)
        tail = jnp.where(
            tail_id == 0,
            info_ref[pl.ds(patch, 1), :],
            jnp.where(tail_id == 1, info_ref[pl.ds(patches + patch, 1), :], 0.0),
        )
        tail = jnp.concatenate([tail, blank], axis=1)
        slots_ref[...] = jnp.concatenate([block, tail], axis=0).astype(BF16)


def pack(targets, local, mult, prec, dep, rows, patches, cap):
    count, members = rows.shape
    operands = (targets.T, local.T, mult, prec, dep, rows)
    return pl.pallas_call(
        pack_kernel,
        out_shape=[jax.ShapeDtypeStruct((cap + TAIL, members), BF16)] * patches,
        in_specs=[pl.BlockSpec(memory_space=pltpu.HBM)] * len(operands),
        scratch_shapes=[pltpu.VMEM(operand.shape, operand.dtype) for operand in operands]
        + [
            pltpu.VMEM((LANES, LANES), F32),
            pltpu.VMEM((patches, count), F32),
            pltpu.SemaphoreType.DMA((len(operands),)),
        ],
        compiler_params=pltpu.CompilerParams(vmem_limit_bytes=VMEM_BYTES),
        cost_estimate=pl.CostEstimate(
            flops=2 * patches * cap * count * members,
            bytes_accessed=2 * (patches * cap + count) * members,
            transcendentals=0,
        ),
        name="pack_rows",
    )(*operands)


def halves(value):
    high = value.astype(BF16)
    return high, (value - high.astype(F32)).astype(BF16)


def product(left_high, left_low, right_high, right_low):
    dot = functools.partial(jnp.dot, preferred_element_type=F32)
    return dot(left_high, right_high) + (dot(left_high, right_low) + dot(left_low, right_high))


def weights_kernel(*refs):
    rows_refs, blended_ref, info_ref = refs[:-8], refs[-8], refs[-7]
    y_high, y_low, z_high, z_low, f_high, f_low = refs[-6:]
    sources = len(rows_refs)
    depth, members = rows_refs[0].shape
    cap = depth - TAIL
    for source in range(sources):
        tail = rows_refs[source][...].astype(F32)[cap:depth, 0:LANES]
        info_ref[source : source + 1, :] = tail[0:1, :]
        info_ref[sources + source : sources + source + 1, :] = tail[1:2, :]
    info = info_ref[...].T[0:depth, :]
    real = lax.broadcasted_iota(jnp.int32, (depth, LANES), 0) < cap
    info = jnp.where(real, info, 0.0)
    gram = jnp.zeros((members, members), F32)
    drive = jnp.zeros((1, members), F32)
    for source in range(sources):
        weight_col = info[:, source : source + 1]
        dep_col = info[:, sources + source : sources + source + 1]
        rows = rows_refs[source][...]
        scaled = (weight_col * rows.astype(F32)).astype(BF16)
        gram += lax.dot_general(rows, scaled, (((0,), (0,)), ((), ())), preferred_element_type=F32)
        drive += jnp.sum(dep_col * scaled.astype(F32), axis=0, keepdims=True)

    row_id = lax.broadcasted_iota(jnp.int32, (members, members), 0)
    col_id = lax.broadcasted_iota(jnp.int32, (members, members), 1)
    diagonal = row_id == col_id
    identity = jnp.where(diagonal, 1.0, 0.0)
    shifted = identity + gram / (members - 1.0)
    squares = jnp.sum(jnp.sum(shifted * shifted, axis=0, keepdims=True), axis=1, keepdims=True)
    frobenius = jnp.sqrt(squares)
    current = shifted / frobenius

    def put(high_ref, low_ref, value):
        high_ref[...], low_ref[...] = halves(value)

    def factor_of(zy):
        return 1.5 * identity - 0.5 * zy

    first = factor_of(current)
    put(y_high, y_low, current)
    put(f_high, f_low, first)
    put(z_high, z_low, first)
    put(y_high, y_low, product(y_high[...], y_low[...], f_high[...], f_low[...]))

    def step(_, carry):
        zy = product(z_high[...], z_low[...], y_high[...], y_low[...])
        put(f_high, f_low, factor_of(zy))
        put(y_high, y_low, product(y_high[...], y_low[...], f_high[...], f_low[...]))
        put(z_high, z_low, product(f_high[...], f_low[...], z_high[...], z_low[...]))
        return carry

    lax.fori_loop(1, NS_STEPS - 1, step, 0)
    zy = product(z_high[...], z_low[...], y_high[...], y_low[...])
    put(f_high, f_low, factor_of(zy))
    root = product(f_high[...], f_low[...], z_high[...], z_low[...]) / jnp.sqrt(frobenius)

    drive_col = jnp.sum(jnp.where(diagonal, drive, 0.0), axis=1, keepdims=True)
    inner = jnp.sum(root * drive_col, axis=0, keepdims=True)
    inner_col = jnp.sum(jnp.where(diagonal, inner, 0.0), axis=1, keepdims=True)
    mean_weight = jnp.sum(root * inner_col, axis=0, keepdims=True) / (members - 1.0)
    blended_ref[...] = (root + mean_weight).astype(BF16)


def patch_weights(rows):
    sources = len(rows)
    depth, members = rows[0].shape
    half = pltpu.VMEM((members, members), BF16)
    return pl.pallas_call(
        weights_kernel,
        out_shape=jax.ShapeDtypeStruct((members, members), BF16),
        scratch_shapes=[pltpu.VMEM((LANES, LANES), F32)] + [half] * 6,
        compiler_params=pltpu.CompilerParams(vmem_limit_bytes=VMEM_BYTES),
        cost_estimate=pl.CostEstimate(
            flops=2 * members * members * (sources * depth + 45 * members),
            bytes_accessed=2 * sources * depth * members,
            transcendentals=0,
        ),
        name="patch_weights",
    )(*rows)


def update_kernel(blended_ref, background_ref, *refs):
    analysis_refs, whole_ref = refs[:-1], refs[-1]
    me = lax.axis_index("space")
    rows = analysis_refs[0].shape[0]
    members, points = background_ref.shape
    tile = min(points, 256)
    for begin in range(0, points, tile):
        columns = slice(begin, begin + tile)
        background = background_ref[:, columns].astype(F32)
        centre = jnp.sum(background, axis=0, keepdims=True) / members
        perturb = (background - centre).astype(BF16)
        update = jnp.dot(blended_ref[...], perturb, preferred_element_type=F32)
        whole_ref[:, columns] = centre + update
    for turn, analysis_ref in enumerate(analysis_refs):
        begin = pl.multiple_of((me ^ turn) * rows, rows)
        analysis_ref[...] = whole_ref[pl.ds(begin, rows), :].astype(BF16)


def update_points(blended, background, holders):
    members, points = background.shape
    return pl.pallas_call(
        update_kernel,
        out_shape=[jax.ShapeDtypeStruct((members // holders, points), BF16)] * holders,
        scratch_shapes=[pltpu.VMEM((members, points), F32)],
        compiler_params=pltpu.CompilerParams(vmem_limit_bytes=VMEM_BYTES),
        cost_estimate=pl.CostEstimate(
            flops=2 * members * members * points,
            bytes_accessed=4 * members * points + 2 * members * members,
            transcendentals=0,
        ),
        name="update_points",
    )(blended, background)


def cut_kernel(states_ref, *cut_refs):
    me = lax.axis_index("space")
    share = cut_refs[0].shape[1]
    region = states_ref.shape[1] // len(cut_refs)
    offset = lax.axis_index("boot") * share
    for turn, cut_ref in enumerate(cut_refs):
        begin = pl.multiple_of((me ^ turn) * region + offset, LANES)
        cut_ref[...] = states_ref[:, pl.ds(begin, share)]


def cut_share(states, patches, share):
    own_members = states.shape[0]
    return pl.pallas_call(
        cut_kernel,
        out_shape=[jax.ShapeDtypeStruct((own_members, share), BF16)] * patches,
        compiler_params=pltpu.CompilerParams(vmem_limit_bytes=VMEM_BYTES),
        cost_estimate=pl.CostEstimate(
            flops=0, bytes_accessed=4 * patches * own_members * share, transcendentals=0
        ),
        name="cut_share",
    )(states)


def join_kernel(*refs):
    piece_refs, joined_ref, whole_ref = refs[:-2], refs[-2], refs[-1]
    me = lax.axis_index("space")
    rows = piece_refs[0].shape[0]
    for turn, piece_ref in enumerate(piece_refs):
        begin = pl.multiple_of((me ^ turn) * rows, rows)
        whole_ref[pl.ds(begin, rows), :] = piece_ref[...].astype(F32)
    joined_ref[...] = whole_ref[...].astype(BF16)


def join_members(pieces):
    rows, share = pieces[0].shape
    members = rows * len(pieces)
    return pl.pallas_call(
        join_kernel,
        out_shape=jax.ShapeDtypeStruct((members, share), BF16),
        scratch_shapes=[pltpu.VMEM((members, share), F32)],
        compiler_params=pltpu.CompilerParams(vmem_limit_bytes=VMEM_BYTES),
        cost_estimate=pl.CostEstimate(
            flops=0, bytes_accessed=4 * members * share, transcendentals=0
        ),
        name="join_members",
    )(*pieces)


def place_kernel(groups, *refs):
    piece_refs, whole_ref = refs[:-1], refs[-1]
    patches = len(piece_refs) // groups
    share = piece_refs[0].shape[1]
    me, group = lax.axis_index("space"), lax.axis_index("boot")
    for place, piece_ref in enumerate(piece_refs):
        shift, turn = divmod(place, patches)
        offset = lax.rem(group + shift, groups) * share
        begin = pl.multiple_of((me ^ turn) * groups * share + offset, LANES)
        whole_ref[:, pl.ds(begin, share)] = piece_ref[...]


def place_pieces(pieces, groups):
    own_members, share = pieces[0].shape
    points = share * len(pieces)
    return pl.pallas_call(
        functools.partial(place_kernel, groups),
        out_shape=jax.ShapeDtypeStruct((own_members, points), BF16),
        compiler_params=pltpu.CompilerParams(vmem_limit_bytes=VMEM_BYTES),
        cost_estimate=pl.CostEstimate(
            flops=0, bytes_accessed=4 * own_members * points, transcendentals=0
        ),
        name="place_pieces",
    )(*pieces)


def swap(pieces):
    devices = len(pieces)
    if devices > MOST_PERMUTES:
        order = lax.axis_index("space") ^ jnp.arange(devices, dtype=jnp.int32)
        stacked = jnp.stack(pieces)[order]
        stacked = lax.all_to_all(stacked, "space", split_axis=0, concat_axis=0, tiled=True)[order]
        return [stacked[turn] for turn in range(devices)]
    return [pieces[0]] + [
        lax.ppermute(pieces[turn], "space", [(d, d ^ turn) for d in range(devices)])
        for turn in range(1, devices)
    ]


def local(
    background_states,
    measurement_anomaly_matrix,
    departure_vector,
    measurement_precision,
    measurement_region_targets,
    localization_factor_scaled,
    bootstrap_multiplicity,
):
    device_count = lax.axis_size("space")
    groups = lax.axis_size("boot")
    local_rows = measurement_anomaly_matrix.shape[0]
    targets_per = measurement_region_targets.shape[1]
    slot_cap = 2 * targets_per * local_rows // device_count
    own_members, points = background_states.shape
    region = points // device_count
    share = region // groups
    slots = pack(
        measurement_region_targets,
        localization_factor_scaled,
        bootstrap_multiplicity,
        measurement_precision,
        departure_vector,
        measurement_anomaly_matrix,
        device_count,
        slot_cap,
    )
    cuts = cut_share(background_states, device_count, share)
    rows_got = swap(slots)
    middle = 5 * device_count // 8
    rows_got[middle], cuts = lax.optimization_barrier((rows_got[middle], cuts))
    own_share = join_members(swap(cuts))
    shares = [own_share]
    for turn in range(1, groups):
        shares.append(
            lax.ppermute(own_share, "boot", [(g, (g - turn) % groups) for g in range(groups)])
        )

    blended = patch_weights(rows_got)
    pieces = []
    for part in shares:
        pieces += swap(update_points(blended, part, device_count))
    return place_pieces(pieces, groups)


def solution(mesh):
    in_specs = (
        P("space", None),
        P("space", None),
        P("space"),
        P("space"),
        P("space", None),
        P("space", None),
        P(("boot", "space")),
    )
    out_specs = P(("boot", "space"), None)
    return jax.shard_map(local, mesh=mesh, in_specs=in_specs, out_specs=out_specs, check_vma=False)
```

```python
import functools

import jax
import jax.numpy as jnp
from jax import lax
from jax.experimental import pallas as pl
from jax.experimental.pallas import tpu as pltpu
from jax.sharding import PartitionSpec as P

NS_STEPS = 6
LANES = 128
TAIL = 8
FULL_STEPS = 2
VMEM_BYTES = 48 * 1024 * 1024
ALL_VMEM_BYTES = 64 * 1024 * 1024
F32 = jnp.float32
BF16 = jnp.bfloat16


def pack_kernel(groups, *refs):
    sources, slots_ref, fetched = refs[:6], refs[6], refs[7:13]
    info_ref, sems = refs[13:]
    run_copies(
        [
            pltpu.make_async_copy(source, target, sems.at[i])
            for i, (source, target) in enumerate(zip(sources, fetched))
        ]
    )
    targets_ref, local_ref, mult_ref, prec_ref, dep_ref, rows_ref = fetched
    patches, depth, members = slots_ref.shape
    share = depth - TAIL
    count = rows_ref.shape[0]
    mult = mult_ref[...].reshape(1, count).astype(F32)
    prec = prec_ref[...].reshape(1, count)
    weight = local_ref[...].astype(F32) / 1024.0 * (mult * prec)
    weight = weight.astype(BF16).astype(F32)
    dep = dep_ref[...].astype(F32).reshape(1, count)
    patch_id = lax.broadcasted_iota(jnp.int32, (patches, count), 0)
    first = patch_id == targets_ref[0:1, :]
    second = patch_id == targets_ref[1:2, :]
    named = jnp.logical_or(first, second)
    earlier = lax.broadcasted_iota(jnp.int32, (count, count), 0) < lax.broadcasted_iota(
        jnp.int32, (count, count), 1
    )
    rank = jnp.dot(
        named.astype(F32).astype(BF16), earlier.astype(F32).astype(BF16), preferred_element_type=F32
    )
    rank = jnp.where(named, rank, -1.0)
    by_patch = jnp.where(first, weight[0:1, :], jnp.where(second, weight[1:2, :], 0.0))
    slot_id = lax.broadcasted_iota(jnp.int32, (groups * share, count), 0).astype(F32)
    lane = lax.broadcasted_iota(jnp.int32, (groups * share, LANES), 1)
    info = jnp.zeros((groups * share, LANES), F32)
    for patch in range(patches):
        pick = slot_id == rank[patch : patch + 1, :]
        weight_col = jnp.sum(
            jnp.where(pick, by_patch[patch : patch + 1, :], 0.0), axis=1, keepdims=True
        )
        dep_col = jnp.sum(jnp.where(pick, dep, 0.0), axis=1, keepdims=True)
        info = jnp.where(lane == patch, weight_col, info)
        info = jnp.where(lane == patches + patch, dep_col, info)
    info_ref[...] = jnp.zeros((LANES, LANES), F32)
    info_ref[0 : groups * share, :] = info
    info = info_ref[...].T
    begin = lax.axis_index("boot") * share
    own_id = (lax.broadcasted_iota(jnp.int32, (share, count), 0) + begin).astype(F32)
    tail_id = lax.broadcasted_iota(jnp.int32, (TAIL, LANES), 0)
    blank = jnp.zeros((TAIL, members - LANES), F32)
    rows = rows_ref[...]
    for patch in range(patches):
        pick = jnp.where(own_id == rank[patch : patch + 1, :], 1.0, 0.0)
        block = jnp.dot(pick.astype(BF16), rows, preferred_element_type=F32)
        tail = jnp.where(
            tail_id == 0,
            info[patch : patch + 1, :],
            jnp.where(tail_id == 1, info[patches + patch : patches + patch + 1, :], 0.0),
        )
        tail = jnp.concatenate([tail, blank], axis=1)
        slots_ref[patch] = jnp.concatenate([block, tail], axis=0).astype(BF16)


def run_copies(copies):
    for copy in copies:
        copy.start()
    for copy in copies:
        copy.wait()


def pack(targets, local, mult, prec, dep, rows, patches, share, groups):
    count, members = rows.shape
    operands = (targets.T, local.T, mult, prec, dep, rows)
    return pl.pallas_call(
        functools.partial(pack_kernel, groups),
        out_shape=jax.ShapeDtypeStruct((patches, share + TAIL, members), BF16),
        in_specs=[pl.BlockSpec(memory_space=pl.ANY)] * len(operands),
        scratch_shapes=[pltpu.VMEM(operand.shape, operand.dtype) for operand in operands]
        + [pltpu.VMEM((LANES, LANES), F32), pltpu.SemaphoreType.DMA((len(operands),))],
        compiler_params=pltpu.CompilerParams(vmem_limit_bytes=ALL_VMEM_BYTES),
        cost_estimate=pl.CostEstimate(
            flops=2 * patches * share * count * members,
            bytes_accessed=2 * (patches * share + count) * members,
            transcendentals=0,
        ),
        name="pack_rows",
    )(*operands)


def halves(value):
    high = value.astype(BF16)
    return high, (value - high.astype(F32)).astype(BF16)


def product(left_high, left_low, right_high, right_low):
    dot = functools.partial(jnp.dot, preferred_element_type=F32)
    return dot(left_high, right_high) + (dot(left_high, right_low) + dot(left_low, right_high))


def weights_kernel(*refs):
    rows_refs, blended_ref, info_ref = refs[:-10], refs[-10], refs[-9]
    y_ref, z_ref, y_high, y_low, z_high, z_low, w_high, w_low = refs[-8:]
    groups = len(rows_refs)
    sources, depth, members = rows_refs[0].shape
    share = depth - TAIL
    for source in range(sources):
        tail = rows_refs[0][source].astype(F32)[share:depth, 0:LANES]
        info_ref[source : source + 1, :] = tail[0:1, :]
        info_ref[sources + source : sources + source + 1, :] = tail[1:2, :]
    info_ref[...] = info_ref[...].T
    gram = jnp.zeros((members, members), F32)
    drive = jnp.zeros((1, members), F32)
    for turn, rows_ref in enumerate(rows_refs):
        begin = lax.rem(lax.axis_index("boot") + turn, groups) * share
        info = info_ref[pl.ds(pl.multiple_of(begin, 8), share), :]
        rows, scaled = [], []
        for source in range(sources):
            block = rows_ref[source].astype(F32)[0:share, :]
            rows.append(block)
            block = (info[:, source : source + 1] * block).astype(BF16).astype(F32)
            scaled.append(block)
            dep_col = info[:, sources + source : sources + source + 1]
            drive += jnp.sum(dep_col * block, axis=0, keepdims=True)
        gram += lax.dot_general(
            jnp.concatenate(rows, axis=0).astype(BF16),
            jnp.concatenate(scaled, axis=0).astype(BF16),
            (((0,), (0,)), ((), ())),
            preferred_element_type=F32,
        )

    row_id = lax.broadcasted_iota(jnp.int32, (members, members), 0)
    col_id = lax.broadcasted_iota(jnp.int32, (members, members), 1)
    diagonal = row_id == col_id
    identity = jnp.where(diagonal, 1.0, 0.0)
    shifted = identity + gram / (members - 1.0)
    squares = jnp.sum(jnp.sum(shifted * shifted, axis=0, keepdims=True), axis=1, keepdims=True)
    frobenius = jnp.sqrt(squares)
    dot = functools.partial(jnp.dot, preferred_element_type=F32)

    def put(high_ref, low_ref, value):
        high_ref[...], low_ref[...] = halves(value)

    def step(_, carry):
        w_high[...] = dot(z_high[...], y_high[...]).astype(BF16)
        current = 1.5 * y_ref[...] - 0.5 * dot(y_high[...], w_high[...])
        root = 1.5 * z_ref[...] - 0.5 * dot(w_high[...], z_high[...])
        y_ref[...], z_ref[...] = current, root
        y_high[...], z_high[...] = current.astype(BF16), root.astype(BF16)
        return carry

    current = shifted / frobenius
    y_high[...] = current.astype(BF16)
    root = 1.5 * identity - 0.5 * current
    current = 1.5 * current - 0.5 * dot(y_high[...], y_high[...])
    y_ref[...], z_ref[...] = current, root
    y_high[...], z_high[...] = current.astype(BF16), root.astype(BF16)
    lax.fori_loop(1, NS_STEPS - FULL_STEPS, step, 0)
    for full in range(FULL_STEPS):
        put(y_high, y_low, y_ref[...])
        put(z_high, z_low, z_ref[...])
        put(w_high, w_low, product(z_high[...], z_low[...], y_high[...], y_low[...]))
        if full < FULL_STEPS - 1:
            change = product(y_high[...], y_low[...], w_high[...], w_low[...])
            y_ref[...] = 1.5 * y_ref[...] - 0.5 * change
        change = product(w_high[...], w_low[...], z_high[...], z_low[...])
        z_ref[...] = 1.5 * z_ref[...] - 0.5 * change
    root = z_ref[...] / jnp.sqrt(frobenius)

    drive_col = jnp.sum(jnp.where(diagonal, drive, 0.0), axis=1, keepdims=True)
    inner = jnp.sum(root * drive_col, axis=0, keepdims=True)
    inner_col = jnp.sum(jnp.where(diagonal, inner, 0.0), axis=1, keepdims=True)
    mean_weight = jnp.sum(root * inner_col, axis=0, keepdims=True) / (members - 1.0)
    blended_ref[...] = (root + mean_weight).astype(BF16)


def patch_weights(rows):
    sources, depth, members = rows[0].shape
    whole = pltpu.VMEM((members, members), F32)
    half = pltpu.VMEM((members, members), BF16)
    return pl.pallas_call(
        weights_kernel,
        out_shape=jax.ShapeDtypeStruct((members, members), BF16),
        scratch_shapes=[pltpu.VMEM((LANES, LANES), F32)] + [whole] * 2 + [half] * 6,
        compiler_params=pltpu.CompilerParams(vmem_limit_bytes=VMEM_BYTES),
        cost_estimate=pl.CostEstimate(
            flops=2 * members * members * (len(rows) * sources * depth + 25 * members),
            bytes_accessed=2 * len(rows) * sources * depth * members,
            transcendentals=0,
        ),
        name="patch_weights",
    )(*rows)


def update_kernel(blended_ref, background_ref, analysis_ref):
    members, points = background_ref.shape
    tile = min(points, 256)
    for begin in range(0, points, tile):
        columns = slice(begin, begin + tile)
        background = background_ref[:, columns].astype(F32)
        centre = jnp.sum(background, axis=0, keepdims=True) / members
        perturb = (background - centre).astype(BF16)
        update = jnp.dot(blended_ref[...], perturb, preferred_element_type=F32)
        analysis_ref[:, columns] = (centre + update).astype(BF16)


def update_points(blended, background):
    members, points = background.shape
    return pl.pallas_call(
        update_kernel,
        out_shape=jax.ShapeDtypeStruct((members, points), BF16),
        compiler_params=pltpu.CompilerParams(vmem_limit_bytes=VMEM_BYTES),
        cost_estimate=pl.CostEstimate(
            flops=2 * members * members * points,
            bytes_accessed=4 * members * points + 2 * members * members,
            transcendentals=0,
        ),
        name="update_points",
    )(blended, background)


def cut_kernel(states_ref, cut_ref):
    patches, _, share = cut_ref.shape
    region = states_ref.shape[1] // patches
    offset = lax.axis_index("boot") * share
    for patch in range(patches):
        begin = pl.multiple_of(patch * region + offset, LANES)
        cut_ref[patch] = states_ref[:, pl.ds(begin, share)]


def cut_share(states, patches, share):
    own_members = states.shape[0]
    return pl.pallas_call(
        cut_kernel,
        out_shape=jax.ShapeDtypeStruct((patches, own_members, share), BF16),
        compiler_params=pltpu.CompilerParams(vmem_limit_bytes=VMEM_BYTES),
        cost_estimate=pl.CostEstimate(
            flops=0, bytes_accessed=4 * patches * own_members * share, transcendentals=0
        ),
        name="cut_share",
    )(states)


def place_kernel(*refs):
    piece_refs, whole_ref = refs[:-1], refs[-1]
    groups = len(piece_refs)
    patches, _, share = piece_refs[0].shape
    for turn, piece_ref in enumerate(piece_refs):
        offset = lax.rem(lax.axis_index("boot") + turn, groups) * share
        for patch in range(patches):
            begin = pl.multiple_of(patch * groups * share + offset, LANES)
            whole_ref[:, pl.ds(begin, share)] = piece_ref[patch]


def place_pieces(pieces):
    patches, own_members, share = pieces[0].shape
    points = patches * share * len(pieces)
    return pl.pallas_call(
        place_kernel,
        out_shape=jax.ShapeDtypeStruct((own_members, points), BF16),
        compiler_params=pltpu.CompilerParams(vmem_limit_bytes=VMEM_BYTES),
        cost_estimate=pl.CostEstimate(
            flops=0, bytes_accessed=4 * own_members * points, transcendentals=0
        ),
        name="place_pieces",
    )(*pieces)


def exchange(blocks):
    return lax.all_to_all(blocks, "space", split_axis=0, concat_axis=0, tiled=True)


def swap_shares(own):
    groups = lax.axis_size("boot")
    return [
        lax.ppermute(own, "boot", [(g, (g - turn) % groups) for g in range(groups)])
        for turn in range(1, groups)
    ]


def local(
    background_states,
    measurement_anomaly_matrix,
    departure_vector,
    measurement_precision,
    measurement_region_targets,
    localization_factor_scaled,
    bootstrap_multiplicity,
):
    device_count = lax.axis_size("space")
    groups = lax.axis_size("boot")
    local_rows = measurement_anomaly_matrix.shape[0]
    targets_per = measurement_region_targets.shape[1]
    slot_cap = 2 * targets_per * local_rows // device_count
    slot_share = -(-slot_cap // (8 * groups)) * 8
    own_members, points = background_states.shape
    share = points // device_count // groups

    slots = pack(
        measurement_region_targets,
        localization_factor_scaled,
        bootstrap_multiplicity,
        measurement_precision,
        departure_vector,
        measurement_anomaly_matrix,
        device_count,
        slot_share,
        groups,
    )
    own_rows = exchange(slots)
    rows = [own_rows] + swap_shares(own_rows[:, :slot_share])
    own_rows, background_states = lax.optimization_barrier((own_rows, background_states))
    own_points = exchange(cut_share(background_states, device_count, share))
    own_points = own_points.reshape(-1, share)
    background = [own_points] + swap_shares(own_points)

    blended = patch_weights(rows)
    pieces = []
    for part in background:
        analysis = update_points(blended, part).reshape(device_count, own_members, share)
        pieces.append(exchange(analysis))
    return place_pieces(pieces)


def solution(mesh):
    in_specs = (
        P("space", None),
        P("space", None),
        P("space"),
        P("space"),
        P("space", None),
        P("space", None),
        P(("boot", "space")),
    )
    out_specs = P(("boot", "space"), None)
    return jax.shard_map(local, mesh=mesh, in_specs=in_specs, out_specs=out_specs, check_vma=False)
```

```python
import functools

import jax
import jax.numpy as jnp
from jax import lax
from jax.experimental import pallas as pl
from jax.experimental.pallas import tpu as pltpu
from jax.sharding import PartitionSpec as P

NS_STEPS = 6
LANES = 128
ROWS = 8
FULL_STEPS = 1
VMEM_BYTES = 48 * 1024 * 1024
ALL_VMEM_BYTES = 64 * 1024 * 1024
F32 = jnp.float32
BF16 = jnp.bfloat16


def pack_kernel(groups, *refs):
    sources, slots_ref, fetched = refs[:6], refs[6], refs[7:13]
    info_ref, sems = refs[13:]
    run_copies(
        [
            pltpu.make_async_copy(source, target, sems.at[i])
            for i, (source, target) in enumerate(zip(sources, fetched))
        ]
    )
    targets_ref, local_ref, mult_ref, prec_ref, dep_ref, rows_ref = fetched
    patches = slots_ref.shape[0]
    count, members = rows_ref.shape
    share = (slots_ref.shape[2] - LANES) // members * ROWS
    mult = mult_ref[...].reshape(1, count).astype(F32)
    prec = prec_ref[...].reshape(1, count)
    weight = local_ref[...].astype(F32) / 1024.0 * (mult * prec)
    weight = weight.astype(BF16).astype(F32)
    dep = dep_ref[...].astype(F32).reshape(1, count)
    patch_id = lax.broadcasted_iota(jnp.int32, (patches, count), 0)
    first = patch_id == targets_ref[0:1, :]
    second = patch_id == targets_ref[1:2, :]
    named = jnp.logical_or(first, second)
    earlier = lax.broadcasted_iota(jnp.int32, (count, count), 0) < lax.broadcasted_iota(
        jnp.int32, (count, count), 1
    )
    rank = jnp.dot(
        named.astype(F32).astype(BF16), earlier.astype(F32).astype(BF16), preferred_element_type=F32
    )
    rank = jnp.where(named, rank, -1.0)
    by_patch = jnp.where(first, weight[0:1, :], jnp.where(second, weight[1:2, :], 0.0))
    slot_id = lax.broadcasted_iota(jnp.int32, (groups * share, count), 0).astype(F32)
    lane = lax.broadcasted_iota(jnp.int32, (groups * share, LANES), 1)
    info = jnp.zeros((groups * share, LANES), F32)
    for patch in range(patches):
        pick = slot_id == rank[patch : patch + 1, :]
        weight_col = jnp.sum(
            jnp.where(pick, by_patch[patch : patch + 1, :], 0.0), axis=1, keepdims=True
        )
        dep_col = jnp.sum(jnp.where(pick, dep, 0.0), axis=1, keepdims=True)
        info = jnp.where(lane == patch, weight_col, info)
        info = jnp.where(lane == patches + patch, dep_col, info)
    info_ref[...] = jnp.zeros((LANES, LANES), F32)
    info_ref[0 : groups * share, :] = info
    info = info_ref[...].T
    begin = lax.axis_index("boot") * share
    own_id = (lax.broadcasted_iota(jnp.int32, (share, count), 0) + begin).astype(F32)
    tail_id = lax.broadcasted_iota(jnp.int32, (ROWS, LANES), 0)
    picks = [
        jnp.where(own_id == rank[patch : patch + 1, :], 1.0, 0.0) for patch in range(patches)
    ]
    picked = jnp.dot(
        jnp.concatenate(picks, axis=0).astype(BF16), rows_ref[...], preferred_element_type=F32
    )
    for patch in range(patches):
        first = patch * share
        blocks = [picked[first + i : first + i + ROWS, :] for i in range(0, share, ROWS)]
        tail = jnp.where(
            tail_id == 0,
            info[patch : patch + 1, :],
            jnp.where(tail_id == 1, info[patches + patch : patches + patch + 1, :], 0.0),
        )
        slots_ref[patch] = jnp.concatenate(blocks + [tail], axis=1).astype(BF16)


def run_copies(copies):
    for copy in copies:
        copy.start()
    for copy in copies:
        copy.wait()


def pack(targets, local, mult, prec, dep, rows, patches, share, groups):
    count, members = rows.shape
    operands = (targets.T, local.T, mult, prec, dep, rows)
    return pl.pallas_call(
        functools.partial(pack_kernel, groups),
        out_shape=jax.ShapeDtypeStruct((patches, ROWS, share // ROWS * members + LANES), BF16),
        in_specs=[pl.BlockSpec(memory_space=pl.ANY)] * len(operands),
        scratch_shapes=[pltpu.VMEM(operand.shape, operand.dtype) for operand in operands]
        + [pltpu.VMEM((LANES, LANES), F32), pltpu.SemaphoreType.DMA((len(operands),))],
        compiler_params=pltpu.CompilerParams(vmem_limit_bytes=ALL_VMEM_BYTES),
        cost_estimate=pl.CostEstimate(
            flops=2 * patches * share * count * members,
            bytes_accessed=2 * (patches * share + count) * members,
            transcendentals=0,
        ),
        name="pack_rows",
    )(*operands)


def halves(value):
    high = value.astype(BF16)
    return high, (value - high.astype(F32)).astype(BF16)


def product(left_high, left_low, right_high, right_low):
    dot = functools.partial(jnp.dot, preferred_element_type=F32)
    return dot(left_high, right_high) + (dot(left_high, right_low) + dot(left_low, right_high))


def add_rows(rows_ref, info, gram, drive):
    sources = rows_ref.shape[0]
    members = gram.shape[0]
    share = info.shape[0]
    rows, scaled = [], []
    for source in range(sources):
        block = rows_ref[source].astype(F32)
        block = jnp.concatenate(
            [block[:, i * members : (i + 1) * members] for i in range(share // ROWS)], axis=0
        )
        rows.append(block)
        block = (info[:, source : source + 1] * block).astype(BF16).astype(F32)
        scaled.append(block)
        dep_col = info[:, sources + source : sources + source + 1]
        drive = drive + jnp.sum(dep_col * block, axis=0, keepdims=True)
    gram = gram + lax.dot_general(
        jnp.concatenate(rows, axis=0).astype(BF16),
        jnp.concatenate(scaled, axis=0).astype(BF16),
        (((0,), (0,)), ((), ())),
        preferred_element_type=F32,
    )
    return gram, drive


def gram_kernel(share, rows_ref, gram_ref, drive_ref, info_ref):
    sources, _, width = rows_ref.shape
    members = gram_ref.shape[0]
    for source in range(sources):
        tail = rows_ref[source].astype(F32)[:, width - LANES :]
        info_ref[source : source + 1, :] = tail[0:1, :]
        info_ref[sources + source : sources + source + 1, :] = tail[1:2, :]
    if 2 * sources < LANES:
        info_ref[2 * sources :, :] = jnp.zeros((LANES - 2 * sources, LANES), F32)
    info_ref[...] = info_ref[...].T
    begin = lax.axis_index("boot") * share
    info = info_ref[pl.ds(pl.multiple_of(begin, ROWS), share), :]
    gram, drive = add_rows(
        rows_ref, info, jnp.zeros((members, members), F32), jnp.zeros((1, members), F32)
    )
    gram_ref[...] = gram
    drive_ref[...] = drive


def own_gram(rows, share, members):
    sources, _, width = rows.shape
    return pl.pallas_call(
        functools.partial(gram_kernel, share),
        out_shape=(
            jax.ShapeDtypeStruct((members, members), F32),
            jax.ShapeDtypeStruct((1, members), F32),
            jax.ShapeDtypeStruct((LANES, LANES), F32),
        ),
        compiler_params=pltpu.CompilerParams(vmem_limit_bytes=VMEM_BYTES),
        cost_estimate=pl.CostEstimate(
            flops=4 * members * members * sources * share,
            bytes_accessed=2 * sources * ROWS * width,
            transcendentals=0,
        ),
        name="own_gram",
    )(rows)


def weights_kernel(share, *refs):
    gram_ref, drive_ref, info_ref = refs[:3]
    rows_refs, blended_ref = refs[3:-9], refs[-9]
    y_ref, z_ref, y_high, y_low, z_high, z_low, w_high, w_low = refs[-8:]
    groups = len(rows_refs) + 1
    members = gram_ref.shape[0]
    gram, drive = gram_ref[...], drive_ref[...]
    for turn, rows_ref in enumerate(rows_refs):
        begin = lax.rem(lax.axis_index("boot") + turn + 1, groups) * share
        info = info_ref[pl.ds(pl.multiple_of(begin, ROWS), share), :]
        gram, drive = add_rows(rows_ref, info, gram, drive)

    row_id = lax.broadcasted_iota(jnp.int32, (members, members), 0)
    col_id = lax.broadcasted_iota(jnp.int32, (members, members), 1)
    diagonal = row_id == col_id
    identity = jnp.where(diagonal, 1.0, 0.0)
    shifted = identity + gram / (members - 1.0)
    squares = jnp.sum(jnp.sum(shifted * shifted, axis=0, keepdims=True), axis=1, keepdims=True)
    frobenius = jnp.sqrt(squares)
    dot = functools.partial(jnp.dot, preferred_element_type=F32)

    def put(high_ref, low_ref, value):
        high_ref[...], low_ref[...] = halves(value)

    def step(_, carry):
        w_high[...] = dot(z_high[...], y_high[...]).astype(BF16)
        current = 1.5 * y_ref[...] - 0.5 * dot(y_high[...], w_high[...])
        root = 1.5 * z_ref[...] - 0.5 * dot(w_high[...], z_high[...])
        y_ref[...], z_ref[...] = current, root
        y_high[...], z_high[...] = current.astype(BF16), root.astype(BF16)
        return carry

    current = shifted / frobenius
    y_high[...] = current.astype(BF16)
    root = 1.5 * identity - 0.5 * current
    current = 1.5 * current - 0.5 * dot(y_high[...], y_high[...])
    y_ref[...], z_ref[...] = current, root
    y_high[...], z_high[...] = current.astype(BF16), root.astype(BF16)
    lax.fori_loop(1, NS_STEPS - FULL_STEPS, step, 0)
    for full in range(FULL_STEPS):
        put(y_high, y_low, y_ref[...])
        put(z_high, z_low, z_ref[...])
        put(w_high, w_low, product(z_high[...], z_low[...], y_high[...], y_low[...]))
        if full < FULL_STEPS - 1:
            change = product(y_high[...], y_low[...], w_high[...], w_low[...])
            y_ref[...] = 1.5 * y_ref[...] - 0.5 * change
        change = product(w_high[...], w_low[...], z_high[...], z_low[...])
        z_ref[...] = 1.5 * z_ref[...] - 0.5 * change
    root = z_ref[...] / jnp.sqrt(frobenius)

    drive_col = jnp.sum(jnp.where(diagonal, drive, 0.0), axis=1, keepdims=True)
    inner = jnp.sum(root * drive_col, axis=0, keepdims=True)
    inner_col = jnp.sum(jnp.where(diagonal, inner, 0.0), axis=1, keepdims=True)
    mean_weight = jnp.sum(root * inner_col, axis=0, keepdims=True) / (members - 1.0)
    blended_ref[...] = (root + mean_weight).astype(BF16)


def patch_weights(gram, drive, info, rows, share):
    members = gram.shape[0]
    whole = pltpu.VMEM((members, members), F32)
    half = pltpu.VMEM((members, members), BF16)
    return pl.pallas_call(
        functools.partial(weights_kernel, share),
        out_shape=jax.ShapeDtypeStruct((members, members), BF16),
        scratch_shapes=[whole] * 2 + [half] * 6,
        compiler_params=pltpu.CompilerParams(vmem_limit_bytes=VMEM_BYTES),
        cost_estimate=pl.CostEstimate(
            flops=80 * members * members * members,
            bytes_accessed=8 * members * members,
            transcendentals=0,
        ),
        name="patch_weights",
    )(gram, drive, info, *rows)


def update_kernel(blended_ref, background_ref, analysis_ref):
    members, points = background_ref.shape
    tile = min(points, 256)
    for begin in range(0, points, tile):
        columns = slice(begin, begin + tile)
        background = background_ref[:, columns].astype(F32)
        centre = jnp.sum(background, axis=0, keepdims=True) / members
        perturb = (background - centre).astype(BF16)
        update = jnp.dot(blended_ref[...], perturb, preferred_element_type=F32)
        analysis_ref[:, columns] = (centre + update).astype(BF16)


def update_points(blended, background):
    members, points = background.shape
    return pl.pallas_call(
        update_kernel,
        out_shape=jax.ShapeDtypeStruct((members, points), BF16),
        compiler_params=pltpu.CompilerParams(vmem_limit_bytes=VMEM_BYTES),
        cost_estimate=pl.CostEstimate(
            flops=2 * members * members * points,
            bytes_accessed=4 * members * points + 2 * members * members,
            transcendentals=0,
        ),
        name="update_points",
    )(blended, background)


def cut_kernel(states_ref, cut_ref):
    patches, _, share = cut_ref.shape
    region = states_ref.shape[1] // patches
    offset = lax.axis_index("boot") * share
    for patch in range(patches):
        begin = pl.multiple_of(patch * region + offset, LANES)
        cut_ref[patch] = states_ref[:, pl.ds(begin, share)]


def cut_share(states, patches, share):
    own_members = states.shape[0]
    return pl.pallas_call(
        cut_kernel,
        out_shape=jax.ShapeDtypeStruct((patches, own_members, share), BF16),
        compiler_params=pltpu.CompilerParams(vmem_limit_bytes=VMEM_BYTES),
        cost_estimate=pl.CostEstimate(
            flops=0, bytes_accessed=4 * patches * own_members * share, transcendentals=0
        ),
        name="cut_share",
    )(states)


def place_kernel(*refs):
    piece_refs, whole_ref = refs[:-1], refs[-1]
    groups = len(piece_refs)
    patches, _, share = piece_refs[0].shape
    for turn, piece_ref in enumerate(piece_refs):
        offset = lax.rem(lax.axis_index("boot") + turn, groups) * share
        for patch in range(patches):
            begin = pl.multiple_of(patch * groups * share + offset, LANES)
            whole_ref[:, pl.ds(begin, share)] = piece_ref[patch]


def place_pieces(pieces):
    patches, own_members, share = pieces[0].shape
    points = patches * share * len(pieces)
    return pl.pallas_call(
        place_kernel,
        out_shape=jax.ShapeDtypeStruct((own_members, points), BF16),
        compiler_params=pltpu.CompilerParams(vmem_limit_bytes=VMEM_BYTES),
        cost_estimate=pl.CostEstimate(
            flops=0, bytes_accessed=4 * own_members * points, transcendentals=0
        ),
        name="place_pieces",
    )(*pieces)


def exchange(blocks):
    return lax.all_to_all(blocks, "space", split_axis=0, concat_axis=0, tiled=True)


def swap_shares(own):
    groups = lax.axis_size("boot")
    return [
        lax.ppermute(own, "boot", [(g, (g - turn) % groups) for g in range(groups)])
        for turn in range(1, groups)
    ]


def local(
    background_states,
    measurement_anomaly_matrix,
    departure_vector,
    measurement_precision,
    measurement_region_targets,
    localization_factor_scaled,
    bootstrap_multiplicity,
):
    device_count = lax.axis_size("space")
    groups = lax.axis_size("boot")
    local_rows = measurement_anomaly_matrix.shape[0]
    targets_per = measurement_region_targets.shape[1]
    slot_cap = 2 * targets_per * local_rows // device_count
    slot_share = -(-slot_cap // (ROWS * groups)) * ROWS
    own_members, points = background_states.shape
    share = points // device_count // groups

    slots = pack(
        measurement_region_targets,
        localization_factor_scaled,
        bootstrap_multiplicity,
        measurement_precision,
        departure_vector,
        measurement_anomaly_matrix,
        device_count,
        slot_share,
        groups,
    )
    own_rows = exchange(slots)
    other_rows = swap_shares(own_rows)
    own_points = cut_share(background_states, device_count, share)
    own_rows, own_points = lax.optimization_barrier((own_rows, own_points))
    own_points = exchange(own_points).reshape(-1, share)
    background = [own_points] + swap_shares(own_points)

    members = measurement_anomaly_matrix.shape[1]
    gram, drive, info = own_gram(own_rows, slot_share, members)
    blended = patch_weights(gram, drive, info, other_rows, slot_share)
    pieces = []
    for part in background:
        analysis = update_points(blended, part).reshape(device_count, own_members, share)
        pieces.append(exchange(analysis))
    return place_pieces(pieces)


def solution(mesh):
    in_specs = (
        P("space", None),
        P("space", None),
        P("space"),
        P("space"),
        P("space", None),
        P("space", None),
        P(("boot", "space")),
    )
    out_specs = P(("boot", "space"), None)
    return jax.shard_map(local, mesh=mesh, in_specs=in_specs, out_specs=out_specs, check_vma=False)
```

```python
import functools

import jax
import jax.numpy as jnp
from jax import lax
from jax.experimental import pallas as pl
from jax.experimental.pallas import tpu as pltpu
from jax.sharding import PartitionSpec as P

NS_STEPS = 6
LANES = 128
ROWS = 8
FULL_STEPS = 1
VMEM_BYTES = 48 * 1024 * 1024
ALL_VMEM_BYTES = 64 * 1024 * 1024
F32 = jnp.float32
BF16 = jnp.bfloat16


def pack_kernel(groups, *refs):
    sources, slots_ref, fetched = refs[:6], refs[6], refs[7:13]
    info_ref, sems = refs[13:]
    run_copies(
        [
            pltpu.make_async_copy(source, target, sems.at[i])
            for i, (source, target) in enumerate(zip(sources, fetched))
        ]
    )
    targets_ref, local_ref, mult_ref, prec_ref, dep_ref, rows_ref = fetched
    patches = slots_ref.shape[0]
    count, members = rows_ref.shape
    share = (slots_ref.shape[2] - LANES) // members * ROWS
    mult = mult_ref[...].reshape(1, count).astype(F32)
    prec = prec_ref[...].reshape(1, count)
    weight = local_ref[...].astype(F32) / 1024.0 * (mult * prec)
    weight = weight.astype(BF16).astype(F32)
    dep = dep_ref[...].astype(F32).reshape(1, count)
    patch_id = lax.broadcasted_iota(jnp.int32, (patches, count), 0)
    first = patch_id == targets_ref[0:1, :]
    second = patch_id == targets_ref[1:2, :]
    named = jnp.logical_or(first, second)
    earlier = lax.broadcasted_iota(jnp.int32, (count, count), 0) < lax.broadcasted_iota(
        jnp.int32, (count, count), 1
    )
    rank = jnp.dot(
        named.astype(F32).astype(BF16), earlier.astype(F32).astype(BF16), preferred_element_type=F32
    )
    rank = jnp.where(named, rank, -1.0)
    by_patch = jnp.where(first, weight[0:1, :], jnp.where(second, weight[1:2, :], 0.0))
    slot_id = lax.broadcasted_iota(jnp.int32, (groups * share, count), 0).astype(F32)
    lane = lax.broadcasted_iota(jnp.int32, (groups * share, LANES), 1)
    info = jnp.zeros((groups * share, LANES), F32)
    for patch in range(patches):
        pick = slot_id == rank[patch : patch + 1, :]
        weight_col = jnp.sum(
            jnp.where(pick, by_patch[patch : patch + 1, :], 0.0), axis=1, keepdims=True
        )
        dep_col = jnp.sum(jnp.where(pick, dep, 0.0), axis=1, keepdims=True)
        info = jnp.where(lane == patch, weight_col, info)
        info = jnp.where(lane == patches + patch, dep_col, info)
    info_ref[...] = jnp.zeros((LANES, LANES), F32)
    info_ref[0 : groups * share, :] = info
    info = info_ref[...].T
    begin = lax.axis_index("boot") * share
    own_id = (lax.broadcasted_iota(jnp.int32, (share, count), 0) + begin).astype(F32)
    tail_id = lax.broadcasted_iota(jnp.int32, (ROWS, LANES), 0)
    picks = [
        jnp.where(own_id == rank[patch : patch + 1, :], 1.0, 0.0) for patch in range(patches)
    ]
    picked = jnp.dot(
        jnp.concatenate(picks, axis=0).astype(BF16), rows_ref[...], preferred_element_type=F32
    )
    for patch in range(patches):
        first = patch * share
        blocks = [picked[first + i : first + i + ROWS, :] for i in range(0, share, ROWS)]
        tail = jnp.where(
            tail_id == 0,
            info[patch : patch + 1, :],
            jnp.where(tail_id == 1, info[patches + patch : patches + patch + 1, :], 0.0),
        )
        slots_ref[patch] = jnp.concatenate(blocks + [tail], axis=1).astype(BF16)


def run_copies(copies):
    for copy in copies:
        copy.start()
    for copy in copies:
        copy.wait()


def pack(targets, local, mult, prec, dep, rows, patches, share, groups):
    count, members = rows.shape
    operands = (targets.T, local.T, mult, prec, dep, rows)
    return pl.pallas_call(
        functools.partial(pack_kernel, groups),
        out_shape=jax.ShapeDtypeStruct((patches, ROWS, share // ROWS * members + LANES), BF16),
        in_specs=[pl.BlockSpec(memory_space=pl.ANY)] * len(operands),
        scratch_shapes=[pltpu.VMEM(operand.shape, operand.dtype) for operand in operands]
        + [pltpu.VMEM((LANES, LANES), F32), pltpu.SemaphoreType.DMA((len(operands),))],
        compiler_params=pltpu.CompilerParams(vmem_limit_bytes=ALL_VMEM_BYTES),
        cost_estimate=pl.CostEstimate(
            flops=2 * patches * share * count * members,
            bytes_accessed=2 * (patches * share + count) * members,
            transcendentals=0,
        ),
        name="pack_rows",
    )(*operands)


def halves(value):
    high = value.astype(BF16)
    return high, (value - high.astype(F32)).astype(BF16)


def product(left_high, left_low, right_high, right_low):
    dot = functools.partial(jnp.dot, preferred_element_type=F32)
    return dot(left_high, right_high) + (dot(left_high, right_low) + dot(left_low, right_high))


def slot_rows(rows_ref, members):
    blocks = []
    for source in range(rows_ref.shape[0]):
        block = rows_ref[source].astype(F32)
        for begin in range(0, block.shape[1] - LANES, members):
            blocks.append(block[:, begin : begin + members])
    return jnp.concatenate(blocks, axis=0)


def slot_info(rows_ref, info_ref):
    sources, _, width = rows_ref.shape
    if 2 * sources < LANES:
        info_ref[2 * sources :, :] = jnp.zeros((LANES - 2 * sources, LANES), F32)
    for source in range(sources):
        tail = rows_ref[source].astype(F32)[:, width - LANES :]
        info_ref[source : source + 1, :] = tail[0:1, :]
        info_ref[sources + source : sources + source + 1, :] = tail[1:2, :]
    info_ref[...] = info_ref[...].T


def add_rows(rows, info_ref, turn, sources, gram, drive):
    share = rows.shape[0] // sources
    begin = lax.rem(lax.axis_index("boot") + turn, lax.axis_size("boot")) * share
    info = info_ref[pl.ds(pl.multiple_of(begin, ROWS), share), :]
    scaled = []
    for source in range(sources):
        block = rows[source * share : (source + 1) * share, :]
        block = (info[:, source : source + 1] * block).astype(BF16).astype(F32)
        scaled.append(block)
        dep_col = info[:, sources + source : sources + source + 1]
        drive = drive + jnp.sum(dep_col * block, axis=0, keepdims=True)
    gram = gram + lax.dot_general(
        rows.astype(BF16),
        jnp.concatenate(scaled, axis=0).astype(BF16),
        (((0,), (0,)), ((), ())),
        preferred_element_type=F32,
    )
    return gram, drive


def gram_kernel(rows_ref, gram_ref, drive_ref, info_ref):
    members = gram_ref.shape[0]
    slot_info(rows_ref, info_ref)
    gram_ref[...], drive_ref[...] = add_rows(
        slot_rows(rows_ref, members),
        info_ref,
        0,
        rows_ref.shape[0],
        jnp.zeros((members, members), F32),
        jnp.zeros((1, members), F32),
    )


def own_gram(rows, members):
    sources, _, width = rows.shape
    return pl.pallas_call(
        gram_kernel,
        out_shape=(
            jax.ShapeDtypeStruct((members, members), F32),
            jax.ShapeDtypeStruct((1, members), F32),
            jax.ShapeDtypeStruct((LANES, LANES), F32),
        ),
        compiler_params=pltpu.CompilerParams(vmem_limit_bytes=VMEM_BYTES),
        cost_estimate=pl.CostEstimate(
            flops=4 * members * sources * ROWS * width,
            bytes_accessed=2 * sources * ROWS * width,
            transcendentals=0,
        ),
        name="own_gram",
    )(rows)


def weights_kernel(*refs):
    gram_ref, drive_ref, own_info_ref = refs[:3]
    rows_refs, blended_ref, info_ref = refs[3:-10], refs[-10], refs[-9]
    y_ref, z_ref, y_high, y_low, z_high, z_low, w_high, w_low = refs[-8:]
    groups, members, _ = blended_ref.shape
    sources = rows_refs[0].shape[0]
    row_id = lax.broadcasted_iota(jnp.int32, (members, members), 0)
    col_id = lax.broadcasted_iota(jnp.int32, (members, members), 1)
    diagonal = row_id == col_id
    identity = jnp.where(diagonal, 1.0, 0.0)
    dot = functools.partial(jnp.dot, preferred_element_type=F32)
    rows = [slot_rows(rows_ref, members) for rows_ref in rows_refs]
    frobenius, drives = [], []
    for chain in range(groups):
        if chain == 0:
            gram, drive = gram_ref[...], drive_ref[...]
        else:
            slot_info(rows_refs[chain], info_ref.at[chain])
            gram, drive = jnp.zeros((members, members), F32), jnp.zeros((1, members), F32)
        for turn in range(groups):
            if chain or turn:
                gram, drive = add_rows(
                    rows[turn],
                    info_ref.at[chain] if chain else own_info_ref,
                    turn,
                    sources,
                    gram,
                    drive,
                )
        shifted = identity + gram / (members - 1.0)
        squares = jnp.sum(jnp.sum(shifted * shifted, axis=0, keepdims=True), axis=1, keepdims=True)
        frobenius.append(jnp.sqrt(squares))
        drives.append(drive)
        current = shifted / frobenius[chain]
        y_high[chain] = current.astype(BF16)
        z_ref[chain] = 1.5 * identity - 0.5 * current
        y_ref[chain] = 1.5 * current - 0.5 * dot(y_high[chain], y_high[chain])
        y_high[chain], z_high[chain] = y_ref[chain].astype(BF16), z_ref[chain].astype(BF16)

    def step(_, carry):
        for chain in range(groups):
            w_high[chain] = dot(z_high[chain], y_high[chain]).astype(BF16)
        for chain in range(groups):
            current = 1.5 * y_ref[chain] - 0.5 * dot(y_high[chain], w_high[chain])
            root = 1.5 * z_ref[chain] - 0.5 * dot(w_high[chain], z_high[chain])
            y_ref[chain], z_ref[chain] = current, root
            y_high[chain], z_high[chain] = current.astype(BF16), root.astype(BF16)
        return carry

    lax.fori_loop(1, NS_STEPS - 1, step, 0)
    for chain in range(groups):
        y_low[chain] = (y_ref[chain] - y_high[chain].astype(F32)).astype(BF16)
        z_low[chain] = (z_ref[chain] - z_high[chain].astype(F32)).astype(BF16)
    for chain in range(groups):
        w_high[chain], w_low[chain] = halves(
            product(z_high[chain], z_low[chain], y_high[chain], y_low[chain])
        )
    for chain in range(groups):
        change = product(w_high[chain], w_low[chain], z_high[chain], z_low[chain])
        root = (1.5 * z_ref[chain] - 0.5 * change) / jnp.sqrt(frobenius[chain])
        drive_col = jnp.sum(jnp.where(diagonal, drives[chain], 0.0), axis=1, keepdims=True)
        inner = jnp.sum(root * drive_col, axis=0, keepdims=True)
        inner_col = jnp.sum(jnp.where(diagonal, inner, 0.0), axis=1, keepdims=True)
        mean_weight = jnp.sum(root * inner_col, axis=0, keepdims=True) / (members - 1.0)
        blended_ref[chain] = (root + mean_weight).astype(BF16)


def patch_weights(gram, drive, info, rows):
    groups, members = len(rows), gram.shape[0]
    whole = pltpu.VMEM((groups, members, members), F32)
    half = pltpu.VMEM((groups, members, members), BF16)
    return pl.pallas_call(
        weights_kernel,
        out_shape=jax.ShapeDtypeStruct((groups, members, members), BF16),
        scratch_shapes=[pltpu.VMEM((groups, LANES, LANES), F32)] + [whole] * 2 + [half] * 6,
        compiler_params=pltpu.CompilerParams(vmem_limit_bytes=VMEM_BYTES),
        cost_estimate=pl.CostEstimate(
            flops=80 * groups * members * members * members,
            bytes_accessed=8 * members * members,
            transcendentals=0,
        ),
        name="patch_weights",
    )(gram, drive, info, *rows)


def update_kernel(blended_ref, background_ref, analysis_ref):
    groups = blended_ref.shape[0]
    members, points = background_ref.shape
    tile = min(points, 256)
    for begin in range(0, points, tile):
        columns = slice(begin, begin + tile)
        background = background_ref[:, columns].astype(F32)
        centre = jnp.sum(background, axis=0, keepdims=True) / members
        perturb = (background - centre).astype(BF16)
        for turn in range(groups):
            update = jnp.dot(blended_ref[turn], perturb, preferred_element_type=F32)
            group = lax.rem(lax.axis_index("boot") + turn, groups)
            analysis_ref[group, :, columns] = (centre + update).astype(BF16)


def update_points(blended, background):
    groups = blended.shape[0]
    members, points = background.shape
    return pl.pallas_call(
        update_kernel,
        out_shape=jax.ShapeDtypeStruct((groups, members, points), BF16),
        compiler_params=pltpu.CompilerParams(vmem_limit_bytes=VMEM_BYTES),
        cost_estimate=pl.CostEstimate(
            flops=2 * groups * members * members * points,
            bytes_accessed=2 * (groups + 1) * members * points,
            transcendentals=0,
        ),
        name="update_points",
    )(blended, background)


def cut_kernel(states_ref, cut_ref):
    patches, _, share = cut_ref.shape
    region = states_ref.shape[1] // patches
    offset = lax.axis_index("boot") * share
    for patch in range(patches):
        begin = pl.multiple_of(patch * region + offset, LANES)
        cut_ref[patch] = states_ref[:, pl.ds(begin, share)]


def cut_share(states, patches, share):
    own_members = states.shape[0]
    return pl.pallas_call(
        cut_kernel,
        out_shape=jax.ShapeDtypeStruct((patches, own_members, share), BF16),
        compiler_params=pltpu.CompilerParams(vmem_limit_bytes=VMEM_BYTES),
        cost_estimate=pl.CostEstimate(
            flops=0, bytes_accessed=4 * patches * own_members * share, transcendentals=0
        ),
        name="cut_share",
    )(states)


def place_kernel(pieces_ref, whole_ref):
    groups, patches, _, share = pieces_ref.shape
    for patch in range(patches):
        for group in range(groups):
            begin = (patch * groups + group) * share
            whole_ref[:, begin : begin + share] = pieces_ref[group, patch]


def place_pieces(pieces):
    groups, patches, own_members, share = pieces.shape
    points = groups * patches * share
    return pl.pallas_call(
        place_kernel,
        out_shape=jax.ShapeDtypeStruct((own_members, points), BF16),
        compiler_params=pltpu.CompilerParams(vmem_limit_bytes=VMEM_BYTES),
        cost_estimate=pl.CostEstimate(
            flops=0, bytes_accessed=4 * own_members * points, transcendentals=0
        ),
        name="place_pieces",
    )(pieces)


def exchange(blocks, axes="space"):
    return lax.all_to_all(blocks, axes, split_axis=0, concat_axis=0, tiled=True)


def swap_shares(own):
    groups = lax.axis_size("boot")
    return [
        lax.ppermute(own, "boot", [(g, (g - turn) % groups) for g in range(groups)])
        for turn in range(1, groups)
    ]


def local(
    background_states,
    measurement_anomaly_matrix,
    departure_vector,
    measurement_precision,
    measurement_region_targets,
    localization_factor_scaled,
    bootstrap_multiplicity,
):
    device_count = lax.axis_size("space")
    groups = lax.axis_size("boot")
    local_rows = measurement_anomaly_matrix.shape[0]
    targets_per = measurement_region_targets.shape[1]
    slot_cap = 2 * targets_per * local_rows // device_count
    slot_share = -(-slot_cap // (ROWS * groups)) * ROWS
    own_members, points = background_states.shape
    share = points // device_count // groups

    slots = pack(
        measurement_region_targets,
        localization_factor_scaled,
        bootstrap_multiplicity,
        measurement_precision,
        departure_vector,
        measurement_anomaly_matrix,
        device_count,
        slot_share,
        groups,
    )
    own_rows = exchange(slots)
    other_rows = swap_shares(own_rows)
    own_points = cut_share(background_states, device_count, share)
    own_rows, own_points = lax.optimization_barrier((own_rows, own_points))
    own_points = exchange(own_points).reshape(-1, share)

    gram, drive, info = own_gram(own_rows, measurement_anomaly_matrix.shape[1])
    blended = patch_weights(gram, drive, info, [own_rows] + other_rows)
    analysis = update_points(blended, own_points)
    analysis = exchange(analysis.reshape(-1, own_members, share), ("boot", "space"))
    return place_pieces(analysis.reshape(groups, device_count, own_members, share))


def solution(mesh):
    in_specs = (
        P("space", None),
        P("space", None),
        P("space"),
        P("space"),
        P("space", None),
        P("space", None),
        P(("boot", "space")),
    )
    out_specs = P(("boot", "space"), None)
    return jax.shard_map(local, mesh=mesh, in_specs=in_specs, out_specs=out_specs, check_vma=False)
```

```python
import functools

import jax
import jax.numpy as jnp
from jax import lax
from jax.experimental import pallas as pl
from jax.experimental.pallas import tpu as pltpu
from jax.sharding import PartitionSpec as P

NS_STEPS = 6
LANES = 128
ROWS = 8
MEBI = 1024 * 1024
F32 = jnp.float32
BF16 = jnp.bfloat16


def pack_kernel(groups, *refs):
    sources, slots_ref, fetched = refs[:6], refs[6], refs[7:13]
    info_ref, sems = refs[13:]
    run_copies(
        [
            pltpu.make_async_copy(source, target, sems.at[i])
            for i, (source, target) in enumerate(zip(sources, fetched))
        ]
    )
    targets_ref, local_ref, mult_ref, prec_ref, dep_ref, rows_ref = fetched
    patches = slots_ref.shape[0]
    count, members = rows_ref.shape
    share = (slots_ref.shape[2] - LANES) // members * ROWS
    mult = mult_ref[...].reshape(1, count).astype(F32)
    prec = prec_ref[...].reshape(1, count)
    weight = local_ref[...].astype(F32) / 1024.0 * (mult * prec)
    weight = weight.astype(BF16).astype(F32)
    dep = dep_ref[...].astype(F32).reshape(1, count)
    patch_id = lax.broadcasted_iota(jnp.int32, (patches, count), 0)
    first = patch_id == targets_ref[0:1, :]
    second = patch_id == targets_ref[1:2, :]
    named = jnp.logical_or(first, second)
    earlier = lax.broadcasted_iota(jnp.int32, (count, count), 0) < lax.broadcasted_iota(
        jnp.int32, (count, count), 1
    )
    rank = jnp.dot(
        named.astype(F32).astype(BF16), earlier.astype(F32).astype(BF16), preferred_element_type=F32
    )
    rank = jnp.where(named, rank, -1.0)
    by_patch = jnp.where(first, weight[0:1, :], jnp.where(second, weight[1:2, :], 0.0))
    slot_id = lax.broadcasted_iota(jnp.int32, (groups * share, count), 0).astype(F32)
    lane = lax.broadcasted_iota(jnp.int32, (groups * share, LANES), 1)
    info = jnp.zeros((groups * share, LANES), F32)
    for patch in range(patches):
        pick = slot_id == rank[patch : patch + 1, :]
        weight_col = jnp.sum(
            jnp.where(pick, by_patch[patch : patch + 1, :], 0.0), axis=1, keepdims=True
        )
        dep_col = jnp.sum(jnp.where(pick, dep, 0.0), axis=1, keepdims=True)
        info = jnp.where(lane == patch, weight_col, info)
        info = jnp.where(lane == patches + patch, dep_col, info)
    info_ref[...] = jnp.zeros((LANES, LANES), F32)
    info_ref[0 : groups * share, :] = info
    info = info_ref[...].T
    begin = lax.axis_index("boot") * share
    own_id = (lax.broadcasted_iota(jnp.int32, (share, count), 0) + begin).astype(F32)
    tail_id = lax.broadcasted_iota(jnp.int32, (ROWS, LANES), 0)
    picks = [
        jnp.where(own_id == rank[patch : patch + 1, :], 1.0, 0.0) for patch in range(patches)
    ]
    picked = jnp.dot(
        jnp.concatenate(picks, axis=0).astype(BF16), rows_ref[...], preferred_element_type=F32
    )
    for patch in range(patches):
        first = patch * share
        blocks = [picked[first + i : first + i + ROWS, :] for i in range(0, share, ROWS)]
        tail = jnp.where(
            tail_id == 0,
            info[patch : patch + 1, :],
            jnp.where(tail_id == 1, info[patches + patch : patches + patch + 1, :], 0.0),
        )
        slots_ref[patch] = jnp.concatenate(blocks + [tail], axis=1).astype(BF16)


def run_copies(copies):
    for copy in copies:
        copy.start()
    for copy in copies:
        copy.wait()


def pack(targets, local, mult, prec, dep, rows, patches, share, groups):
    count, members = rows.shape
    operands = (targets.T, local.T, mult, prec, dep, rows)
    return pl.pallas_call(
        functools.partial(pack_kernel, groups),
        out_shape=jax.ShapeDtypeStruct((patches, ROWS, share // ROWS * members + LANES), BF16),
        in_specs=[pl.BlockSpec(memory_space=pl.ANY)] * len(operands),
        scratch_shapes=[pltpu.VMEM(operand.shape, operand.dtype) for operand in operands]
        + [pltpu.VMEM((LANES, LANES), F32), pltpu.SemaphoreType.DMA((len(operands),))],
        compiler_params=pltpu.CompilerParams(vmem_limit_bytes=64 * MEBI),
        cost_estimate=pl.CostEstimate(
            flops=2 * patches * share * count * members,
            bytes_accessed=2 * (patches * share + count) * members,
            transcendentals=0,
        ),
        name="pack_rows",
    )(*operands)


def slot_rows(rows_ref, members):
    blocks = []
    for source in range(rows_ref.shape[0]):
        block = rows_ref[source].astype(F32)
        for begin in range(0, block.shape[1] - LANES, members):
            blocks.append(block[:, begin : begin + members])
    return jnp.concatenate(blocks, axis=0)


def slot_info(rows_ref, info_ref):
    sources, _, width = rows_ref.shape
    if 2 * sources < LANES:
        info_ref[2 * sources :, :] = jnp.zeros((LANES - 2 * sources, LANES), F32)
    for source in range(sources):
        tail = rows_ref[source].astype(F32)[:, width - LANES :]
        info_ref[source : source + 1, :] = tail[0:1, :]
        info_ref[sources + source : sources + source + 1, :] = tail[1:2, :]
    info_ref[...] = info_ref[...].T


def scaled_rows(rows, info_ref, turn, sources):
    share = rows.shape[0] // sources
    begin = lax.rem(lax.axis_index("boot") + turn, lax.axis_size("boot")) * share
    info = info_ref[pl.ds(pl.multiple_of(begin, ROWS), share), :]
    blocks, drive = [], jnp.zeros((1, rows.shape[1]), F32)
    for source in range(sources):
        block = rows[source * share : (source + 1) * share, :]
        block = (info[:, source : source + 1] * block).astype(BF16).astype(F32)
        blocks.append(block)
        dep_col = info[:, sources + source : sources + source + 1]
        drive = drive + jnp.sum(dep_col * block, axis=0, keepdims=True)
    return jnp.concatenate(blocks, axis=0).astype(BF16), drive


def outer_sum(rows, scaled):
    return lax.dot_general(
        rows.astype(BF16), scaled, (((0,), (0,)), ((), ())), preferred_element_type=F32
    )


def gram_kernel(rows_ref, gram_ref, drive_ref, info_ref):
    members = gram_ref.shape[0]
    slot_info(rows_ref, info_ref)
    rows = slot_rows(rows_ref, members)
    scaled, drive_ref[...] = scaled_rows(rows, info_ref, 0, rows_ref.shape[0])
    gram_ref[...] = outer_sum(rows, scaled)


def own_gram(rows, members):
    sources, _, width = rows.shape
    return pl.pallas_call(
        gram_kernel,
        out_shape=(
            jax.ShapeDtypeStruct((members, members), F32),
            jax.ShapeDtypeStruct((1, members), F32),
            jax.ShapeDtypeStruct((LANES, LANES), F32),
        ),
        compiler_params=pltpu.CompilerParams(vmem_limit_bytes=16 * MEBI),
        cost_estimate=pl.CostEstimate(
            flops=4 * members * sources * ROWS * width,
            bytes_accessed=2 * sources * ROWS * width,
            transcendentals=0,
        ),
        name="own_gram",
    )(rows)


def diagonal_column(value, eye):
    size = value.shape[1]
    parts = []
    for begin in range(0, size, LANES):
        block = value[:, begin : begin + LANES]
        block = block if value.shape[0] == 1 else block[begin : begin + LANES, :]
        parts.append(jnp.sum(jnp.where(eye, block, 0.0), axis=1, keepdims=True))
    return jnp.concatenate(parts, axis=0)


def weights_kernel(*refs):
    gram_ref, drive_ref, own_info_ref = refs[:3]
    rows_refs, blended_ref, info_ref = refs[3:-8], refs[-8], refs[-7]
    y_ref, z_ref, y_high, z_high, low, w_high = refs[-6:]
    groups, members, _ = blended_ref.shape
    sources = rows_refs[0].shape[0]
    row_id = lax.broadcasted_iota(jnp.int32, (members, members), 0)
    col_id = lax.broadcasted_iota(jnp.int32, (members, members), 1)
    identity = jnp.where(row_id == col_id, 1.0, 0.0)
    eye = lax.broadcasted_iota(jnp.int32, (LANES, LANES), 0) == lax.broadcasted_iota(
        jnp.int32, (LANES, LANES), 1
    )
    dot = functools.partial(jnp.dot, preferred_element_type=F32)

    def split(chain, value):
        w_high[chain] = value.astype(BF16)
        for begin in range(0, members, LANES):
            block = slice(begin, begin + LANES)
            w_high[chain, block, block] = jnp.where(eye, 0.0, value[block, block]).astype(BF16)
        return 1.5 - 0.5 * diagonal_column(value, eye)

    grams = [gram_ref[...]] + [jnp.zeros((members, members), F32)] * (groups - 1)
    drives = [drive_ref[...]] + [jnp.zeros((1, members), F32)] * (groups - 1)
    for chain in range(1, groups):
        slot_info(rows_refs[chain], info_ref.at[chain])
    for turn, rows_ref in enumerate(rows_refs):
        rows = slot_rows(rows_ref, members)
        chains = [chain for chain in range(groups) if chain or turn]
        scaled = []
        for chain in chains:
            info = info_ref.at[chain] if chain else own_info_ref
            block, drive = scaled_rows(rows, info, turn, sources)
            scaled.append(block)
            drives[chain] = drives[chain] + drive
        sums = outer_sum(rows, jnp.concatenate(scaled, axis=1))
        for place, chain in enumerate(chains):
            columns = slice(place * members, (place + 1) * members)
            grams[chain] = grams[chain] + sums[:, columns]

    frobenius = []
    for chain in range(groups):
        shifted = identity + grams[chain] / (members - 1.0)
        squares = jnp.sum(jnp.sum(shifted * shifted, axis=0, keepdims=True), axis=1, keepdims=True)
        frobenius.append(jnp.sqrt(squares))
        current = shifted / frobenius[chain]
        factor = split(chain, current)
        y_high[chain] = current.astype(BF16)
        z_ref[chain] = 1.5 * identity - 0.5 * current
        y_ref[chain] = factor * current - 0.5 * dot(w_high[chain], y_high[chain])
        y_high[chain], z_high[chain] = y_ref[chain].astype(BF16), z_ref[chain].astype(BF16)

    def step(_, carry):
        factors = [split(c, dot(z_high[c], y_high[c])) for c in range(groups)]
        for chain in range(groups):
            current = factors[chain] * y_ref[chain] - 0.5 * dot(w_high[chain], y_high[chain])
            root = factors[chain] * z_ref[chain] - 0.5 * dot(w_high[chain], z_high[chain])
            y_ref[chain], z_ref[chain] = current, root
            y_high[chain], z_high[chain] = current.astype(BF16), root.astype(BF16)
        return carry

    lax.fori_loop(1, NS_STEPS - 1, step, 0)
    for chain in range(groups):
        low[2 * chain] = (y_ref[chain] - y_high[chain].astype(F32)).astype(BF16)
        low[2 * chain + 1] = (z_ref[chain] - z_high[chain].astype(F32)).astype(BF16)
    factors = []
    for chain in range(groups):
        small = dot(z_high[chain], low[2 * chain]) + dot(low[2 * chain + 1], y_high[chain])
        factors.append(split(chain, dot(z_high[chain], y_high[chain]) + small))
    for chain in range(groups):
        root = factors[chain] * z_ref[chain] - 0.5 * dot(w_high[chain], z_high[chain])
        root = root / jnp.sqrt(frobenius[chain])
        inner = jnp.sum(root * diagonal_column(drives[chain], eye), axis=0, keepdims=True)
        mean_weight = jnp.sum(root * diagonal_column(inner, eye), axis=0, keepdims=True)
        blended_ref[chain] = (root + mean_weight / (members - 1.0)).astype(BF16)


def patch_weights(gram, drive, info, rows):
    groups, members = len(rows), gram.shape[0]
    whole = pltpu.VMEM((groups, members, members), F32)
    half = pltpu.VMEM((groups, members, members), BF16)
    return pl.pallas_call(
        weights_kernel,
        out_shape=jax.ShapeDtypeStruct((groups, members, members), BF16),
        scratch_shapes=[
            pltpu.VMEM((groups, LANES, LANES), F32),
            whole,
            whole,
            half,
            half,
            pltpu.VMEM((2 * groups, members, members), BF16),
            half,
        ],
        compiler_params=pltpu.CompilerParams(vmem_limit_bytes=(8 + 10 * groups) * MEBI),
        cost_estimate=pl.CostEstimate(
            flops=80 * groups * members * members * members,
            bytes_accessed=8 * members * members,
            transcendentals=0,
        ),
        name="patch_weights",
    )(gram, drive, info, *rows)


def update_kernel(blended_ref, background_ref, analysis_ref):
    groups = blended_ref.shape[0]
    members, points = background_ref.shape
    tile = min(points, 256)
    for begin in range(0, points, tile):
        columns = slice(begin, begin + tile)
        background = background_ref[:, columns].astype(F32)
        centre = jnp.sum(background, axis=0, keepdims=True) / members
        perturb = (background - centre).astype(BF16)
        for turn in range(groups):
            update = jnp.dot(blended_ref[turn], perturb, preferred_element_type=F32)
            group = lax.rem(lax.axis_index("boot") + turn, groups)
            analysis_ref[group, :, columns] = (centre + update).astype(BF16)


def update_points(blended, background):
    groups = blended.shape[0]
    members, points = background.shape
    return pl.pallas_call(
        update_kernel,
        out_shape=jax.ShapeDtypeStruct((groups, members, points), BF16),
        compiler_params=pltpu.CompilerParams(vmem_limit_bytes=16 * MEBI),
        cost_estimate=pl.CostEstimate(
            flops=2 * groups * members * members * points,
            bytes_accessed=2 * (groups + 1) * members * points,
            transcendentals=0,
        ),
        name="update_points",
    )(blended, background)


def cut_kernel(states_ref, cut_ref):
    patches, _, share = cut_ref.shape
    region = states_ref.shape[1] // patches
    offset = lax.axis_index("boot") * share
    for patch in range(patches):
        begin = pl.multiple_of(patch * region + offset, LANES)
        cut_ref[patch] = states_ref[:, pl.ds(begin, share)]


def cut_share(states, patches, share):
    own_members = states.shape[0]
    return pl.pallas_call(
        cut_kernel,
        out_shape=jax.ShapeDtypeStruct((patches, own_members, share), BF16),
        compiler_params=pltpu.CompilerParams(vmem_limit_bytes=16 * MEBI),
        cost_estimate=pl.CostEstimate(
            flops=0, bytes_accessed=4 * patches * own_members * share, transcendentals=0
        ),
        name="cut_share",
    )(states)


def place_kernel(pieces_ref, whole_ref):
    groups, patches, _, share = pieces_ref.shape
    for patch in range(patches):
        for group in range(groups):
            begin = (patch * groups + group) * share
            whole_ref[:, begin : begin + share] = pieces_ref[group, patch]


def place_pieces(pieces):
    groups, patches, own_members, share = pieces.shape
    points = groups * patches * share
    return pl.pallas_call(
        place_kernel,
        out_shape=jax.ShapeDtypeStruct((own_members, points), BF16),
        compiler_params=pltpu.CompilerParams(vmem_limit_bytes=16 * MEBI),
        cost_estimate=pl.CostEstimate(
            flops=0, bytes_accessed=4 * own_members * points, transcendentals=0
        ),
        name="place_pieces",
    )(pieces)


def exchange(blocks, axes="space"):
    return lax.all_to_all(blocks, axes, split_axis=0, concat_axis=0, tiled=True)


def swap_shares(own):
    groups = lax.axis_size("boot")
    return [
        lax.ppermute(own, "boot", [(g, (g - turn) % groups) for g in range(groups)])
        for turn in range(1, groups)
    ]


def local(
    background_states,
    measurement_anomaly_matrix,
    departure_vector,
    measurement_precision,
    measurement_region_targets,
    localization_factor_scaled,
    bootstrap_multiplicity,
):
    device_count = lax.axis_size("space")
    groups = lax.axis_size("boot")
    local_rows = measurement_anomaly_matrix.shape[0]
    targets_per = measurement_region_targets.shape[1]
    slot_cap = 2 * targets_per * local_rows // device_count
    slot_share = -(-slot_cap // (ROWS * groups)) * ROWS
    own_members, points = background_states.shape
    share = points // device_count // groups

    slots = pack(
        measurement_region_targets,
        localization_factor_scaled,
        bootstrap_multiplicity,
        measurement_precision,
        departure_vector,
        measurement_anomaly_matrix,
        device_count,
        slot_share,
        groups,
    )
    own_points = cut_share(background_states, device_count, share)
    own_rows, own_points = lax.optimization_barrier((exchange(slots), own_points))
    other_rows = swap_shares(own_rows)
    own_points = exchange(own_points).reshape(-1, share)

    gram, drive, info = own_gram(own_rows, measurement_anomaly_matrix.shape[1])
    blended = patch_weights(gram, drive, info, [own_rows] + other_rows)
    analysis = update_points(blended, own_points)
    analysis = exchange(analysis.reshape(-1, own_members, share), ("boot", "space"))
    return place_pieces(analysis.reshape(groups, device_count, own_members, share))


def solution(mesh):
    in_specs = (
        P("space", None),
        P("space", None),
        P("space"),
        P("space"),
        P("space", None),
        P("space", None),
        P(("boot", "space")),
    )
    out_specs = P(("boot", "space"), None)
    return jax.shard_map(local, mesh=mesh, in_specs=in_specs, out_specs=out_specs, check_vma=False)
```

```python
import functools

import jax
import jax.numpy as jnp
from jax import lax
from jax.experimental import pallas as pl
from jax.experimental.pallas import tpu as pltpu
from jax.sharding import PartitionSpec as P

NS_STEPS = 6
LANES = 128
ROWS = 16
MEBI = 1024 * 1024
F32 = jnp.float32
BF16 = jnp.bfloat16


def pack_kernel(groups, *refs):
    sources, slots_ref, fetched = refs[:6], refs[6], refs[7:13]
    info_ref, sems = refs[13:]
    copies = [
        pltpu.make_async_copy(source, target, sems.at[i])
        for i, (source, target) in enumerate(zip(sources, fetched))
    ]
    for copy in copies:
        copy.start()
    for copy in copies[:-1]:
        copy.wait()
    targets_ref, local_ref, mult_ref, prec_ref, dep_ref, rows_ref = fetched
    patches = slots_ref.shape[0]
    count, members = rows_ref.shape
    share = (slots_ref.shape[2] - LANES) // members * ROWS
    mult = mult_ref[...].reshape(1, count).astype(F32)
    prec = prec_ref[...].reshape(1, count)
    weight = local_ref[...].astype(F32) / 1024.0 * (mult * prec)
    weight = weight.astype(BF16).astype(F32)
    dep = dep_ref[...].astype(F32).reshape(1, count)
    patch_id = lax.broadcasted_iota(jnp.int32, (patches, count), 0)
    first = patch_id == targets_ref[0:1, :]
    second = patch_id == targets_ref[1:2, :]
    named = jnp.logical_or(first, second)
    earlier = lax.broadcasted_iota(jnp.int32, (count, count), 0) < lax.broadcasted_iota(
        jnp.int32, (count, count), 1
    )
    rank = jnp.dot(
        named.astype(F32).astype(BF16), earlier.astype(F32).astype(BF16), preferred_element_type=F32
    )
    rank = jnp.where(named, rank, -1.0)
    by_patch = jnp.where(first, weight[0:1, :], jnp.where(second, weight[1:2, :], 0.0))
    slot_id = lax.broadcasted_iota(jnp.int32, (groups * share, count), 0).astype(F32)
    lane = lax.broadcasted_iota(jnp.int32, (groups * share, LANES), 1)
    info = jnp.zeros((groups * share, LANES), F32)
    for patch in range(patches):
        pick = slot_id == rank[patch : patch + 1, :]
        weight_col = jnp.sum(
            jnp.where(pick, by_patch[patch : patch + 1, :], 0.0), axis=1, keepdims=True
        )
        dep_col = jnp.sum(jnp.where(pick, dep, 0.0), axis=1, keepdims=True)
        info = jnp.where(lane == patch, weight_col, info)
        info = jnp.where(lane == patches + patch, dep_col, info)
    info_ref[...] = jnp.zeros((LANES, LANES), F32)
    info_ref[0 : groups * share, :] = info
    info = info_ref[...].T
    begin = lax.axis_index("boot") * share
    own_id = (lax.broadcasted_iota(jnp.int32, (share, count), 0) + begin).astype(F32)
    tail_id = lax.broadcasted_iota(jnp.int32, (ROWS, LANES), 0)
    picks = [
        jnp.where(own_id == rank[patch : patch + 1, :], 1.0, 0.0) for patch in range(patches)
    ]
    copies[-1].wait()
    picked = jnp.dot(
        jnp.concatenate(picks, axis=0).astype(BF16), rows_ref[...], preferred_element_type=F32
    )
    for patch in range(patches):
        first = patch * share
        blocks = [picked[first + i : first + i + ROWS, :] for i in range(0, share, ROWS)]
        tail = jnp.where(
            tail_id == 0,
            info[patch : patch + 1, :],
            jnp.where(tail_id == 1, info[patches + patch : patches + patch + 1, :], 0.0),
        )
        slots_ref[patch] = jnp.concatenate(blocks + [tail], axis=1).astype(BF16)


def pack(targets, local, mult, prec, dep, rows, patches, share, groups):
    count, members = rows.shape
    operands = (targets.T, local.T, mult, prec, dep, rows)
    return pl.pallas_call(
        functools.partial(pack_kernel, groups),
        out_shape=jax.ShapeDtypeStruct((patches, ROWS, share // ROWS * members + LANES), BF16),
        in_specs=[pl.BlockSpec(memory_space=pl.ANY)] * len(operands),
        scratch_shapes=[pltpu.VMEM(operand.shape, operand.dtype) for operand in operands]
        + [pltpu.VMEM((LANES, LANES), F32), pltpu.SemaphoreType.DMA((len(operands),))],
        compiler_params=pltpu.CompilerParams(vmem_limit_bytes=64 * MEBI),
        cost_estimate=pl.CostEstimate(
            flops=2 * patches * share * count * members,
            bytes_accessed=2 * (patches * share + count) * members,
            transcendentals=0,
        ),
        name="pack_rows",
    )(*operands)


def slot_rows(rows_ref, members):
    sources, _, width = rows_ref.shape
    return jnp.concatenate(
        [
            rows_ref[source, :, begin : begin + members]
            for source in range(sources)
            for begin in range(0, width - LANES, members)
        ],
        axis=0,
    )


def slot_info(rows_ref, info_ref):
    sources, _, width = rows_ref.shape
    if 2 * sources < LANES:
        info_ref[2 * sources :, :] = jnp.zeros((LANES - 2 * sources, LANES), F32)
    for source in range(sources):
        tail = rows_ref[source, :, width - LANES :].astype(F32)
        info_ref[source : source + 1, :] = tail[0:1, :]
        info_ref[sources + source : sources + source + 1, :] = tail[1:2, :]
    info_ref[...] = info_ref[...].T


def scaled_rows(rows, info_ref, turn, sources):
    share, members = rows.shape[0] // sources, rows.shape[1]
    begin = lax.rem(lax.axis_index("boot") + turn, lax.axis_size("boot")) * share
    info = info_ref[pl.ds(pl.multiple_of(begin, ROWS), share), :]
    weights, drives = [], []
    for source in range(sources):
        weight = jnp.broadcast_to(info[:, source : source + 1], (share, LANES))
        dep = jnp.broadcast_to(info[:, sources + source : sources + source + 1], (share, LANES))
        weights.append(weight.astype(BF16))
        drives.append(weight * dep)
    weights = jnp.concatenate(weights, axis=0)
    weights = jnp.concatenate([weights] * (members // LANES), axis=1)
    return rows * weights, jnp.concatenate(drives, axis=0)


def outer_sum(rows, right):
    return lax.dot_general(rows, right, (((0,), (0,)), ((), ())), preferred_element_type=F32)


def drive_sum(drives, rows):
    lane = lax.broadcasted_iota(jnp.int32, drives[0].shape, 1)
    parts = jnp.zeros(drives[0].shape, F32)
    for place, weight in enumerate(drives):
        high = weight.astype(BF16).astype(F32)
        parts = jnp.where(lane == 2 * place, high, parts)
        parts = jnp.where(lane == 2 * place + 1, weight - high, parts)
    sums = outer_sum(parts.astype(BF16), rows)
    return [
        sums[2 * place : 2 * place + 1, :] + sums[2 * place + 1 : 2 * place + 2, :]
        for place in range(len(drives))
    ]


def gram_kernel(rows_ref, gram_ref, drive_ref, info_ref):
    members = gram_ref.shape[0]
    slot_info(rows_ref, info_ref)
    rows = slot_rows(rows_ref, members)
    scaled, drive = scaled_rows(rows, info_ref, 0, rows_ref.shape[0])
    (drive_ref[...],) = drive_sum([drive], rows)
    gram_ref[...] = outer_sum(rows, scaled)


def own_gram(rows, members):
    sources, _, width = rows.shape
    return pl.pallas_call(
        gram_kernel,
        out_shape=(
            jax.ShapeDtypeStruct((members, members), F32),
            jax.ShapeDtypeStruct((1, members), F32),
            jax.ShapeDtypeStruct((LANES, LANES), F32),
        ),
        compiler_params=pltpu.CompilerParams(vmem_limit_bytes=16 * MEBI),
        cost_estimate=pl.CostEstimate(
            flops=4 * members * sources * ROWS * width,
            bytes_accessed=2 * sources * ROWS * width,
            transcendentals=0,
        ),
        name="own_gram",
    )(rows)


def diagonal_column(value, eye):
    size = value.shape[1]
    parts = []
    for begin in range(0, size, LANES):
        block = value[:, begin : begin + LANES]
        block = block if value.shape[0] == 1 else block[begin : begin + LANES, :]
        parts.append(jnp.sum(jnp.where(eye, block, 0.0), axis=1, keepdims=True))
    return jnp.concatenate(parts, axis=0)


def weights_kernel(*refs):
    gram_ref, drive_ref, own_info_ref, own_rows_ref = refs[:4]
    far_refs, blended_ref, info_ref = refs[4:-10], refs[-10], refs[-9]
    y_ref, z_ref, y_high, z_high, low, w_high, near_ref, sems = refs[-8:]
    groups, members, _ = blended_ref.shape
    sources = own_rows_ref.shape[0]
    copies = [
        pltpu.make_async_copy(far_ref, near_ref.at[place], sems.at[place])
        for place, far_ref in enumerate(far_refs)
    ]
    for copy in copies:
        copy.start()
    rows_refs = [own_rows_ref] + [near_ref.at[place] for place in range(groups - 1)]
    row_id = lax.broadcasted_iota(jnp.int32, (members, members), 0)
    col_id = lax.broadcasted_iota(jnp.int32, (members, members), 1)
    identity = jnp.where(row_id == col_id, 1.0, 0.0)
    eye = lax.broadcasted_iota(jnp.int32, (LANES, LANES), 0) == lax.broadcasted_iota(
        jnp.int32, (LANES, LANES), 1
    )
    dot = functools.partial(jnp.dot, preferred_element_type=F32)

    def split(chain, value):
        w_high[chain] = value.astype(BF16)
        for begin in range(0, members, LANES):
            block = slice(begin, begin + LANES)
            w_high[chain, block, block] = jnp.where(eye, 0.0, value[block, block]).astype(BF16)
        return 1.5 - 0.5 * diagonal_column(value, eye)

    grams = [gram_ref[...]] + [jnp.zeros((members, members), F32)] * (groups - 1)
    drives = [drive_ref[...]] + [jnp.zeros((1, members), F32)] * (groups - 1)
    for chain in range(1, groups):
        copies[chain - 1].wait()
        slot_info(rows_refs[chain], info_ref.at[chain])
    for turn, rows_ref in enumerate(rows_refs):
        rows = slot_rows(rows_ref, members)
        chains = [chain for chain in range(groups) if chain or turn]
        scaled, parts = [], []
        for chain in chains:
            info = info_ref.at[chain] if chain else own_info_ref
            block, part = scaled_rows(rows, info, turn, sources)
            scaled.append(block)
            parts.append(part)
        sums = outer_sum(rows, jnp.concatenate(scaled, axis=1))
        for place, (chain, drive) in enumerate(zip(chains, drive_sum(parts, rows))):
            columns = slice(place * members, (place + 1) * members)
            grams[chain] = grams[chain] + sums[:, columns]
            drives[chain] = drives[chain] + drive

    frobenius = []
    for chain in range(groups):
        shifted = identity + grams[chain] / (members - 1.0)
        squares = jnp.sum(jnp.sum(shifted * shifted, axis=0, keepdims=True), axis=1, keepdims=True)
        frobenius.append(jnp.sqrt(squares))
        current = shifted / frobenius[chain]
        factor = split(chain, current)
        y_high[chain] = current.astype(BF16)
        z_ref[chain] = 1.5 * identity - 0.5 * current
        y_ref[chain] = factor * current - 0.5 * dot(w_high[chain], y_high[chain])
        y_high[chain], z_high[chain] = y_ref[chain].astype(BF16), z_ref[chain].astype(BF16)

    def step(_, carry):
        factors = [split(c, dot(z_high[c], y_high[c])) for c in range(groups)]
        for chain in range(groups):
            current = factors[chain] * y_ref[chain] - 0.5 * dot(w_high[chain], y_high[chain])
            root = factors[chain] * z_ref[chain] - 0.5 * dot(w_high[chain], z_high[chain])
            y_ref[chain], z_ref[chain] = current, root
            y_high[chain], z_high[chain] = current.astype(BF16), root.astype(BF16)
        return carry

    lax.fori_loop(1, NS_STEPS - 1, step, 0, unroll=True)
    for chain in range(groups):
        low[2 * chain] = (y_ref[chain] - y_high[chain].astype(F32)).astype(BF16)
        low[2 * chain + 1] = (z_ref[chain] - z_high[chain].astype(F32)).astype(BF16)
    factors = []
    for chain in range(groups):
        small = dot(z_high[chain], low[2 * chain]) + dot(low[2 * chain + 1], y_high[chain])
        factors.append(split(chain, dot(z_high[chain], y_high[chain]) + small))
    for chain in range(groups):
        root = factors[chain] * z_ref[chain] - 0.5 * dot(w_high[chain], z_high[chain])
        root = root / jnp.sqrt(frobenius[chain])
        inner = jnp.sum(root * diagonal_column(drives[chain], eye), axis=0, keepdims=True)
        mean_weight = jnp.sum(root * diagonal_column(inner, eye), axis=0, keepdims=True)
        blended_ref[chain] = (root + mean_weight / (members - 1.0)).astype(BF16)


def patch_weights(gram, drive, info, own_rows, other_rows):
    groups, members = len(other_rows) + 1, gram.shape[0]
    resident, far = pl.BlockSpec(memory_space=pltpu.VMEM), pl.BlockSpec(memory_space=pl.ANY)
    whole = pltpu.VMEM((groups, members, members), F32)
    half = pltpu.VMEM((groups, members, members), BF16)
    return pl.pallas_call(
        weights_kernel,
        in_specs=[resident] * 4 + [far] * (groups - 1),
        out_shape=jax.ShapeDtypeStruct((groups, members, members), BF16),
        scratch_shapes=[
            pltpu.VMEM((groups, LANES, LANES), F32),
            whole,
            whole,
            half,
            half,
            pltpu.VMEM((2 * groups, members, members), BF16),
            half,
            pltpu.VMEM((max(groups - 1, 1),) + own_rows.shape, BF16),
            pltpu.SemaphoreType.DMA((max(groups - 1, 1),)),
        ],
        compiler_params=pltpu.CompilerParams(vmem_limit_bytes=(8 + 10 * groups) * MEBI),
        cost_estimate=pl.CostEstimate(
            flops=80 * groups * members * members * members,
            bytes_accessed=8 * members * members,
            transcendentals=0,
        ),
        name="patch_weights",
    )(gram, drive, info, own_rows, *other_rows)


def update_kernel(blended_ref, background_ref, analysis_ref):
    groups = blended_ref.shape[0]
    members, points = background_ref.shape
    tile = min(points, 256)
    for begin in range(0, points, tile):
        columns = slice(begin, begin + tile)
        background = background_ref[:, columns].astype(F32)
        centre = jnp.sum(background, axis=0, keepdims=True) / members
        perturb = (background - centre).astype(BF16)
        for turn in range(groups):
            update = jnp.dot(blended_ref[turn], perturb, preferred_element_type=F32)
            group = lax.rem(lax.axis_index("boot") + turn, groups)
            analysis_ref[group, :, columns] = (centre + update).astype(BF16)


def update_points(blended, background):
    groups = blended.shape[0]
    members, points = background.shape
    return pl.pallas_call(
        update_kernel,
        out_shape=jax.ShapeDtypeStruct((groups, members, points), BF16),
        compiler_params=pltpu.CompilerParams(vmem_limit_bytes=16 * MEBI),
        cost_estimate=pl.CostEstimate(
            flops=2 * groups * members * members * points,
            bytes_accessed=2 * (groups + 1) * members * points,
            transcendentals=0,
        ),
        name="update_points",
    )(blended, background)


def cut_kernel(states_ref, cut_ref):
    patches, _, share = cut_ref.shape
    region = states_ref.shape[1] // patches
    offset = lax.axis_index("boot") * share
    for patch in range(patches):
        begin = pl.multiple_of(patch * region + offset, LANES)
        cut_ref[patch] = states_ref[:, pl.ds(begin, share)]


def cut_share(states, patches, share):
    own_members = states.shape[0]
    return pl.pallas_call(
        cut_kernel,
        out_shape=jax.ShapeDtypeStruct((patches, own_members, share), BF16),
        compiler_params=pltpu.CompilerParams(vmem_limit_bytes=16 * MEBI),
        cost_estimate=pl.CostEstimate(
            flops=0, bytes_accessed=4 * patches * own_members * share, transcendentals=0
        ),
        name="cut_share",
    )(states)


def place_kernel(pieces_ref, whole_ref):
    groups, patches, _, share = pieces_ref.shape
    for patch in range(patches):
        for group in range(groups):
            begin = (patch * groups + group) * share
            whole_ref[:, begin : begin + share] = pieces_ref[group, patch]


def place_pieces(pieces):
    groups, patches, own_members, share = pieces.shape
    points = groups * patches * share
    return pl.pallas_call(
        place_kernel,
        out_shape=jax.ShapeDtypeStruct((own_members, points), BF16),
        compiler_params=pltpu.CompilerParams(vmem_limit_bytes=16 * MEBI),
        cost_estimate=pl.CostEstimate(
            flops=0, bytes_accessed=4 * own_members * points, transcendentals=0
        ),
        name="place_pieces",
    )(pieces)


def exchange(blocks, axes="space"):
    return lax.all_to_all(blocks, axes, split_axis=0, concat_axis=0, tiled=True)


def swap_shares(own):
    groups = lax.axis_size("boot")
    return [
        lax.ppermute(own, "boot", [(g, (g - turn) % groups) for g in range(groups)])
        for turn in range(1, groups)
    ]


def local(
    background_states,
    measurement_anomaly_matrix,
    departure_vector,
    measurement_precision,
    measurement_region_targets,
    localization_factor_scaled,
    bootstrap_multiplicity,
):
    device_count = lax.axis_size("space")
    groups = lax.axis_size("boot")
    local_rows = measurement_anomaly_matrix.shape[0]
    targets_per = measurement_region_targets.shape[1]
    slot_cap = 2 * targets_per * local_rows // device_count
    slot_share = -(-slot_cap // (ROWS * groups)) * ROWS
    own_members, points = background_states.shape
    share = points // device_count // groups

    slots = pack(
        measurement_region_targets,
        localization_factor_scaled,
        bootstrap_multiplicity,
        measurement_precision,
        departure_vector,
        measurement_anomaly_matrix,
        device_count,
        slot_share,
        groups,
    )
    own_points = cut_share(background_states, device_count, share)
    own_rows, own_points = lax.optimization_barrier((exchange(slots), own_points))
    other_rows = swap_shares(own_rows)
    own_points = exchange(own_points).reshape(-1, share)

    gram, drive, info = own_gram(own_rows, measurement_anomaly_matrix.shape[1])
    blended = patch_weights(gram, drive, info, own_rows, other_rows)
    analysis = update_points(blended, own_points)
    analysis = exchange(analysis.reshape(-1, own_members, share), ("boot", "space"))
    return place_pieces(analysis.reshape(groups, device_count, own_members, share))


def solution(mesh):
    in_specs = (
        P("space", None),
        P("space", None),
        P("space"),
        P("space"),
        P("space", None),
        P("space", None),
        P(("boot", "space")),
    )
    out_specs = P(("boot", "space"), None)
    return jax.shard_map(local, mesh=mesh, in_specs=in_specs, out_specs=out_specs, check_vma=False)
```

```python
import functools

import jax
import jax.numpy as jnp
from jax import lax
from jax.experimental import pallas as pl
from jax.experimental.pallas import tpu as pltpu
from jax.sharding import PartitionSpec as P

NS_STEPS = 6
LANES = 128
ROWS = 8
MEBI = 1024 * 1024
F32 = jnp.float32
BF16 = jnp.bfloat16


def pack_kernel(groups, *refs):
    sources, slots_ref, fetched = refs[:6], refs[6], refs[7:13]
    info_ref, sems = refs[13:]
    run_copies(
        [
            pltpu.make_async_copy(source, target, sems.at[i])
            for i, (source, target) in enumerate(zip(sources, fetched))
        ]
    )
    targets_ref, local_ref, mult_ref, prec_ref, dep_ref, rows_ref = fetched
    patches = slots_ref.shape[0]
    count, members = rows_ref.shape
    share = (slots_ref.shape[2] - LANES) // members * ROWS
    mult = mult_ref[...].reshape(1, count).astype(F32)
    prec = prec_ref[...].reshape(1, count)
    weight = local_ref[...].astype(F32) / 1024.0 * (mult * prec)
    weight = weight.astype(BF16).astype(F32)
    dep = dep_ref[...].astype(F32).reshape(1, count)
    patch_id = lax.broadcasted_iota(jnp.int32, (patches, count), 0)
    first = patch_id == targets_ref[0:1, :]
    second = patch_id == targets_ref[1:2, :]
    named = jnp.logical_or(first, second)
    earlier = lax.broadcasted_iota(jnp.int32, (count, count), 0) < lax.broadcasted_iota(
        jnp.int32, (count, count), 1
    )
    rank = jnp.dot(
        named.astype(F32).astype(BF16), earlier.astype(F32).astype(BF16), preferred_element_type=F32
    )
    rank = jnp.where(named, rank, -1.0)
    by_patch = jnp.where(first, weight[0:1, :], jnp.where(second, weight[1:2, :], 0.0))
    slot_id = lax.broadcasted_iota(jnp.int32, (groups * share, count), 0).astype(F32)
    lane = lax.broadcasted_iota(jnp.int32, (groups * share, LANES), 1)
    info = jnp.zeros((groups * share, LANES), F32)
    for patch in range(patches):
        pick = slot_id == rank[patch : patch + 1, :]
        weight_col = jnp.sum(
            jnp.where(pick, by_patch[patch : patch + 1, :], 0.0), axis=1, keepdims=True
        )
        dep_col = jnp.sum(jnp.where(pick, dep, 0.0), axis=1, keepdims=True)
        info = jnp.where(lane == patch, weight_col, info)
        info = jnp.where(lane == patches + patch, dep_col, info)
    info_ref[...] = jnp.zeros((LANES, LANES), F32)
    info_ref[0 : groups * share, :] = info
    info = info_ref[...].T
    begin = lax.axis_index("boot") * share
    own_id = (lax.broadcasted_iota(jnp.int32, (share, count), 0) + begin).astype(F32)
    tail_id = lax.broadcasted_iota(jnp.int32, (ROWS, LANES), 0)
    picks = [
        jnp.where(own_id == rank[patch : patch + 1, :], 1.0, 0.0) for patch in range(patches)
    ]
    picked = jnp.dot(
        jnp.concatenate(picks, axis=0).astype(BF16), rows_ref[...], preferred_element_type=F32
    )
    for patch in range(patches):
        first = patch * share
        blocks = [picked[first + i : first + i + ROWS, :] for i in range(0, share, ROWS)]
        tail = jnp.where(
            tail_id == 0,
            info[patch : patch + 1, :],
            jnp.where(tail_id == 1, info[patches + patch : patches + patch + 1, :], 0.0),
        )
        slots_ref[patch] = jnp.concatenate(blocks + [tail], axis=1).astype(BF16)


def run_copies(copies):
    for copy in copies:
        copy.start()
    for copy in copies:
        copy.wait()


def pack(targets, local, mult, prec, dep, rows, patches, share, groups):
    count, members = rows.shape
    operands = (targets.T, local.T, mult, prec, dep, rows)
    return pl.pallas_call(
        functools.partial(pack_kernel, groups),
        out_shape=jax.ShapeDtypeStruct((patches, ROWS, share // ROWS * members + LANES), BF16),
        in_specs=[pl.BlockSpec(memory_space=pl.ANY)] * len(operands),
        scratch_shapes=[pltpu.VMEM(operand.shape, operand.dtype) for operand in operands]
        + [pltpu.VMEM((LANES, LANES), F32), pltpu.SemaphoreType.DMA((len(operands),))],
        compiler_params=pltpu.CompilerParams(vmem_limit_bytes=64 * MEBI),
        cost_estimate=pl.CostEstimate(
            flops=2 * patches * share * count * members,
            bytes_accessed=2 * (patches * share + count) * members,
            transcendentals=0,
        ),
        name="pack_rows",
    )(*operands)


def slot_rows(rows_ref, members):
    blocks = []
    for source in range(rows_ref.shape[0]):
        block = rows_ref[source].astype(F32)
        for begin in range(0, block.shape[1] - LANES, members):
            blocks.append(block[:, begin : begin + members])
    return jnp.concatenate(blocks, axis=0)


def slot_info(rows_ref, info_ref):
    sources, _, width = rows_ref.shape
    if 2 * sources < LANES:
        info_ref[2 * sources :, :] = jnp.zeros((LANES - 2 * sources, LANES), F32)
    for source in range(sources):
        tail = rows_ref[source].astype(F32)[:, width - LANES :]
        info_ref[source : source + 1, :] = tail[0:1, :]
        info_ref[sources + source : sources + source + 1, :] = tail[1:2, :]
    info_ref[...] = info_ref[...].T


def share_info(info_ref, turn, share):
    begin = lax.rem(lax.axis_index("boot") + turn, lax.axis_size("boot")) * share
    return info_ref[pl.ds(pl.multiple_of(begin, ROWS), share), :]


def scaled_rows(rows, info, sources):
    share = rows.shape[0] // sources
    blocks = [
        info[:, source : source + 1] * rows[source * share : (source + 1) * share, :]
        for source in range(sources)
    ]
    return jnp.concatenate(blocks, axis=0).astype(BF16)


def gram_sums(rows, info, scaled, sources):
    share, members = rows.shape[0] // sources, rows.shape[1]
    deps = [
        jnp.broadcast_to(info[:, sources + source : sources + source + 1], (share, LANES))
        for source in range(sources)
    ]
    left = jnp.concatenate([rows, jnp.concatenate(deps, axis=0)], axis=1).astype(BF16)
    sums = lax.dot_general(left, scaled, (((0,), (0,)), ((), ())), preferred_element_type=F32)
    return sums[0:members, :], sums[members : members + 1, :]


def gram_kernel(rows_ref, gram_ref, drive_ref, info_ref):
    members = gram_ref.shape[0]
    slot_info(rows_ref, info_ref)
    rows = slot_rows(rows_ref, members)
    sources = rows_ref.shape[0]
    info = share_info(info_ref, 0, rows.shape[0] // sources)
    gram_ref[...], drive_ref[...] = gram_sums(
        rows, info, scaled_rows(rows, info, sources), sources
    )


def own_gram(rows, members):
    sources, _, width = rows.shape
    return pl.pallas_call(
        gram_kernel,
        out_shape=(
            jax.ShapeDtypeStruct((members, members), F32),
            jax.ShapeDtypeStruct((1, members), F32),
            jax.ShapeDtypeStruct((LANES, LANES), F32),
        ),
        compiler_params=pltpu.CompilerParams(vmem_limit_bytes=16 * MEBI),
        cost_estimate=pl.CostEstimate(
            flops=4 * members * sources * ROWS * width,
            bytes_accessed=2 * sources * ROWS * width,
            transcendentals=0,
        ),
        name="own_gram",
    )(rows)


def diagonal_column(value, eye):
    size = value.shape[1]
    parts = []
    for begin in range(0, size, LANES):
        block = value[:, begin : begin + LANES]
        block = block if value.shape[0] == 1 else block[begin : begin + LANES, :]
        parts.append(jnp.sum(jnp.where(eye, block, 0.0), axis=1, keepdims=True))
    return jnp.concatenate(parts, axis=0)


def weights_kernel(*refs):
    count = (len(refs) - 7) // 2
    far_refs, blended_ref, refs = refs[:count], refs[count], refs[count + 1 :]
    gram_ref, drive_ref, own_info_ref, rows_refs = refs[0], refs[1], refs[2], refs[3:count]
    info_ref, yz_ref, yz_high, low, w_high, sems = refs[count:]
    groups, members, _ = blended_ref.shape
    sources = rows_refs[0].shape[0]
    copies = [
        pltpu.make_async_copy(far_ref, near_ref, sems.at[place])
        for place, (far_ref, near_ref) in enumerate(zip(far_refs, refs[:count]))
    ]
    for copy in reversed(copies):
        copy.start()
    for copy in reversed(copies):
        copy.wait()
    y_part, z_part = slice(0, members), slice(members, 2 * members)
    row_id = lax.broadcasted_iota(jnp.int32, (members, members), 0)
    col_id = lax.broadcasted_iota(jnp.int32, (members, members), 1)
    identity = jnp.where(row_id == col_id, 1.0, 0.0)
    eye = lax.broadcasted_iota(jnp.int32, (LANES, LANES), 0) == lax.broadcasted_iota(
        jnp.int32, (LANES, LANES), 1
    )
    dot = functools.partial(jnp.dot, preferred_element_type=F32)

    def split(chain, value):
        value = -0.5 * value
        w_high[chain] = value.astype(BF16)
        for begin in range(0, members, LANES):
            block = slice(begin, begin + LANES)
            w_high[chain, block, block] = jnp.where(eye, 0.0, value[block, block]).astype(BF16)
        return 1.5 + diagonal_column(value, eye)

    grams = [gram_ref[...]] + [jnp.zeros((members, members), F32)] * (groups - 1)
    drives = [drive_ref[...]] + [jnp.zeros((1, members), F32)] * (groups - 1)
    for chain in range(1, groups):
        slot_info(rows_refs[chain], info_ref.at[chain])
    for turn, rows_ref in enumerate(rows_refs):
        rows = slot_rows(rows_ref, members)
        share = rows.shape[0] // sources
        chains = [chain for chain in range(groups) if chain or turn]
        infos = [
            share_info(info_ref.at[chain] if chain else own_info_ref, turn, share)
            for chain in chains
        ]
        scaled = jnp.concatenate([scaled_rows(rows, info, sources) for info in infos], axis=1)
        gram, drive = gram_sums(rows, infos[0], scaled, sources)
        for place, chain in enumerate(chains):
            columns = slice(place * members, (place + 1) * members)
            grams[chain] = grams[chain] + gram[:, columns]
            drives[chain] = drives[chain] + drive[:, columns]

    frobenius = []
    for chain in range(groups):
        shifted = identity + grams[chain] / (members - 1.0)
        squares = jnp.sum(jnp.sum(shifted * shifted, axis=0, keepdims=True), axis=1, keepdims=True)
        frobenius.append(jnp.sqrt(squares))
        current = shifted / frobenius[chain]
        factor = split(chain, current)
        yz_high[chain, :, y_part] = current.astype(BF16)
        yz_ref[chain, :, z_part] = 1.5 * identity - 0.5 * current
        change = dot(w_high[chain], yz_high[chain, :, y_part])
        yz_ref[chain, :, y_part] = factor * current + change
        yz_high[chain] = yz_ref[chain].astype(BF16)

    def high_product(chain):
        return dot(yz_high[chain, :, z_part], yz_high[chain, :, y_part])

    def step(_, carry):
        factors = [split(chain, high_product(chain)) for chain in range(groups)]
        for chain in range(groups):
            value = factors[chain] * yz_ref[chain] + dot(w_high[chain], yz_high[chain])
            yz_ref[chain] = value
            yz_high[chain] = value.astype(BF16)
        return carry

    lax.fori_loop(1, NS_STEPS - 1, step, 0, unroll=True)
    for chain in range(groups):
        low[chain] = (yz_ref[chain] - yz_high[chain].astype(F32)).astype(BF16)
    factors = []
    for chain in range(groups):
        small = dot(yz_high[chain, :, z_part], low[chain, :, y_part])
        small += dot(low[chain, :, z_part], yz_high[chain, :, y_part])
        factors.append(split(chain, high_product(chain) + small))
    for chain in range(groups):
        root = factors[chain] * yz_ref[chain, :, z_part]
        root += dot(w_high[chain], yz_high[chain, :, z_part])
        root = root / jnp.sqrt(frobenius[chain])
        inner = jnp.sum(root * diagonal_column(drives[chain], eye), axis=0, keepdims=True)
        mean_weight = jnp.sum(root * diagonal_column(inner, eye), axis=0, keepdims=True)
        blended_ref[chain] = (root + mean_weight / (members - 1.0)).astype(BF16)


def patch_weights(gram, drive, info, rows):
    groups, members = len(rows), gram.shape[0]
    operands = (gram, drive, info, *rows)
    half = pltpu.VMEM((groups, members, 2 * members), BF16)
    return pl.pallas_call(
        weights_kernel,
        in_specs=[pl.BlockSpec(memory_space=pl.ANY)] * len(operands),
        out_shape=jax.ShapeDtypeStruct((groups, members, members), BF16),
        scratch_shapes=[pltpu.VMEM(operand.shape, operand.dtype) for operand in operands]
        + [
            pltpu.VMEM((groups, LANES, LANES), F32),
            pltpu.VMEM((groups, members, 2 * members), F32),
            half,
            half,
            pltpu.VMEM((groups, members, members), BF16),
            pltpu.SemaphoreType.DMA((len(operands),)),
        ],
        compiler_params=pltpu.CompilerParams(vmem_limit_bytes=64 * MEBI),
        cost_estimate=pl.CostEstimate(
            flops=80 * groups * members * members * members,
            bytes_accessed=8 * members * members,
            transcendentals=0,
        ),
        name="patch_weights",
    )(*operands)


def update_kernel(blended_ref, background_ref, analysis_ref):
    groups = blended_ref.shape[0]
    members, points = background_ref.shape
    tile = min(points, 256)
    for begin in range(0, points, tile):
        columns = slice(begin, begin + tile)
        background = background_ref[:, columns].astype(F32)
        centre = jnp.sum(background, axis=0, keepdims=True) / members
        perturb = (background - centre).astype(BF16)
        for turn in range(groups):
            update = jnp.dot(blended_ref[turn], perturb, preferred_element_type=F32)
            group = lax.rem(lax.axis_index("boot") + turn, groups)
            analysis_ref[group, :, columns] = (centre + update).astype(BF16)


def update_points(blended, background):
    groups = blended.shape[0]
    members, points = background.shape
    return pl.pallas_call(
        update_kernel,
        out_shape=jax.ShapeDtypeStruct((groups, members, points), BF16),
        compiler_params=pltpu.CompilerParams(vmem_limit_bytes=16 * MEBI),
        cost_estimate=pl.CostEstimate(
            flops=2 * groups * members * members * points,
            bytes_accessed=2 * (groups + 1) * members * points,
            transcendentals=0,
        ),
        name="update_points",
    )(blended, background)


def cut_kernel(states_ref, cut_ref):
    patches, _, share = cut_ref.shape
    region = states_ref.shape[1] // patches
    offset = lax.axis_index("boot") * share
    for patch in range(patches):
        begin = pl.multiple_of(patch * region + offset, LANES)
        cut_ref[patch] = states_ref[:, pl.ds(begin, share)]


def cut_share(states, patches, share):
    own_members = states.shape[0]
    return pl.pallas_call(
        cut_kernel,
        out_shape=jax.ShapeDtypeStruct((patches, own_members, share), BF16),
        compiler_params=pltpu.CompilerParams(vmem_limit_bytes=16 * MEBI),
        cost_estimate=pl.CostEstimate(
            flops=0, bytes_accessed=4 * patches * own_members * share, transcendentals=0
        ),
        name="cut_share",
    )(states)


def place_kernel(pieces_ref, whole_ref):
    groups, patches, _, share = pieces_ref.shape
    for patch in range(patches):
        for group in range(groups):
            begin = (patch * groups + group) * share
            whole_ref[:, begin : begin + share] = pieces_ref[group, patch]


def place_pieces(pieces):
    groups, patches, own_members, share = pieces.shape
    points = groups * patches * share
    steps = 4
    held = patches // steps
    return pl.pallas_call(
        place_kernel,
        grid=(steps,),
        in_specs=[pl.BlockSpec((groups, held, own_members, share), lambda i: (0, i, 0, 0))],
        out_specs=pl.BlockSpec((own_members, points // steps), lambda i: (0, i)),
        out_shape=jax.ShapeDtypeStruct((own_members, points), BF16),
        compiler_params=pltpu.CompilerParams(vmem_limit_bytes=16 * MEBI),
        cost_estimate=pl.CostEstimate(
            flops=0, bytes_accessed=4 * own_members * points, transcendentals=0
        ),
        name="place_pieces",
    )(pieces)


def exchange(blocks, axes="space"):
    return lax.all_to_all(blocks, axes, split_axis=0, concat_axis=0, tiled=True)


def swap_shares(own):
    groups = lax.axis_size("boot")
    return [
        lax.ppermute(own, "boot", [(g, (g - turn) % groups) for g in range(groups)])
        for turn in range(1, groups)
    ]


def local(
    background_states,
    measurement_anomaly_matrix,
    departure_vector,
    measurement_precision,
    measurement_region_targets,
    localization_factor_scaled,
    bootstrap_multiplicity,
):
    device_count = lax.axis_size("space")
    groups = lax.axis_size("boot")
    local_rows = measurement_anomaly_matrix.shape[0]
    targets_per = measurement_region_targets.shape[1]
    slot_cap = 2 * targets_per * local_rows // device_count
    slot_share = -(-slot_cap // (ROWS * groups)) * ROWS
    own_members, points = background_states.shape
    share = points // device_count // groups

    slots = pack(
        measurement_region_targets,
        localization_factor_scaled,
        bootstrap_multiplicity,
        measurement_precision,
        departure_vector,
        measurement_anomaly_matrix,
        device_count,
        slot_share,
        groups,
    )
    own_points = cut_share(background_states, device_count, share)
    own_rows, own_points = lax.optimization_barrier((exchange(slots), own_points))
    other_rows = swap_shares(own_rows)
    own_points = exchange(own_points).reshape(-1, share)

    gram, drive, info = own_gram(own_rows, measurement_anomaly_matrix.shape[1])
    blended = patch_weights(gram, drive, info, [own_rows] + other_rows)
    analysis = update_points(blended, own_points)
    analysis = exchange(analysis.reshape(-1, own_members, share), ("boot", "space"))
    return place_pieces(analysis.reshape(groups, device_count, own_members, share))


def solution(mesh):
    in_specs = (
        P("space", None),
        P("space", None),
        P("space"),
        P("space"),
        P("space", None),
        P("space", None),
        P(("boot", "space")),
    )
    out_specs = P(("boot", "space"), None)
    return jax.shard_map(local, mesh=mesh, in_specs=in_specs, out_specs=out_specs, check_vma=False)
```

```python
import functools

import jax
import jax.numpy as jnp
from jax import lax
from jax.experimental import pallas as pl
from jax.experimental.pallas import tpu as pltpu
from jax.sharding import PartitionSpec as P

NS_STEPS = 6
LANES = 128
ROWS = 8
MEBI = 1024 * 1024
F32 = jnp.float32
BF16 = jnp.bfloat16


def pack_kernel(groups, *refs):
    sources, slots_ref, fetched = refs[:6], refs[6], refs[7:13]
    info_ref, sems = refs[13:]
    run_copies(
        [
            pltpu.make_async_copy(source, target, sems.at[i])
            for i, (source, target) in enumerate(zip(sources, fetched))
        ]
    )
    targets_ref, local_ref, mult_ref, prec_ref, dep_ref, rows_ref = fetched
    patches = slots_ref.shape[0]
    count, members = rows_ref.shape
    share = (slots_ref.shape[2] - LANES) // members * ROWS
    mult = mult_ref[...].reshape(1, count).astype(F32)
    prec = prec_ref[...].reshape(1, count)
    weight = local_ref[...].astype(F32) / 1024.0 * (mult * prec)
    weight = weight.astype(BF16).astype(F32)
    dep = dep_ref[...].astype(F32).reshape(1, count)
    patch_id = lax.broadcasted_iota(jnp.int32, (patches, count), 0)
    first = patch_id == targets_ref[0:1, :]
    second = patch_id == targets_ref[1:2, :]
    named = jnp.logical_or(first, second)
    earlier = lax.broadcasted_iota(jnp.int32, (count, count), 0) < lax.broadcasted_iota(
        jnp.int32, (count, count), 1
    )
    rank = jnp.dot(
        named.astype(F32).astype(BF16), earlier.astype(F32).astype(BF16), preferred_element_type=F32
    )
    rank = jnp.where(named, rank, -1.0)
    by_patch = jnp.where(first, weight[0:1, :], jnp.where(second, weight[1:2, :], 0.0))
    slot_id = lax.broadcasted_iota(jnp.int32, (groups * share, count), 0).astype(F32)
    lane = lax.broadcasted_iota(jnp.int32, (groups * share, LANES), 1)
    info = jnp.zeros((groups * share, LANES), F32)
    for patch in range(patches):
        pick = slot_id == rank[patch : patch + 1, :]
        weight_col = jnp.sum(
            jnp.where(pick, by_patch[patch : patch + 1, :], 0.0), axis=1, keepdims=True
        )
        dep_col = jnp.sum(jnp.where(pick, dep, 0.0), axis=1, keepdims=True)
        info = jnp.where(lane == patch, weight_col, info)
        info = jnp.where(lane == patches + patch, dep_col, info)
    info_ref[...] = jnp.zeros((LANES, LANES), F32)
    info_ref[0 : groups * share, :] = info
    info = info_ref[...].T
    begin = lax.axis_index("boot") * share
    own_id = (lax.broadcasted_iota(jnp.int32, (share, count), 0) + begin).astype(F32)
    tail_id = lax.broadcasted_iota(jnp.int32, (ROWS, LANES), 0)
    picks = [
        jnp.where(own_id == rank[patch : patch + 1, :], 1.0, 0.0) for patch in range(patches)
    ]
    picked = jnp.dot(
        jnp.concatenate(picks, axis=0).astype(BF16), rows_ref[...], preferred_element_type=F32
    )
    for patch in range(patches):
        first = patch * share
        blocks = [picked[first + i : first + i + ROWS, :] for i in range(0, share, ROWS)]
        tail = jnp.where(
            tail_id == 0,
            info[patch : patch + 1, :],
            jnp.where(tail_id == 1, info[patches + patch : patches + patch + 1, :], 0.0),
        )
        slots_ref[patch] = jnp.concatenate(blocks + [tail], axis=1).astype(BF16)


def run_copies(copies):
    for copy in copies:
        copy.start()
    for copy in copies:
        copy.wait()


def pack(targets, local, mult, prec, dep, rows, patches, share, groups):
    count, members = rows.shape
    operands = (targets.T, local.T, mult, prec, dep, rows)
    return pl.pallas_call(
        functools.partial(pack_kernel, groups),
        out_shape=jax.ShapeDtypeStruct((patches, ROWS, share // ROWS * members + LANES), BF16),
        in_specs=[pl.BlockSpec(memory_space=pl.ANY)] * len(operands),
        scratch_shapes=[pltpu.VMEM(operand.shape, operand.dtype) for operand in operands]
        + [pltpu.VMEM((LANES, LANES), F32), pltpu.SemaphoreType.DMA((len(operands),))],
        compiler_params=pltpu.CompilerParams(vmem_limit_bytes=64 * MEBI),
        cost_estimate=pl.CostEstimate(
            flops=2 * patches * share * count * members,
            bytes_accessed=2 * (patches * share + count) * members,
            transcendentals=0,
        ),
        name="pack_rows",
    )(*operands)


def slot_rows(rows_ref, members):
    blocks = []
    for source in range(rows_ref.shape[0]):
        block = rows_ref[source].astype(F32)
        for begin in range(0, block.shape[1] - LANES, members):
            blocks.append(block[:, begin : begin + members])
    return jnp.concatenate(blocks, axis=0)


def slot_info(rows_ref, info_ref):
    sources, _, width = rows_ref.shape
    if 2 * sources < LANES:
        info_ref[2 * sources :, :] = jnp.zeros((LANES - 2 * sources, LANES), F32)
    for source in range(sources):
        tail = rows_ref[source].astype(F32)[:, width - LANES :]
        info_ref[source : source + 1, :] = tail[0:1, :]
        info_ref[sources + source : sources + source + 1, :] = tail[1:2, :]
    info_ref[...] = info_ref[...].T


def scaled_rows(rows, info_ref, turn, sources):
    share = rows.shape[0] // sources
    begin = lax.rem(lax.axis_index("boot") + turn, lax.axis_size("boot")) * share
    info = info_ref[pl.ds(pl.multiple_of(begin, ROWS), share), :]
    blocks, drive = [], jnp.zeros((1, rows.shape[1]), F32)
    for source in range(sources):
        block = rows[source * share : (source + 1) * share, :]
        block = (info[:, source : source + 1] * block).astype(BF16).astype(F32)
        blocks.append(block)
        dep_col = info[:, sources + source : sources + source + 1]
        drive = drive + jnp.sum(dep_col * block, axis=0, keepdims=True)
    return jnp.concatenate(blocks, axis=0).astype(BF16), drive


def gram_kernel(rows_ref, gram_ref, drive_ref, info_ref, ordered_ref, turned_ref):
    members = gram_ref.shape[0]
    slot_info(rows_ref, info_ref)
    rows = slot_rows(rows_ref, members)
    ordered_ref[...] = rows.astype(BF16)
    turned_ref[...] = rows.T.astype(BF16)
    scaled, drive_ref[...] = scaled_rows(rows, info_ref, 0, rows_ref.shape[0])
    gram_ref[...] = jnp.dot(turned_ref[...], scaled, preferred_element_type=F32)


def own_gram(rows, members):
    sources, height, width = rows.shape
    slots = sources * height * ((width - LANES) // members)
    return pl.pallas_call(
        gram_kernel,
        out_shape=(
            jax.ShapeDtypeStruct((members, members), F32),
            jax.ShapeDtypeStruct((1, members), F32),
            jax.ShapeDtypeStruct((LANES, LANES), F32),
            jax.ShapeDtypeStruct((slots, members), BF16),
            jax.ShapeDtypeStruct((members, slots), BF16),
        ),
        compiler_params=pltpu.CompilerParams(vmem_limit_bytes=16 * MEBI),
        cost_estimate=pl.CostEstimate(
            flops=4 * members * members * slots,
            bytes_accessed=6 * slots * members,
            transcendentals=0,
        ),
        name="own_gram",
    )(rows)


def diagonal_column(value, eye):
    size = value.shape[1]
    parts = []
    for begin in range(0, size, LANES):
        block = value[:, begin : begin + LANES]
        block = block if value.shape[0] == 1 else block[begin : begin + LANES, :]
        parts.append(jnp.sum(jnp.where(eye, block, 0.0), axis=1, keepdims=True))
    return jnp.concatenate(parts, axis=0)


def weights_kernel(*refs):
    gram_ref, drive_ref, own_info_ref, ordered_ref, turned_ref = refs[:5]
    rows_refs, blended_ref, info_ref = refs[5:-8], refs[-8], refs[-7]
    y_ref, z_ref, y_high, z_high, low, w_high = refs[-6:]
    groups, members, _ = blended_ref.shape
    sources = rows_refs[0].shape[0] if rows_refs else 1
    row_id = lax.broadcasted_iota(jnp.int32, (members, members), 0)
    col_id = lax.broadcasted_iota(jnp.int32, (members, members), 1)
    identity = jnp.where(row_id == col_id, 1.0, 0.0)
    eye = lax.broadcasted_iota(jnp.int32, (LANES, LANES), 0) == lax.broadcasted_iota(
        jnp.int32, (LANES, LANES), 1
    )
    dot = functools.partial(jnp.dot, preferred_element_type=F32)

    def split(chain, value):
        w_high[chain] = value.astype(BF16)
        for begin in range(0, members, LANES):
            block = slice(begin, begin + LANES)
            w_high[chain, block, block] = jnp.where(eye, 0.0, value[block, block]).astype(BF16)
        return 1.5 - 0.5 * diagonal_column(value, eye)

    grams = [gram_ref[...]] + [jnp.zeros((members, members), F32)] * (groups - 1)
    drives = [drive_ref[...]] + [jnp.zeros((1, members), F32)] * (groups - 1)
    infos = [own_info_ref] + [info_ref.at[chain] for chain in range(1, groups)]
    for chain in range(1, groups):
        slot_info(rows_refs[chain - 1], infos[chain])
    for chain in range(1, groups):
        scaled, drive = scaled_rows(ordered_ref[...].astype(F32), infos[chain], 0, sources)
        grams[chain] = grams[chain] + dot(turned_ref[...], scaled)
        drives[chain] = drives[chain] + drive
    for turn, rows_ref in enumerate(rows_refs, 1):
        rows = slot_rows(rows_ref, members)
        scaled = []
        for chain in range(groups):
            block, drive = scaled_rows(rows, infos[chain], turn, sources)
            scaled.append(block)
            drives[chain] = drives[chain] + drive
        sums = lax.dot_general(
            rows.astype(BF16),
            jnp.concatenate(scaled, axis=1),
            (((0,), (0,)), ((), ())),
            preferred_element_type=F32,
        )
        for chain in range(groups):
            columns = slice(chain * members, (chain + 1) * members)
            grams[chain] = grams[chain] + sums[:, columns]

    frobenius = []
    for chain in range(groups):
        shifted = identity + grams[chain] / (members - 1.0)
        squares = jnp.sum(jnp.sum(shifted * shifted, axis=0, keepdims=True), axis=1, keepdims=True)
        frobenius.append(jnp.sqrt(squares))
        current = shifted / frobenius[chain]
        factor = split(chain, current)
        y_high[chain] = current.astype(BF16)
        z_ref[chain] = 1.5 * identity - 0.5 * current
        y_ref[chain] = factor * current - 0.5 * dot(w_high[chain], y_high[chain])
        y_high[chain], z_high[chain] = y_ref[chain].astype(BF16), z_ref[chain].astype(BF16)

    def step(_, carry):
        factors = [split(c, dot(z_high[c], y_high[c])) for c in range(groups)]
        for chain in range(groups):
            current = factors[chain] * y_ref[chain] - 0.5 * dot(w_high[chain], y_high[chain])
            root = factors[chain] * z_ref[chain] - 0.5 * dot(w_high[chain], z_high[chain])
            y_ref[chain], z_ref[chain] = current, root
            y_high[chain], z_high[chain] = current.astype(BF16), root.astype(BF16)
        return carry

    lax.fori_loop(1, NS_STEPS - 1, step, 0, unroll=True)
    for chain in range(groups):
        low[2 * chain] = (y_ref[chain] - y_high[chain].astype(F32)).astype(BF16)
        low[2 * chain + 1] = (z_ref[chain] - z_high[chain].astype(F32)).astype(BF16)
    factors = []
    for chain in range(groups):
        small = dot(z_high[chain], low[2 * chain]) + dot(low[2 * chain + 1], y_high[chain])
        factors.append(split(chain, dot(z_high[chain], y_high[chain]) + small))
    for chain in range(groups):
        root = factors[chain] * z_ref[chain] - 0.5 * dot(w_high[chain], z_high[chain])
        root = root / jnp.sqrt(frobenius[chain])
        inner = jnp.sum(root * diagonal_column(drives[chain], eye), axis=0, keepdims=True)
        mean_weight = jnp.sum(root * diagonal_column(inner, eye), axis=0, keepdims=True)
        blended_ref[chain] = (root + mean_weight / (members - 1.0)).astype(BF16)


def patch_weights(own, other_rows):
    groups, members = len(other_rows) + 1, own[0].shape[0]
    whole = pltpu.VMEM((groups, members, members), F32)
    half = pltpu.VMEM((groups, members, members), BF16)
    return pl.pallas_call(
        weights_kernel,
        out_shape=jax.ShapeDtypeStruct((groups, members, members), BF16),
        scratch_shapes=[
            pltpu.VMEM((groups, LANES, LANES), F32),
            whole,
            whole,
            half,
            half,
            pltpu.VMEM((2 * groups, members, members), BF16),
            half,
        ],
        compiler_params=pltpu.CompilerParams(vmem_limit_bytes=(8 + 10 * groups) * MEBI),
        cost_estimate=pl.CostEstimate(
            flops=80 * groups * members * members * members,
            bytes_accessed=8 * members * members,
            transcendentals=0,
        ),
        name="patch_weights",
    )(*own, *other_rows)


def update_kernel(blended_ref, background_ref, analysis_ref):
    groups = blended_ref.shape[0]
    members, points = background_ref.shape
    tile = min(points, 256)
    for begin in range(0, points, tile):
        columns = slice(begin, begin + tile)
        background = background_ref[:, columns].astype(F32)
        centre = jnp.sum(background, axis=0, keepdims=True) / members
        perturb = (background - centre).astype(BF16)
        for turn in range(groups):
            update = jnp.dot(blended_ref[turn], perturb, preferred_element_type=F32)
            group = lax.rem(lax.axis_index("boot") + turn, groups)
            analysis_ref[group, :, columns] = (centre + update).astype(BF16)


def update_points(blended, background):
    groups = blended.shape[0]
    members, points = background.shape
    return pl.pallas_call(
        update_kernel,
        out_shape=jax.ShapeDtypeStruct((groups, members, points), BF16),
        compiler_params=pltpu.CompilerParams(vmem_limit_bytes=16 * MEBI),
        cost_estimate=pl.CostEstimate(
            flops=2 * groups * members * members * points,
            bytes_accessed=2 * (groups + 1) * members * points,
            transcendentals=0,
        ),
        name="update_points",
    )(blended, background)


def cut_kernel(states_ref, cut_ref):
    patches, _, share = cut_ref.shape
    region = states_ref.shape[1] // patches
    offset = lax.axis_index("boot") * share
    for patch in range(patches):
        begin = pl.multiple_of(patch * region + offset, LANES)
        cut_ref[patch] = states_ref[:, pl.ds(begin, share)]


def cut_share(states, patches, share):
    own_members = states.shape[0]
    return pl.pallas_call(
        cut_kernel,
        out_shape=jax.ShapeDtypeStruct((patches, own_members, share), BF16),
        compiler_params=pltpu.CompilerParams(vmem_limit_bytes=16 * MEBI),
        cost_estimate=pl.CostEstimate(
            flops=0, bytes_accessed=4 * patches * own_members * share, transcendentals=0
        ),
        name="cut_share",
    )(states)


def place_kernel(pieces_ref, whole_ref):
    groups, patches, _, share = pieces_ref.shape
    for patch in range(patches):
        for group in range(groups):
            begin = (patch * groups + group) * share
            whole_ref[:, begin : begin + share] = pieces_ref[group, patch]


def place_pieces(pieces):
    groups, patches, own_members, share = pieces.shape
    points = groups * patches * share
    return pl.pallas_call(
        place_kernel,
        out_shape=jax.ShapeDtypeStruct((own_members, points), BF16),
        compiler_params=pltpu.CompilerParams(vmem_limit_bytes=16 * MEBI),
        cost_estimate=pl.CostEstimate(
            flops=0, bytes_accessed=4 * own_members * points, transcendentals=0
        ),
        name="place_pieces",
    )(pieces)


def exchange(blocks, axes="space"):
    return lax.all_to_all(blocks, axes, split_axis=0, concat_axis=0, tiled=True)


def swap_shares(own):
    groups = lax.axis_size("boot")
    return [
        lax.ppermute(own, "boot", [(g, (g - turn) % groups) for g in range(groups)])
        for turn in range(1, groups)
    ]


def local(
    background_states,
    measurement_anomaly_matrix,
    departure_vector,
    measurement_precision,
    measurement_region_targets,
    localization_factor_scaled,
    bootstrap_multiplicity,
):
    device_count = lax.axis_size("space")
    groups = lax.axis_size("boot")
    local_rows = measurement_anomaly_matrix.shape[0]
    targets_per = measurement_region_targets.shape[1]
    slot_cap = 2 * targets_per * local_rows // device_count
    slot_share = -(-slot_cap // (ROWS * groups)) * ROWS
    own_members, points = background_states.shape
    share = points // device_count // groups

    slots = pack(
        measurement_region_targets,
        localization_factor_scaled,
        bootstrap_multiplicity,
        measurement_precision,
        departure_vector,
        measurement_anomaly_matrix,
        device_count,
        slot_share,
        groups,
    )
    own_points = cut_share(background_states, device_count, share)
    own_rows, own_points = lax.optimization_barrier((exchange(slots), own_points))
    other_rows = swap_shares(own_rows)
    own_points = exchange(own_points).reshape(-1, share)

    own = own_gram(own_rows, measurement_anomaly_matrix.shape[1])
    blended = patch_weights(own, other_rows)
    analysis = update_points(blended, own_points)
    analysis = exchange(analysis.reshape(-1, own_members, share), ("boot", "space"))
    return place_pieces(analysis.reshape(groups, device_count, own_members, share))


def solution(mesh):
    in_specs = (
        P("space", None),
        P("space", None),
        P("space"),
        P("space"),
        P("space", None),
        P("space", None),
        P(("boot", "space")),
    )
    out_specs = P(("boot", "space"), None)
    return jax.shard_map(local, mesh=mesh, in_specs=in_specs, out_specs=out_specs, check_vma=False)
```

```python
import functools

import jax
import jax.numpy as jnp
from jax import lax
from jax.experimental import pallas as pl
from jax.experimental.pallas import tpu as pltpu
from jax.sharding import PartitionSpec as P

NS_STEPS = 6
LANES = 128
ROWS = 8
MEBI = 1024 * 1024
F32 = jnp.float32
BF16 = jnp.bfloat16


def pack_kernel(groups, *refs):
    sources, slots_ref, fetched = refs[:6], refs[6], refs[7:13]
    info_ref, sems = refs[13:]
    run_copies(
        [
            pltpu.make_async_copy(source, target, sems.at[i])
            for i, (source, target) in enumerate(zip(sources, fetched))
        ]
    )
    targets_ref, local_ref, mult_ref, prec_ref, dep_ref, rows_ref = fetched
    patches = slots_ref.shape[0]
    count, members = rows_ref.shape
    share = (slots_ref.shape[2] - LANES) // members * ROWS
    mult = mult_ref[...].reshape(1, count).astype(F32)
    prec = prec_ref[...].reshape(1, count)
    weight = local_ref[...].astype(F32) / 1024.0 * (mult * prec)
    weight = weight.astype(BF16).astype(F32)
    dep = dep_ref[...].astype(F32).reshape(1, count)
    patch_id = lax.broadcasted_iota(jnp.int32, (patches, count), 0)
    first = patch_id == targets_ref[0:1, :]
    second = patch_id == targets_ref[1:2, :]
    named = jnp.logical_or(first, second)
    earlier = lax.broadcasted_iota(jnp.int32, (count, count), 0) < lax.broadcasted_iota(
        jnp.int32, (count, count), 1
    )
    rank = jnp.dot(
        named.astype(F32).astype(BF16), earlier.astype(F32).astype(BF16), preferred_element_type=F32
    )
    rank = jnp.where(named, rank, -1.0)
    by_patch = jnp.where(first, weight[0:1, :], jnp.where(second, weight[1:2, :], 0.0))
    slot_id = lax.broadcasted_iota(jnp.int32, (groups * share, count), 0).astype(F32)
    lane = lax.broadcasted_iota(jnp.int32, (groups * share, LANES), 1)
    info = jnp.zeros((groups * share, LANES), F32)
    for patch in range(patches):
        pick = slot_id == rank[patch : patch + 1, :]
        weight_col = jnp.sum(
            jnp.where(pick, by_patch[patch : patch + 1, :], 0.0), axis=1, keepdims=True
        )
        dep_col = jnp.sum(jnp.where(pick, dep, 0.0), axis=1, keepdims=True)
        info = jnp.where(lane == patch, weight_col, info)
        info = jnp.where(lane == patches + patch, dep_col, info)
    info_ref[...] = jnp.zeros((LANES, LANES), F32)
    info_ref[0 : groups * share, :] = info
    info = info_ref[...].T
    begin = lax.axis_index("boot") * share
    own_id = (lax.broadcasted_iota(jnp.int32, (share, count), 0) + begin).astype(F32)
    tail_id = lax.broadcasted_iota(jnp.int32, (ROWS, LANES), 0)
    picks = [
        jnp.where(own_id == rank[patch : patch + 1, :], 1.0, 0.0) for patch in range(patches)
    ]
    picked = jnp.dot(
        jnp.concatenate(picks, axis=0).astype(BF16), rows_ref[...], preferred_element_type=F32
    )
    for patch in range(patches):
        first = patch * share
        blocks = [picked[first + i : first + i + ROWS, :] for i in range(0, share, ROWS)]
        tail = jnp.where(
            tail_id == 0,
            info[patch : patch + 1, :],
            jnp.where(tail_id == 1, info[patches + patch : patches + patch + 1, :], 0.0),
        )
        slots_ref[patch] = jnp.concatenate(blocks + [tail], axis=1).astype(BF16)


def run_copies(copies):
    for copy in copies:
        copy.start()
    for copy in copies:
        copy.wait()


def pack(targets, local, mult, prec, dep, rows, patches, share, groups):
    count, members = rows.shape
    operands = (targets.T, local.T, mult, prec, dep, rows)
    return pl.pallas_call(
        functools.partial(pack_kernel, groups),
        out_shape=jax.ShapeDtypeStruct((patches, ROWS, share // ROWS * members + LANES), BF16),
        in_specs=[pl.BlockSpec(memory_space=pl.ANY)] * len(operands),
        scratch_shapes=[pltpu.VMEM(operand.shape, operand.dtype) for operand in operands]
        + [pltpu.VMEM((LANES, LANES), F32), pltpu.SemaphoreType.DMA((len(operands),))],
        compiler_params=pltpu.CompilerParams(vmem_limit_bytes=64 * MEBI),
        cost_estimate=pl.CostEstimate(
            flops=2 * patches * share * count * members,
            bytes_accessed=2 * (patches * share + count) * members,
            transcendentals=0,
        ),
        name="pack_rows",
    )(*operands)


def slot_rows(rows_ref, members):
    blocks = []
    for source in range(rows_ref.shape[0]):
        block = rows_ref[source].astype(F32)
        for begin in range(0, block.shape[1] - LANES, members):
            blocks.append(block[:, begin : begin + members])
    return jnp.concatenate(blocks, axis=0)


def slot_info(rows_ref, info_ref):
    sources, _, width = rows_ref.shape
    if 2 * sources < LANES:
        info_ref[2 * sources :, :] = jnp.zeros((LANES - 2 * sources, LANES), F32)
    for source in range(sources):
        tail = rows_ref[source].astype(F32)[:, width - LANES :]
        info_ref[source : source + 1, :] = tail[0:1, :]
        info_ref[sources + source : sources + source + 1, :] = tail[1:2, :]
    info_ref[...] = info_ref[...].T


def scaled_rows(rows, info_ref, turn, sources):
    share = rows.shape[0] // sources
    begin = lax.rem(lax.axis_index("boot") + turn, lax.axis_size("boot")) * share
    info = info_ref[pl.ds(pl.multiple_of(begin, ROWS), share), :]
    blocks, drive = [], jnp.zeros((1, rows.shape[1]), F32)
    for source in range(sources):
        block = rows[source * share : (source + 1) * share, :]
        block = (info[:, source : source + 1] * block).astype(BF16).astype(F32)
        blocks.append(block)
        dep_col = info[:, sources + source : sources + source + 1]
        drive = drive + jnp.sum(dep_col * block, axis=0, keepdims=True)
    return jnp.concatenate(blocks, axis=0).astype(BF16), drive


def gram_kernel(rows_ref, gram_ref, drive_ref, info_ref, ordered_ref, turned_ref):
    members = gram_ref.shape[0]
    slot_info(rows_ref, info_ref)
    rows = slot_rows(rows_ref, members)
    ordered_ref[...] = rows.astype(BF16)
    turned_ref[...] = rows.T.astype(BF16)
    scaled, drive_ref[...] = scaled_rows(rows, info_ref, 0, rows_ref.shape[0])
    gram_ref[...] = jnp.dot(turned_ref[...], scaled, preferred_element_type=F32)


def own_gram(rows, members):
    sources, height, width = rows.shape
    slots = sources * height * ((width - LANES) // members)
    return pl.pallas_call(
        gram_kernel,
        out_shape=(
            jax.ShapeDtypeStruct((members, members), F32),
            jax.ShapeDtypeStruct((1, members), F32),
            jax.ShapeDtypeStruct((LANES, LANES), F32),
            jax.ShapeDtypeStruct((slots, members), BF16),
            jax.ShapeDtypeStruct((members, slots), BF16),
        ),
        compiler_params=pltpu.CompilerParams(vmem_limit_bytes=16 * MEBI),
        cost_estimate=pl.CostEstimate(
            flops=4 * members * members * slots,
            bytes_accessed=6 * slots * members,
            transcendentals=0,
        ),
        name="own_gram",
    )(rows)


def diagonal_column(value, eye):
    size = value.shape[1]
    parts = []
    for begin in range(0, size, LANES):
        block = value[:, begin : begin + LANES]
        block = block if value.shape[0] == 1 else block[begin : begin + LANES, :]
        parts.append(jnp.sum(jnp.where(eye, block, 0.0), axis=1, keepdims=True))
    return jnp.concatenate(parts, axis=0)


def symmetric_product(left_ref, right_ref):
    half = left_ref.shape[0] // 2
    dot = functools.partial(jnp.dot, preferred_element_type=F32)
    return (
        dot(left_ref[...], right_ref[:, half:]),
        dot(left_ref[0:half, :], right_ref[:, 0:half]),
    )


def put_symmetric(ref, right, corner):
    half = corner.shape[0]
    right = right.astype(BF16)
    ref[:, half:] = right
    ref[0:half, 0:half] = corner.astype(BF16)
    ref[half:, 0:half] = right[0:half, :].T


def weights_kernel(*refs):
    gram_ref, drive_ref, own_info_ref, ordered_ref, turned_ref = refs[:5]
    groups = (len(refs) - 5) // 11
    rows_refs, blended_ref = refs[5 : 4 + groups], refs[4 + groups]
    info_refs = refs[5 + groups : 5 + 2 * groups]
    chains = [refs[5 + 2 * groups + 9 * c : 14 + 2 * groups + 9 * c] for c in range(groups)]
    members = gram_ref.shape[0]
    half = members // 2
    sources = rows_refs[0].shape[0] if rows_refs else 1
    row_id = lax.broadcasted_iota(jnp.int32, (members, members), 0)
    col_id = lax.broadcasted_iota(jnp.int32, (members, members), 1)
    identity = jnp.where(row_id == col_id, 1.0, 0.0)
    eye = lax.broadcasted_iota(jnp.int32, (LANES, LANES), 0) == lax.broadcasted_iota(
        jnp.int32, (LANES, LANES), 1
    )
    dot = functools.partial(jnp.dot, preferred_element_type=F32)

    def split(w_high, right, corner):
        right, corner = -0.5 * right, -0.5 * corner
        put_symmetric(w_high, right, corner)
        for begin in range(0, half, LANES):
            block = slice(begin, begin + LANES)
            for first, part in ((0, corner), (half, right[half:, :])):
                place = slice(first + begin, first + begin + LANES)
                w_high[place, place] = jnp.where(eye, 0.0, part[block, block]).astype(BF16)
        return 1.5 + jnp.concatenate(
            [diagonal_column(corner, eye), diagonal_column(right[half:, :], eye)], axis=0
        )

    grams = [gram_ref[...]] + [jnp.zeros((members, members), F32)] * (groups - 1)
    drives = [drive_ref[...]] + [jnp.zeros((1, members), F32)] * (groups - 1)
    infos = [own_info_ref] + list(info_refs[1:])
    for chain in range(1, groups):
        slot_info(rows_refs[chain - 1], infos[chain])
    for chain in range(1, groups):
        scaled, drive = scaled_rows(ordered_ref[...].astype(F32), infos[chain], 0, sources)
        grams[chain] = grams[chain] + dot(turned_ref[...], scaled)
        drives[chain] = drives[chain] + drive
    for turn, rows_ref in enumerate(rows_refs, 1):
        rows = slot_rows(rows_ref, members)
        scaled = []
        for chain in range(groups):
            block, drive = scaled_rows(rows, infos[chain], turn, sources)
            scaled.append(block)
            drives[chain] = drives[chain] + drive
        sums = lax.dot_general(
            rows.astype(BF16),
            jnp.concatenate(scaled, axis=1),
            (((0,), (0,)), ((), ())),
            preferred_element_type=F32,
        )
        for chain in range(groups):
            columns = slice(chain * members, (chain + 1) * members)
            grams[chain] = grams[chain] + sums[:, columns]

    frobenius = []
    for chain, (y_right, y_corner, z_right, z_corner, y_high, z_high, _, _, w_high) in enumerate(
        chains
    ):
        shifted = identity + grams[chain] / (members - 1.0)
        squares = jnp.sum(jnp.sum(shifted * shifted, axis=0, keepdims=True), axis=1, keepdims=True)
        frobenius.append(jnp.sqrt(squares))
        current = shifted / frobenius[chain]
        right, corner = current[:, half:], current[0:half, 0:half]
        factor = split(w_high, right, corner)
        put_symmetric(y_high, right, corner)
        z_right[...] = 1.5 * identity[:, half:] - 0.5 * right
        z_corner[...] = 1.5 * identity[0:half, 0:half] - 0.5 * corner
        change_right, change_corner = symmetric_product(w_high, y_high)
        y_right[...] = factor * right + change_right
        y_corner[...] = factor[0:half, :] * corner + change_corner
        put_symmetric(y_high, y_right[...], y_corner[...])
        put_symmetric(z_high, z_right[...], z_corner[...])

    def step(_, carry):
        factors = [
            split(chain[8], *symmetric_product(chain[5], chain[4])) for chain in chains
        ]
        for factor, chain in zip(factors, chains):
            w_high = chain[8]
            for right, corner, high in (
                (chain[0], chain[1], chain[4]),
                (chain[2], chain[3], chain[5]),
            ):
                change_right, change_corner = symmetric_product(w_high, high)
                new_right = factor * right[...] + change_right
                new_corner = factor[0:half, :] * corner[...] + change_corner
                right[...], corner[...] = new_right, new_corner
                put_symmetric(high, new_right, new_corner)
        return carry

    lax.fori_loop(1, NS_STEPS - 1, step, 0)
    factors = []
    for y_right, y_corner, z_right, z_corner, y_high, z_high, y_low, z_low, w_high in chains:
        for right, corner, high, low in (
            (y_right, y_corner, y_high, y_low),
            (z_right, z_corner, z_high, z_low),
        ):
            put_symmetric(
                low,
                right[...] - high[:, half:].astype(F32),
                corner[...] - high[0:half, 0:half].astype(F32),
            )
        large = symmetric_product(z_high, y_high)
        small = zip(symmetric_product(z_high, y_low), symmetric_product(z_low, y_high))
        factors.append(
            split(w_high, *[first + (one + two) for first, (one, two) in zip(large, small)])
        )
    for chain, (_, _, z_right, z_corner, _, z_high, _, _, w_high) in enumerate(chains):
        right, corner = symmetric_product(w_high, z_high)
        right = factors[chain] * z_right[...] + right
        corner = factors[chain][0:half, :] * z_corner[...] + corner
        left = jnp.concatenate([corner, right[0:half, :].T], axis=0)
        root = jnp.concatenate([left, right], axis=1) / jnp.sqrt(frobenius[chain])
        inner = jnp.sum(root * diagonal_column(drives[chain], eye), axis=0, keepdims=True)
        mean_weight = jnp.sum(root * diagonal_column(inner, eye), axis=0, keepdims=True)
        blended_ref[chain] = (root + mean_weight / (members - 1.0)).astype(BF16)


def patch_weights(own, other_rows):
    groups, members = len(other_rows) + 1, own[0].shape[0]
    half = members // 2
    right, corner = pltpu.VMEM((members, half), F32), pltpu.VMEM((half, half), F32)
    chain = [right, corner] * 2 + [pltpu.VMEM((members, members), BF16)] * 5
    return pl.pallas_call(
        weights_kernel,
        out_shape=jax.ShapeDtypeStruct((groups, members, members), BF16),
        scratch_shapes=[pltpu.VMEM((LANES, LANES), F32)] * groups + chain * groups,
        compiler_params=pltpu.CompilerParams(vmem_limit_bytes=(8 + 10 * groups) * MEBI),
        cost_estimate=pl.CostEstimate(
            flops=80 * groups * members * members * members,
            bytes_accessed=8 * members * members,
            transcendentals=0,
        ),
        name="patch_weights",
    )(*own, *other_rows)


def update_kernel(blended_ref, background_ref, analysis_ref):
    groups = blended_ref.shape[0]
    members, points = background_ref.shape
    tile = min(points, 256)
    for begin in range(0, points, tile):
        columns = slice(begin, begin + tile)
        background = background_ref[:, columns].astype(F32)
        centre = jnp.sum(background, axis=0, keepdims=True) / members
        perturb = (background - centre).astype(BF16)
        for turn in range(groups):
            update = jnp.dot(blended_ref[turn], perturb, preferred_element_type=F32)
            group = lax.rem(lax.axis_index("boot") + turn, groups)
            analysis_ref[group, :, columns] = (centre + update).astype(BF16)


def update_points(blended, background):
    groups = blended.shape[0]
    members, points = background.shape
    return pl.pallas_call(
        update_kernel,
        out_shape=jax.ShapeDtypeStruct((groups, members, points), BF16),
        compiler_params=pltpu.CompilerParams(vmem_limit_bytes=16 * MEBI),
        cost_estimate=pl.CostEstimate(
            flops=2 * groups * members * members * points,
            bytes_accessed=2 * (groups + 1) * members * points,
            transcendentals=0,
        ),
        name="update_points",
    )(blended, background)


def cut_kernel(states_ref, cut_ref):
    patches, _, share = cut_ref.shape
    region = states_ref.shape[1] // patches
    offset = lax.axis_index("boot") * share
    for patch in range(patches):
        begin = pl.multiple_of(patch * region + offset, LANES)
        cut_ref[patch] = states_ref[:, pl.ds(begin, share)]


def cut_share(states, patches, share):
    own_members = states.shape[0]
    return pl.pallas_call(
        cut_kernel,
        out_shape=jax.ShapeDtypeStruct((patches, own_members, share), BF16),
        compiler_params=pltpu.CompilerParams(vmem_limit_bytes=16 * MEBI),
        cost_estimate=pl.CostEstimate(
            flops=0, bytes_accessed=4 * patches * own_members * share, transcendentals=0
        ),
        name="cut_share",
    )(states)


def place_kernel(pieces_ref, whole_ref):
    groups, patches, _, share = pieces_ref.shape
    for patch in range(patches):
        for group in range(groups):
            begin = (patch * groups + group) * share
            whole_ref[:, begin : begin + share] = pieces_ref[group, patch]


def place_pieces(pieces):
    groups, patches, own_members, share = pieces.shape
    points = groups * patches * share
    return pl.pallas_call(
        place_kernel,
        out_shape=jax.ShapeDtypeStruct((own_members, points), BF16),
        compiler_params=pltpu.CompilerParams(vmem_limit_bytes=16 * MEBI),
        cost_estimate=pl.CostEstimate(
            flops=0, bytes_accessed=4 * own_members * points, transcendentals=0
        ),
        name="place_pieces",
    )(pieces)


def exchange(blocks, axes="space"):
    return lax.all_to_all(blocks, axes, split_axis=0, concat_axis=0, tiled=True)


def swap_shares(own):
    groups = lax.axis_size("boot")
    return [
        lax.ppermute(own, "boot", [(g, (g - turn) % groups) for g in range(groups)])
        for turn in range(1, groups)
    ]


def local(
    background_states,
    measurement_anomaly_matrix,
    departure_vector,
    measurement_precision,
    measurement_region_targets,
    localization_factor_scaled,
    bootstrap_multiplicity,
):
    device_count = lax.axis_size("space")
    groups = lax.axis_size("boot")
    local_rows = measurement_anomaly_matrix.shape[0]
    targets_per = measurement_region_targets.shape[1]
    slot_cap = 2 * targets_per * local_rows // device_count
    slot_share = -(-slot_cap // (ROWS * groups)) * ROWS
    own_members, points = background_states.shape
    share = points // device_count // groups

    slots = pack(
        measurement_region_targets,
        localization_factor_scaled,
        bootstrap_multiplicity,
        measurement_precision,
        departure_vector,
        measurement_anomaly_matrix,
        device_count,
        slot_share,
        groups,
    )
    own_points = cut_share(background_states, device_count, share)
    own_rows, own_points = lax.optimization_barrier((exchange(slots), own_points))
    other_rows = swap_shares(own_rows)
    own_points = exchange(own_points).reshape(-1, share)

    own = own_gram(own_rows, measurement_anomaly_matrix.shape[1])
    blended = patch_weights(own, other_rows)
    analysis = update_points(blended, own_points)
    analysis = exchange(analysis.reshape(-1, own_members, share), ("boot", "space"))
    return place_pieces(analysis.reshape(groups, device_count, own_members, share))


def solution(mesh):
    in_specs = (
        P("space", None),
        P("space", None),
        P("space"),
        P("space"),
        P("space", None),
        P("space", None),
        P(("boot", "space")),
    )
    out_specs = P(("boot", "space"), None)
    return jax.shard_map(local, mesh=mesh, in_specs=in_specs, out_specs=out_specs, check_vma=False)
```

```python
import functools

import jax
import jax.numpy as jnp
from jax import lax
from jax.experimental import pallas as pl
from jax.experimental.pallas import tpu as pltpu
from jax.sharding import PartitionSpec as P

NS_STEPS = 6
LANES = 128
ROWS = 8
MEBI = 1024 * 1024
F32 = jnp.float32
BF16 = jnp.bfloat16


def pack_kernel(groups, *refs):
    sources, slots_ref, fetched = refs[:6], refs[6], refs[7:13]
    info_ref, sems = refs[13:]
    run_copies(
        [
            pltpu.make_async_copy(source, target, sems.at[i])
            for i, (source, target) in enumerate(zip(sources, fetched))
        ]
    )
    targets_ref, local_ref, mult_ref, prec_ref, dep_ref, rows_ref = fetched
    patches = slots_ref.shape[0]
    count, members = rows_ref.shape
    share = (slots_ref.shape[2] - LANES) // members * ROWS
    mult = mult_ref[...].reshape(1, count).astype(F32)
    prec = prec_ref[...].reshape(1, count)
    weight = local_ref[...].astype(F32) / 1024.0 * (mult * prec)
    weight = weight.astype(BF16).astype(F32)
    dep = dep_ref[...].astype(F32).reshape(1, count)
    patch_id = lax.broadcasted_iota(jnp.int32, (patches, count), 0)
    first = patch_id == targets_ref[0:1, :]
    second = patch_id == targets_ref[1:2, :]
    named = jnp.logical_or(first, second)
    earlier = lax.broadcasted_iota(jnp.int32, (count, count), 0) < lax.broadcasted_iota(
        jnp.int32, (count, count), 1
    )
    rank = jnp.dot(
        named.astype(F32).astype(BF16), earlier.astype(F32).astype(BF16), preferred_element_type=F32
    )
    rank = jnp.where(named, rank, -1.0)
    by_patch = jnp.where(first, weight[0:1, :], jnp.where(second, weight[1:2, :], 0.0))
    slot_id = lax.broadcasted_iota(jnp.int32, (groups * share, count), 0).astype(F32)
    lane = lax.broadcasted_iota(jnp.int32, (groups * share, LANES), 1)
    info = jnp.zeros((groups * share, LANES), F32)
    for patch in range(patches):
        pick = slot_id == rank[patch : patch + 1, :]
        weight_col = jnp.sum(
            jnp.where(pick, by_patch[patch : patch + 1, :], 0.0), axis=1, keepdims=True
        )
        dep_col = jnp.sum(jnp.where(pick, dep, 0.0), axis=1, keepdims=True)
        info = jnp.where(lane == patch, weight_col, info)
        info = jnp.where(lane == patches + patch, dep_col, info)
    info_ref[...] = jnp.zeros((LANES, LANES), F32)
    info_ref[0 : groups * share, :] = info
    info = info_ref[...].T
    begin = lax.axis_index("boot") * share
    own_id = (lax.broadcasted_iota(jnp.int32, (share, count), 0) + begin).astype(F32)
    tail_id = lax.broadcasted_iota(jnp.int32, (ROWS, LANES), 0)
    picks = [
        jnp.where(own_id == rank[patch : patch + 1, :], 1.0, 0.0) for patch in range(patches)
    ]
    picked = jnp.dot(
        jnp.concatenate(picks, axis=0).astype(BF16), rows_ref[...], preferred_element_type=F32
    )
    for patch in range(patches):
        first = patch * share
        blocks = [picked[first + i : first + i + ROWS, :] for i in range(0, share, ROWS)]
        tail = jnp.where(
            tail_id == 0,
            info[patch : patch + 1, :],
            jnp.where(tail_id == 1, info[patches + patch : patches + patch + 1, :], 0.0),
        )
        slots_ref[patch] = jnp.concatenate(blocks + [tail], axis=1).astype(BF16)


def run_copies(copies):
    for copy in copies:
        copy.start()
    for copy in copies:
        copy.wait()


def pack(targets, local, mult, prec, dep, rows, patches, share, groups):
    count, members = rows.shape
    operands = (targets.T, local.T, mult, prec, dep, rows)
    return pl.pallas_call(
        functools.partial(pack_kernel, groups),
        out_shape=jax.ShapeDtypeStruct((patches, ROWS, share // ROWS * members + LANES), BF16),
        in_specs=[pl.BlockSpec(memory_space=pl.ANY)] * len(operands),
        scratch_shapes=[pltpu.VMEM(operand.shape, operand.dtype) for operand in operands]
        + [pltpu.VMEM((LANES, LANES), F32), pltpu.SemaphoreType.DMA((len(operands),))],
        compiler_params=pltpu.CompilerParams(vmem_limit_bytes=64 * MEBI),
        cost_estimate=pl.CostEstimate(
            flops=2 * patches * share * count * members,
            bytes_accessed=2 * (patches * share + count) * members,
            transcendentals=0,
        ),
        name="pack_rows",
    )(*operands)


def slot_rows(rows_ref, members):
    blocks = []
    for source in range(rows_ref.shape[0]):
        block = rows_ref[source].astype(F32)
        for begin in range(0, block.shape[1] - LANES, members):
            blocks.append(block[:, begin : begin + members])
    return jnp.concatenate(blocks, axis=0)


def slot_info(rows_ref, info_ref):
    sources, _, width = rows_ref.shape
    if 2 * sources < LANES:
        info_ref[2 * sources :, :] = jnp.zeros((LANES - 2 * sources, LANES), F32)
    for source in range(sources):
        tail = rows_ref[source].astype(F32)[:, width - LANES :]
        info_ref[source : source + 1, :] = tail[0:1, :]
        info_ref[sources + source : sources + source + 1, :] = tail[1:2, :]
    info_ref[...] = info_ref[...].T


def scaled_rows(rows, info_ref, turn, sources):
    share = rows.shape[0] // sources
    begin = lax.rem(lax.axis_index("boot") + turn, lax.axis_size("boot")) * share
    info = info_ref[pl.ds(pl.multiple_of(begin, ROWS), share), :]
    blocks, drive = [], jnp.zeros((1, rows.shape[1]), F32)
    for source in range(sources):
        block = rows[source * share : (source + 1) * share, :]
        block = (info[:, source : source + 1] * block).astype(BF16).astype(F32)
        blocks.append(block)
        dep_col = info[:, sources + source : sources + source + 1]
        drive = drive + jnp.sum(dep_col * block, axis=0, keepdims=True)
    return jnp.concatenate(blocks, axis=0).astype(BF16), drive


def gram_kernel(rows_ref, gram_ref, drive_ref, info_ref, ordered_ref, turned_ref):
    members = gram_ref.shape[0]
    slot_info(rows_ref, info_ref)
    rows = slot_rows(rows_ref, members)
    ordered_ref[...] = rows.astype(BF16)
    turned_ref[...] = rows.T.astype(BF16)
    scaled, drive_ref[...] = scaled_rows(rows, info_ref, 0, rows_ref.shape[0])
    gram_ref[...] = jnp.dot(turned_ref[...], scaled, preferred_element_type=F32)


def own_gram(rows, members):
    sources, height, width = rows.shape
    slots = sources * height * ((width - LANES) // members)
    return pl.pallas_call(
        gram_kernel,
        out_shape=(
            jax.ShapeDtypeStruct((members, members), F32),
            jax.ShapeDtypeStruct((1, members), F32),
            jax.ShapeDtypeStruct((LANES, LANES), F32),
            jax.ShapeDtypeStruct((slots, members), BF16),
            jax.ShapeDtypeStruct((members, slots), BF16),
        ),
        compiler_params=pltpu.CompilerParams(vmem_limit_bytes=16 * MEBI),
        cost_estimate=pl.CostEstimate(
            flops=4 * members * members * slots,
            bytes_accessed=6 * slots * members,
            transcendentals=0,
        ),
        name="own_gram",
    )(rows)


def diagonal_column(value, eye):
    size = value.shape[1]
    parts = []
    for begin in range(0, size, LANES):
        block = value[:, begin : begin + LANES]
        block = block if value.shape[0] == 1 else block[begin : begin + LANES, :]
        parts.append(jnp.sum(jnp.where(eye, block, 0.0), axis=1, keepdims=True))
    return jnp.concatenate(parts, axis=0)


def symmetric_product(left_ref, right_ref):
    half = left_ref.shape[0] // 2
    dot = functools.partial(jnp.dot, preferred_element_type=F32)
    return (
        dot(left_ref[...], right_ref[:, half:]),
        dot(left_ref[0:half, :], right_ref[:, 0:half]),
    )


def put_symmetric(ref, right, corner):
    half = corner.shape[0]
    right = right.astype(BF16)
    ref[:, half:] = right
    ref[0:half, 0:half] = corner.astype(BF16)
    ref[half:, 0:half] = right[0:half, :].T


def weights_kernel(*refs):
    gram_ref, drive_ref, own_info_ref, ordered_ref, turned_ref = refs[:5]
    groups = (len(refs) - 5) // 11
    rows_refs, blended_ref = refs[5 : 4 + groups], refs[4 + groups]
    info_refs = refs[5 + groups : 5 + 2 * groups]
    chains = [refs[5 + 2 * groups + 9 * c : 14 + 2 * groups + 9 * c] for c in range(groups)]
    members = gram_ref.shape[0]
    half = members // 2
    sources = rows_refs[0].shape[0] if rows_refs else 1
    row_id = lax.broadcasted_iota(jnp.int32, (members, members), 0)
    col_id = lax.broadcasted_iota(jnp.int32, (members, members), 1)
    identity = jnp.where(row_id == col_id, 1.0, 0.0)
    eye = lax.broadcasted_iota(jnp.int32, (LANES, LANES), 0) == lax.broadcasted_iota(
        jnp.int32, (LANES, LANES), 1
    )
    dot = functools.partial(jnp.dot, preferred_element_type=F32)

    def split(w_high, right, corner):
        put_symmetric(w_high, right, corner)
        diagonal = []
        for first, part in ((0, corner), (half, right[half:, :])):
            for begin in range(0, half, LANES):
                block = part[begin : begin + LANES, begin : begin + LANES]
                place = slice(first + begin, first + begin + LANES)
                w_high[place, place] = jnp.where(eye, 0.0, block).astype(BF16)
                diagonal.append(jnp.sum(jnp.where(eye, block, 0.0), axis=0, keepdims=True))
        return 1.5 + jnp.concatenate(diagonal, axis=1)

    def advance(factor, w_high, right, corner, high):
        change_right, change_corner = symmetric_product(high, w_high)
        return (
            factor[:, half:] * right + change_right,
            factor[:, 0:half] * corner + change_corner,
        )

    grams = [gram_ref[...]] + [jnp.zeros((members, members), F32)] * (groups - 1)
    drives = [drive_ref[...]] + [jnp.zeros((1, members), F32)] * (groups - 1)
    infos = [own_info_ref] + list(info_refs[1:])
    for chain in range(1, groups):
        slot_info(rows_refs[chain - 1], infos[chain])
    for chain in range(1, groups):
        scaled, drive = scaled_rows(ordered_ref[...].astype(F32), infos[chain], 0, sources)
        grams[chain] = grams[chain] + dot(turned_ref[...], scaled)
        drives[chain] = drives[chain] + drive
    for turn, rows_ref in enumerate(rows_refs, 1):
        rows = slot_rows(rows_ref, members)
        scaled = []
        for chain in range(groups):
            block, drive = scaled_rows(rows, infos[chain], turn, sources)
            scaled.append(block)
            drives[chain] = drives[chain] + drive
        sums = lax.dot_general(
            rows.astype(BF16),
            jnp.concatenate(scaled, axis=1),
            (((0,), (0,)), ((), ())),
            preferred_element_type=F32,
        )
        for chain in range(groups):
            columns = slice(chain * members, (chain + 1) * members)
            grams[chain] = grams[chain] + sums[:, columns]

    frobenius = []
    for chain, (y_right, y_corner, z_right, z_corner, y_high, z_high, _, _, w_high) in enumerate(
        chains
    ):
        shifted = identity + grams[chain] / (members - 1.0)
        squares = jnp.sum(jnp.sum(shifted * shifted, axis=0, keepdims=True), axis=1, keepdims=True)
        frobenius.append(jnp.sqrt(squares))
        current = shifted / frobenius[chain]
        right, corner = current[:, half:], current[0:half, 0:half]
        factor = split(w_high, -0.5 * right, -0.5 * corner)
        put_symmetric(y_high, right, corner)
        y_right[...], y_corner[...] = advance(factor, w_high, right, corner, y_high)
        z_right[...] = 0.25 * right - 0.75 * identity[:, half:]
        z_corner[...] = 0.25 * corner - 0.75 * identity[0:half, 0:half]
        put_symmetric(y_high, y_right[...], y_corner[...])
        put_symmetric(z_high, z_right[...], z_corner[...])

    def step(_, carry):
        factors = [
            split(chain[8], *symmetric_product(chain[5], chain[4])) for chain in chains
        ]
        for factor, chain in zip(factors, chains):
            for right, corner, high in (
                (chain[0], chain[1], chain[4]),
                (chain[2], chain[3], chain[5]),
            ):
                new_right, new_corner = advance(factor, chain[8], right[...], corner[...], high)
                right[...], corner[...] = new_right, new_corner
                put_symmetric(high, new_right, new_corner)
        return carry

    lax.fori_loop(1, NS_STEPS - 1, step, 0)
    factors = []
    for y_right, y_corner, z_right, z_corner, y_high, z_high, y_low, z_low, w_high in chains:
        for right, corner, high, low in (
            (y_right, y_corner, y_high, y_low),
            (z_right, z_corner, z_high, z_low),
        ):
            put_symmetric(
                low,
                right[...] - high[:, half:].astype(F32),
                corner[...] - high[0:half, 0:half].astype(F32),
            )
        large = symmetric_product(z_high, y_high)
        small = zip(symmetric_product(z_high, y_low), symmetric_product(z_low, y_high))
        factors.append(
            split(w_high, *[first + (one + two) for first, (one, two) in zip(large, small)])
        )
    for chain, (_, _, z_right, z_corner, _, z_high, _, _, w_high) in enumerate(chains):
        right, corner = advance(factors[chain], w_high, z_right[...], z_corner[...], z_high)
        left = jnp.concatenate([corner, right[0:half, :].T], axis=0)
        root = jnp.concatenate([left, right], axis=1) * (-2.0 / jnp.sqrt(frobenius[chain]))
        inner = jnp.sum(root * diagonal_column(drives[chain], eye), axis=0, keepdims=True)
        mean_weight = jnp.sum(root * diagonal_column(inner, eye), axis=0, keepdims=True)
        blended_ref[chain] = (root + mean_weight / (members - 1.0)).astype(BF16)


def patch_weights(own, other_rows):
    groups, members = len(other_rows) + 1, own[0].shape[0]
    half = members // 2
    right, corner = pltpu.VMEM((members, half), F32), pltpu.VMEM((half, half), F32)
    chain = [right, corner] * 2 + [pltpu.VMEM((members, members), BF16)] * 5
    return pl.pallas_call(
        weights_kernel,
        out_shape=jax.ShapeDtypeStruct((groups, members, members), BF16),
        scratch_shapes=[pltpu.VMEM((LANES, LANES), F32)] * groups + chain * groups,
        compiler_params=pltpu.CompilerParams(vmem_limit_bytes=(8 + 10 * groups) * MEBI),
        cost_estimate=pl.CostEstimate(
            flops=80 * groups * members * members * members,
            bytes_accessed=8 * members * members,
            transcendentals=0,
        ),
        name="patch_weights",
    )(*own, *other_rows)


def update_kernel(blended_ref, background_ref, analysis_ref):
    groups = blended_ref.shape[0]
    members, points = background_ref.shape
    tile = min(points, 256)
    for begin in range(0, points, tile):
        columns = slice(begin, begin + tile)
        background = background_ref[:, columns].astype(F32)
        centre = jnp.sum(background, axis=0, keepdims=True) / members
        perturb = (background - centre).astype(BF16)
        for turn in range(groups):
            update = jnp.dot(blended_ref[turn], perturb, preferred_element_type=F32)
            group = lax.rem(lax.axis_index("boot") + turn, groups)
            analysis_ref[group, :, columns] = (centre + update).astype(BF16)


def update_points(blended, background):
    groups = blended.shape[0]
    members, points = background.shape
    return pl.pallas_call(
        update_kernel,
        out_shape=jax.ShapeDtypeStruct((groups, members, points), BF16),
        compiler_params=pltpu.CompilerParams(vmem_limit_bytes=16 * MEBI),
        cost_estimate=pl.CostEstimate(
            flops=2 * groups * members * members * points,
            bytes_accessed=2 * (groups + 1) * members * points,
            transcendentals=0,
        ),
        name="update_points",
    )(blended, background)


def cut_kernel(states_ref, cut_ref):
    patches, _, share = cut_ref.shape
    region = states_ref.shape[1] // patches
    offset = lax.axis_index("boot") * share
    for patch in range(patches):
        begin = pl.multiple_of(patch * region + offset, LANES)
        cut_ref[patch] = states_ref[:, pl.ds(begin, share)]


def cut_share(states, patches, share):
    own_members = states.shape[0]
    return pl.pallas_call(
        cut_kernel,
        out_shape=jax.ShapeDtypeStruct((patches, own_members, share), BF16),
        compiler_params=pltpu.CompilerParams(vmem_limit_bytes=16 * MEBI),
        cost_estimate=pl.CostEstimate(
            flops=0, bytes_accessed=4 * patches * own_members * share, transcendentals=0
        ),
        name="cut_share",
    )(states)


def place_kernel(pieces_ref, whole_ref, sems):
    groups, patches, _, share = pieces_ref.shape
    copies = []
    for group in range(groups):
        for patch in range(patches):
            begin = (patch * groups + group) * share
            copies.append(
                pltpu.make_async_copy(
                    pieces_ref.at[group, patch],
                    whole_ref.at[:, begin : begin + share],
                    sems.at[group, patch],
                )
            )
    for copy in copies:
        copy.start()
    for copy in copies:
        copy.wait()


def place_pieces(pieces):
    groups, patches, own_members, share = pieces.shape
    points = groups * patches * share
    return pl.pallas_call(
        place_kernel,
        in_specs=[pl.BlockSpec(memory_space=pltpu.VMEM)],
        out_specs=pl.BlockSpec(memory_space=pl.ANY),
        out_shape=jax.ShapeDtypeStruct((own_members, points), BF16),
        scratch_shapes=[pltpu.SemaphoreType.DMA((groups, patches))],
        compiler_params=pltpu.CompilerParams(vmem_limit_bytes=16 * MEBI),
        cost_estimate=pl.CostEstimate(
            flops=0, bytes_accessed=4 * own_members * points, transcendentals=0
        ),
        name="place_pieces",
    )(pieces)


def exchange(blocks, axes="space"):
    return lax.all_to_all(blocks, axes, split_axis=0, concat_axis=0, tiled=True)


def swap_shares(own):
    groups = lax.axis_size("boot")
    return [
        lax.ppermute(own, "boot", [(g, (g - turn) % groups) for g in range(groups)])
        for turn in range(1, groups)
    ]


def local(
    background_states,
    measurement_anomaly_matrix,
    departure_vector,
    measurement_precision,
    measurement_region_targets,
    localization_factor_scaled,
    bootstrap_multiplicity,
):
    device_count = lax.axis_size("space")
    groups = lax.axis_size("boot")
    local_rows = measurement_anomaly_matrix.shape[0]
    targets_per = measurement_region_targets.shape[1]
    slot_cap = 2 * targets_per * local_rows // device_count
    slot_share = -(-slot_cap // (ROWS * groups)) * ROWS
    own_members, points = background_states.shape
    share = points // device_count // groups

    slots = pack(
        measurement_region_targets,
        localization_factor_scaled,
        bootstrap_multiplicity,
        measurement_precision,
        departure_vector,
        measurement_anomaly_matrix,
        device_count,
        slot_share,
        groups,
    )
    own_points = cut_share(background_states, device_count, share)
    own_rows, own_points = lax.optimization_barrier((exchange(slots), own_points))
    other_rows = swap_shares(own_rows)
    own_points = exchange(own_points).reshape(-1, share)

    own = own_gram(own_rows, measurement_anomaly_matrix.shape[1])
    blended = patch_weights(own, other_rows)
    analysis = update_points(blended, own_points)
    analysis = exchange(analysis.reshape(-1, own_members, share), ("boot", "space"))
    return place_pieces(analysis.reshape(groups, device_count, own_members, share))


def solution(mesh):
    in_specs = (
        P("space", None),
        P("space", None),
        P("space"),
        P("space"),
        P("space", None),
        P("space", None),
        P(("boot", "space")),
    )
    out_specs = P(("boot", "space"), None)
    return jax.shard_map(local, mesh=mesh, in_specs=in_specs, out_specs=out_specs, check_vma=False)
```

```python
import functools

import jax
import jax.numpy as jnp
from jax import lax
from jax.experimental import pallas as pl
from jax.experimental.pallas import tpu as pltpu
from jax.sharding import PartitionSpec as P

NS_STEPS = 6
LANES = 128
ROWS = 8
MEBI = 1024 * 1024
F32 = jnp.float32
BF16 = jnp.bfloat16


def pack_kernel(groups, *refs):
    sources, slots_ref, fetched = refs[:6], refs[6], refs[7:13]
    block_ref, tail_ref, info_ref, sems = refs[13:]
    copies = [
        pltpu.make_async_copy(source, target, sems.at[i])
        for i, (source, target) in enumerate(zip(sources, fetched))
    ]
    for copy in copies:
        copy.start()
    for copy in copies[:-1]:
        copy.wait()
    targets_ref, local_ref, mult_ref, prec_ref, dep_ref, rows_ref = fetched
    patches, _, width = block_ref.shape
    count, members = rows_ref.shape
    share = width // members * ROWS
    patch_id = lax.broadcasted_iota(jnp.int32, (patches, count), 0)
    first = patch_id == targets_ref[0:1, :]
    second = patch_id == targets_ref[1:2, :]
    named = jnp.logical_or(first, second)
    earlier = lax.broadcasted_iota(jnp.int32, (count, count), 0) < lax.broadcasted_iota(
        jnp.int32, (count, count), 1
    )
    rank = jnp.dot(
        named.astype(F32).astype(BF16), earlier.astype(F32).astype(BF16), preferred_element_type=F32
    )
    rank = jnp.where(named, rank, -1.0)

    begin = lax.axis_index("boot") * share
    own_id = (lax.broadcasted_iota(jnp.int32, (share, count), 0) + begin).astype(F32)
    picks = [
        jnp.where(own_id == rank[patch : patch + 1, :], 1.0, 0.0) for patch in range(patches)
    ]
    picks = jnp.concatenate(picks, axis=0).astype(BF16)
    copies[-1].wait()
    picked = jnp.dot(picks, rows_ref[...], preferred_element_type=F32)
    for patch in range(patches):
        place = patch * share
        blocks = [picked[place + i : place + i + ROWS, :] for i in range(0, share, ROWS)]
        block_ref[patch] = jnp.concatenate(blocks, axis=1).astype(BF16)
    blocks_out = pltpu.make_async_copy(block_ref, slots_ref.at[:, :, 0:width], sems.at[6])
    blocks_out.start()

    mult = mult_ref[...].reshape(1, count).astype(F32)
    prec = prec_ref[...].reshape(1, count)
    weight = local_ref[...].astype(F32) / 1024.0 * (mult * prec)
    weight = weight.astype(BF16).astype(F32)
    dep = dep_ref[...].astype(F32).reshape(1, count)
    by_patch = jnp.where(first, weight[0:1, :], jnp.where(second, weight[1:2, :], 0.0))
    slot_id = lax.broadcasted_iota(jnp.int32, (groups * share, count), 0).astype(F32)
    lane = lax.broadcasted_iota(jnp.int32, (groups * share, LANES), 1)
    info = jnp.zeros((groups * share, LANES), F32)
    for patch in range(patches):
        pick = slot_id == rank[patch : patch + 1, :]
        weight_col = jnp.sum(
            jnp.where(pick, by_patch[patch : patch + 1, :], 0.0), axis=1, keepdims=True
        )
        dep_col = jnp.sum(jnp.where(pick, dep, 0.0), axis=1, keepdims=True)
        info = jnp.where(lane == patch, weight_col, info)
        info = jnp.where(lane == patches + patch, dep_col, info)
    info_ref[...] = jnp.zeros((LANES, LANES), F32)
    info_ref[0 : groups * share, :] = info
    info = info_ref[...].T
    tail_id = lax.broadcasted_iota(jnp.int32, (ROWS, LANES), 0)
    for patch in range(patches):
        tail = jnp.where(
            tail_id == 0,
            info[patch : patch + 1, :],
            jnp.where(tail_id == 1, info[patches + patch : patches + patch + 1, :], 0.0),
        )
        tail_ref[patch] = tail.astype(BF16)
    tails_out = pltpu.make_async_copy(tail_ref, slots_ref.at[:, :, width:], sems.at[7])
    tails_out.start()
    blocks_out.wait()
    tails_out.wait()


def pack(targets, local, mult, prec, dep, rows, patches, share, groups):
    count, members = rows.shape
    operands = (targets.T, local.T, mult, prec, dep, rows)
    width = share // ROWS * members
    return pl.pallas_call(
        functools.partial(pack_kernel, groups),
        out_shape=jax.ShapeDtypeStruct((patches, ROWS, width + LANES), BF16),
        in_specs=[pl.BlockSpec(memory_space=pl.ANY)] * len(operands),
        out_specs=pl.BlockSpec(memory_space=pl.ANY),
        scratch_shapes=[pltpu.VMEM(operand.shape, operand.dtype) for operand in operands]
        + [
            pltpu.VMEM((patches, ROWS, width), BF16),
            pltpu.VMEM((patches, ROWS, LANES), BF16),
            pltpu.VMEM((LANES, LANES), F32),
            pltpu.SemaphoreType.DMA((len(operands) + 2,)),
        ],
        compiler_params=pltpu.CompilerParams(vmem_limit_bytes=64 * MEBI),
        cost_estimate=pl.CostEstimate(
            flops=2 * patches * share * count * members,
            bytes_accessed=2 * (patches * share + count) * members,
            transcendentals=0,
        ),
        name="pack_rows",
    )(*operands)


def slot_rows(rows_ref, members):
    blocks = []
    for source in range(rows_ref.shape[0]):
        block = rows_ref[source].astype(F32)
        for begin in range(0, block.shape[1] - LANES, members):
            blocks.append(block[:, begin : begin + members])
    return jnp.concatenate(blocks, axis=0)


def slot_info(rows_ref, info_ref):
    sources, _, width = rows_ref.shape
    if 2 * sources < LANES:
        info_ref[2 * sources :, :] = jnp.zeros((LANES - 2 * sources, LANES), F32)
    for source in range(sources):
        tail = rows_ref[source].astype(F32)[:, width - LANES :]
        info_ref[source : source + 1, :] = tail[0:1, :]
        info_ref[sources + source : sources + source + 1, :] = tail[1:2, :]
    info_ref[...] = info_ref[...].T


def scaled_rows(rows, info_ref, turn, sources):
    share = rows.shape[0] // sources
    begin = lax.rem(lax.axis_index("boot") + turn, lax.axis_size("boot")) * share
    info = info_ref[pl.ds(pl.multiple_of(begin, ROWS), share), :]
    blocks, drive = [], jnp.zeros((1, rows.shape[1]), F32)
    for source in range(sources):
        block = rows[source * share : (source + 1) * share, :]
        block = (info[:, source : source + 1] * block).astype(BF16).astype(F32)
        blocks.append(block)
        dep_col = info[:, sources + source : sources + source + 1]
        drive = drive + jnp.sum(dep_col * block, axis=0, keepdims=True)
    return jnp.concatenate(blocks, axis=0).astype(BF16), drive


def gram_kernel(rows_ref, right_ref, corner_ref, drive_ref, info_ref, ordered_ref, turned_ref):
    members, half = right_ref.shape
    slot_info(rows_ref, info_ref)
    rows = slot_rows(rows_ref, members)
    ordered_ref[...] = rows.astype(BF16)
    turned_ref[...] = rows.T.astype(BF16)
    scaled, drive_ref[...] = scaled_rows(rows, info_ref, 0, rows_ref.shape[0])
    dot = functools.partial(jnp.dot, preferred_element_type=F32)
    right_ref[...] = dot(turned_ref[...], scaled[:, half:])
    corner_ref[...] = dot(turned_ref[0:half, :], scaled[:, 0:half])


def own_gram(rows, members):
    sources, height, width = rows.shape
    slots = sources * height * ((width - LANES) // members)
    return pl.pallas_call(
        gram_kernel,
        out_shape=(
            jax.ShapeDtypeStruct((members, members // 2), F32),
            jax.ShapeDtypeStruct((members // 2, members // 2), F32),
            jax.ShapeDtypeStruct((1, members), F32),
            jax.ShapeDtypeStruct((LANES, LANES), F32),
            jax.ShapeDtypeStruct((slots, members), BF16),
            jax.ShapeDtypeStruct((members, slots), BF16),
        ),
        compiler_params=pltpu.CompilerParams(vmem_limit_bytes=16 * MEBI),
        cost_estimate=pl.CostEstimate(
            flops=4 * members * members * slots,
            bytes_accessed=6 * slots * members,
            transcendentals=0,
        ),
        name="own_gram",
    )(rows)


def diagonal_column(value, eye):
    size = value.shape[1]
    parts = []
    for begin in range(0, size, LANES):
        block = value[:, begin : begin + LANES]
        block = block if value.shape[0] == 1 else block[begin : begin + LANES, :]
        parts.append(jnp.sum(jnp.where(eye, block, 0.0), axis=1, keepdims=True))
    return jnp.concatenate(parts, axis=0)


def symmetric_product(left_ref, right_ref):
    half = left_ref.shape[0] // 2
    dot = functools.partial(jnp.dot, preferred_element_type=F32)
    return (
        dot(left_ref[...], right_ref[:, half:]),
        dot(left_ref[0:half, :], right_ref[:, 0:half]),
    )


def put_symmetric(ref, right, corner):
    half = corner.shape[0]
    right = right.astype(BF16)
    ref[:, half:] = right
    ref[0:half, 0:half] = corner.astype(BF16)
    ref[half:, 0:half] = right[0:half, :].T


def weights_kernel(*refs):
    right_ref, corner_ref, drive_ref, own_info_ref, ordered_ref, turned_ref = refs[:6]
    groups = (len(refs) - 6) // 11
    rows_refs, blended_ref = refs[6 : 5 + groups], refs[5 + groups]
    info_refs = refs[6 + groups : 6 + 2 * groups]
    chains = [refs[6 + 2 * groups + 9 * c : 15 + 2 * groups + 9 * c] for c in range(groups)]
    members, half = right_ref.shape
    sources = rows_refs[0].shape[0] if rows_refs else 1
    row_id = lax.broadcasted_iota(jnp.int32, (members, members), 0)
    col_id = lax.broadcasted_iota(jnp.int32, (members, members), 1)
    identity = jnp.where(row_id == col_id, 1.0, 0.0)
    eye = lax.broadcasted_iota(jnp.int32, (LANES, LANES), 0) == lax.broadcasted_iota(
        jnp.int32, (LANES, LANES), 1
    )
    dot = functools.partial(jnp.dot, preferred_element_type=F32)

    def split(w_high, right, corner):
        put_symmetric(w_high, right, corner)
        diagonal = []
        for first, part in ((0, corner), (half, right[half:, :])):
            for begin in range(0, half, LANES):
                block = part[begin : begin + LANES, begin : begin + LANES]
                place = slice(first + begin, first + begin + LANES)
                w_high[place, place] = jnp.where(eye, 0.0, block).astype(BF16)
                diagonal.append(jnp.sum(jnp.where(eye, block, 0.0), axis=0, keepdims=True))
        return 1.5 + jnp.concatenate(diagonal, axis=1)

    def advance(factor, w_high, right, corner, high):
        change_right, change_corner = symmetric_product(high, w_high)
        return (
            factor[:, half:] * right + change_right,
            factor[:, 0:half] * corner + change_corner,
        )

    infos = [own_info_ref] + list(info_refs[1:])
    rights, corners, drives = [right_ref[...]], [corner_ref[...]], [drive_ref[...]]
    for chain in range(1, groups):
        slot_info(rows_refs[chain - 1], infos[chain])
        scaled, drive = scaled_rows(ordered_ref[...].astype(F32), infos[chain], 0, sources)
        rights.append(dot(turned_ref[...], scaled[:, half:]))
        corners.append(dot(turned_ref[0:half, :], scaled[:, 0:half]))
        drives.append(drive)
    for turn, rows_ref in enumerate(rows_refs, 1):
        rows = slot_rows(rows_ref, members)
        turned = rows.T.astype(BF16)
        for chain in range(groups):
            scaled, drive = scaled_rows(rows, infos[chain], turn, sources)
            rights[chain] = rights[chain] + dot(turned, scaled[:, half:])
            corners[chain] = corners[chain] + dot(turned[0:half, :], scaled[:, 0:half])
            drives[chain] = drives[chain] + drive

    frobenius = []
    for chain, (y_right, y_corner, z_right, z_corner, y_high, z_high, _, _, w_high) in enumerate(
        chains
    ):
        right = identity[:, half:] + rights[chain] / (members - 1.0)
        corner = identity[0:half, 0:half] + corners[chain] / (members - 1.0)
        squares = right * right
        squares = 2.0 * squares[0:half, :] + squares[half:, :] + corner * corner
        squares = jnp.sum(jnp.sum(squares, axis=0, keepdims=True), axis=1, keepdims=True)
        frobenius.append(jnp.sqrt(squares))
        right, corner = right / frobenius[chain], corner / frobenius[chain]
        factor = split(w_high, -0.5 * right, -0.5 * corner)
        put_symmetric(y_high, right, corner)
        y_right[...], y_corner[...] = advance(factor, w_high, right, corner, y_high)
        z_right[...] = 0.25 * right - 0.75 * identity[:, half:]
        z_corner[...] = 0.25 * corner - 0.75 * identity[0:half, 0:half]
        put_symmetric(y_high, y_right[...], y_corner[...])
        put_symmetric(z_high, z_right[...], z_corner[...])

    def step(_, carry):
        factors = [
            split(chain[8], *symmetric_product(chain[5], chain[4])) for chain in chains
        ]
        for factor, chain in zip(factors, chains):
            for right, corner, high in (
                (chain[0], chain[1], chain[4]),
                (chain[2], chain[3], chain[5]),
            ):
                new_right, new_corner = advance(factor, chain[8], right[...], corner[...], high)
                right[...], corner[...] = new_right, new_corner
                put_symmetric(high, new_right, new_corner)
        return carry

    lax.fori_loop(1, NS_STEPS - 1, step, 0)
    factors = []
    for y_right, y_corner, z_right, z_corner, y_high, z_high, y_low, z_low, w_high in chains:
        for right, corner, high, low in (
            (y_right, y_corner, y_high, y_low),
            (z_right, z_corner, z_high, z_low),
        ):
            put_symmetric(
                low,
                right[...] - high[:, half:].astype(F32),
                corner[...] - high[0:half, 0:half].astype(F32),
            )
        large = symmetric_product(z_high, y_high)
        small = zip(symmetric_product(z_high, y_low), symmetric_product(z_low, y_high))
        factors.append(
            split(w_high, *[first + (one + two) for first, (one, two) in zip(large, small)])
        )
    for chain, (_, _, z_right, z_corner, _, z_high, _, _, w_high) in enumerate(chains):
        right, corner = advance(factors[chain], w_high, z_right[...], z_corner[...], z_high)
        left = jnp.concatenate([corner, right[0:half, :].T], axis=0)
        root = jnp.concatenate([left, right], axis=1) * (-2.0 / jnp.sqrt(frobenius[chain]))
        inner = jnp.sum(root * diagonal_column(drives[chain], eye), axis=0, keepdims=True)
        mean_weight = jnp.sum(root * diagonal_column(inner, eye), axis=0, keepdims=True)
        blended_ref[chain] = (root + mean_weight / (members - 1.0)).astype(BF16)


def patch_weights(own, other_rows):
    groups, members = len(other_rows) + 1, own[0].shape[0]
    half = members // 2
    right, corner = pltpu.VMEM((members, half), F32), pltpu.VMEM((half, half), F32)
    chain = [right, corner] * 2 + [pltpu.VMEM((members, members), BF16)] * 5
    return pl.pallas_call(
        weights_kernel,
        out_shape=jax.ShapeDtypeStruct((groups, members, members), BF16),
        scratch_shapes=[pltpu.VMEM((LANES, LANES), F32)] * groups + chain * groups,
        compiler_params=pltpu.CompilerParams(vmem_limit_bytes=(8 + 10 * groups) * MEBI),
        cost_estimate=pl.CostEstimate(
            flops=80 * groups * members * members * members,
            bytes_accessed=8 * members * members,
            transcendentals=0,
        ),
        name="patch_weights",
    )(*own, *other_rows)


def update_kernel(blended_ref, background_ref, analysis_ref):
    groups = blended_ref.shape[0]
    members, points = background_ref.shape
    tile = min(points, 256)
    for begin in range(0, points, tile):
        columns = slice(begin, begin + tile)
        background = background_ref[:, columns].astype(F32)
        centre = jnp.sum(background, axis=0, keepdims=True) / members
        perturb = (background - centre).astype(BF16)
        for turn in range(groups):
            update = jnp.dot(blended_ref[turn], perturb, preferred_element_type=F32)
            group = lax.rem(lax.axis_index("boot") + turn, groups)
            analysis_ref[group, :, columns] = (centre + update).astype(BF16)


def update_points(blended, background):
    groups = blended.shape[0]
    members, points = background.shape
    return pl.pallas_call(
        update_kernel,
        out_shape=jax.ShapeDtypeStruct((groups, members, points), BF16),
        compiler_params=pltpu.CompilerParams(vmem_limit_bytes=16 * MEBI),
        cost_estimate=pl.CostEstimate(
            flops=2 * groups * members * members * points,
            bytes_accessed=2 * (groups + 1) * members * points,
            transcendentals=0,
        ),
        name="update_points",
    )(blended, background)


def cut_kernel(states_ref, cut_ref):
    patches, _, share = cut_ref.shape
    region = states_ref.shape[1] // patches
    offset = lax.axis_index("boot") * share
    for patch in range(patches):
        begin = pl.multiple_of(patch * region + offset, LANES)
        cut_ref[patch] = states_ref[:, pl.ds(begin, share)]


def cut_share(states, patches, share):
    own_members = states.shape[0]
    return pl.pallas_call(
        cut_kernel,
        out_shape=jax.ShapeDtypeStruct((patches, own_members, share), BF16),
        compiler_params=pltpu.CompilerParams(vmem_limit_bytes=16 * MEBI),
        cost_estimate=pl.CostEstimate(
            flops=0, bytes_accessed=4 * patches * own_members * share, transcendentals=0
        ),
        name="cut_share",
    )(states)


def place_kernel(pieces_ref, whole_ref):
    groups, patches, _, share = pieces_ref.shape
    for patch in range(patches):
        for group in range(groups):
            begin = (patch * groups + group) * share
            whole_ref[:, begin : begin + share] = pieces_ref[group, patch]


def place_pieces(pieces):
    groups, patches, own_members, share = pieces.shape
    points = groups * patches * share
    return pl.pallas_call(
        place_kernel,
        out_shape=jax.ShapeDtypeStruct((own_members, points), BF16),
        compiler_params=pltpu.CompilerParams(vmem_limit_bytes=16 * MEBI),
        cost_estimate=pl.CostEstimate(
            flops=0, bytes_accessed=4 * own_members * points, transcendentals=0
        ),
        name="place_pieces",
    )(pieces)


def exchange(blocks, axes="space"):
    return lax.all_to_all(blocks, axes, split_axis=0, concat_axis=0, tiled=True)


def swap_shares(own):
    groups = lax.axis_size("boot")
    return [
        lax.ppermute(own, "boot", [(g, (g - turn) % groups) for g in range(groups)])
        for turn in range(1, groups)
    ]


def local(
    background_states,
    measurement_anomaly_matrix,
    departure_vector,
    measurement_precision,
    measurement_region_targets,
    localization_factor_scaled,
    bootstrap_multiplicity,
):
    device_count = lax.axis_size("space")
    groups = lax.axis_size("boot")
    local_rows = measurement_anomaly_matrix.shape[0]
    targets_per = measurement_region_targets.shape[1]
    slot_cap = 2 * targets_per * local_rows // device_count
    slot_share = -(-slot_cap // (ROWS * groups)) * ROWS
    own_members, points = background_states.shape
    share = points // device_count // groups

    slots = pack(
        measurement_region_targets,
        localization_factor_scaled,
        bootstrap_multiplicity,
        measurement_precision,
        departure_vector,
        measurement_anomaly_matrix,
        device_count,
        slot_share,
        groups,
    )
    own_points = cut_share(background_states, device_count, share)
    own_rows, own_points = lax.optimization_barrier((exchange(slots), own_points))
    other_rows = swap_shares(own_rows)
    own_points = exchange(own_points).reshape(-1, share)

    own = own_gram(own_rows, measurement_anomaly_matrix.shape[1])
    blended = patch_weights(own, other_rows)
    analysis = update_points(blended, own_points)
    analysis = exchange(analysis.reshape(-1, own_members, share), ("boot", "space"))
    return place_pieces(analysis.reshape(groups, device_count, own_members, share))


def solution(mesh):
    in_specs = (
        P("space", None),
        P("space", None),
        P("space"),
        P("space"),
        P("space", None),
        P("space", None),
        P(("boot", "space")),
    )
    out_specs = P(("boot", "space"), None)
    return jax.shard_map(local, mesh=mesh, in_specs=in_specs, out_specs=out_specs, check_vma=False)
```

```python
import functools

import jax
import jax.numpy as jnp
from jax import lax
from jax.experimental import pallas as pl
from jax.experimental.pallas import tpu as pltpu
from jax.sharding import PartitionSpec as P

NS_STEPS = 6
LANES = 128
ROWS = 8
MEBI = 1024 * 1024
F32 = jnp.float32
BF16 = jnp.bfloat16


def pack_kernel(groups, *refs):
    sources, slots_ref, fetched = refs[:6], refs[6], refs[7:13]
    block_ref, tail_ref, info_ref, sems = refs[13:]
    copies = [
        pltpu.make_async_copy(source, target, sems.at[i])
        for i, (source, target) in enumerate(zip(sources, fetched))
    ]
    for copy in copies:
        copy.start()
    for copy in copies[:-1]:
        copy.wait()
    targets_ref, local_ref, mult_ref, prec_ref, dep_ref, rows_ref = fetched
    patches, _, width = block_ref.shape
    count, members = rows_ref.shape
    share = width // members * ROWS
    patch_id = lax.broadcasted_iota(jnp.int32, (patches, count), 0)
    first = patch_id == targets_ref[0:1, :]
    second = patch_id == targets_ref[1:2, :]
    named = jnp.logical_or(first, second)
    earlier = lax.broadcasted_iota(jnp.int32, (count, count), 0) < lax.broadcasted_iota(
        jnp.int32, (count, count), 1
    )
    rank = jnp.dot(
        named.astype(F32).astype(BF16), earlier.astype(F32).astype(BF16), preferred_element_type=F32
    )
    rank = jnp.where(named, rank, -1.0)

    begin = lax.axis_index("boot") * share
    own_id = (lax.broadcasted_iota(jnp.int32, (share, count), 0) + begin).astype(F32)
    picks = [
        jnp.where(own_id == rank[patch : patch + 1, :], 1.0, 0.0) for patch in range(patches)
    ]
    picks = jnp.concatenate(picks, axis=0).astype(BF16)
    copies[-1].wait()
    picked = jnp.dot(picks, rows_ref[...], preferred_element_type=F32)
    for patch in range(patches):
        place = patch * share
        blocks = [picked[place + i : place + i + ROWS, :] for i in range(0, share, ROWS)]
        block_ref[patch] = jnp.concatenate(blocks, axis=1).astype(BF16)
    blocks_out = pltpu.make_async_copy(block_ref, slots_ref.at[:, :, 0:width], sems.at[6])
    blocks_out.start()

    mult = mult_ref[...].reshape(1, count).astype(F32)
    prec = prec_ref[...].reshape(1, count)
    weight = local_ref[...].astype(F32) / 1024.0 * (mult * prec)
    weight = weight.astype(BF16).astype(F32)
    dep = dep_ref[...].astype(F32).reshape(1, count)
    by_patch = jnp.where(first, weight[0:1, :], jnp.where(second, weight[1:2, :], 0.0))
    slot_id = lax.broadcasted_iota(jnp.int32, (groups * share, count), 0).astype(F32)
    lane = lax.broadcasted_iota(jnp.int32, (groups * share, LANES), 1)
    info = jnp.zeros((groups * share, LANES), F32)
    for patch in range(patches):
        pick = slot_id == rank[patch : patch + 1, :]
        weight_col = jnp.sum(
            jnp.where(pick, by_patch[patch : patch + 1, :], 0.0), axis=1, keepdims=True
        )
        dep_col = jnp.sum(jnp.where(pick, dep, 0.0), axis=1, keepdims=True)
        info = jnp.where(lane == patch, weight_col, info)
        info = jnp.where(lane == patches + patch, dep_col, info)
    info_ref[...] = jnp.zeros((LANES, LANES), F32)
    info_ref[0 : groups * share, :] = info
    info = info_ref[...].T
    tail_id = lax.broadcasted_iota(jnp.int32, (ROWS, LANES), 0)
    for patch in range(patches):
        tail = jnp.where(
            tail_id == 0,
            info[patch : patch + 1, :],
            jnp.where(tail_id == 1, info[patches + patch : patches + patch + 1, :], 0.0),
        )
        tail_ref[patch] = tail.astype(BF16)
    tails_out = pltpu.make_async_copy(tail_ref, slots_ref.at[:, :, width:], sems.at[7])
    tails_out.start()
    blocks_out.wait()
    tails_out.wait()


def pack(targets, local, mult, prec, dep, rows, patches, share, groups):
    count, members = rows.shape
    operands = (targets.T, local.T, mult, prec, dep, rows)
    width = share // ROWS * members
    return pl.pallas_call(
        functools.partial(pack_kernel, groups),
        out_shape=jax.ShapeDtypeStruct((patches, ROWS, width + LANES), BF16),
        in_specs=[pl.BlockSpec(memory_space=pl.ANY)] * len(operands),
        out_specs=pl.BlockSpec(memory_space=pl.ANY),
        scratch_shapes=[pltpu.VMEM(operand.shape, operand.dtype) for operand in operands]
        + [
            pltpu.VMEM((patches, ROWS, width), BF16),
            pltpu.VMEM((patches, ROWS, LANES), BF16),
            pltpu.VMEM((LANES, LANES), F32),
            pltpu.SemaphoreType.DMA((len(operands) + 2,)),
        ],
        compiler_params=pltpu.CompilerParams(vmem_limit_bytes=64 * MEBI),
        cost_estimate=pl.CostEstimate(
            flops=2 * patches * share * count * members,
            bytes_accessed=2 * (patches * share + count) * members,
            transcendentals=0,
        ),
        name="pack_rows",
    )(*operands)


def slot_rows(rows_ref, members):
    blocks = []
    for source in range(rows_ref.shape[0]):
        block = rows_ref[source].astype(F32)
        for begin in range(0, block.shape[1] - LANES, members):
            blocks.append(block[:, begin : begin + members])
    return jnp.concatenate(blocks, axis=0)


def slot_info(rows_ref, info_ref):
    sources, _, width = rows_ref.shape
    if 2 * sources < LANES:
        info_ref[2 * sources :, :] = jnp.zeros((LANES - 2 * sources, LANES), F32)
    for source in range(sources):
        tail = rows_ref[source].astype(F32)[:, width - LANES :]
        info_ref[source : source + 1, :] = tail[0:1, :]
        info_ref[sources + source : sources + source + 1, :] = tail[1:2, :]
    info_ref[...] = info_ref[...].T


def scaled_rows(rows, info_ref, turn, sources):
    share = rows.shape[0] // sources
    begin = lax.rem(lax.axis_index("boot") + turn, lax.axis_size("boot")) * share
    info = info_ref[pl.ds(pl.multiple_of(begin, ROWS), share), :]
    blocks, drive = [], jnp.zeros((1, rows.shape[1]), F32)
    for source in range(sources):
        block = rows[source * share : (source + 1) * share, :]
        block = (info[:, source : source + 1] * block).astype(BF16).astype(F32)
        blocks.append(block)
        dep_col = info[:, sources + source : sources + source + 1]
        drive = drive + jnp.sum(dep_col * block, axis=0, keepdims=True)
    return jnp.concatenate(blocks, axis=0).astype(BF16), drive


def gram_kernel(rows_ref, right_ref, corner_ref, drive_ref, info_ref, ordered_ref, turned_ref):
    members, half = right_ref.shape
    slot_info(rows_ref, info_ref)
    rows = slot_rows(rows_ref, members)
    ordered_ref[...] = rows.astype(BF16)
    turned_ref[...] = rows.T.astype(BF16)
    scaled, drive_ref[...] = scaled_rows(rows, info_ref, 0, rows_ref.shape[0])
    dot = functools.partial(jnp.dot, preferred_element_type=F32)
    right_ref[...] = dot(turned_ref[...], scaled[:, half:])
    corner_ref[...] = dot(turned_ref[0:half, :], scaled[:, 0:half])


def own_gram(rows, members):
    sources, height, width = rows.shape
    slots = sources * height * ((width - LANES) // members)
    return pl.pallas_call(
        gram_kernel,
        out_shape=(
            jax.ShapeDtypeStruct((members, members // 2), F32),
            jax.ShapeDtypeStruct((members // 2, members // 2), F32),
            jax.ShapeDtypeStruct((1, members), F32),
            jax.ShapeDtypeStruct((LANES, LANES), F32),
            jax.ShapeDtypeStruct((slots, members), BF16),
            jax.ShapeDtypeStruct((members, slots), BF16),
        ),
        compiler_params=pltpu.CompilerParams(vmem_limit_bytes=16 * MEBI),
        cost_estimate=pl.CostEstimate(
            flops=4 * members * members * slots,
            bytes_accessed=6 * slots * members,
            transcendentals=0,
        ),
        name="own_gram",
    )(rows)


def diagonal_column(value, eye):
    size = value.shape[1]
    parts = []
    for begin in range(0, size, LANES):
        block = value[:, begin : begin + LANES]
        block = block if value.shape[0] == 1 else block[begin : begin + LANES, :]
        parts.append(jnp.sum(jnp.where(eye, block, 0.0), axis=1, keepdims=True))
    return jnp.concatenate(parts, axis=0)


def symmetric_product(left_ref, right_ref):
    half = left_ref.shape[0] // 2
    dot = functools.partial(jnp.dot, preferred_element_type=F32)
    return (
        dot(left_ref[...], right_ref[:, half:]),
        dot(left_ref[0:half, :], right_ref[:, 0:half]),
    )


def put_symmetric(ref, right, corner):
    half = corner.shape[0]
    right = right.astype(BF16)
    ref[:, half:] = right
    ref[0:half, 0:half] = corner.astype(BF16)
    ref[half:, 0:half] = right[0:half, :].T


def weights_kernel(*refs):
    right_ref, corner_ref, drive_ref, own_info_ref, ordered_ref, turned_ref = refs[:6]
    groups = (len(refs) - 6) // 10
    rows_refs, blended_ref = refs[6 : 5 + groups], refs[5 + groups]
    info_refs = refs[6 + groups : 6 + 2 * groups]
    chains = [refs[6 + 2 * groups + 8 * c : 14 + 2 * groups + 8 * c] for c in range(groups)]
    members, half = right_ref.shape
    sources = rows_refs[0].shape[0] if rows_refs else 1
    row_id = lax.broadcasted_iota(jnp.int32, (members, members), 0)
    col_id = lax.broadcasted_iota(jnp.int32, (members, members), 1)
    identity = jnp.where(row_id == col_id, 1.0, 0.0)
    eye = lax.broadcasted_iota(jnp.int32, (LANES, LANES), 0) == lax.broadcasted_iota(
        jnp.int32, (LANES, LANES), 1
    )
    dot = functools.partial(jnp.dot, preferred_element_type=F32)

    def diagonal_row(lower, corner):
        return jnp.concatenate(
            [
                jnp.sum(
                    jnp.where(eye, part[begin : begin + LANES, begin : begin + LANES], 0.0),
                    axis=0,
                    keepdims=True,
                )
                for part in (corner, lower)
                for begin in range(0, half, LANES)
            ],
            axis=1,
        )

    def split(w_high, right, corner):
        put_symmetric(w_high, right, corner)
        for first, part in ((0, corner), (half, right[half:, :])):
            for begin in range(0, half, LANES):
                block = part[begin : begin + LANES, begin : begin + LANES]
                place = slice(first + begin, first + begin + LANES)
                w_high[place, place] = jnp.where(eye, 0.0, block).astype(BF16)
        return 1.5 + diagonal_row(right[half:, :], corner)

    def advance(factor, w_high, right, corner, high):
        change_right, change_corner = symmetric_product(high, w_high)
        return (
            factor[:, half:] * right + change_right,
            factor[:, 0:half] * corner + change_corner,
        )

    infos = [own_info_ref] + list(info_refs[1:])
    rights, corners, drives = [right_ref[...]], [corner_ref[...]], [drive_ref[...]]
    for chain in range(1, groups):
        slot_info(rows_refs[chain - 1], infos[chain])
        scaled, drive = scaled_rows(ordered_ref[...].astype(F32), infos[chain], 0, sources)
        rights.append(dot(turned_ref[...], scaled[:, half:]))
        corners.append(dot(turned_ref[0:half, :], scaled[:, 0:half]))
        drives.append(drive)
    for turn, rows_ref in enumerate(rows_refs, 1):
        rows = slot_rows(rows_ref, members)
        turned = rows.T.astype(BF16)
        for chain in range(groups):
            scaled, drive = scaled_rows(rows, infos[chain], turn, sources)
            rights[chain] = rights[chain] + dot(turned, scaled[:, half:])
            corners[chain] = corners[chain] + dot(turned[0:half, :], scaled[:, 0:half])
            drives[chain] = drives[chain] + drive

    frobenius = []
    for chain, (y_right, y_corner, z_right, z_corner, y_high, z_high, _, w_high) in enumerate(
        chains
    ):
        right = identity[:, half:] + rights[chain] / (members - 1.0)
        corner = identity[0:half, 0:half] + corners[chain] / (members - 1.0)
        squares = right * right
        squares = 2.0 * squares[0:half, :] + squares[half:, :] + corner * corner
        squares = jnp.sum(jnp.sum(squares, axis=0, keepdims=True), axis=1, keepdims=True)
        frobenius.append(jnp.sqrt(squares))
        right, corner = right / frobenius[chain], corner / frobenius[chain]
        factor = split(w_high, -0.5 * right, -0.5 * corner)
        put_symmetric(y_high, right, corner)
        y_right[...], y_corner[...] = advance(factor, w_high, right, corner, y_high)
        z_right[...] = 0.25 * right - 0.75 * identity[:, half:]
        z_corner[...] = 0.25 * corner - 0.75 * identity[0:half, 0:half]
        put_symmetric(y_high, y_right[...], y_corner[...])
        put_symmetric(z_high, z_right[...], z_corner[...])

    def step(_, carry):
        factors = [
            split(chain[7], *symmetric_product(chain[5], chain[4])) for chain in chains
        ]
        for factor, chain in zip(factors, chains):
            for right, corner, high in (
                (chain[0], chain[1], chain[4]),
                (chain[2], chain[3], chain[5]),
            ):
                new_right, new_corner = advance(factor, chain[7], right[...], corner[...], high)
                right[...], corner[...] = new_right, new_corner
                put_symmetric(high, new_right, new_corner)
        return carry

    lax.fori_loop(1, NS_STEPS - 1, step, 0)
    factors = []
    for y_right, y_corner, z_right, z_corner, y_high, z_high, z_off, w_high in chains:
        z_off[...] = z_high[...]
        for right, corner, off in ((y_right, y_corner, y_high), (z_right, z_corner, z_off)):
            for first, part in ((0, corner), (half, right)):
                for begin in range(0, half, LANES):
                    place = slice(first + begin, first + begin + LANES)
                    block = part[place, begin : begin + LANES]
                    off[place, place] = jnp.where(eye, 0.0, block).astype(BF16)
        y_row = diagonal_row(y_right[half:, :], y_corner[...])
        z_row = diagonal_row(z_right[half:, :], z_corner[...])
        z_column = diagonal_column(z_row, eye)
        right, corner = symmetric_product(z_off, y_high)
        right += z_column * y_right[...] + z_right[...] * y_row[:, half:]
        corner += z_column[0:half, :] * y_corner[...] + z_corner[...] * y_row[:, 0:half]
        factors.append(split(w_high, right, corner) - z_row * y_row)
    for chain, (_, _, z_right, z_corner, _, z_high, _, w_high) in enumerate(chains):
        right, corner = advance(factors[chain], w_high, z_right[...], z_corner[...], z_high)
        left = jnp.concatenate([corner, right[0:half, :].T], axis=0)
        root = jnp.concatenate([left, right], axis=1) * (-2.0 / jnp.sqrt(frobenius[chain]))
        inner = jnp.sum(root * diagonal_column(drives[chain], eye), axis=0, keepdims=True)
        mean_weight = jnp.sum(root * diagonal_column(inner, eye), axis=0, keepdims=True)
        blended_ref[chain] = (root + mean_weight / (members - 1.0)).astype(BF16)


def patch_weights(own, other_rows):
    groups, members = len(other_rows) + 1, own[0].shape[0]
    half = members // 2
    right, corner = pltpu.VMEM((members, half), F32), pltpu.VMEM((half, half), F32)
    chain = [right, corner] * 2 + [pltpu.VMEM((members, members), BF16)] * 4
    return pl.pallas_call(
        weights_kernel,
        out_shape=jax.ShapeDtypeStruct((groups, members, members), BF16),
        scratch_shapes=[pltpu.VMEM((LANES, LANES), F32)] * groups + chain * groups,
        compiler_params=pltpu.CompilerParams(vmem_limit_bytes=(8 + 10 * groups) * MEBI),
        cost_estimate=pl.CostEstimate(
            flops=80 * groups * members * members * members,
            bytes_accessed=8 * members * members,
            transcendentals=0,
        ),
        name="patch_weights",
    )(*own, *other_rows)


def update_kernel(blended_ref, background_ref, analysis_ref):
    groups = blended_ref.shape[0]
    members, points = background_ref.shape
    tile = min(points, 256)
    for begin in range(0, points, tile):
        columns = slice(begin, begin + tile)
        background = background_ref[:, columns].astype(F32)
        centre = jnp.sum(background, axis=0, keepdims=True) / members
        perturb = (background - centre).astype(BF16)
        for turn in range(groups):
            update = jnp.dot(blended_ref[turn], perturb, preferred_element_type=F32)
            group = lax.rem(lax.axis_index("boot") + turn, groups)
            analysis_ref[group, :, columns] = (centre + update).astype(BF16)


def update_points(blended, background):
    groups = blended.shape[0]
    members, points = background.shape
    return pl.pallas_call(
        update_kernel,
        out_shape=jax.ShapeDtypeStruct((groups, members, points), BF16),
        compiler_params=pltpu.CompilerParams(vmem_limit_bytes=16 * MEBI),
        cost_estimate=pl.CostEstimate(
            flops=2 * groups * members * members * points,
            bytes_accessed=2 * (groups + 1) * members * points,
            transcendentals=0,
        ),
        name="update_points",
    )(blended, background)


def cut_kernel(states_ref, cut_ref):
    patches, _, share = cut_ref.shape
    region = states_ref.shape[1] // patches
    offset = lax.axis_index("boot") * share
    for patch in range(patches):
        begin = pl.multiple_of(patch * region + offset, LANES)
        cut_ref[patch] = states_ref[:, pl.ds(begin, share)]


def cut_share(states, patches, share):
    own_members = states.shape[0]
    return pl.pallas_call(
        cut_kernel,
        out_shape=jax.ShapeDtypeStruct((patches, own_members, share), BF16),
        compiler_params=pltpu.CompilerParams(vmem_limit_bytes=16 * MEBI),
        cost_estimate=pl.CostEstimate(
            flops=0, bytes_accessed=4 * patches * own_members * share, transcendentals=0
        ),
        name="cut_share",
    )(states)


def place_kernel(pieces_ref, whole_ref):
    groups, patches, _, share = pieces_ref.shape
    for patch in range(patches):
        for group in range(groups):
            begin = (patch * groups + group) * share
            whole_ref[:, begin : begin + share] = pieces_ref[group, patch]


def place_pieces(pieces):
    groups, patches, own_members, share = pieces.shape
    points = groups * patches * share
    return pl.pallas_call(
        place_kernel,
        out_shape=jax.ShapeDtypeStruct((own_members, points), BF16),
        compiler_params=pltpu.CompilerParams(vmem_limit_bytes=16 * MEBI),
        cost_estimate=pl.CostEstimate(
            flops=0, bytes_accessed=4 * own_members * points, transcendentals=0
        ),
        name="place_pieces",
    )(pieces)


def exchange(blocks, axes="space"):
    return lax.all_to_all(blocks, axes, split_axis=0, concat_axis=0, tiled=True)


def swap_shares(own):
    groups = lax.axis_size("boot")
    return [
        lax.ppermute(own, "boot", [(g, (g - turn) % groups) for g in range(groups)])
        for turn in range(1, groups)
    ]


def local(
    background_states,
    measurement_anomaly_matrix,
    departure_vector,
    measurement_precision,
    measurement_region_targets,
    localization_factor_scaled,
    bootstrap_multiplicity,
):
    device_count = lax.axis_size("space")
    groups = lax.axis_size("boot")
    local_rows = measurement_anomaly_matrix.shape[0]
    targets_per = measurement_region_targets.shape[1]
    slot_cap = 2 * targets_per * local_rows // device_count
    slot_share = -(-slot_cap // (ROWS * groups)) * ROWS
    own_members, points = background_states.shape
    share = points // device_count // groups

    slots = pack(
        measurement_region_targets,
        localization_factor_scaled,
        bootstrap_multiplicity,
        measurement_precision,
        departure_vector,
        measurement_anomaly_matrix,
        device_count,
        slot_share,
        groups,
    )
    own_points = cut_share(background_states, device_count, share)
    own_rows, own_points = lax.optimization_barrier((exchange(slots), own_points))
    other_rows = swap_shares(own_rows)
    own_points = exchange(own_points).reshape(-1, share)

    own = own_gram(own_rows, measurement_anomaly_matrix.shape[1])
    blended = patch_weights(own, other_rows)
    analysis = update_points(blended, own_points)
    analysis = exchange(analysis.reshape(-1, own_members, share), ("boot", "space"))
    return place_pieces(analysis.reshape(groups, device_count, own_members, share))


def solution(mesh):
    in_specs = (
        P("space", None),
        P("space", None),
        P("space"),
        P("space"),
        P("space", None),
        P("space", None),
        P(("boot", "space")),
    )
    out_specs = P(("boot", "space"), None)
    return jax.shard_map(local, mesh=mesh, in_specs=in_specs, out_specs=out_specs, check_vma=False)
```

```python
import functools

import jax
import jax.numpy as jnp
from jax import lax
from jax.experimental import pallas as pl
from jax.experimental.pallas import tpu as pltpu
from jax.sharding import Mesh
from jax.sharding import PartitionSpec as P

NS_STEPS = 6
SPACE = ("za", "zb", "near")
PARTNERS = ("near", "zb", "za")
LANES = 128
ROWS = 8
MEBI = 1024 * 1024
F32 = jnp.float32
BF16 = jnp.bfloat16


def partner_order(sizes):
    za, zb, near = sizes
    return [(a * zb + b) * near + c for c in range(near) for b in range(zb) for a in range(za)]


def pack_kernel(groups, order, *refs):
    sources, slots_ref, fetched = refs[:6], refs[6], refs[7:13]
    block_ref, tail_ref, info_ref, sems = refs[13:]
    copies = [
        pltpu.make_async_copy(source, target, sems.at[i])
        for i, (source, target) in enumerate(zip(sources, fetched))
    ]
    for copy in copies:
        copy.start()
    for copy in copies[:-1]:
        copy.wait()
    targets_ref, local_ref, mult_ref, prec_ref, dep_ref, rows_ref = fetched
    patches, _, width = block_ref.shape
    count, members = rows_ref.shape
    share = width // members * ROWS
    patch_id = lax.broadcasted_iota(jnp.int32, (patches, count), 0)
    first = patch_id == targets_ref[0:1, :]
    second = patch_id == targets_ref[1:2, :]
    named = jnp.logical_or(first, second)
    earlier = lax.broadcasted_iota(jnp.int32, (count, count), 0) < lax.broadcasted_iota(
        jnp.int32, (count, count), 1
    )
    rank = jnp.dot(
        named.astype(F32).astype(BF16), earlier.astype(F32).astype(BF16), preferred_element_type=F32
    )
    rank = jnp.where(named, rank, -1.0)

    begin = lax.axis_index("boot") * share
    own_id = (lax.broadcasted_iota(jnp.int32, (share, count), 0) + begin).astype(F32)
    picks = [
        jnp.where(own_id == rank[patch : patch + 1, :], 1.0, 0.0) for patch in order
    ]
    picks = jnp.concatenate(picks, axis=0).astype(BF16)
    copies[-1].wait()
    picked = jnp.dot(picks, rows_ref[...], preferred_element_type=F32)
    for patch in range(patches):
        place = patch * share
        blocks = [picked[place + i : place + i + ROWS, :] for i in range(0, share, ROWS)]
        block_ref[patch] = jnp.concatenate(blocks, axis=1).astype(BF16)
    blocks_out = pltpu.make_async_copy(block_ref, slots_ref.at[:, :, 0:width], sems.at[6])
    blocks_out.start()

    mult = mult_ref[...].reshape(1, count).astype(F32)
    prec = prec_ref[...].reshape(1, count)
    weight = local_ref[...].astype(F32) / 1024.0 * (mult * prec)
    weight = weight.astype(BF16).astype(F32)
    dep = dep_ref[...].astype(F32).reshape(1, count)
    by_patch = jnp.where(first, weight[0:1, :], jnp.where(second, weight[1:2, :], 0.0))
    slot_id = lax.broadcasted_iota(jnp.int32, (groups * share, count), 0).astype(F32)
    lane = lax.broadcasted_iota(jnp.int32, (groups * share, LANES), 1)
    info = jnp.zeros((groups * share, LANES), F32)
    for patch in range(patches):
        pick = slot_id == rank[patch : patch + 1, :]
        weight_col = jnp.sum(
            jnp.where(pick, by_patch[patch : patch + 1, :], 0.0), axis=1, keepdims=True
        )
        dep_col = jnp.sum(jnp.where(pick, dep, 0.0), axis=1, keepdims=True)
        info = jnp.where(lane == patch, weight_col, info)
        info = jnp.where(lane == patches + patch, dep_col, info)
    info_ref[...] = jnp.zeros((LANES, LANES), F32)
    info_ref[0 : groups * share, :] = info
    info = info_ref[...].T
    tail_id = lax.broadcasted_iota(jnp.int32, (ROWS, LANES), 0)
    for place, patch in enumerate(order):
        tail = jnp.where(
            tail_id == 0,
            info[patch : patch + 1, :],
            jnp.where(tail_id == 1, info[patches + patch : patches + patch + 1, :], 0.0),
        )
        tail_ref[place] = tail.astype(BF16)
    tails_out = pltpu.make_async_copy(tail_ref, slots_ref.at[:, :, width:], sems.at[7])
    tails_out.start()
    blocks_out.wait()
    tails_out.wait()


def pack(targets, local, mult, prec, dep, rows, order, share, groups):
    count, members = rows.shape
    patches = len(order)
    operands = (targets.T, local.T, mult, prec, dep, rows)
    width = share // ROWS * members
    return pl.pallas_call(
        functools.partial(pack_kernel, groups, order),
        out_shape=jax.ShapeDtypeStruct((patches, ROWS, width + LANES), BF16),
        in_specs=[pl.BlockSpec(memory_space=pl.ANY)] * len(operands),
        out_specs=pl.BlockSpec(memory_space=pl.ANY),
        scratch_shapes=[pltpu.VMEM(operand.shape, operand.dtype) for operand in operands]
        + [
            pltpu.VMEM((patches, ROWS, width), BF16),
            pltpu.VMEM((patches, ROWS, LANES), BF16),
            pltpu.VMEM((LANES, LANES), F32),
            pltpu.SemaphoreType.DMA((len(operands) + 2,)),
        ],
        compiler_params=pltpu.CompilerParams(vmem_limit_bytes=64 * MEBI),
        cost_estimate=pl.CostEstimate(
            flops=2 * patches * share * count * members,
            bytes_accessed=2 * (patches * share + count) * members,
            transcendentals=0,
        ),
        name="pack_rows",
    )(*operands)


def slot_rows(rows_ref, members):
    blocks = []
    for source in range(rows_ref.shape[0]):
        block = rows_ref[source].astype(F32)
        for begin in range(0, block.shape[1] - LANES, members):
            blocks.append(block[:, begin : begin + members])
    return jnp.concatenate(blocks, axis=0)


def slot_info(rows_ref, info_ref):
    sources, _, width = rows_ref.shape
    if 2 * sources < LANES:
        info_ref[2 * sources :, :] = jnp.zeros((LANES - 2 * sources, LANES), F32)
    for source in range(sources):
        tail = rows_ref[source].astype(F32)[:, width - LANES :]
        info_ref[source : source + 1, :] = tail[0:1, :]
        info_ref[sources + source : sources + source + 1, :] = tail[1:2, :]
    info_ref[...] = info_ref[...].T


def scaled_rows(rows, info_ref, turn, sources):
    share = rows.shape[0] // sources
    begin = lax.rem(lax.axis_index("boot") + turn, lax.axis_size("boot")) * share
    info = info_ref[pl.ds(pl.multiple_of(begin, ROWS), share), :]
    blocks, drive = [], jnp.zeros((1, rows.shape[1]), F32)
    for source in range(sources):
        block = rows[source * share : (source + 1) * share, :]
        block = (info[:, source : source + 1] * block).astype(BF16).astype(F32)
        blocks.append(block)
        dep_col = info[:, sources + source : sources + source + 1]
        drive = drive + jnp.sum(dep_col * block, axis=0, keepdims=True)
    return jnp.concatenate(blocks, axis=0).astype(BF16), drive


def gram_kernel(rows_ref, right_ref, corner_ref, drive_ref, info_ref, ordered_ref, turned_ref):
    members, half = right_ref.shape
    slot_info(rows_ref, info_ref)
    rows = slot_rows(rows_ref, members)
    ordered_ref[...] = rows.astype(BF16)
    turned_ref[...] = rows.T.astype(BF16)
    scaled, drive_ref[...] = scaled_rows(rows, info_ref, 0, rows_ref.shape[0])
    dot = functools.partial(jnp.dot, preferred_element_type=F32)
    right_ref[...] = dot(turned_ref[...], scaled[:, half:])
    corner_ref[...] = dot(turned_ref[0:half, :], scaled[:, 0:half])


def own_gram(rows, members):
    sources, height, width = rows.shape
    slots = sources * height * ((width - LANES) // members)
    return pl.pallas_call(
        gram_kernel,
        out_shape=(
            jax.ShapeDtypeStruct((members, members // 2), F32),
            jax.ShapeDtypeStruct((members // 2, members // 2), F32),
            jax.ShapeDtypeStruct((1, members), F32),
            jax.ShapeDtypeStruct((LANES, LANES), F32),
            jax.ShapeDtypeStruct((slots, members), BF16),
            jax.ShapeDtypeStruct((members, slots), BF16),
        ),
        compiler_params=pltpu.CompilerParams(vmem_limit_bytes=16 * MEBI),
        cost_estimate=pl.CostEstimate(
            flops=4 * members * members * slots,
            bytes_accessed=6 * slots * members,
            transcendentals=0,
        ),
        name="own_gram",
    )(rows)


def diagonal_column(value, eye):
    size = value.shape[1]
    parts = []
    for begin in range(0, size, LANES):
        block = value[:, begin : begin + LANES]
        block = block if value.shape[0] == 1 else block[begin : begin + LANES, :]
        parts.append(jnp.sum(jnp.where(eye, block, 0.0), axis=1, keepdims=True))
    return jnp.concatenate(parts, axis=0)


def symmetric_product(left_ref, right_ref):
    half = left_ref.shape[0] // 2
    dot = functools.partial(jnp.dot, preferred_element_type=F32)
    return (
        dot(left_ref[...], right_ref[:, half:]),
        dot(left_ref[0:half, :], right_ref[:, 0:half]),
    )


def put_symmetric(ref, right, corner):
    half = corner.shape[0]
    right = right.astype(BF16)
    ref[:, half:] = right
    ref[0:half, 0:half] = corner.astype(BF16)
    ref[half:, 0:half] = right[0:half, :].T


def weights_kernel(*refs):
    right_ref, corner_ref, drive_ref, own_info_ref, ordered_ref, turned_ref = refs[:6]
    groups = (len(refs) - 6) // 10
    rows_refs, blended_ref = refs[6 : 5 + groups], refs[5 + groups]
    info_refs = refs[6 + groups : 6 + 2 * groups]
    chains = [refs[6 + 2 * groups + 8 * c : 14 + 2 * groups + 8 * c] for c in range(groups)]
    members, half = right_ref.shape
    sources = rows_refs[0].shape[0] if rows_refs else 1
    row_id = lax.broadcasted_iota(jnp.int32, (members, members), 0)
    col_id = lax.broadcasted_iota(jnp.int32, (members, members), 1)
    identity = jnp.where(row_id == col_id, 1.0, 0.0)
    eye = lax.broadcasted_iota(jnp.int32, (LANES, LANES), 0) == lax.broadcasted_iota(
        jnp.int32, (LANES, LANES), 1
    )
    dot = functools.partial(jnp.dot, preferred_element_type=F32)

    def diagonal_row(lower, corner):
        return jnp.concatenate(
            [
                jnp.sum(
                    jnp.where(eye, part[begin : begin + LANES, begin : begin + LANES], 0.0),
                    axis=0,
                    keepdims=True,
                )
                for part in (corner, lower)
                for begin in range(0, half, LANES)
            ],
            axis=1,
        )

    def split(w_high, right, corner):
        put_symmetric(w_high, right, corner)
        for first, part in ((0, corner), (half, right[half:, :])):
            for begin in range(0, half, LANES):
                block = part[begin : begin + LANES, begin : begin + LANES]
                place = slice(first + begin, first + begin + LANES)
                w_high[place, place] = jnp.where(eye, 0.0, block).astype(BF16)
        return 1.5 + diagonal_row(right[half:, :], corner)

    def advance(factor, w_high, right, corner, high):
        change_right, change_corner = symmetric_product(high, w_high)
        return (
            factor[:, half:] * right + change_right,
            factor[:, 0:half] * corner + change_corner,
        )

    infos = [own_info_ref] + list(info_refs[1:])
    rights, corners, drives = [right_ref[...]], [corner_ref[...]], [drive_ref[...]]
    for chain in range(1, groups):
        slot_info(rows_refs[chain - 1], infos[chain])
        scaled, drive = scaled_rows(ordered_ref[...].astype(F32), infos[chain], 0, sources)
        rights.append(dot(turned_ref[...], scaled[:, half:]))
        corners.append(dot(turned_ref[0:half, :], scaled[:, 0:half]))
        drives.append(drive)
    for turn, rows_ref in enumerate(rows_refs, 1):
        rows = slot_rows(rows_ref, members)
        turned = rows.T.astype(BF16)
        for chain in range(groups):
            scaled, drive = scaled_rows(rows, infos[chain], turn, sources)
            rights[chain] = rights[chain] + dot(turned, scaled[:, half:])
            corners[chain] = corners[chain] + dot(turned[0:half, :], scaled[:, 0:half])
            drives[chain] = drives[chain] + drive

    frobenius = []
    for chain, (y_right, y_corner, z_right, z_corner, y_high, z_high, _, w_high) in enumerate(
        chains
    ):
        right = identity[:, half:] + rights[chain] / (members - 1.0)
        corner = identity[0:half, 0:half] + corners[chain] / (members - 1.0)
        squares = right * right
        squares = 2.0 * squares[0:half, :] + squares[half:, :] + corner * corner
        squares = jnp.sum(jnp.sum(squares, axis=0, keepdims=True), axis=1, keepdims=True)
        frobenius.append(jnp.sqrt(squares))
        right, corner = right / frobenius[chain], corner / frobenius[chain]
        factor = split(w_high, -0.5 * right, -0.5 * corner)
        put_symmetric(y_high, right, corner)
        y_right[...], y_corner[...] = advance(factor, w_high, right, corner, y_high)
        z_right[...] = 0.25 * right - 0.75 * identity[:, half:]
        z_corner[...] = 0.25 * corner - 0.75 * identity[0:half, 0:half]
        put_symmetric(y_high, y_right[...], y_corner[...])
        put_symmetric(z_high, z_right[...], z_corner[...])

    def step(_, carry):
        factors = [
            split(chain[7], *symmetric_product(chain[5], chain[4])) for chain in chains
        ]
        for factor, chain in zip(factors, chains):
            for right, corner, high in (
                (chain[0], chain[1], chain[4]),
                (chain[2], chain[3], chain[5]),
            ):
                new_right, new_corner = advance(factor, chain[7], right[...], corner[...], high)
                right[...], corner[...] = new_right, new_corner
                put_symmetric(high, new_right, new_corner)
        return carry

    lax.fori_loop(1, NS_STEPS - 1, step, 0)
    factors = []
    for y_right, y_corner, z_right, z_corner, y_high, z_high, z_off, w_high in chains:
        z_off[...] = z_high[...]
        for right, corner, off in ((y_right, y_corner, y_high), (z_right, z_corner, z_off)):
            for first, part in ((0, corner), (half, right)):
                for begin in range(0, half, LANES):
                    place = slice(first + begin, first + begin + LANES)
                    block = part[place, begin : begin + LANES]
                    off[place, place] = jnp.where(eye, 0.0, block).astype(BF16)
        y_row = diagonal_row(y_right[half:, :], y_corner[...])
        z_row = diagonal_row(z_right[half:, :], z_corner[...])
        z_column = diagonal_column(z_row, eye)
        right, corner = symmetric_product(z_off, y_high)
        right += z_column * y_right[...] + z_right[...] * y_row[:, half:]
        corner += z_column[0:half, :] * y_corner[...] + z_corner[...] * y_row[:, 0:half]
        factors.append(split(w_high, right, corner) - z_row * y_row)
    for chain, (_, _, z_right, z_corner, _, z_high, _, w_high) in enumerate(chains):
        right, corner = advance(factors[chain], w_high, z_right[...], z_corner[...], z_high)
        left = jnp.concatenate([corner, right[0:half, :].T], axis=0)
        root = jnp.concatenate([left, right], axis=1) * (-2.0 / jnp.sqrt(frobenius[chain]))
        inner = jnp.sum(root * diagonal_column(drives[chain], eye), axis=0, keepdims=True)
        mean_weight = jnp.sum(root * diagonal_column(inner, eye), axis=0, keepdims=True)
        blended_ref[chain] = (root + mean_weight / (members - 1.0)).astype(BF16)


def patch_weights(own, other_rows):
    groups, members = len(other_rows) + 1, own[0].shape[0]
    half = members // 2
    right, corner = pltpu.VMEM((members, half), F32), pltpu.VMEM((half, half), F32)
    chain = [right, corner] * 2 + [pltpu.VMEM((members, members), BF16)] * 4
    return pl.pallas_call(
        weights_kernel,
        out_shape=jax.ShapeDtypeStruct((groups, members, members), BF16),
        scratch_shapes=[pltpu.VMEM((LANES, LANES), F32)] * groups + chain * groups,
        compiler_params=pltpu.CompilerParams(vmem_limit_bytes=(8 + 10 * groups) * MEBI),
        cost_estimate=pl.CostEstimate(
            flops=80 * groups * members * members * members,
            bytes_accessed=8 * members * members,
            transcendentals=0,
        ),
        name="patch_weights",
    )(*own, *other_rows)


def update_kernel(order, blended_ref, background_ref, analysis_ref):
    groups = blended_ref.shape[0]
    members, points = background_ref.shape
    rows = members // len(order)
    places = [order.index(holder) for holder in range(len(order))]
    tile = min(points, 256)
    for begin in range(0, points, tile):
        columns = slice(begin, begin + tile)
        background = background_ref[:, columns].astype(F32)
        background = jnp.concatenate(
            [background[place * rows : (place + 1) * rows, :] for place in places], axis=0
        )
        centre = jnp.sum(background, axis=0, keepdims=True) / members
        perturb = (background - centre).astype(BF16)
        for turn in range(groups):
            update = jnp.dot(blended_ref[turn], perturb, preferred_element_type=F32)
            group = lax.rem(lax.axis_index("boot") + turn, groups)
            update = centre + update
            update = jnp.concatenate(
                [update[holder * rows : (holder + 1) * rows, :] for holder in order], axis=0
            )
            analysis_ref[group, :, columns] = update.astype(BF16)


def update_points(blended, background, order):
    groups = blended.shape[0]
    members, points = background.shape
    return pl.pallas_call(
        functools.partial(update_kernel, order),
        out_shape=jax.ShapeDtypeStruct((groups, members, points), BF16),
        compiler_params=pltpu.CompilerParams(vmem_limit_bytes=16 * MEBI),
        cost_estimate=pl.CostEstimate(
            flops=2 * groups * members * members * points,
            bytes_accessed=2 * (groups + 1) * members * points,
            transcendentals=0,
        ),
        name="update_points",
    )(blended, background)


def cut_kernel(order, states_ref, cut_ref):
    patches, _, share = cut_ref.shape
    region = states_ref.shape[1] // patches
    offset = lax.axis_index("boot") * share
    for place, patch in enumerate(order):
        begin = pl.multiple_of(patch * region + offset, LANES)
        cut_ref[place] = states_ref[:, pl.ds(begin, share)]


def cut_share(states, order, share):
    own_members, patches = states.shape[0], len(order)
    return pl.pallas_call(
        functools.partial(cut_kernel, order),
        out_shape=jax.ShapeDtypeStruct((patches, own_members, share), BF16),
        compiler_params=pltpu.CompilerParams(vmem_limit_bytes=16 * MEBI),
        cost_estimate=pl.CostEstimate(
            flops=0, bytes_accessed=4 * patches * own_members * share, transcendentals=0
        ),
        name="cut_share",
    )(states)


def place_kernel(order, pieces_ref, whole_ref):
    groups, _, _, share = pieces_ref.shape
    for place, patch in enumerate(order):
        for group in range(groups):
            begin = (patch * groups + group) * share
            whole_ref[:, begin : begin + share] = pieces_ref[group, place]


def place_pieces(pieces, order):
    groups, patches, own_members, share = pieces.shape
    points = groups * patches * share
    return pl.pallas_call(
        functools.partial(place_kernel, order),
        out_shape=jax.ShapeDtypeStruct((own_members, points), BF16),
        compiler_params=pltpu.CompilerParams(vmem_limit_bytes=16 * MEBI),
        cost_estimate=pl.CostEstimate(
            flops=0, bytes_accessed=4 * own_members * points, transcendentals=0
        ),
        name="place_pieces",
    )(pieces)


def exchange(blocks, axes=PARTNERS):
    return lax.all_to_all(blocks, axes, split_axis=0, concat_axis=0, tiled=True)


def swap_shares(own):
    groups = lax.axis_size("boot")
    return [
        lax.ppermute(own, "boot", [(g, (g - turn) % groups) for g in range(groups)])
        for turn in range(1, groups)
    ]


def local(
    background_states,
    measurement_anomaly_matrix,
    departure_vector,
    measurement_precision,
    measurement_region_targets,
    localization_factor_scaled,
    bootstrap_multiplicity,
):
    order = partner_order([lax.axis_size(axis) for axis in SPACE])
    device_count = len(order)
    groups = lax.axis_size("boot")
    local_rows = measurement_anomaly_matrix.shape[0]
    targets_per = measurement_region_targets.shape[1]
    slot_cap = 2 * targets_per * local_rows // device_count
    slot_share = -(-slot_cap // (ROWS * groups)) * ROWS
    own_members, points = background_states.shape
    share = points // device_count // groups

    slots = pack(
        measurement_region_targets,
        localization_factor_scaled,
        bootstrap_multiplicity,
        measurement_precision,
        departure_vector,
        measurement_anomaly_matrix,
        order,
        slot_share,
        groups,
    )
    own_points = cut_share(background_states, order, share)
    own_rows, own_points = lax.optimization_barrier((exchange(slots), own_points))
    other_rows = swap_shares(own_rows)
    own_points = exchange(own_points).reshape(-1, share)

    own = own_gram(own_rows, measurement_anomaly_matrix.shape[1])
    blended = patch_weights(own, other_rows)
    analysis = update_points(blended, own_points, order)
    analysis = exchange(analysis.reshape(-1, own_members, share), ("boot",) + PARTNERS)
    return place_pieces(analysis.reshape(groups, device_count, own_members, share), order)


def solution(mesh):
    groups, devices = mesh.shape["boot"], mesh.shape["space"]
    cut = 2 if devices % 4 == 0 else 1
    mesh = Mesh(
        mesh.devices.reshape(groups, cut, cut, devices // cut**2), ("boot",) + SPACE
    )
    in_specs = (
        P(SPACE, None),
        P(SPACE, None),
        P(SPACE),
        P(SPACE),
        P(SPACE, None),
        P(SPACE, None),
        P(("boot",) + SPACE),
    )
    out_specs = P(("boot",) + SPACE, None)
    return jax.shard_map(local, mesh=mesh, in_specs=in_specs, out_specs=out_specs, check_vma=False)
```

```python
import functools

import jax
import jax.numpy as jnp
from jax import lax
from jax.experimental import pallas as pl
from jax.experimental.pallas import tpu as pltpu
from jax.sharding import Mesh
from jax.sharding import PartitionSpec as P

NS_STEPS = 6
SPACE = ("za", "zb", "near")
PARTNERS = ("near", "zb", "za")
LANES = 128
ROWS = 8
MEBI = 1024 * 1024
F32 = jnp.float32
BF16 = jnp.bfloat16


def partner_order(sizes):
    za, zb, near = sizes
    return [(a * zb + b) * near + c for c in range(near) for b in range(zb) for a in range(za)]


def pack_kernel(groups, order, *refs):
    sources, slots_ref, fetched = refs[:6], refs[6], refs[7:13]
    block_ref, tail_ref, info_ref, sems = refs[13:]
    copies = [
        pltpu.make_async_copy(source, target, sems.at[i])
        for i, (source, target) in enumerate(zip(sources, fetched))
    ]
    for copy in copies:
        copy.start()
    for copy in copies[:-1]:
        copy.wait()
    targets_ref, local_ref, mult_ref, prec_ref, dep_ref, rows_ref = fetched
    patches, _, width = block_ref.shape
    count, members = rows_ref.shape
    share = width // members * ROWS
    patch_id = lax.broadcasted_iota(jnp.int32, (patches, count), 0)
    first = patch_id == targets_ref[0:1, :]
    second = patch_id == targets_ref[1:2, :]
    named = jnp.logical_or(first, second)
    earlier = lax.broadcasted_iota(jnp.int32, (count, count), 0) < lax.broadcasted_iota(
        jnp.int32, (count, count), 1
    )
    rank = jnp.dot(
        named.astype(F32).astype(BF16), earlier.astype(F32).astype(BF16), preferred_element_type=F32
    )
    rank = jnp.where(named, rank, -1.0)

    begin = lax.axis_index("boot") * share
    own_id = (lax.broadcasted_iota(jnp.int32, (share, count), 0) + begin).astype(F32)
    picks = [
        jnp.where(own_id == rank[patch : patch + 1, :], 1.0, 0.0) for patch in order
    ]
    picks = jnp.concatenate(picks, axis=0).astype(BF16)
    copies[-1].wait()
    picked = jnp.dot(picks, rows_ref[...], preferred_element_type=F32)
    for patch in range(patches):
        place = patch * share
        blocks = [picked[place + i : place + i + ROWS, :] for i in range(0, share, ROWS)]
        block_ref[patch] = jnp.concatenate(blocks, axis=1).astype(BF16)
    blocks_out = pltpu.make_async_copy(block_ref, slots_ref.at[:, :, 0:width], sems.at[6])
    blocks_out.start()

    mult = mult_ref[...].reshape(1, count).astype(F32)
    prec = prec_ref[...].reshape(1, count)
    weight = local_ref[...].astype(F32) / 1024.0 * (mult * prec)
    weight = weight.astype(BF16).astype(F32)
    dep = dep_ref[...].astype(F32).reshape(1, count)
    by_patch = jnp.where(first, weight[0:1, :], jnp.where(second, weight[1:2, :], 0.0))
    slot_id = lax.broadcasted_iota(jnp.int32, (groups * share, count), 0).astype(F32)
    lane = lax.broadcasted_iota(jnp.int32, (groups * share, LANES), 1)
    info = jnp.zeros((groups * share, LANES), F32)
    for patch in range(patches):
        pick = slot_id == rank[patch : patch + 1, :]
        weight_col = jnp.sum(
            jnp.where(pick, by_patch[patch : patch + 1, :], 0.0), axis=1, keepdims=True
        )
        dep_col = jnp.sum(jnp.where(pick, dep, 0.0), axis=1, keepdims=True)
        info = jnp.where(lane == patch, weight_col, info)
        info = jnp.where(lane == patches + patch, dep_col, info)
    info_ref[...] = jnp.zeros((LANES, LANES), F32)
    info_ref[0 : groups * share, :] = info
    info = info_ref[...].T
    tail_id = lax.broadcasted_iota(jnp.int32, (ROWS, LANES), 0)
    for place, patch in enumerate(order):
        tail = jnp.where(
            tail_id == 0,
            info[patch : patch + 1, :],
            jnp.where(tail_id == 1, info[patches + patch : patches + patch + 1, :], 0.0),
        )
        tail_ref[place] = tail.astype(BF16)
    tails_out = pltpu.make_async_copy(tail_ref, slots_ref.at[:, :, width:], sems.at[7])
    tails_out.start()
    blocks_out.wait()
    tails_out.wait()


def pack(targets, local, mult, prec, dep, rows, order, share, groups):
    count, members = rows.shape
    patches = len(order)
    operands = (targets.T, local.T, mult, prec, dep, rows)
    width = share // ROWS * members
    return pl.pallas_call(
        functools.partial(pack_kernel, groups, order),
        out_shape=jax.ShapeDtypeStruct((patches, ROWS, width + LANES), BF16),
        in_specs=[pl.BlockSpec(memory_space=pl.ANY)] * len(operands),
        out_specs=pl.BlockSpec(memory_space=pl.ANY),
        scratch_shapes=[pltpu.VMEM(operand.shape, operand.dtype) for operand in operands]
        + [
            pltpu.VMEM((patches, ROWS, width), BF16),
            pltpu.VMEM((patches, ROWS, LANES), BF16),
            pltpu.VMEM((LANES, LANES), F32),
            pltpu.SemaphoreType.DMA((len(operands) + 2,)),
        ],
        compiler_params=pltpu.CompilerParams(vmem_limit_bytes=64 * MEBI),
        cost_estimate=pl.CostEstimate(
            flops=2 * patches * share * count * members,
            bytes_accessed=2 * (patches * share + count) * members,
            transcendentals=0,
        ),
        name="pack_rows",
    )(*operands)


def slot_rows(rows_ref, members):
    blocks = []
    for source in range(rows_ref.shape[0]):
        block = rows_ref[source].astype(F32)
        for begin in range(0, block.shape[1] - LANES, members):
            blocks.append(block[:, begin : begin + members])
    return jnp.concatenate(blocks, axis=0)


def slot_info(rows_ref, info_ref):
    sources, _, width = rows_ref.shape
    if 2 * sources < LANES:
        info_ref[2 * sources :, :] = jnp.zeros((LANES - 2 * sources, LANES), F32)
    for source in range(sources):
        tail = rows_ref[source].astype(F32)[:, width - LANES :]
        info_ref[source : source + 1, :] = tail[0:1, :]
        info_ref[sources + source : sources + source + 1, :] = tail[1:2, :]
    info_ref[...] = info_ref[...].T


def scaled_rows(rows, info_ref, turn, sources):
    share = rows.shape[0] // sources
    begin = lax.rem(lax.axis_index("boot") + turn, lax.axis_size("boot")) * share
    info = info_ref[pl.ds(pl.multiple_of(begin, ROWS), share), :]
    blocks, drive = [], jnp.zeros((1, rows.shape[1]), F32)
    for source in range(sources):
        block = rows[source * share : (source + 1) * share, :]
        block = (info[:, source : source + 1] * block).astype(BF16).astype(F32)
        blocks.append(block)
        dep_col = info[:, sources + source : sources + source + 1]
        drive = drive + jnp.sum(dep_col * block, axis=0, keepdims=True)
    return jnp.concatenate(blocks, axis=0).astype(BF16), drive


def gram_kernel(rows_ref, right_ref, corner_ref, drive_ref, info_ref, ordered_ref, turned_ref):
    members, half = right_ref.shape
    slot_info(rows_ref, info_ref)
    rows = slot_rows(rows_ref, members)
    ordered_ref[...] = rows.astype(BF16)
    turned_ref[...] = rows.T.astype(BF16)
    scaled, drive_ref[...] = scaled_rows(rows, info_ref, 0, rows_ref.shape[0])
    dot = functools.partial(jnp.dot, preferred_element_type=F32)
    right_ref[...] = dot(turned_ref[...], scaled[:, half:])
    corner_ref[...] = dot(turned_ref[0:half, :], scaled[:, 0:half])


def own_gram(rows, members):
    sources, height, width = rows.shape
    slots = sources * height * ((width - LANES) // members)
    return pl.pallas_call(
        gram_kernel,
        out_shape=(
            jax.ShapeDtypeStruct((members, members // 2), F32),
            jax.ShapeDtypeStruct((members // 2, members // 2), F32),
            jax.ShapeDtypeStruct((1, members), F32),
            jax.ShapeDtypeStruct((LANES, LANES), F32),
            jax.ShapeDtypeStruct((slots, members), BF16),
            jax.ShapeDtypeStruct((members, slots), BF16),
        ),
        compiler_params=pltpu.CompilerParams(vmem_limit_bytes=16 * MEBI),
        cost_estimate=pl.CostEstimate(
            flops=4 * members * members * slots,
            bytes_accessed=6 * slots * members,
            transcendentals=0,
        ),
        name="own_gram",
    )(rows)


def diagonal_column(value, eye):
    size = value.shape[1]
    parts = []
    for begin in range(0, size, LANES):
        block = value[:, begin : begin + LANES]
        block = block if value.shape[0] == 1 else block[begin : begin + LANES, :]
        parts.append(jnp.sum(jnp.where(eye, block, 0.0), axis=1, keepdims=True))
    return jnp.concatenate(parts, axis=0)


def symmetric_product(left_ref, right_ref):
    half = left_ref.shape[0] // 2
    dot = functools.partial(jnp.dot, preferred_element_type=F32)
    return (
        dot(left_ref[...], right_ref[:, half:]),
        dot(left_ref[0:half, :], right_ref[:, 0:half]),
    )


def put_symmetric(ref, right, corner):
    half = corner.shape[0]
    right = right.astype(BF16)
    ref[:, half:] = right
    ref[0:half, 0:half] = corner.astype(BF16)
    ref[half:, 0:half] = right[0:half, :].T


def weights_kernel(*refs):
    right_ref, corner_ref, drive_ref, own_info_ref, ordered_ref, turned_ref = refs[:6]
    groups = (len(refs) - 6) // 10
    rows_refs, blended_ref = refs[6 : 5 + groups], refs[5 + groups]
    info_refs = refs[6 + groups : 6 + 2 * groups]
    chains = [refs[6 + 2 * groups + 8 * c : 14 + 2 * groups + 8 * c] for c in range(groups)]
    members, half = right_ref.shape
    sources = rows_refs[0].shape[0] if rows_refs else 1
    row_id = lax.broadcasted_iota(jnp.int32, (members, members), 0)
    col_id = lax.broadcasted_iota(jnp.int32, (members, members), 1)
    identity = jnp.where(row_id == col_id, 1.0, 0.0)
    eye = lax.broadcasted_iota(jnp.int32, (LANES, LANES), 0) == lax.broadcasted_iota(
        jnp.int32, (LANES, LANES), 1
    )
    dot = functools.partial(jnp.dot, preferred_element_type=F32)

    def diagonal_row(lower, corner):
        return jnp.concatenate(
            [
                jnp.sum(
                    jnp.where(eye, part[begin : begin + LANES, begin : begin + LANES], 0.0),
                    axis=0,
                    keepdims=True,
                )
                for part in (corner, lower)
                for begin in range(0, half, LANES)
            ],
            axis=1,
        )

    def split(w_high, right, corner):
        put_symmetric(w_high, right, corner)
        for first, part in ((0, corner), (half, right[half:, :])):
            for begin in range(0, half, LANES):
                block = part[begin : begin + LANES, begin : begin + LANES]
                place = slice(first + begin, first + begin + LANES)
                w_high[place, place] = jnp.where(eye, 0.0, block).astype(BF16)
        return 1.5 + diagonal_row(right[half:, :], corner)

    def advance(factor, w_high, right, corner, high):
        change_right, change_corner = symmetric_product(high, w_high)
        return (
            factor[:, half:] * right + change_right,
            factor[:, 0:half] * corner + change_corner,
        )

    infos = [own_info_ref] + list(info_refs[1:])
    rights, corners, drives = [right_ref[...]], [corner_ref[...]], [drive_ref[...]]
    for chain in range(1, groups):
        slot_info(rows_refs[chain - 1], infos[chain])
        scaled, drive = scaled_rows(ordered_ref[...].astype(F32), infos[chain], 0, sources)
        rights.append(dot(turned_ref[...], scaled[:, half:]))
        corners.append(dot(turned_ref[0:half, :], scaled[:, 0:half]))
        drives.append(drive)
    for turn, rows_ref in enumerate(rows_refs, 1):
        rows = slot_rows(rows_ref, members)
        turned = rows.T.astype(BF16)
        for chain in range(groups):
            scaled, drive = scaled_rows(rows, infos[chain], turn, sources)
            rights[chain] = rights[chain] + dot(turned, scaled[:, half:])
            corners[chain] = corners[chain] + dot(turned[0:half, :], scaled[:, 0:half])
            drives[chain] = drives[chain] + drive

    frobenius = []
    for chain, (y_right, y_corner, z_right, z_corner, y_high, z_high, _, w_high) in enumerate(
        chains
    ):
        right = identity[:, half:] + rights[chain] / (members - 1.0)
        corner = identity[0:half, 0:half] + corners[chain] / (members - 1.0)
        squares = right * right
        squares = 2.0 * squares[0:half, :] + squares[half:, :] + corner * corner
        squares = jnp.sum(jnp.sum(squares, axis=0, keepdims=True), axis=1, keepdims=True)
        frobenius.append(jnp.sqrt(squares))
        right, corner = right / frobenius[chain], corner / frobenius[chain]
        factor = split(w_high, -0.5 * right, -0.5 * corner)
        put_symmetric(y_high, right, corner)
        y_right[...], y_corner[...] = advance(factor, w_high, right, corner, y_high)
        z_right[...] = 0.25 * right - 0.75 * identity[:, half:]
        z_corner[...] = 0.25 * corner - 0.75 * identity[0:half, 0:half]
        put_symmetric(y_high, y_right[...], y_corner[...])
        put_symmetric(z_high, z_right[...], z_corner[...])

    def step(_, carry):
        factors = [
            split(chain[7], *symmetric_product(chain[5], chain[4])) for chain in chains
        ]
        for factor, chain in zip(factors, chains):
            for right, corner, high in (
                (chain[0], chain[1], chain[4]),
                (chain[2], chain[3], chain[5]),
            ):
                new_right, new_corner = advance(factor, chain[7], right[...], corner[...], high)
                right[...], corner[...] = new_right, new_corner
                put_symmetric(high, new_right, new_corner)
        return carry

    lax.fori_loop(1, NS_STEPS - 1, step, 0)
    factors = []
    for y_right, y_corner, z_right, z_corner, y_high, z_high, z_off, w_high in chains:
        z_off[...] = z_high[...]
        for right, corner, off in ((y_right, y_corner, y_high), (z_right, z_corner, z_off)):
            for first, part in ((0, corner), (half, right)):
                for begin in range(0, half, LANES):
                    place = slice(first + begin, first + begin + LANES)
                    block = part[place, begin : begin + LANES]
                    off[place, place] = jnp.where(eye, 0.0, block).astype(BF16)
        y_row = diagonal_row(y_right[half:, :], y_corner[...])
        z_row = diagonal_row(z_right[half:, :], z_corner[...])
        z_column = diagonal_column(z_row, eye)
        right, corner = symmetric_product(z_off, y_high)
        right += z_column * y_right[...] + z_right[...] * y_row[:, half:]
        corner += z_column[0:half, :] * y_corner[...] + z_corner[...] * y_row[:, 0:half]
        factors.append(split(w_high, right, corner) - z_row * y_row)
    for chain, (_, _, z_right, z_corner, _, z_high, _, w_high) in enumerate(chains):
        right, corner = advance(factors[chain], w_high, z_right[...], z_corner[...], z_high)
        left = jnp.concatenate([corner, right[0:half, :].T], axis=0)
        root = jnp.concatenate([left, right], axis=1) * (-2.0 / jnp.sqrt(frobenius[chain]))
        inner = jnp.sum(root * diagonal_column(drives[chain], eye), axis=0, keepdims=True)
        mean_weight = jnp.sum(root * diagonal_column(inner, eye), axis=0, keepdims=True)
        blended_ref[chain] = (root + mean_weight / (members - 1.0)).astype(BF16)


def patch_weights(own, other_rows):
    groups, members = len(other_rows) + 1, own[0].shape[0]
    half = members // 2
    right, corner = pltpu.VMEM((members, half), F32), pltpu.VMEM((half, half), F32)
    chain = [right, corner] * 2 + [pltpu.VMEM((members, members), BF16)] * 4
    return pl.pallas_call(
        weights_kernel,
        out_shape=jax.ShapeDtypeStruct((groups, members, members), BF16),
        scratch_shapes=[pltpu.VMEM((LANES, LANES), F32)] * groups + chain * groups,
        compiler_params=pltpu.CompilerParams(vmem_limit_bytes=(8 + 10 * groups) * MEBI),
        cost_estimate=pl.CostEstimate(
            flops=8 * groups * members * members * members,
            bytes_accessed=8 * members * members,
            transcendentals=0,
        ),
        name="patch_weights",
    )(*own, *other_rows)


def update_kernel(order, blended_ref, *refs):
    piece_refs, analysis_ref, members_ref = refs[:-2], refs[-2], refs[-1]
    groups = blended_ref.shape[0]
    near, rows, points = piece_refs[0].shape
    slabs = len(piece_refs)
    members = slabs * near * rows
    slab, place = lax.axis_index(SPACE[:2]), lax.axis_index(SPACE[2])
    for far, piece_ref in enumerate(piece_refs):
        for step in range(near):
            holder = lax.rem(slab + slabs - far, slabs) * near + lax.rem(place + near - step, near)
            begin = pl.multiple_of(holder * rows, rows)
            members_ref[pl.ds(begin, rows), :] = piece_ref[step].astype(members_ref.dtype)
    tile = min(points, 256)
    for begin in range(0, points, tile):
        columns = slice(begin, begin + tile)
        background = members_ref[:, columns].astype(F32)
        centre = jnp.sum(background, axis=0, keepdims=True) / members
        perturb = (background - centre).astype(BF16)
        for turn in range(groups):
            update = jnp.dot(blended_ref[turn], perturb, preferred_element_type=F32)
            group = lax.rem(lax.axis_index("boot") + turn, groups)
            update = centre + update
            update = jnp.concatenate(
                [update[holder * rows : (holder + 1) * rows, :] for holder in order], axis=0
            )
            analysis_ref[group, :, columns] = update.astype(BF16)


def update_points(blended, pieces, order):
    groups, members, _ = blended.shape
    rows, points = pieces[0].shape[1:]
    held = BF16 if rows % 16 == 0 else F32
    return pl.pallas_call(
        functools.partial(update_kernel, order),
        out_shape=jax.ShapeDtypeStruct((groups, members, points), BF16),
        scratch_shapes=[pltpu.VMEM((members, points), held)],
        compiler_params=pltpu.CompilerParams(vmem_limit_bytes=16 * MEBI),
        cost_estimate=pl.CostEstimate(
            flops=2 * groups * members * members * points,
            bytes_accessed=2 * (groups + 1) * members * points,
            transcendentals=0,
        ),
        name="update_points",
    )(blended, *pieces)


def slab_sizes():
    return lax.axis_size(SPACE[:2]), lax.axis_size(SPACE[2])


def cut_kernel(slabs, states_ref, *cut_refs):
    share = cut_refs[0].shape[2]
    near = len(cut_refs)
    region = states_ref.shape[1] // (slabs * near)
    offset = lax.axis_index("boot") * share
    slab, place = lax.axis_index(SPACE[:2]), lax.axis_index(SPACE[2])
    for step, cut_ref in enumerate(cut_refs):
        for far in range(slabs):
            patch = lax.rem(slab + far, slabs) * near + lax.rem(place + step, near)
            begin = pl.multiple_of(patch * region + offset, LANES)
            cut_ref[far] = states_ref[:, pl.ds(begin, share)]


def cut_share(states, share):
    slabs, near = slab_sizes()
    own_members = states.shape[0]
    return pl.pallas_call(
        functools.partial(cut_kernel, slabs),
        out_shape=[jax.ShapeDtypeStruct((slabs, own_members, share), BF16)] * near,
        compiler_params=pltpu.CompilerParams(vmem_limit_bytes=16 * MEBI),
        cost_estimate=pl.CostEstimate(
            flops=0, bytes_accessed=4 * slabs * near * own_members * share, transcendentals=0
        ),
        name="cut_share",
    )(states)


def regroup_kernel(near, *refs):
    for far, group_ref in enumerate(refs[near:]):
        for step, cut_ref in enumerate(refs[:near]):
            group_ref[step] = cut_ref[far]


def regroup(cuts):
    slabs, own_members, share = cuts[0].shape
    return pl.pallas_call(
        functools.partial(regroup_kernel, len(cuts)),
        out_shape=[jax.ShapeDtypeStruct((len(cuts), own_members, share), BF16)] * slabs,
        compiler_params=pltpu.CompilerParams(vmem_limit_bytes=16 * MEBI),
        cost_estimate=pl.CostEstimate(
            flops=0, bytes_accessed=4 * len(cuts) * slabs * own_members * share, transcendentals=0
        ),
        name="regroup",
    )(*cuts)


def shift_all(pieces, axes):
    count = len(pieces)
    return [pieces[0]] + [
        lax.ppermute(pieces[step], axes, [(d, (d + step) % count) for d in range(count)])
        for step in range(1, count)
    ]


def place_kernel(order, pieces_ref, whole_ref, held_ref, sems):
    groups, _, _, share = pieces_ref.shape
    steps = sems.shape[0]
    width = held_ref.shape[1] // steps
    copies = []
    for step in range(steps):
        for patch in range(step * len(order) // steps, (step + 1) * len(order) // steps):
            for group in range(groups):
                begin = (patch * groups + group) * share
                held_ref[:, begin : begin + share] = pieces_ref[group, order.index(patch)]
        columns = slice(step * width, (step + 1) * width)
        copies.append(
            pltpu.make_async_copy(held_ref.at[:, columns], whole_ref.at[:, columns], sems.at[step])
        )
        copies[step].start()
    for copy in copies:
        copy.wait()


def place_pieces(pieces, order):
    groups, patches, own_members, share = pieces.shape
    points = groups * patches * share
    return pl.pallas_call(
        functools.partial(place_kernel, order),
        out_specs=pl.BlockSpec(memory_space=pl.ANY),
        out_shape=jax.ShapeDtypeStruct((own_members, points), BF16),
        scratch_shapes=[pltpu.VMEM((own_members, points), BF16), pltpu.SemaphoreType.DMA((4,))],
        compiler_params=pltpu.CompilerParams(vmem_limit_bytes=16 * MEBI),
        cost_estimate=pl.CostEstimate(
            flops=0, bytes_accessed=4 * own_members * points, transcendentals=0
        ),
        name="place_pieces",
    )(pieces)


def exchange(blocks, axes=PARTNERS):
    return lax.all_to_all(blocks, axes, split_axis=0, concat_axis=0, tiled=True)


def swap_shares(own):
    groups = lax.axis_size("boot")
    return [
        lax.ppermute(own, "boot", [(g, (g - turn) % groups) for g in range(groups)])
        for turn in range(1, groups)
    ]


def local(
    background_states,
    measurement_anomaly_matrix,
    departure_vector,
    measurement_precision,
    measurement_region_targets,
    localization_factor_scaled,
    bootstrap_multiplicity,
):
    order = partner_order([lax.axis_size(axis) for axis in SPACE])
    device_count = len(order)
    groups = lax.axis_size("boot")
    local_rows = measurement_anomaly_matrix.shape[0]
    targets_per = measurement_region_targets.shape[1]
    slot_cap = 2 * targets_per * local_rows // device_count
    slot_share = -(-slot_cap // (ROWS * groups)) * ROWS
    own_members, points = background_states.shape
    share = points // device_count // groups

    slots = pack(
        measurement_region_targets,
        localization_factor_scaled,
        bootstrap_multiplicity,
        measurement_precision,
        departure_vector,
        measurement_anomaly_matrix,
        order,
        slot_share,
        groups,
    )
    slots, background_states = lax.optimization_barrier((slots, background_states))
    by_slab = regroup(shift_all(cut_share(background_states, share), SPACE[2]))
    own_rows, by_slab = lax.optimization_barrier((exchange(slots), by_slab))
    other_rows = swap_shares(own_rows)
    points_by_slab = shift_all(by_slab, SPACE[:2])

    own = own_gram(own_rows, measurement_anomaly_matrix.shape[1])
    blended = patch_weights(own, other_rows)
    analysis = update_points(blended, points_by_slab, order)
    analysis = exchange(analysis.reshape(-1, own_members, share), ("boot",) + PARTNERS)
    return place_pieces(analysis.reshape(groups, device_count, own_members, share), order)


def solution(mesh):
    groups, devices = mesh.shape["boot"], mesh.shape["space"]
    cut = 2 if devices % 4 == 0 else 1
    mesh = Mesh(
        mesh.devices.reshape(groups, cut, cut, devices // cut**2), ("boot",) + SPACE
    )
    in_specs = (
        P(SPACE, None),
        P(SPACE, None),
        P(SPACE),
        P(SPACE),
        P(SPACE, None),
        P(SPACE, None),
        P(("boot",) + SPACE),
    )
    out_specs = P(("boot",) + SPACE, None)
    return jax.shard_map(local, mesh=mesh, in_specs=in_specs, out_specs=out_specs, check_vma=False)
```

```python
import functools

import jax
import jax.numpy as jnp
from jax import lax
from jax.experimental import pallas as pl
from jax.experimental.pallas import tpu as pltpu
from jax.sharding import Mesh
from jax.sharding import PartitionSpec as P

NS_STEPS = 6
SPACE = ("za", "zb", "near")
PARTNERS = ("near", "zb", "za")
LANES = 128
ROWS = 8
MEBI = 1024 * 1024
F32 = jnp.float32
BF16 = jnp.bfloat16


def partner_order(sizes):
    za, zb, near = sizes
    return [(a * zb + b) * near + c for c in range(near) for b in range(zb) for a in range(za)]


def pack_kernel(groups, order, *refs):
    sources, slots_ref, fetched = refs[:6], refs[6], refs[7:13]
    block_ref, tail_ref, info_ref, sems = refs[13:]
    copies = [
        pltpu.make_async_copy(source, target, sems.at[i])
        for i, (source, target) in enumerate(zip(sources, fetched))
    ]
    for copy in copies:
        copy.start()
    for copy in copies[:-1]:
        copy.wait()
    targets_ref, local_ref, mult_ref, prec_ref, dep_ref, rows_ref = fetched
    patches, _, width = block_ref.shape
    count, members = rows_ref.shape
    share = width // members * ROWS
    patch_id = lax.broadcasted_iota(jnp.int32, (patches, count), 0)
    first = patch_id == targets_ref[0:1, :]
    second = patch_id == targets_ref[1:2, :]
    named = jnp.logical_or(first, second)
    earlier = lax.broadcasted_iota(jnp.int32, (count, count), 0) < lax.broadcasted_iota(
        jnp.int32, (count, count), 1
    )
    rank = jnp.dot(
        named.astype(F32).astype(BF16), earlier.astype(F32).astype(BF16), preferred_element_type=F32
    )
    rank = jnp.where(named, rank, -1.0)

    begin = lax.axis_index("boot") * share
    own_id = (lax.broadcasted_iota(jnp.int32, (share, count), 0) + begin).astype(F32)
    picks = [
        jnp.where(own_id == rank[patch : patch + 1, :], 1.0, 0.0) for patch in order
    ]
    picks = jnp.concatenate(picks, axis=0).astype(BF16)
    copies[-1].wait()
    picked = jnp.dot(picks, rows_ref[...], preferred_element_type=F32)
    for patch in range(patches):
        place = patch * share
        blocks = [picked[place + i : place + i + ROWS, :] for i in range(0, share, ROWS)]
        block_ref[patch] = jnp.concatenate(blocks, axis=1).astype(BF16)
    blocks_out = pltpu.make_async_copy(block_ref, slots_ref.at[:, :, 0:width], sems.at[6])
    blocks_out.start()

    mult = mult_ref[...].reshape(1, count).astype(F32)
    prec = prec_ref[...].reshape(1, count)
    weight = local_ref[...].astype(F32) / 1024.0 * (mult * prec)
    weight = weight.astype(BF16).astype(F32)
    dep = dep_ref[...].astype(F32).reshape(1, count)
    by_patch = jnp.where(first, weight[0:1, :], jnp.where(second, weight[1:2, :], 0.0))
    slot_id = lax.broadcasted_iota(jnp.int32, (groups * share, count), 0).astype(F32)
    lane = lax.broadcasted_iota(jnp.int32, (groups * share, LANES), 1)
    info = jnp.zeros((groups * share, LANES), F32)
    for patch in range(patches):
        pick = slot_id == rank[patch : patch + 1, :]
        weight_col = jnp.sum(
            jnp.where(pick, by_patch[patch : patch + 1, :], 0.0), axis=1, keepdims=True
        )
        dep_col = jnp.sum(jnp.where(pick, dep, 0.0), axis=1, keepdims=True)
        info = jnp.where(lane == patch, weight_col, info)
        info = jnp.where(lane == patches + patch, dep_col, info)
    info_ref[...] = jnp.zeros((LANES, LANES), F32)
    info_ref[0 : groups * share, :] = info
    info = info_ref[...].T
    tail_id = lax.broadcasted_iota(jnp.int32, (ROWS, LANES), 0)
    for place, patch in enumerate(order):
        tail = jnp.where(
            tail_id == 0,
            info[patch : patch + 1, :],
            jnp.where(tail_id == 1, info[patches + patch : patches + patch + 1, :], 0.0),
        )
        tail_ref[place] = tail.astype(BF16)
    tails_out = pltpu.make_async_copy(tail_ref, slots_ref.at[:, :, width:], sems.at[7])
    tails_out.start()
    blocks_out.wait()
    tails_out.wait()


def pack(targets, local, mult, prec, dep, rows, order, share, groups):
    count, members = rows.shape
    patches = len(order)
    operands = (targets.T, local.T, mult, prec, dep, rows)
    width = share // ROWS * members
    return pl.pallas_call(
        functools.partial(pack_kernel, groups, order),
        out_shape=jax.ShapeDtypeStruct((patches, ROWS, width + LANES), BF16),
        in_specs=[pl.BlockSpec(memory_space=pl.ANY)] * len(operands),
        out_specs=pl.BlockSpec(memory_space=pl.ANY),
        scratch_shapes=[pltpu.VMEM(operand.shape, operand.dtype) for operand in operands]
        + [
            pltpu.VMEM((patches, ROWS, width), BF16),
            pltpu.VMEM((patches, ROWS, LANES), BF16),
            pltpu.VMEM((LANES, LANES), F32),
            pltpu.SemaphoreType.DMA((len(operands) + 2,)),
        ],
        compiler_params=pltpu.CompilerParams(vmem_limit_bytes=64 * MEBI),
        cost_estimate=pl.CostEstimate(
            flops=2 * patches * share * count * members,
            bytes_accessed=2 * (patches * share + count) * members,
            transcendentals=0,
        ),
        name="pack_rows",
    )(*operands)


def slot_rows(rows_ref, members):
    blocks = []
    for source in range(rows_ref.shape[0]):
        block = rows_ref[source].astype(F32)
        for begin in range(0, block.shape[1] - LANES, members):
            blocks.append(block[:, begin : begin + members])
    return jnp.concatenate(blocks, axis=0)


def slot_info(rows_ref, info_ref):
    sources, _, width = rows_ref.shape
    if 2 * sources < LANES:
        info_ref[2 * sources :, :] = jnp.zeros((LANES - 2 * sources, LANES), F32)
    for source in range(sources):
        tail = rows_ref[source].astype(F32)[:, width - LANES :]
        info_ref[source : source + 1, :] = tail[0:1, :]
        info_ref[sources + source : sources + source + 1, :] = tail[1:2, :]
    info_ref[...] = info_ref[...].T


def scaled_rows(rows, info_ref, turn, sources):
    share = rows.shape[0] // sources
    begin = lax.rem(lax.axis_index("boot") + turn, lax.axis_size("boot")) * share
    info = info_ref[pl.ds(pl.multiple_of(begin, ROWS), share), :]
    blocks, drive = [], jnp.zeros((1, rows.shape[1]), F32)
    for source in range(sources):
        block = rows[source * share : (source + 1) * share, :]
        block = (info[:, source : source + 1] * block).astype(BF16).astype(F32)
        blocks.append(block)
        dep_col = info[:, sources + source : sources + source + 1]
        drive = drive + jnp.sum(dep_col * block, axis=0, keepdims=True)
    return jnp.concatenate(blocks, axis=0).astype(BF16), drive


def gram_kernel(rows_ref, right_ref, corner_ref, drive_ref, info_ref, ordered_ref, turned_ref):
    members, half = right_ref.shape
    slot_info(rows_ref, info_ref)
    rows = slot_rows(rows_ref, members)
    ordered_ref[...] = rows.astype(BF16)
    turned_ref[...] = rows.T.astype(BF16)
    scaled, drive_ref[...] = scaled_rows(rows, info_ref, 0, rows_ref.shape[0])
    dot = functools.partial(jnp.dot, preferred_element_type=F32)
    right_ref[...] = dot(turned_ref[...], scaled[:, half:])
    corner_ref[...] = dot(turned_ref[0:half, :], scaled[:, 0:half])


def own_gram(rows, members):
    sources, height, width = rows.shape
    slots = sources * height * ((width - LANES) // members)
    return pl.pallas_call(
        gram_kernel,
        out_shape=(
            jax.ShapeDtypeStruct((members, members // 2), F32),
            jax.ShapeDtypeStruct((members // 2, members // 2), F32),
            jax.ShapeDtypeStruct((1, members), F32),
            jax.ShapeDtypeStruct((LANES, LANES), F32),
            jax.ShapeDtypeStruct((slots, members), BF16),
            jax.ShapeDtypeStruct((members, slots), BF16),
        ),
        compiler_params=pltpu.CompilerParams(vmem_limit_bytes=16 * MEBI),
        cost_estimate=pl.CostEstimate(
            flops=4 * members * members * slots,
            bytes_accessed=6 * slots * members,
            transcendentals=0,
        ),
        name="own_gram",
    )(rows)


def diagonal_column(value, eye):
    size = value.shape[1]
    parts = []
    for begin in range(0, size, LANES):
        block = value[:, begin : begin + LANES]
        block = block if value.shape[0] == 1 else block[begin : begin + LANES, :]
        parts.append(jnp.sum(jnp.where(eye, block, 0.0), axis=1, keepdims=True))
    return jnp.concatenate(parts, axis=0)


def symmetric_product(left_ref, right_ref):
    half = left_ref.shape[0] // 2
    dot = functools.partial(jnp.dot, preferred_element_type=F32)
    return (
        dot(left_ref[...], right_ref[:, half:]),
        dot(left_ref[0:half, :], right_ref[:, 0:half]),
    )


def put_symmetric(ref, right, corner):
    half = corner.shape[0]
    right = right.astype(BF16)
    ref[:, half:] = right
    ref[0:half, 0:half] = corner.astype(BF16)
    ref[half:, 0:half] = right[0:half, :].T


def weights_kernel(*refs):
    right_ref, corner_ref, drive_ref, own_info_ref, ordered_ref, turned_ref = refs[:6]
    groups = (len(refs) - 6) // 10
    rows_refs, blended_ref = refs[6 : 5 + groups], refs[5 + groups]
    info_refs = refs[6 + groups : 6 + 2 * groups]
    chains = [refs[6 + 2 * groups + 8 * c : 14 + 2 * groups + 8 * c] for c in range(groups)]
    members, half = right_ref.shape
    sources = rows_refs[0].shape[0] if rows_refs else 1
    row_id = lax.broadcasted_iota(jnp.int32, (members, members), 0)
    col_id = lax.broadcasted_iota(jnp.int32, (members, members), 1)
    identity = jnp.where(row_id == col_id, 1.0, 0.0)
    eye = lax.broadcasted_iota(jnp.int32, (LANES, LANES), 0) == lax.broadcasted_iota(
        jnp.int32, (LANES, LANES), 1
    )
    dot = functools.partial(jnp.dot, preferred_element_type=F32)

    def diagonal_row(lower, corner):
        return jnp.concatenate(
            [
                jnp.sum(
                    jnp.where(eye, part[begin : begin + LANES, begin : begin + LANES], 0.0),
                    axis=0,
                    keepdims=True,
                )
                for part in (corner, lower)
                for begin in range(0, half, LANES)
            ],
            axis=1,
        )

    def split(w_high, right, corner):
        put_symmetric(w_high, right, corner)
        for first, part in ((0, corner), (half, right[half:, :])):
            for begin in range(0, half, LANES):
                block = part[begin : begin + LANES, begin : begin + LANES]
                place = slice(first + begin, first + begin + LANES)
                w_high[place, place] = jnp.where(eye, 0.0, block).astype(BF16)
        return 1.5 + diagonal_row(right[half:, :], corner)

    def advance(factor, w_high, right, corner, high):
        change_right, change_corner = symmetric_product(high, w_high)
        return (
            factor[:, half:] * right + change_right,
            factor[:, 0:half] * corner + change_corner,
        )

    infos = [own_info_ref] + list(info_refs[1:])
    rights, corners, drives = [right_ref[...]], [corner_ref[...]], [drive_ref[...]]
    for chain in range(1, groups):
        slot_info(rows_refs[chain - 1], infos[chain])
        scaled, drive = scaled_rows(ordered_ref[...].astype(F32), infos[chain], 0, sources)
        rights.append(dot(turned_ref[...], scaled[:, half:]))
        corners.append(dot(turned_ref[0:half, :], scaled[:, 0:half]))
        drives.append(drive)
    for turn, rows_ref in enumerate(rows_refs, 1):
        rows = slot_rows(rows_ref, members)
        turned = rows.T.astype(BF16)
        for chain in range(groups):
            scaled, drive = scaled_rows(rows, infos[chain], turn, sources)
            rights[chain] = rights[chain] + dot(turned, scaled[:, half:])
            corners[chain] = corners[chain] + dot(turned[0:half, :], scaled[:, 0:half])
            drives[chain] = drives[chain] + drive

    frobenius = []
    for chain, (y_right, y_corner, z_right, z_corner, y_high, z_high, _, w_high) in enumerate(
        chains
    ):
        right = identity[:, half:] + rights[chain] / (members - 1.0)
        corner = identity[0:half, 0:half] + corners[chain] / (members - 1.0)
        squares = right * right
        squares = 2.0 * squares[0:half, :] + squares[half:, :] + corner * corner
        squares = jnp.sum(jnp.sum(squares, axis=0, keepdims=True), axis=1, keepdims=True)
        frobenius.append(jnp.sqrt(squares))
        right, corner = right / frobenius[chain], corner / frobenius[chain]
        factor = split(w_high, -0.5 * right, -0.5 * corner)
        put_symmetric(y_high, right, corner)
        y_right[...], y_corner[...] = advance(factor, w_high, right, corner, y_high)
        z_right[...] = 0.25 * right - 0.75 * identity[:, half:]
        z_corner[...] = 0.25 * corner - 0.75 * identity[0:half, 0:half]
        put_symmetric(y_high, y_right[...], y_corner[...])
        put_symmetric(z_high, z_right[...], z_corner[...])

    def step(_, carry):
        factors = [
            split(chain[7], *symmetric_product(chain[5], chain[4])) for chain in chains
        ]
        for factor, chain in zip(factors, chains):
            for right, corner, high in (
                (chain[0], chain[1], chain[4]),
                (chain[2], chain[3], chain[5]),
            ):
                new_right, new_corner = advance(factor, chain[7], right[...], corner[...], high)
                right[...], corner[...] = new_right, new_corner
                put_symmetric(high, new_right, new_corner)
        return carry

    lax.fori_loop(1, NS_STEPS - 1, step, 0)
    factors = []
    for y_right, y_corner, z_right, z_corner, y_high, z_high, z_off, w_high in chains:
        z_off[...] = z_high[...]
        for right, corner, off in ((y_right, y_corner, y_high), (z_right, z_corner, z_off)):
            for first, part in ((0, corner), (half, right)):
                for begin in range(0, half, LANES):
                    place = slice(first + begin, first + begin + LANES)
                    block = part[place, begin : begin + LANES]
                    off[place, place] = jnp.where(eye, 0.0, block).astype(BF16)
        y_row = diagonal_row(y_right[half:, :], y_corner[...])
        z_row = diagonal_row(z_right[half:, :], z_corner[...])
        z_column = diagonal_column(z_row, eye)
        right, corner = symmetric_product(z_off, y_high)
        right += z_column * y_right[...] + z_right[...] * y_row[:, half:]
        corner += z_column[0:half, :] * y_corner[...] + z_corner[...] * y_row[:, 0:half]
        factors.append(split(w_high, right, corner) - z_row * y_row)
    for chain, (_, _, z_right, z_corner, _, z_high, _, w_high) in enumerate(chains):
        right, corner = advance(factors[chain], w_high, z_right[...], z_corner[...], z_high)
        left = jnp.concatenate([corner, right[0:half, :].T], axis=0)
        root = jnp.concatenate([left, right], axis=1) * (-2.0 / jnp.sqrt(frobenius[chain]))
        inner = jnp.sum(root * diagonal_column(drives[chain], eye), axis=0, keepdims=True)
        mean_weight = jnp.sum(root * diagonal_column(inner, eye), axis=0, keepdims=True)
        blended_ref[chain] = (root + mean_weight / (members - 1.0)).astype(BF16)


def patch_weights(own, other_rows):
    groups, members = len(other_rows) + 1, own[0].shape[0]
    half = members // 2
    right, corner = pltpu.VMEM((members, half), F32), pltpu.VMEM((half, half), F32)
    chain = [right, corner] * 2 + [pltpu.VMEM((members, members), BF16)] * 4
    return pl.pallas_call(
        weights_kernel,
        out_shape=jax.ShapeDtypeStruct((groups, members, members), BF16),
        scratch_shapes=[pltpu.VMEM((LANES, LANES), F32)] * groups + chain * groups,
        compiler_params=pltpu.CompilerParams(vmem_limit_bytes=(8 + 10 * groups) * MEBI),
        cost_estimate=pl.CostEstimate(
            flops=80 * groups * members * members * members,
            bytes_accessed=8 * members * members,
            transcendentals=0,
        ),
        name="patch_weights",
    )(*own, *other_rows)


def update_kernel(order, blended_ref, background_ref, analysis_ref):
    groups = blended_ref.shape[0]
    members, points = background_ref.shape
    rows = members // len(order)
    places = [order.index(holder) for holder in range(len(order))]
    tile = min(points, 256)
    for begin in range(0, points, tile):
        columns = slice(begin, begin + tile)
        background = background_ref[:, columns].astype(F32)
        background = jnp.concatenate(
            [background[place * rows : (place + 1) * rows, :] for place in places], axis=0
        )
        centre = jnp.sum(background, axis=0, keepdims=True) / members
        perturb = (background - centre).astype(BF16)
        for turn in range(groups):
            update = jnp.dot(blended_ref[turn], perturb, preferred_element_type=F32)
            group = lax.rem(lax.axis_index("boot") + turn, groups)
            update = centre + update
            update = jnp.concatenate(
                [update[holder * rows : (holder + 1) * rows, :] for holder in order], axis=0
            )
            update = update.astype(BF16).reshape(len(order), rows, tile)
            analysis_ref[:, group, :, columns] = update


def update_points(blended, background, order):
    groups = blended.shape[0]
    members, points = background.shape
    return pl.pallas_call(
        functools.partial(update_kernel, order),
        out_shape=jax.ShapeDtypeStruct(
            (len(order), groups, members // len(order), points), BF16
        ),
        compiler_params=pltpu.CompilerParams(vmem_limit_bytes=16 * MEBI),
        cost_estimate=pl.CostEstimate(
            flops=2 * groups * members * members * points,
            bytes_accessed=2 * (groups + 1) * members * points,
            transcendentals=0,
        ),
        name="update_points",
    )(blended, background)


def cut_kernel(order, states_ref, cut_ref):
    patches, _, share = cut_ref.shape
    region = states_ref.shape[1] // patches
    offset = lax.axis_index("boot") * share
    for place, patch in enumerate(order):
        begin = pl.multiple_of(patch * region + offset, LANES)
        cut_ref[place] = states_ref[:, pl.ds(begin, share)]


def cut_share(states, order, share):
    own_members, patches = states.shape[0], len(order)
    return pl.pallas_call(
        functools.partial(cut_kernel, order),
        out_shape=jax.ShapeDtypeStruct((patches, own_members, share), BF16),
        compiler_params=pltpu.CompilerParams(vmem_limit_bytes=16 * MEBI),
        cost_estimate=pl.CostEstimate(
            flops=0, bytes_accessed=4 * patches * own_members * share, transcendentals=0
        ),
        name="cut_share",
    )(states)


def place_kernel(order, pieces_ref, whole_ref, held_ref, sems):
    groups, share = pieces_ref.shape[1], pieces_ref.shape[3]
    steps = sems.shape[0]
    width = held_ref.shape[1] // steps
    copies = []
    for step in range(steps):
        for patch in range(step * len(order) // steps, (step + 1) * len(order) // steps):
            for group in range(groups):
                begin = (patch * groups + group) * share
                held_ref[:, begin : begin + share] = pieces_ref[order.index(patch), group]
        columns = slice(step * width, (step + 1) * width)
        copies.append(
            pltpu.make_async_copy(held_ref.at[:, columns], whole_ref.at[:, columns], sems.at[step])
        )
        copies[step].start()
    for copy in copies:
        copy.wait()


def place_pieces(pieces, order):
    patches, groups, own_members, share = pieces.shape
    points = groups * patches * share
    return pl.pallas_call(
        functools.partial(place_kernel, order),
        out_specs=pl.BlockSpec(memory_space=pl.ANY),
        out_shape=jax.ShapeDtypeStruct((own_members, points), BF16),
        scratch_shapes=[pltpu.VMEM((own_members, points), BF16), pltpu.SemaphoreType.DMA((4,))],
        compiler_params=pltpu.CompilerParams(vmem_limit_bytes=16 * MEBI),
        cost_estimate=pl.CostEstimate(
            flops=0, bytes_accessed=4 * own_members * points, transcendentals=0
        ),
        name="place_pieces",
    )(pieces)


def exchange(blocks, axes=PARTNERS):
    return lax.all_to_all(blocks, axes, split_axis=0, concat_axis=0, tiled=True)


def swap_shares(own):
    groups = lax.axis_size("boot")
    return [
        lax.ppermute(own, "boot", [(g, (g - turn) % groups) for g in range(groups)])
        for turn in range(1, groups)
    ]


def local(
    background_states,
    measurement_anomaly_matrix,
    departure_vector,
    measurement_precision,
    measurement_region_targets,
    localization_factor_scaled,
    bootstrap_multiplicity,
):
    order = partner_order([lax.axis_size(axis) for axis in SPACE])
    device_count = len(order)
    groups = lax.axis_size("boot")
    local_rows = measurement_anomaly_matrix.shape[0]
    targets_per = measurement_region_targets.shape[1]
    slot_cap = 2 * targets_per * local_rows // device_count
    slot_share = -(-slot_cap // (ROWS * groups)) * ROWS
    own_members, points = background_states.shape
    share = points // device_count // groups

    slots = pack(
        measurement_region_targets,
        localization_factor_scaled,
        bootstrap_multiplicity,
        measurement_precision,
        departure_vector,
        measurement_anomaly_matrix,
        order,
        slot_share,
        groups,
    )
    own_points = cut_share(background_states, order, share)
    own_rows, own_points = lax.optimization_barrier((exchange(slots), own_points))
    other_rows = swap_shares(own_rows)
    own_points = exchange(own_points).reshape(-1, share)

    own = own_gram(own_rows, measurement_anomaly_matrix.shape[1])
    blended = patch_weights(own, other_rows)
    analysis = update_points(blended, own_points, order)
    analysis = exchange(analysis.reshape(-1, own_members, share), PARTNERS + ("boot",))
    return place_pieces(analysis.reshape(device_count, groups, own_members, share), order)


def solution(mesh):
    groups, devices = mesh.shape["boot"], mesh.shape["space"]
    cut = 2 if devices % 4 == 0 else 1
    mesh = Mesh(
        mesh.devices.reshape(groups, cut, cut, devices // cut**2), ("boot",) + SPACE
    )
    in_specs = (
        P(SPACE, None),
        P(SPACE, None),
        P(SPACE),
        P(SPACE),
        P(SPACE, None),
        P(SPACE, None),
        P(("boot",) + SPACE),
    )
    out_specs = P(("boot",) + SPACE, None)
    return jax.shard_map(local, mesh=mesh, in_specs=in_specs, out_specs=out_specs, check_vma=False)
```

```python
import functools

import jax
import jax.numpy as jnp
from jax import lax
from jax.experimental import pallas as pl
from jax.experimental.pallas import tpu as pltpu
from jax.sharding import Mesh
from jax.sharding import PartitionSpec as P

NS_STEPS = 6
SPACE = ("za", "zb", "near")
PARTNERS = ("near", "za", "zb")
LANES = 128
ROWS = 8
MEBI = 1024 * 1024
F32 = jnp.float32
BF16 = jnp.bfloat16


def partner_order(sizes):
    za, zb, near = sizes
    return [(a * zb + b) * near + c for c in range(near) for a in range(za) for b in range(zb)]


def pack_kernel(groups, order, *refs):
    sources, slots_ref, fetched = refs[:6], refs[6], refs[7:13]
    block_ref, tail_ref, info_ref, sems = refs[13:]
    copies = [
        pltpu.make_async_copy(source, target, sems.at[i])
        for i, (source, target) in enumerate(zip(sources, fetched))
    ]
    for copy in copies:
        copy.start()
    for copy in copies[:-1]:
        copy.wait()
    targets_ref, local_ref, mult_ref, prec_ref, dep_ref, rows_ref = fetched
    patches, _, width = block_ref.shape
    count, members = rows_ref.shape
    share = width // members * ROWS
    patch_id = lax.broadcasted_iota(jnp.int32, (patches, count), 0)
    first = patch_id == targets_ref[0:1, :]
    second = patch_id == targets_ref[1:2, :]
    named = jnp.logical_or(first, second)
    earlier = lax.broadcasted_iota(jnp.int32, (count, count), 0) < lax.broadcasted_iota(
        jnp.int32, (count, count), 1
    )
    rank = jnp.dot(
        named.astype(F32).astype(BF16), earlier.astype(F32).astype(BF16), preferred_element_type=F32
    )
    rank = jnp.where(named, rank, -1.0)

    begin = lax.axis_index("boot") * share
    own_id = (lax.broadcasted_iota(jnp.int32, (share, count), 0) + begin).astype(F32)
    picks = [
        jnp.where(own_id == rank[patch : patch + 1, :], 1.0, 0.0) for patch in order
    ]
    picks = jnp.concatenate(picks, axis=0).astype(BF16)
    copies[-1].wait()
    picked = jnp.dot(picks, rows_ref[...], preferred_element_type=F32)
    for patch in range(patches):
        place = patch * share
        blocks = [picked[place + i : place + i + ROWS, :] for i in range(0, share, ROWS)]
        block_ref[patch] = jnp.concatenate(blocks, axis=1).astype(BF16)
    blocks_out = pltpu.make_async_copy(block_ref, slots_ref.at[:, :, 0:width], sems.at[6])
    blocks_out.start()

    mult = mult_ref[...].reshape(1, count).astype(F32)
    prec = prec_ref[...].reshape(1, count)
    weight = local_ref[...].astype(F32) / 1024.0 * (mult * prec)
    weight = weight.astype(BF16).astype(F32)
    dep = dep_ref[...].astype(F32).reshape(1, count)
    by_patch = jnp.where(first, weight[0:1, :], jnp.where(second, weight[1:2, :], 0.0))
    slot_id = lax.broadcasted_iota(jnp.int32, (groups * share, count), 0).astype(F32)
    lane = lax.broadcasted_iota(jnp.int32, (groups * share, LANES), 1)
    info = jnp.zeros((groups * share, LANES), F32)
    for patch in range(patches):
        pick = slot_id == rank[patch : patch + 1, :]
        weight_col = jnp.sum(
            jnp.where(pick, by_patch[patch : patch + 1, :], 0.0), axis=1, keepdims=True
        )
        dep_col = jnp.sum(jnp.where(pick, dep, 0.0), axis=1, keepdims=True)
        info = jnp.where(lane == patch, weight_col, info)
        info = jnp.where(lane == patches + patch, dep_col, info)
    info_ref[...] = jnp.zeros((LANES, LANES), F32)
    info_ref[0 : groups * share, :] = info
    info = info_ref[...].T
    tail_id = lax.broadcasted_iota(jnp.int32, (ROWS, LANES), 0)
    for place, patch in enumerate(order):
        tail = jnp.where(
            tail_id == 0,
            info[patch : patch + 1, :],
            jnp.where(tail_id == 1, info[patches + patch : patches + patch + 1, :], 0.0),
        )
        tail_ref[place] = tail.astype(BF16)
    tails_out = pltpu.make_async_copy(tail_ref, slots_ref.at[:, :, width:], sems.at[7])
    tails_out.start()
    blocks_out.wait()
    tails_out.wait()


def pack(targets, local, mult, prec, dep, rows, order, share, groups):
    count, members = rows.shape
    patches = len(order)
    operands = (targets.T, local.T, mult, prec, dep, rows)
    width = share // ROWS * members
    return pl.pallas_call(
        functools.partial(pack_kernel, groups, order),
        out_shape=jax.ShapeDtypeStruct((patches, ROWS, width + LANES), BF16),
        in_specs=[pl.BlockSpec(memory_space=pl.ANY)] * len(operands),
        out_specs=pl.BlockSpec(memory_space=pl.ANY),
        scratch_shapes=[pltpu.VMEM(operand.shape, operand.dtype) for operand in operands]
        + [
            pltpu.VMEM((patches, ROWS, width), BF16),
            pltpu.VMEM((patches, ROWS, LANES), BF16),
            pltpu.VMEM((LANES, LANES), F32),
            pltpu.SemaphoreType.DMA((len(operands) + 2,)),
        ],
        compiler_params=pltpu.CompilerParams(vmem_limit_bytes=64 * MEBI),
        cost_estimate=pl.CostEstimate(
            flops=2 * patches * share * count * members,
            bytes_accessed=2 * (patches * share + count) * members,
            transcendentals=0,
        ),
        name="pack_rows",
    )(*operands)


def slot_rows(rows_ref, members):
    blocks = []
    for source in range(rows_ref.shape[0]):
        block = rows_ref[source].astype(F32)
        for begin in range(0, block.shape[1] - LANES, members):
            blocks.append(block[:, begin : begin + members])
    return jnp.concatenate(blocks, axis=0)


def slot_info(rows_ref, info_ref):
    sources, _, width = rows_ref.shape
    if 2 * sources < LANES:
        info_ref[2 * sources :, :] = jnp.zeros((LANES - 2 * sources, LANES), F32)
    for source in range(sources):
        tail = rows_ref[source].astype(F32)[:, width - LANES :]
        info_ref[source : source + 1, :] = tail[0:1, :]
        info_ref[sources + source : sources + source + 1, :] = tail[1:2, :]
    info_ref[...] = info_ref[...].T


def scaled_rows(rows, info_ref, turn, sources):
    share = rows.shape[0] // sources
    begin = lax.rem(lax.axis_index("boot") + turn, lax.axis_size("boot")) * share
    info = info_ref[pl.ds(pl.multiple_of(begin, ROWS), share), :]
    blocks, drive = [], jnp.zeros((1, rows.shape[1]), F32)
    for source in range(sources):
        block = rows[source * share : (source + 1) * share, :]
        block = (info[:, source : source + 1] * block).astype(BF16).astype(F32)
        blocks.append(block)
        dep_col = info[:, sources + source : sources + source + 1]
        drive = drive + jnp.sum(dep_col * block, axis=0, keepdims=True)
    return jnp.concatenate(blocks, axis=0).astype(BF16), drive


def gram_kernel(rows_ref, right_ref, corner_ref, drive_ref, info_ref, ordered_ref, turned_ref):
    members, half = right_ref.shape
    slot_info(rows_ref, info_ref)
    rows = slot_rows(rows_ref, members)
    ordered_ref[...] = rows.astype(BF16)
    turned_ref[...] = rows.T.astype(BF16)
    scaled, drive_ref[...] = scaled_rows(rows, info_ref, 0, rows_ref.shape[0])
    dot = functools.partial(jnp.dot, preferred_element_type=F32)
    right_ref[...] = dot(turned_ref[...], scaled[:, half:])
    corner_ref[...] = dot(turned_ref[0:half, :], scaled[:, 0:half])


def own_gram(rows, members):
    sources, height, width = rows.shape
    slots = sources * height * ((width - LANES) // members)
    return pl.pallas_call(
        gram_kernel,
        out_shape=(
            jax.ShapeDtypeStruct((members, members // 2), F32),
            jax.ShapeDtypeStruct((members // 2, members // 2), F32),
            jax.ShapeDtypeStruct((1, members), F32),
            jax.ShapeDtypeStruct((LANES, LANES), F32),
            jax.ShapeDtypeStruct((slots, members), BF16),
            jax.ShapeDtypeStruct((members, slots), BF16),
        ),
        compiler_params=pltpu.CompilerParams(vmem_limit_bytes=16 * MEBI),
        cost_estimate=pl.CostEstimate(
            flops=4 * members * members * slots,
            bytes_accessed=6 * slots * members,
            transcendentals=0,
        ),
        name="own_gram",
    )(rows)


def diagonal_column(value, eye):
    size = value.shape[1]
    parts = []
    for begin in range(0, size, LANES):
        block = value[:, begin : begin + LANES]
        block = block if value.shape[0] == 1 else block[begin : begin + LANES, :]
        parts.append(jnp.sum(jnp.where(eye, block, 0.0), axis=1, keepdims=True))
    return jnp.concatenate(parts, axis=0)


def symmetric_product(left_ref, right_ref):
    half = left_ref.shape[0] // 2
    dot = functools.partial(jnp.dot, preferred_element_type=F32)
    return (
        dot(left_ref[...], right_ref[:, half:]),
        dot(left_ref[0:half, :], right_ref[:, 0:half]),
    )


def put_symmetric(ref, right, corner):
    half = corner.shape[0]
    right = right.astype(BF16)
    ref[:, half:] = right
    ref[0:half, 0:half] = corner.astype(BF16)
    ref[half:, 0:half] = right[0:half, :].T


def weights_kernel(*refs):
    right_ref, corner_ref, drive_ref, own_info_ref, ordered_ref, turned_ref = refs[:6]
    groups = (len(refs) - 6) // 10
    rows_refs, blended_ref = refs[6 : 5 + groups], refs[5 + groups]
    info_refs = refs[6 + groups : 6 + 2 * groups]
    chains = [refs[6 + 2 * groups + 8 * c : 14 + 2 * groups + 8 * c] for c in range(groups)]
    members, half = right_ref.shape
    sources = rows_refs[0].shape[0] if rows_refs else 1
    row_id = lax.broadcasted_iota(jnp.int32, (members, members), 0)
    col_id = lax.broadcasted_iota(jnp.int32, (members, members), 1)
    identity = jnp.where(row_id == col_id, 1.0, 0.0)
    eye = lax.broadcasted_iota(jnp.int32, (LANES, LANES), 0) == lax.broadcasted_iota(
        jnp.int32, (LANES, LANES), 1
    )
    dot = functools.partial(jnp.dot, preferred_element_type=F32)

    def diagonal_row(lower, corner):
        return jnp.concatenate(
            [
                jnp.sum(
                    jnp.where(eye, part[begin : begin + LANES, begin : begin + LANES], 0.0),
                    axis=0,
                    keepdims=True,
                )
                for part in (corner, lower)
                for begin in range(0, half, LANES)
            ],
            axis=1,
        )

    def split(w_high, right, corner):
        put_symmetric(w_high, right, corner)
        for first, part in ((0, corner), (half, right[half:, :])):
            for begin in range(0, half, LANES):
                block = part[begin : begin + LANES, begin : begin + LANES]
                place = slice(first + begin, first + begin + LANES)
                w_high[place, place] = jnp.where(eye, 0.0, block).astype(BF16)
        return 1.5 + diagonal_row(right[half:, :], corner)

    def advance(factor, w_high, right, corner, high):
        change_right, change_corner = symmetric_product(high, w_high)
        return (
            factor[:, half:] * right + change_right,
            factor[:, 0:half] * corner + change_corner,
        )

    infos = [own_info_ref] + list(info_refs[1:])
    rights, corners, drives = [right_ref[...]], [corner_ref[...]], [drive_ref[...]]
    for chain in range(1, groups):
        slot_info(rows_refs[chain - 1], infos[chain])
        scaled, drive = scaled_rows(ordered_ref[...].astype(F32), infos[chain], 0, sources)
        rights.append(dot(turned_ref[...], scaled[:, half:]))
        corners.append(dot(turned_ref[0:half, :], scaled[:, 0:half]))
        drives.append(drive)
    for turn, rows_ref in enumerate(rows_refs, 1):
        rows = slot_rows(rows_ref, members)
        turned = rows.T.astype(BF16)
        for chain in range(groups):
            scaled, drive = scaled_rows(rows, infos[chain], turn, sources)
            rights[chain] = rights[chain] + dot(turned, scaled[:, half:])
            corners[chain] = corners[chain] + dot(turned[0:half, :], scaled[:, 0:half])
            drives[chain] = drives[chain] + drive

    frobenius = []
    for chain, (y_right, y_corner, z_right, z_corner, y_high, z_high, _, w_high) in enumerate(
        chains
    ):
        right = identity[:, half:] + rights[chain] / (members - 1.0)
        corner = identity[0:half, 0:half] + corners[chain] / (members - 1.0)
        squares = right * right
        squares = 2.0 * squares[0:half, :] + squares[half:, :] + corner * corner
        squares = jnp.sum(jnp.sum(squares, axis=0, keepdims=True), axis=1, keepdims=True)
        frobenius.append(jnp.sqrt(squares))
        right, corner = right / frobenius[chain], corner / frobenius[chain]
        factor = split(w_high, -0.5 * right, -0.5 * corner)
        put_symmetric(y_high, right, corner)
        y_right[...], y_corner[...] = advance(factor, w_high, right, corner, y_high)
        z_right[...] = 0.25 * right - 0.75 * identity[:, half:]
        z_corner[...] = 0.25 * corner - 0.75 * identity[0:half, 0:half]
        put_symmetric(y_high, y_right[...], y_corner[...])
        put_symmetric(z_high, z_right[...], z_corner[...])

    def step(_, carry):
        factors = [
            split(chain[7], *symmetric_product(chain[5], chain[4])) for chain in chains
        ]
        for factor, chain in zip(factors, chains):
            for right, corner, high in (
                (chain[0], chain[1], chain[4]),
                (chain[2], chain[3], chain[5]),
            ):
                new_right, new_corner = advance(factor, chain[7], right[...], corner[...], high)
                right[...], corner[...] = new_right, new_corner
                put_symmetric(high, new_right, new_corner)
        return carry

    lax.fori_loop(1, NS_STEPS - 1, step, 0)
    factors = []
    for y_right, y_corner, z_right, z_corner, y_high, z_high, z_off, w_high in chains:
        z_off[...] = z_high[...]
        for right, corner, off in ((y_right, y_corner, y_high), (z_right, z_corner, z_off)):
            for first, part in ((0, corner), (half, right)):
                for begin in range(0, half, LANES):
                    place = slice(first + begin, first + begin + LANES)
                    block = part[place, begin : begin + LANES]
                    off[place, place] = jnp.where(eye, 0.0, block).astype(BF16)
        y_row = diagonal_row(y_right[half:, :], y_corner[...])
        z_row = diagonal_row(z_right[half:, :], z_corner[...])
        z_column = diagonal_column(z_row, eye)
        right, corner = symmetric_product(z_off, y_high)
        right += z_column * y_right[...] + z_right[...] * y_row[:, half:]
        corner += z_column[0:half, :] * y_corner[...] + z_corner[...] * y_row[:, 0:half]
        factors.append(split(w_high, right, corner) - z_row * y_row)
    for chain, (_, _, z_right, z_corner, _, z_high, _, w_high) in enumerate(chains):
        right, corner = advance(factors[chain], w_high, z_right[...], z_corner[...], z_high)
        left = jnp.concatenate([corner, right[0:half, :].T], axis=0)
        root = jnp.concatenate([left, right], axis=1) * (-2.0 / jnp.sqrt(frobenius[chain]))
        inner = jnp.sum(root * diagonal_column(drives[chain], eye), axis=0, keepdims=True)
        mean_weight = jnp.sum(root * diagonal_column(inner, eye), axis=0, keepdims=True)
        blended_ref[chain] = (root + mean_weight / (members - 1.0)).astype(BF16)


def patch_weights(own, other_rows):
    groups, members = len(other_rows) + 1, own[0].shape[0]
    half = members // 2
    right, corner = pltpu.VMEM((members, half), F32), pltpu.VMEM((half, half), F32)
    chain = [right, corner] * 2 + [pltpu.VMEM((members, members), BF16)] * 4
    return pl.pallas_call(
        weights_kernel,
        out_shape=jax.ShapeDtypeStruct((groups, members, members), BF16),
        scratch_shapes=[pltpu.VMEM((LANES, LANES), F32)] * groups + chain * groups,
        compiler_params=pltpu.CompilerParams(vmem_limit_bytes=(8 + 10 * groups) * MEBI),
        cost_estimate=pl.CostEstimate(
            flops=80 * groups * members * members * members,
            bytes_accessed=8 * members * members,
            transcendentals=0,
        ),
        name="patch_weights",
    )(*own, *other_rows)


def update_kernel(order, blended_ref, background_ref, analysis_ref):
    groups = blended_ref.shape[0]
    members, points = background_ref.shape
    rows = members // len(order)
    places = [order.index(holder) for holder in range(len(order))]
    tile = min(points, 256)
    for begin in range(0, points, tile):
        columns = slice(begin, begin + tile)
        background = background_ref[:, columns].astype(F32)
        background = jnp.concatenate(
            [background[place * rows : (place + 1) * rows, :] for place in places], axis=0
        )
        centre = jnp.sum(background, axis=0, keepdims=True) / members
        perturb = (background - centre).astype(BF16)
        for turn in range(groups):
            update = jnp.dot(blended_ref[turn], perturb, preferred_element_type=F32)
            group = lax.rem(lax.axis_index("boot") + turn, groups)
            update = centre + update
            update = jnp.concatenate(
                [update[holder * rows : (holder + 1) * rows, :] for holder in order], axis=0
            )
            update = update.astype(BF16).reshape(len(order), rows, tile)
            analysis_ref[:, group, :, columns] = update


def update_points(blended, background, order):
    groups = blended.shape[0]
    members, points = background.shape
    return pl.pallas_call(
        functools.partial(update_kernel, order),
        out_shape=jax.ShapeDtypeStruct(
            (len(order), groups, members // len(order), points), BF16
        ),
        compiler_params=pltpu.CompilerParams(vmem_limit_bytes=16 * MEBI),
        cost_estimate=pl.CostEstimate(
            flops=2 * groups * members * members * points,
            bytes_accessed=2 * (groups + 1) * members * points,
            transcendentals=0,
        ),
        name="update_points",
    )(blended, background)


def cut_kernel(order, states_ref, cut_ref):
    patches, _, share = cut_ref.shape
    region = states_ref.shape[1] // patches
    offset = lax.axis_index("boot") * share
    for place, patch in enumerate(order):
        begin = pl.multiple_of(patch * region + offset, LANES)
        cut_ref[place] = states_ref[:, pl.ds(begin, share)]


def cut_share(states, order, share):
    own_members, patches = states.shape[0], len(order)
    return pl.pallas_call(
        functools.partial(cut_kernel, order),
        out_shape=jax.ShapeDtypeStruct((patches, own_members, share), BF16),
        compiler_params=pltpu.CompilerParams(vmem_limit_bytes=16 * MEBI),
        cost_estimate=pl.CostEstimate(
            flops=0, bytes_accessed=4 * patches * own_members * share, transcendentals=0
        ),
        name="cut_share",
    )(states)


def place_kernel(order, pieces_ref, whole_ref, held_ref, sems):
    groups, share = pieces_ref.shape[1], pieces_ref.shape[3]
    steps = sems.shape[0]
    width = held_ref.shape[1] // steps
    copies = []
    for step in range(steps):
        for patch in range(step * len(order) // steps, (step + 1) * len(order) // steps):
            for group in range(groups):
                begin = (patch * groups + group) * share
                held_ref[:, begin : begin + share] = pieces_ref[order.index(patch), group]
        columns = slice(step * width, (step + 1) * width)
        copies.append(
            pltpu.make_async_copy(held_ref.at[:, columns], whole_ref.at[:, columns], sems.at[step])
        )
        copies[step].start()
    for copy in copies:
        copy.wait()


def place_pieces(pieces, order):
    patches, groups, own_members, share = pieces.shape
    points = groups * patches * share
    return pl.pallas_call(
        functools.partial(place_kernel, order),
        out_specs=pl.BlockSpec(memory_space=pl.ANY),
        out_shape=jax.ShapeDtypeStruct((own_members, points), BF16),
        scratch_shapes=[pltpu.VMEM((own_members, points), BF16), pltpu.SemaphoreType.DMA((4,))],
        compiler_params=pltpu.CompilerParams(vmem_limit_bytes=16 * MEBI),
        cost_estimate=pl.CostEstimate(
            flops=0, bytes_accessed=4 * own_members * points, transcendentals=0
        ),
        name="place_pieces",
    )(pieces)


def exchange(blocks, axes=PARTNERS):
    return lax.all_to_all(blocks, axes, split_axis=0, concat_axis=0, tiled=True)


def swap_shares(own):
    groups = lax.axis_size("boot")
    return [
        lax.ppermute(own, "boot", [(g, (g - turn) % groups) for g in range(groups)])
        for turn in range(1, groups)
    ]


def local(
    background_states,
    measurement_anomaly_matrix,
    departure_vector,
    measurement_precision,
    measurement_region_targets,
    localization_factor_scaled,
    bootstrap_multiplicity,
):
    order = partner_order([lax.axis_size(axis) for axis in SPACE])
    device_count = len(order)
    groups = lax.axis_size("boot")
    local_rows = measurement_anomaly_matrix.shape[0]
    targets_per = measurement_region_targets.shape[1]
    slot_cap = 2 * targets_per * local_rows // device_count
    slot_share = -(-slot_cap // (ROWS * groups)) * ROWS
    own_members, points = background_states.shape
    share = points // device_count // groups

    slots = pack(
        measurement_region_targets,
        localization_factor_scaled,
        bootstrap_multiplicity,
        measurement_precision,
        departure_vector,
        measurement_anomaly_matrix,
        order,
        slot_share,
        groups,
    )
    own_points = cut_share(background_states, order, share)
    own_rows, own_points = lax.optimization_barrier((exchange(slots), own_points))
    other_rows = swap_shares(own_rows)
    own_points = exchange(own_points).reshape(-1, share)

    own = own_gram(own_rows, measurement_anomaly_matrix.shape[1])
    blended = patch_weights(own, other_rows)
    analysis = update_points(blended, own_points, order)
    analysis = exchange(analysis.reshape(-1, own_members, share), PARTNERS + ("boot",))
    return place_pieces(analysis.reshape(device_count, groups, own_members, share), order)


def solution(mesh):
    groups, devices = mesh.shape["boot"], mesh.shape["space"]
    cut = 2 if devices % 4 == 0 else 1
    mesh = Mesh(
        mesh.devices.reshape(groups, cut, cut, devices // cut**2), ("boot",) + SPACE
    )
    in_specs = (
        P(SPACE, None),
        P(SPACE, None),
        P(SPACE),
        P(SPACE),
        P(SPACE, None),
        P(SPACE, None),
        P(("boot",) + SPACE),
    )
    out_specs = P(("boot",) + SPACE, None)
    return jax.shard_map(local, mesh=mesh, in_specs=in_specs, out_specs=out_specs, check_vma=False)
```

```python
import functools

import jax
import jax.numpy as jnp
from jax import lax
from jax.experimental import pallas as pl
from jax.experimental.pallas import tpu as pltpu
from jax.sharding import Mesh
from jax.sharding import PartitionSpec as P

NS_STEPS = 6
SPACE = ("za", "zb", "near")
PARTNERS = ("near", "zb", "za")
LANES = 128
ROWS = 8
MEBI = 1024 * 1024
F32 = jnp.float32
BF16 = jnp.bfloat16


def partner_order(sizes):
    za, zb, near = sizes
    return [(a * zb + b) * near + c for c in range(near) for b in range(zb) for a in range(za)]


def pack_kernel(groups, order, *refs):
    sources, slots_ref, fetched = refs[:6], refs[6], refs[7:13]
    block_ref, tail_ref, info_ref, sems = refs[13:]
    copies = [
        pltpu.make_async_copy(source, target, sems.at[i])
        for i, (source, target) in enumerate(zip(sources, fetched))
    ]
    for copy in copies:
        copy.start()
    for copy in copies[:-1]:
        copy.wait()
    targets_ref, local_ref, mult_ref, prec_ref, dep_ref, rows_ref = fetched
    patches, _, width = block_ref.shape
    count, members = rows_ref.shape
    share = width // members * ROWS
    patch_id = lax.broadcasted_iota(jnp.int32, (patches, count), 0)
    first = patch_id == targets_ref[0:1, :]
    second = patch_id == targets_ref[1:2, :]
    named = jnp.logical_or(first, second)
    earlier = lax.broadcasted_iota(jnp.int32, (count, count), 0) < lax.broadcasted_iota(
        jnp.int32, (count, count), 1
    )
    rank = jnp.dot(
        named.astype(F32).astype(BF16), earlier.astype(F32).astype(BF16), preferred_element_type=F32
    )
    rank = jnp.where(named, rank, -1.0)

    slots = groups * share
    slot_id = lax.broadcasted_iota(jnp.int32, (slots, count), 0) + lax.axis_index("boot") * share
    slot_id = jnp.where(slot_id < slots, slot_id, slot_id - slots).astype(F32)
    named_by = [
        jnp.where(slot_id == rank[patch : patch + 1, :], 1.0, 0.0) for patch in order
    ]
    picks = jnp.concatenate([pick[0:share, :] for pick in named_by], axis=0).astype(BF16)
    copies[-1].wait()
    picked = jnp.dot(picks, rows_ref[...], preferred_element_type=F32)
    for patch in range(patches):
        place = patch * share
        blocks = [picked[place + i : place + i + ROWS, :] for i in range(0, share, ROWS)]
        block_ref[patch] = jnp.concatenate(blocks, axis=1).astype(BF16)
    blocks_out = pltpu.make_async_copy(block_ref, slots_ref.at[:, :, 0:width], sems.at[6])
    blocks_out.start()

    mult = mult_ref[...].reshape(1, count).astype(F32)
    prec = prec_ref[...].reshape(1, count)
    weight = local_ref[...].astype(F32) / 1024.0 * (mult * prec)
    weight = weight.astype(BF16).astype(F32)
    dep = dep_ref[...].astype(F32).reshape(1, count)
    by_patch = jnp.where(first, weight[0:1, :], jnp.where(second, weight[1:2, :], 0.0))
    info_ref[...] = jnp.zeros(info_ref.shape, F32)
    info_ref[0:patches, :] = by_patch
    info_ref[patches : patches + 1, :] = dep
    info = jnp.dot(
        jnp.concatenate(named_by, axis=0).astype(BF16),
        info_ref[...].T.astype(BF16),
        preferred_element_type=F32,
    )
    lane = lax.broadcasted_iota(jnp.int32, (ROWS, LANES), 1)
    height = slots // ROWS
    for place, patch in enumerate(order):
        tail = jnp.zeros((ROWS, LANES), F32)
        for i in range(height):
            begin = place * slots + i * ROWS
            block = info[begin : begin + ROWS, :]
            tail = jnp.where(lane == i, block[:, patch : patch + 1], tail)
            tail = jnp.where(lane == height + i, block[:, patches : patches + 1], tail)
        tail_ref[place] = tail.astype(BF16)
    tails_out = pltpu.make_async_copy(tail_ref, slots_ref.at[:, :, width:], sems.at[7])
    tails_out.start()
    blocks_out.wait()
    tails_out.wait()


def pack(targets, local, mult, prec, dep, rows, order, share, groups):
    count, members = rows.shape
    patches = len(order)
    operands = (targets.T, local.T, mult, prec, dep, rows)
    width = share // ROWS * members
    return pl.pallas_call(
        functools.partial(pack_kernel, groups, order),
        out_shape=jax.ShapeDtypeStruct((patches, ROWS, width + LANES), BF16),
        in_specs=[pl.BlockSpec(memory_space=pl.ANY)] * len(operands),
        out_specs=pl.BlockSpec(memory_space=pl.ANY),
        scratch_shapes=[pltpu.VMEM(operand.shape, operand.dtype) for operand in operands]
        + [
            pltpu.VMEM((patches, ROWS, width), BF16),
            pltpu.VMEM((patches, ROWS, LANES), BF16),
            pltpu.VMEM((LANES, count), F32),
            pltpu.SemaphoreType.DMA((len(operands) + 2,)),
        ],
        compiler_params=pltpu.CompilerParams(vmem_limit_bytes=64 * MEBI),
        cost_estimate=pl.CostEstimate(
            flops=2 * patches * share * count * members,
            bytes_accessed=2 * (patches * share + count) * members,
            transcendentals=0,
        ),
        name="pack_rows",
    )(*operands)


def slot_rows(rows_ref, members):
    blocks = []
    for source in range(rows_ref.shape[0]):
        block = rows_ref[source].astype(F32)
        for begin in range(0, block.shape[1] - LANES, members):
            blocks.append(block[:, begin : begin + members])
    return jnp.concatenate(blocks, axis=0)


def slot_tails(rows_ref):
    return [
        rows_ref[source, :, rows_ref.shape[2] - LANES :].astype(F32)
        for source in range(rows_ref.shape[0])
    ]


def scaled_rows(rows, tails, position, groups):
    height = rows.shape[0] // len(tails) // ROWS
    blocks, drive = [], jnp.zeros((ROWS, rows.shape[1]), F32)
    for source, tail in enumerate(tails):
        for i in range(height):
            begin = (source * height + i) * ROWS
            column = position * height + i
            block = tail[:, column : column + 1] * rows[begin : begin + ROWS, :]
            block = block.astype(BF16).astype(F32)
            blocks.append(block)
            column += groups * height
            drive = drive + tail[:, column : column + 1] * block
    return jnp.concatenate(blocks, axis=0).astype(BF16), jnp.sum(drive, axis=0, keepdims=True)


def gram_kernel(groups, *refs):
    rows_ref, right_ref, corner_ref, drive_ref, tails_ref, ordered_ref, turned_ref = refs
    members, half = right_ref.shape
    rows = slot_rows(rows_ref, members)
    ordered_ref[...] = rows.astype(BF16)
    turned_ref[...] = rows.T.astype(BF16)
    tails = slot_tails(rows_ref)
    for source, tail in enumerate(tails):
        tails_ref[source] = tail
    scaled, drive_ref[...] = scaled_rows(rows, tails, 0, groups)
    dot = functools.partial(jnp.dot, preferred_element_type=F32)
    right_ref[...] = dot(turned_ref[...], scaled[:, half:])
    corner_ref[...] = dot(turned_ref[0:half, :], scaled[:, 0:half])


def own_gram(rows, members, groups):
    sources, height, width = rows.shape
    slots = sources * height * ((width - LANES) // members)
    return pl.pallas_call(
        functools.partial(gram_kernel, groups),
        out_shape=(
            jax.ShapeDtypeStruct((members, members // 2), F32),
            jax.ShapeDtypeStruct((members // 2, members // 2), F32),
            jax.ShapeDtypeStruct((1, members), F32),
            jax.ShapeDtypeStruct((sources, height, LANES), F32),
            jax.ShapeDtypeStruct((slots, members), BF16),
            jax.ShapeDtypeStruct((members, slots), BF16),
        ),
        compiler_params=pltpu.CompilerParams(vmem_limit_bytes=16 * MEBI),
        cost_estimate=pl.CostEstimate(
            flops=4 * members * members * slots,
            bytes_accessed=6 * slots * members,
            transcendentals=0,
        ),
        name="own_gram",
    )(rows)


def diagonal_column(value, eye):
    size = value.shape[1]
    parts = []
    for begin in range(0, size, LANES):
        block = value[:, begin : begin + LANES]
        block = block if value.shape[0] == 1 else block[begin : begin + LANES, :]
        parts.append(jnp.sum(jnp.where(eye, block, 0.0), axis=1, keepdims=True))
    return jnp.concatenate(parts, axis=0)


def symmetric_product(left_ref, right_ref):
    half = left_ref.shape[0] // 2
    dot = functools.partial(jnp.dot, preferred_element_type=F32)
    return (
        dot(left_ref[...], right_ref[:, half:]),
        dot(left_ref[0:half, :], right_ref[:, 0:half]),
    )


def put_symmetric(ref, right, corner):
    half = corner.shape[0]
    right = right.astype(BF16)
    ref[:, half:] = right
    ref[0:half, 0:half] = corner.astype(BF16)
    ref[half:, 0:half] = right[0:half, :].T


def weights_kernel(*refs):
    right_ref, corner_ref, drive_ref, tails_ref, ordered_ref, turned_ref = refs[:6]
    groups = (len(refs) - 6) // 9
    rows_refs, blended_ref = refs[6 : 5 + groups], refs[5 + groups]
    chains = [refs[6 + groups + 8 * c : 14 + groups + 8 * c] for c in range(groups)]
    members, half = right_ref.shape
    row_id = lax.broadcasted_iota(jnp.int32, (members, members), 0)
    col_id = lax.broadcasted_iota(jnp.int32, (members, members), 1)
    identity = jnp.where(row_id == col_id, 1.0, 0.0)
    eye = lax.broadcasted_iota(jnp.int32, (LANES, LANES), 0) == lax.broadcasted_iota(
        jnp.int32, (LANES, LANES), 1
    )
    dot = functools.partial(jnp.dot, preferred_element_type=F32)

    def diagonal_row(lower, corner):
        return jnp.concatenate(
            [
                jnp.sum(
                    jnp.where(eye, part[begin : begin + LANES, begin : begin + LANES], 0.0),
                    axis=0,
                    keepdims=True,
                )
                for part in (corner, lower)
                for begin in range(0, half, LANES)
            ],
            axis=1,
        )

    def split(w_high, right, corner):
        put_symmetric(w_high, right, corner)
        for first, part in ((0, corner), (half, right[half:, :])):
            for begin in range(0, half, LANES):
                block = part[begin : begin + LANES, begin : begin + LANES]
                place = slice(first + begin, first + begin + LANES)
                w_high[place, place] = jnp.where(eye, 0.0, block).astype(BF16)
        return 1.5 + diagonal_row(right[half:, :], corner)

    def advance(factor, w_high, right, corner, high):
        change_right, change_corner = symmetric_product(high, w_high)
        return (
            factor[:, half:] * right + change_right,
            factor[:, 0:half] * corner + change_corner,
        )

    tails = [[tails_ref[source] for source in range(tails_ref.shape[0])]]
    tails += [slot_tails(rows_ref) for rows_ref in rows_refs]
    rights, corners, drives = [right_ref[...]], [corner_ref[...]], [drive_ref[...]]
    rows = ordered_ref[...].astype(F32)
    for chain in range(1, groups):
        scaled, drive = scaled_rows(rows, tails[chain], groups - chain, groups)
        rights.append(dot(turned_ref[...], scaled[:, half:]))
        corners.append(dot(turned_ref[0:half, :], scaled[:, 0:half]))
        drives.append(drive)
    for turn, rows_ref in enumerate(rows_refs, 1):
        rows = slot_rows(rows_ref, members)
        turned = rows.T.astype(BF16)
        for chain in range(groups):
            scaled, drive = scaled_rows(rows, tails[chain], (turn - chain) % groups, groups)
            rights[chain] = rights[chain] + dot(turned, scaled[:, half:])
            corners[chain] = corners[chain] + dot(turned[0:half, :], scaled[:, 0:half])
            drives[chain] = drives[chain] + drive

    frobenius = []
    for chain, (y_right, y_corner, z_right, z_corner, y_high, z_high, _, w_high) in enumerate(
        chains
    ):
        right = identity[:, half:] + rights[chain] / (members - 1.0)
        corner = identity[0:half, 0:half] + corners[chain] / (members - 1.0)
        squares = right * right
        squares = 2.0 * squares[0:half, :] + squares[half:, :] + corner * corner
        squares = jnp.sum(jnp.sum(squares, axis=0, keepdims=True), axis=1, keepdims=True)
        frobenius.append(jnp.sqrt(squares))
        right, corner = right / frobenius[chain], corner / frobenius[chain]
        factor = split(w_high, -0.5 * right, -0.5 * corner)
        put_symmetric(y_high, right, corner)
        y_right[...], y_corner[...] = advance(factor, w_high, right, corner, y_high)
        z_right[...] = 0.25 * right - 0.75 * identity[:, half:]
        z_corner[...] = 0.25 * corner - 0.75 * identity[0:half, 0:half]
        put_symmetric(y_high, y_right[...], y_corner[...])
        put_symmetric(z_high, z_right[...], z_corner[...])

    def step(_, carry):
        factors = [
            split(chain[7], *symmetric_product(chain[5], chain[4])) for chain in chains
        ]
        for factor, chain in zip(factors, chains):
            for right, corner, high in (
                (chain[0], chain[1], chain[4]),
                (chain[2], chain[3], chain[5]),
            ):
                new_right, new_corner = advance(factor, chain[7], right[...], corner[...], high)
                right[...], corner[...] = new_right, new_corner
                put_symmetric(high, new_right, new_corner)
        return carry

    lax.fori_loop(1, NS_STEPS - 1, step, 0)
    factors = []
    for y_right, y_corner, z_right, z_corner, y_high, z_high, z_off, w_high in chains:
        z_off[...] = z_high[...]
        for right, corner, off in ((y_right, y_corner, y_high), (z_right, z_corner, z_off)):
            for first, part in ((0, corner), (half, right)):
                for begin in range(0, half, LANES):
                    place = slice(first + begin, first + begin + LANES)
                    block = part[place, begin : begin + LANES]
                    off[place, place] = jnp.where(eye, 0.0, block).astype(BF16)
        y_row = diagonal_row(y_right[half:, :], y_corner[...])
        z_row = diagonal_row(z_right[half:, :], z_corner[...])
        z_column = diagonal_column(z_row, eye)
        right, corner = symmetric_product(z_off, y_high)
        right += z_column * y_right[...] + z_right[...] * y_row[:, half:]
        corner += z_column[0:half, :] * y_corner[...] + z_corner[...] * y_row[:, 0:half]
        factors.append(split(w_high, right, corner) - z_row * y_row)
    for chain, (_, _, z_right, z_corner, _, z_high, _, w_high) in enumerate(chains):
        right, corner = advance(factors[chain], w_high, z_right[...], z_corner[...], z_high)
        left = jnp.concatenate([corner, right[0:half, :].T], axis=0)
        root = jnp.concatenate([left, right], axis=1) * (-2.0 / jnp.sqrt(frobenius[chain]))
        inner = jnp.sum(root * diagonal_column(drives[chain], eye), axis=0, keepdims=True)
        mean_weight = jnp.sum(root * diagonal_column(inner, eye), axis=0, keepdims=True)
        blended_ref[chain] = (root + mean_weight / (members - 1.0)).astype(BF16)


def patch_weights(own, other_rows):
    groups, members = len(other_rows) + 1, own[0].shape[0]
    half = members // 2
    right, corner = pltpu.VMEM((members, half), F32), pltpu.VMEM((half, half), F32)
    chain = [right, corner] * 2 + [pltpu.VMEM((members, members), BF16)] * 4
    return pl.pallas_call(
        weights_kernel,
        out_shape=jax.ShapeDtypeStruct((groups, members, members), BF16),
        scratch_shapes=chain * groups,
        compiler_params=pltpu.CompilerParams(vmem_limit_bytes=(8 + 10 * groups) * MEBI),
        cost_estimate=pl.CostEstimate(
            flops=80 * groups * members * members * members,
            bytes_accessed=8 * members * members,
            transcendentals=0,
        ),
        name="patch_weights",
    )(*own, *other_rows)


def update_kernel(order, blended_ref, background_ref, analysis_ref):
    groups = blended_ref.shape[0]
    members, points = background_ref.shape
    rows = members // len(order)
    places = [order.index(holder) for holder in range(len(order))]
    tile = min(points, 256)
    for begin in range(0, points, tile):
        columns = slice(begin, begin + tile)
        background = background_ref[:, columns].astype(F32)
        background = jnp.concatenate(
            [background[place * rows : (place + 1) * rows, :] for place in places], axis=0
        )
        centre = jnp.sum(background, axis=0, keepdims=True) / members
        perturb = (background - centre).astype(BF16)
        for turn in range(groups):
            update = jnp.dot(blended_ref[turn], perturb, preferred_element_type=F32)
            group = lax.rem(lax.axis_index("boot") + turn, groups)
            update = centre + update
            update = jnp.concatenate(
                [update[holder * rows : (holder + 1) * rows, :] for holder in order], axis=0
            )
            update = update.astype(BF16).reshape(len(order), rows, tile)
            analysis_ref[:, group, :, columns] = update


def update_points(blended, background, order):
    groups = blended.shape[0]
    members, points = background.shape
    return pl.pallas_call(
        functools.partial(update_kernel, order),
        out_shape=jax.ShapeDtypeStruct(
            (len(order), groups, members // len(order), points), BF16
        ),
        compiler_params=pltpu.CompilerParams(vmem_limit_bytes=16 * MEBI),
        cost_estimate=pl.CostEstimate(
            flops=2 * groups * members * members * points,
            bytes_accessed=2 * (groups + 1) * members * points,
            transcendentals=0,
        ),
        name="update_points",
    )(blended, background)


def cut_kernel(order, states_ref, cut_ref):
    patches, _, share = cut_ref.shape
    region = states_ref.shape[1] // patches
    offset = lax.axis_index("boot") * share
    for place, patch in enumerate(order):
        begin = pl.multiple_of(patch * region + offset, LANES)
        cut_ref[place] = states_ref[:, pl.ds(begin, share)]


def cut_share(states, order, share):
    own_members, patches = states.shape[0], len(order)
    return pl.pallas_call(
        functools.partial(cut_kernel, order),
        out_shape=jax.ShapeDtypeStruct((patches, own_members, share), BF16),
        compiler_params=pltpu.CompilerParams(vmem_limit_bytes=16 * MEBI),
        cost_estimate=pl.CostEstimate(
            flops=0, bytes_accessed=4 * patches * own_members * share, transcendentals=0
        ),
        name="cut_share",
    )(states)


def place_kernel(order, pieces_ref, whole_ref, held_ref, sems):
    groups, share = pieces_ref.shape[1], pieces_ref.shape[3]
    steps = sems.shape[0]
    width = held_ref.shape[1] // steps
    copies = []
    for step in range(steps):
        for patch in range(step * len(order) // steps, (step + 1) * len(order) // steps):
            for group in range(groups):
                begin = (patch * groups + group) * share
                held_ref[:, begin : begin + share] = pieces_ref[order.index(patch), group]
        columns = slice(step * width, (step + 1) * width)
        copies.append(
            pltpu.make_async_copy(held_ref.at[:, columns], whole_ref.at[:, columns], sems.at[step])
        )
        copies[step].start()
    for copy in copies:
        copy.wait()


def place_pieces(pieces, order):
    patches, groups, own_members, share = pieces.shape
    points = groups * patches * share
    return pl.pallas_call(
        functools.partial(place_kernel, order),
        out_specs=pl.BlockSpec(memory_space=pl.ANY),
        out_shape=jax.ShapeDtypeStruct((own_members, points), BF16),
        scratch_shapes=[pltpu.VMEM((own_members, points), BF16), pltpu.SemaphoreType.DMA((4,))],
        compiler_params=pltpu.CompilerParams(vmem_limit_bytes=16 * MEBI),
        cost_estimate=pl.CostEstimate(
            flops=0, bytes_accessed=4 * own_members * points, transcendentals=0
        ),
        name="place_pieces",
    )(pieces)


def exchange(blocks, axes=PARTNERS):
    return lax.all_to_all(blocks, axes, split_axis=0, concat_axis=0, tiled=True)


def swap_shares(own):
    groups = lax.axis_size("boot")
    return [
        lax.ppermute(own, "boot", [(g, (g - turn) % groups) for g in range(groups)])
        for turn in range(1, groups)
    ]


def local(
    background_states,
    measurement_anomaly_matrix,
    departure_vector,
    measurement_precision,
    measurement_region_targets,
    localization_factor_scaled,
    bootstrap_multiplicity,
):
    order = partner_order([lax.axis_size(axis) for axis in SPACE])
    device_count = len(order)
    groups = lax.axis_size("boot")
    local_rows = measurement_anomaly_matrix.shape[0]
    targets_per = measurement_region_targets.shape[1]
    slot_cap = 2 * targets_per * local_rows // device_count
    slot_share = -(-slot_cap // (ROWS * groups)) * ROWS
    own_members, points = background_states.shape
    share = points // device_count // groups

    slots = pack(
        measurement_region_targets,
        localization_factor_scaled,
        bootstrap_multiplicity,
        measurement_precision,
        departure_vector,
        measurement_anomaly_matrix,
        order,
        slot_share,
        groups,
    )
    own_points = cut_share(background_states, order, share)
    own_rows, own_points = lax.optimization_barrier((exchange(slots), own_points))
    other_rows = swap_shares(own_rows)
    own_points = exchange(own_points).reshape(-1, share)

    own = own_gram(own_rows, measurement_anomaly_matrix.shape[1], groups)
    blended = patch_weights(own, other_rows)
    analysis = update_points(blended, own_points, order)
    analysis = exchange(analysis.reshape(-1, own_members, share), PARTNERS + ("boot",))
    return place_pieces(analysis.reshape(device_count, groups, own_members, share), order)


def solution(mesh):
    groups, devices = mesh.shape["boot"], mesh.shape["space"]
    cut = 2 if devices % 4 == 0 else 1
    mesh = Mesh(
        mesh.devices.reshape(groups, cut, cut, devices // cut**2), ("boot",) + SPACE
    )
    in_specs = (
        P(SPACE, None),
        P(SPACE, None),
        P(SPACE),
        P(SPACE),
        P(SPACE, None),
        P(SPACE, None),
        P(("boot",) + SPACE),
    )
    out_specs = P(("boot",) + SPACE, None)
    return jax.shard_map(local, mesh=mesh, in_specs=in_specs, out_specs=out_specs, check_vma=False)
```

```python
import functools

import jax
import jax.numpy as jnp
from jax import lax
from jax.experimental import pallas as pl
from jax.experimental.pallas import tpu as pltpu
from jax.sharding import Mesh
from jax.sharding import PartitionSpec as P

NS_STEPS = 6
SPACE = ("za", "zb", "near")
PARTNERS = ("near", "zb", "za")
LANES = 128
ROWS = 8
MEBI = 1024 * 1024
F32 = jnp.float32
BF16 = jnp.bfloat16


def partner_order(sizes):
    za, zb, near = sizes
    return [(a * zb + b) * near + c for c in range(near) for b in range(zb) for a in range(za)]


def pack_kernel(groups, order, *refs):
    sources, slots_ref, fetched = refs[:6], refs[6], refs[7:13]
    block_ref, tail_ref, info_ref, sems = refs[13:]
    copies = [
        pltpu.make_async_copy(source, target, sems.at[i])
        for i, (source, target) in enumerate(zip(sources, fetched))
    ]
    for copy in copies:
        copy.start()
    for copy in copies[:-1]:
        copy.wait()
    targets_ref, local_ref, mult_ref, prec_ref, dep_ref, rows_ref = fetched
    patches, _, width = block_ref.shape
    count, members = rows_ref.shape
    share = width // members * ROWS
    patch_id = lax.broadcasted_iota(jnp.int32, (patches, count), 0)
    first = patch_id == targets_ref[0:1, :]
    second = patch_id == targets_ref[1:2, :]
    named = jnp.logical_or(first, second)
    earlier = lax.broadcasted_iota(jnp.int32, (count, count), 0) < lax.broadcasted_iota(
        jnp.int32, (count, count), 1
    )
    rank = jnp.dot(
        named.astype(F32).astype(BF16), earlier.astype(F32).astype(BF16), preferred_element_type=F32
    )
    rank = jnp.where(named, rank, -1.0)

    slots = groups * share
    slot_id = lax.broadcasted_iota(jnp.int32, (slots, count), 0) + lax.axis_index("boot") * share
    slot_id = jnp.where(slot_id < slots, slot_id, slot_id - slots).astype(F32)
    named_by = [
        jnp.where(slot_id == rank[patch : patch + 1, :], 1.0, 0.0) for patch in order
    ]
    picks = jnp.concatenate([pick[0:share, :] for pick in named_by], axis=0).astype(BF16)
    copies[-1].wait()
    picked = jnp.dot(picks, rows_ref[...], preferred_element_type=F32)
    for patch in range(patches):
        place = patch * share
        blocks = [picked[place + i : place + i + ROWS, :] for i in range(0, share, ROWS)]
        block_ref[patch] = jnp.concatenate(blocks, axis=1).astype(BF16)
    blocks_out = pltpu.make_async_copy(block_ref, slots_ref.at[:, :, 0:width], sems.at[6])
    blocks_out.start()

    mult = mult_ref[...].reshape(1, count).astype(F32)
    prec = prec_ref[...].reshape(1, count)
    weight = local_ref[...].astype(F32) / 1024.0 * (mult * prec)
    weight = weight.astype(BF16).astype(F32)
    dep = dep_ref[...].astype(F32).reshape(1, count)
    by_patch = jnp.where(first, weight[0:1, :], jnp.where(second, weight[1:2, :], 0.0))
    info_ref[...] = jnp.zeros(info_ref.shape, F32)
    info_ref[0:patches, :] = by_patch
    info_ref[patches : patches + 1, :] = dep
    info = jnp.dot(
        jnp.concatenate(named_by, axis=0).astype(BF16),
        info_ref[...].T.astype(BF16),
        preferred_element_type=F32,
    )
    lane = lax.broadcasted_iota(jnp.int32, (ROWS, LANES), 1)
    height = slots // ROWS
    for place, patch in enumerate(order):
        tail = jnp.zeros((ROWS, LANES), F32)
        for i in range(height):
            begin = place * slots + i * ROWS
            block = info[begin : begin + ROWS, :]
            tail = jnp.where(lane == i, block[:, patch : patch + 1], tail)
            tail = jnp.where(lane == height + i, block[:, patches : patches + 1], tail)
        tail_ref[place] = tail.astype(BF16)
    tails_out = pltpu.make_async_copy(tail_ref, slots_ref.at[:, :, width:], sems.at[7])
    tails_out.start()
    blocks_out.wait()
    tails_out.wait()


def pack(targets, local, mult, prec, dep, rows, order, share, groups):
    count, members = rows.shape
    patches = len(order)
    operands = (targets.T, local.T, mult, prec, dep, rows)
    width = share // ROWS * members
    return pl.pallas_call(
        functools.partial(pack_kernel, groups, order),
        out_shape=jax.ShapeDtypeStruct((patches, ROWS, width + LANES), BF16),
        in_specs=[pl.BlockSpec(memory_space=pl.ANY)] * len(operands),
        out_specs=pl.BlockSpec(memory_space=pl.ANY),
        scratch_shapes=[pltpu.VMEM(operand.shape, operand.dtype) for operand in operands]
        + [
            pltpu.VMEM((patches, ROWS, width), BF16),
            pltpu.VMEM((patches, ROWS, LANES), BF16),
            pltpu.VMEM((LANES, count), F32),
            pltpu.SemaphoreType.DMA((len(operands) + 2,)),
        ],
        compiler_params=pltpu.CompilerParams(vmem_limit_bytes=64 * MEBI),
        cost_estimate=pl.CostEstimate(
            flops=2 * patches * share * count * members,
            bytes_accessed=2 * (patches * share + count) * members,
            transcendentals=0,
        ),
        name="pack_rows",
    )(*operands)


def slot_rows(rows_ref, members):
    blocks = []
    for source in range(rows_ref.shape[0]):
        block = rows_ref[source].astype(F32)
        for begin in range(0, block.shape[1] - LANES, members):
            blocks.append(block[:, begin : begin + members])
    return jnp.concatenate(blocks, axis=0)


def slot_tails(rows_ref):
    return [
        rows_ref[source, :, rows_ref.shape[2] - LANES :].astype(F32)
        for source in range(rows_ref.shape[0])
    ]


def scaled_rows(rows, tails, position, groups):
    height = rows.shape[0] // len(tails) // ROWS
    blocks, drive = [], jnp.zeros((ROWS, rows.shape[1]), F32)
    for source, tail in enumerate(tails):
        for i in range(height):
            begin = (source * height + i) * ROWS
            column = position * height + i
            block = tail[:, column : column + 1] * rows[begin : begin + ROWS, :]
            block = block.astype(BF16).astype(F32)
            blocks.append(block)
            column += groups * height
            drive = drive + tail[:, column : column + 1] * block
    return jnp.concatenate(blocks, axis=0).astype(BF16), jnp.sum(drive, axis=0, keepdims=True)


def gram_kernel(groups, *refs):
    rows_ref, right_ref, corner_ref, drive_ref, tails_ref, ordered_ref, turned_ref = refs
    members, half = right_ref.shape
    rows = slot_rows(rows_ref, members)
    ordered_ref[...] = rows.astype(BF16)
    turned_ref[...] = rows.T.astype(BF16)
    tails = slot_tails(rows_ref)
    for source, tail in enumerate(tails):
        tails_ref[source] = tail
    scaled, drive_ref[...] = scaled_rows(rows, tails, 0, groups)
    dot = functools.partial(jnp.dot, preferred_element_type=F32)
    right_ref[...] = dot(turned_ref[...], scaled[:, half:])
    corner_ref[...] = dot(turned_ref[0:half, :], scaled[:, 0:half])


def own_gram(rows, members, groups):
    sources, height, width = rows.shape
    slots = sources * height * ((width - LANES) // members)
    return pl.pallas_call(
        functools.partial(gram_kernel, groups),
        out_shape=(
            jax.ShapeDtypeStruct((members, members // 2), F32),
            jax.ShapeDtypeStruct((members // 2, members // 2), F32),
            jax.ShapeDtypeStruct((1, members), F32),
            jax.ShapeDtypeStruct((sources, height, LANES), F32),
            jax.ShapeDtypeStruct((slots, members), BF16),
            jax.ShapeDtypeStruct((members, slots), BF16),
        ),
        compiler_params=pltpu.CompilerParams(vmem_limit_bytes=16 * MEBI),
        cost_estimate=pl.CostEstimate(
            flops=4 * members * members * slots,
            bytes_accessed=6 * slots * members,
            transcendentals=0,
        ),
        name="own_gram",
    )(rows)


def diagonal_column(value, eye):
    size = value.shape[1]
    parts = []
    for begin in range(0, size, LANES):
        block = value[:, begin : begin + LANES]
        block = block if value.shape[0] == 1 else block[begin : begin + LANES, :]
        parts.append(jnp.sum(jnp.where(eye, block, 0.0), axis=1, keepdims=True))
    return jnp.concatenate(parts, axis=0)


def symmetric_product(left_ref, right_ref):
    half = left_ref.shape[0] // 2
    dot = functools.partial(jnp.dot, preferred_element_type=F32)
    return (
        dot(left_ref[...], right_ref[:, half:]),
        dot(left_ref[0:half, :], right_ref[:, 0:half]),
    )


def put_symmetric(ref, right, corner):
    half = corner.shape[0]
    right = right.astype(BF16)
    ref[:, half:] = right
    ref[0:half, 0:half] = corner.astype(BF16)
    ref[half:, 0:half] = right[0:half, :].T


def weights_kernel(*refs):
    right_ref, corner_ref, drive_ref, tails_ref, ordered_ref, turned_ref = refs[:6]
    groups = (len(refs) - 6) // 9
    rows_refs, blended_ref = refs[6 : 5 + groups], refs[5 + groups]
    chains = [refs[6 + groups + 8 * c : 14 + groups + 8 * c] for c in range(groups)]
    members, half = right_ref.shape
    row_id = lax.broadcasted_iota(jnp.int32, (members, members), 0)
    col_id = lax.broadcasted_iota(jnp.int32, (members, members), 1)
    identity = jnp.where(row_id == col_id, 1.0, 0.0)
    eye = lax.broadcasted_iota(jnp.int32, (LANES, LANES), 0) == lax.broadcasted_iota(
        jnp.int32, (LANES, LANES), 1
    )
    dot = functools.partial(jnp.dot, preferred_element_type=F32)

    def diagonal_row(lower, corner):
        return jnp.concatenate(
            [
                jnp.sum(
                    jnp.where(eye, part[begin : begin + LANES, begin : begin + LANES], 0.0),
                    axis=0,
                    keepdims=True,
                )
                for part in (corner, lower)
                for begin in range(0, half, LANES)
            ],
            axis=1,
        )

    def split(w_high, right, corner):
        put_symmetric(w_high, right, corner)
        for first, part in ((0, corner), (half, right[half:, :])):
            for begin in range(0, half, LANES):
                block = part[begin : begin + LANES, begin : begin + LANES]
                place = slice(first + begin, first + begin + LANES)
                w_high[place, place] = jnp.where(eye, 0.0, block).astype(BF16)
        return 1.5 + diagonal_row(right[half:, :], corner)

    def advance(factor, w_high, right, corner, high):
        change_right, change_corner = symmetric_product(high, w_high)
        return (
            factor[:, half:] * right + change_right,
            factor[:, 0:half] * corner + change_corner,
        )

    tails = [[tails_ref[source] for source in range(tails_ref.shape[0])]]
    tails += [slot_tails(rows_ref) for rows_ref in rows_refs]
    rights, corners, drives = [right_ref[...]], [corner_ref[...]], [drive_ref[...]]
    rows = ordered_ref[...].astype(F32)
    for chain in range(1, groups):
        scaled, drive = scaled_rows(rows, tails[chain], groups - chain, groups)
        rights.append(dot(turned_ref[...], scaled[:, half:]))
        corners.append(dot(turned_ref[0:half, :], scaled[:, 0:half]))
        drives.append(drive)
    for turn, rows_ref in enumerate(rows_refs, 1):
        rows = slot_rows(rows_ref, members)
        turned = rows.T.astype(BF16)
        for chain in range(groups):
            scaled, drive = scaled_rows(rows, tails[chain], (turn - chain) % groups, groups)
            rights[chain] = rights[chain] + dot(turned, scaled[:, half:])
            corners[chain] = corners[chain] + dot(turned[0:half, :], scaled[:, 0:half])
            drives[chain] = drives[chain] + drive

    frobenius = []
    for chain, (y_right, y_corner, z_right, z_corner, y_high, z_high, _, w_high) in enumerate(
        chains
    ):
        right = identity[:, half:] + rights[chain] / (members - 1.0)
        corner = identity[0:half, 0:half] + corners[chain] / (members - 1.0)
        squares = right * right
        squares = 2.0 * squares[0:half, :] + squares[half:, :] + corner * corner
        squares = jnp.sum(jnp.sum(squares, axis=0, keepdims=True), axis=1, keepdims=True)
        frobenius.append(jnp.sqrt(squares))
        right, corner = right / frobenius[chain], corner / frobenius[chain]
        factor = split(w_high, -0.5 * right, -0.5 * corner)
        put_symmetric(y_high, right, corner)
        y_right[...], y_corner[...] = advance(factor, w_high, right, corner, y_high)
        z_right[...] = 0.25 * right - 0.75 * identity[:, half:]
        z_corner[...] = 0.25 * corner - 0.75 * identity[0:half, 0:half]
        put_symmetric(y_high, y_right[...], y_corner[...])
        put_symmetric(z_high, z_right[...], z_corner[...])

    def step(_, carry):
        factors = [
            split(chain[7], *symmetric_product(chain[5], chain[4])) for chain in chains
        ]
        for factor, chain in zip(factors, chains):
            for right, corner, high in (
                (chain[0], chain[1], chain[4]),
                (chain[2], chain[3], chain[5]),
            ):
                new_right, new_corner = advance(factor, chain[7], right[...], corner[...], high)
                right[...], corner[...] = new_right, new_corner
                put_symmetric(high, new_right, new_corner)
        return carry

    lax.fori_loop(1, NS_STEPS - 1, step, 0)
    factors = []
    for y_right, y_corner, z_right, z_corner, y_high, z_high, z_off, w_high in chains:
        z_off[...] = z_high[...]
        for right, corner, off in ((y_right, y_corner, y_high), (z_right, z_corner, z_off)):
            for first, part in ((0, corner), (half, right)):
                for begin in range(0, half, LANES):
                    place = slice(first + begin, first + begin + LANES)
                    block = part[place, begin : begin + LANES]
                    off[place, place] = jnp.where(eye, 0.0, block).astype(BF16)
        y_row = diagonal_row(y_right[half:, :], y_corner[...])
        z_row = diagonal_row(z_right[half:, :], z_corner[...])
        z_column = diagonal_column(z_row, eye)
        right, corner = symmetric_product(z_off, y_high)
        right += z_column * y_right[...] + z_right[...] * y_row[:, half:]
        corner += z_column[0:half, :] * y_corner[...] + z_corner[...] * y_row[:, 0:half]
        factors.append(split(w_high, right, corner) - z_row * y_row)
    for chain, (_, _, z_right, z_corner, _, z_high, _, w_high) in enumerate(chains):
        right, corner = advance(factors[chain], w_high, z_right[...], z_corner[...], z_high)
        left = jnp.concatenate([corner, right[0:half, :].T], axis=0)
        root = jnp.concatenate([left, right], axis=1) * (-2.0 / jnp.sqrt(frobenius[chain]))
        inner = jnp.sum(root * diagonal_column(drives[chain], eye), axis=0, keepdims=True)
        mean_weight = jnp.sum(root * diagonal_column(inner, eye), axis=0, keepdims=True)
        blended_ref[chain] = (root + mean_weight / (members - 1.0)).astype(BF16)


def patch_weights(own, other_rows):
    groups, members = len(other_rows) + 1, own[0].shape[0]
    half = members // 2
    right, corner = pltpu.VMEM((members, half), F32), pltpu.VMEM((half, half), F32)
    chain = [right, corner] * 2 + [pltpu.VMEM((members, members), BF16)] * 4
    return pl.pallas_call(
        weights_kernel,
        out_shape=jax.ShapeDtypeStruct((groups, members, members), BF16),
        scratch_shapes=chain * groups,
        compiler_params=pltpu.CompilerParams(vmem_limit_bytes=(8 + 10 * groups) * MEBI),
        cost_estimate=pl.CostEstimate(
            flops=8 * groups * members * members * members,
            bytes_accessed=8 * members * members,
            transcendentals=0,
        ),
        name="patch_weights",
    )(*own, *other_rows)


def update_kernel(order, blended_ref, *refs):
    piece_refs, analysis_ref, members_ref = refs[:-2], refs[-2], refs[-1]
    groups = blended_ref.shape[0]
    near, rows, points = piece_refs[0].shape
    slabs = len(piece_refs)
    members = slabs * near * rows
    slab, place = lax.axis_index(SPACE[:2]), lax.axis_index(SPACE[2])
    for far, piece_ref in enumerate(piece_refs):
        for step in range(near):
            holder = lax.rem(slab + slabs - far, slabs) * near + lax.rem(place + near - step, near)
            begin = pl.multiple_of(holder * rows, rows)
            members_ref[pl.ds(begin, rows), :] = piece_ref[step].astype(members_ref.dtype)
    tile = min(points, 256)
    for begin in range(0, points, tile):
        columns = slice(begin, begin + tile)
        background = members_ref[:, columns].astype(F32)
        centre = jnp.sum(background, axis=0, keepdims=True) / members
        perturb = (background - centre).astype(BF16)
        for turn in range(groups):
            update = jnp.dot(blended_ref[turn], perturb, preferred_element_type=F32)
            group = lax.rem(lax.axis_index("boot") + turn, groups)
            update = centre + update
            update = jnp.concatenate(
                [update[holder * rows : (holder + 1) * rows, :] for holder in order], axis=0
            )
            update = update.astype(BF16).reshape(len(order), rows, tile)
            analysis_ref[:, group, :, columns] = update


def update_points(blended, pieces, order):
    groups, members, _ = blended.shape
    rows, points = pieces[0].shape[1:]
    held = BF16 if rows % 16 == 0 else F32
    return pl.pallas_call(
        functools.partial(update_kernel, order),
        out_shape=jax.ShapeDtypeStruct((len(order), groups, rows, points), BF16),
        scratch_shapes=[pltpu.VMEM((members, points), held)],
        compiler_params=pltpu.CompilerParams(vmem_limit_bytes=16 * MEBI),
        cost_estimate=pl.CostEstimate(
            flops=2 * groups * members * members * points,
            bytes_accessed=2 * (groups + 1) * members * points,
            transcendentals=0,
        ),
        name="update_points",
    )(blended, *pieces)


def slab_sizes():
    return lax.axis_size(SPACE[:2]), lax.axis_size(SPACE[2])


def cut_kernel(slabs, states_ref, *cut_refs):
    share = cut_refs[0].shape[2]
    near = len(cut_refs)
    region = states_ref.shape[1] // (slabs * near)
    offset = lax.axis_index("boot") * share
    slab, place = lax.axis_index(SPACE[:2]), lax.axis_index(SPACE[2])
    for step, cut_ref in enumerate(cut_refs):
        for far in range(slabs):
            patch = lax.rem(slab + far, slabs) * near + lax.rem(place + step, near)
            begin = pl.multiple_of(patch * region + offset, LANES)
            cut_ref[far] = states_ref[:, pl.ds(begin, share)]


def cut_share(states, share):
    slabs, near = slab_sizes()
    own_members = states.shape[0]
    return pl.pallas_call(
        functools.partial(cut_kernel, slabs),
        out_shape=[jax.ShapeDtypeStruct((slabs, own_members, share), BF16)] * near,
        compiler_params=pltpu.CompilerParams(vmem_limit_bytes=16 * MEBI),
        cost_estimate=pl.CostEstimate(
            flops=0, bytes_accessed=4 * slabs * near * own_members * share, transcendentals=0
        ),
        name="cut_share",
    )(states)


def regroup_kernel(near, *refs):
    for far, group_ref in enumerate(refs[near:]):
        for step, cut_ref in enumerate(refs[:near]):
            group_ref[step] = cut_ref[far]


def regroup(cuts):
    slabs, own_members, share = cuts[0].shape
    return pl.pallas_call(
        functools.partial(regroup_kernel, len(cuts)),
        out_shape=[jax.ShapeDtypeStruct((len(cuts), own_members, share), BF16)] * slabs,
        compiler_params=pltpu.CompilerParams(vmem_limit_bytes=16 * MEBI),
        cost_estimate=pl.CostEstimate(
            flops=0, bytes_accessed=4 * len(cuts) * slabs * own_members * share, transcendentals=0
        ),
        name="regroup",
    )(*cuts)


def shift_all(pieces, axes):
    count = len(pieces)
    return [pieces[0]] + [
        lax.ppermute(pieces[step], axes, [(d, (d + step) % count) for d in range(count)])
        for step in range(1, count)
    ]


def place_kernel(order, pieces_ref, whole_ref, held_ref, sems):
    groups, share = pieces_ref.shape[1], pieces_ref.shape[3]
    steps = sems.shape[0]
    width = held_ref.shape[1] // steps
    copies = []
    for step in range(steps):
        for patch in range(step * len(order) // steps, (step + 1) * len(order) // steps):
            for group in range(groups):
                begin = (patch * groups + group) * share
                held_ref[:, begin : begin + share] = pieces_ref[order.index(patch), group]
        columns = slice(step * width, (step + 1) * width)
        copies.append(
            pltpu.make_async_copy(held_ref.at[:, columns], whole_ref.at[:, columns], sems.at[step])
        )
        copies[step].start()
    for copy in copies:
        copy.wait()


def place_pieces(pieces, order):
    patches, groups, own_members, share = pieces.shape
    points = groups * patches * share
    return pl.pallas_call(
        functools.partial(place_kernel, order),
        out_specs=pl.BlockSpec(memory_space=pl.ANY),
        out_shape=jax.ShapeDtypeStruct((own_members, points), BF16),
        scratch_shapes=[pltpu.VMEM((own_members, points), BF16), pltpu.SemaphoreType.DMA((4,))],
        compiler_params=pltpu.CompilerParams(vmem_limit_bytes=16 * MEBI),
        cost_estimate=pl.CostEstimate(
            flops=0, bytes_accessed=4 * own_members * points, transcendentals=0
        ),
        name="place_pieces",
    )(pieces)


def exchange(blocks, axes=PARTNERS):
    return lax.all_to_all(blocks, axes, split_axis=0, concat_axis=0, tiled=True)


def swap_shares(own):
    groups = lax.axis_size("boot")
    return [
        lax.ppermute(own, "boot", [(g, (g - turn) % groups) for g in range(groups)])
        for turn in range(1, groups)
    ]


def local(
    background_states,
    measurement_anomaly_matrix,
    departure_vector,
    measurement_precision,
    measurement_region_targets,
    localization_factor_scaled,
    bootstrap_multiplicity,
):
    order = partner_order([lax.axis_size(axis) for axis in SPACE])
    device_count = len(order)
    groups = lax.axis_size("boot")
    local_rows = measurement_anomaly_matrix.shape[0]
    targets_per = measurement_region_targets.shape[1]
    slot_cap = 2 * targets_per * local_rows // device_count
    slot_share = -(-slot_cap // (ROWS * groups)) * ROWS
    own_members, points = background_states.shape
    share = points // device_count // groups

    slots = pack(
        measurement_region_targets,
        localization_factor_scaled,
        bootstrap_multiplicity,
        measurement_precision,
        departure_vector,
        measurement_anomaly_matrix,
        order,
        slot_share,
        groups,
    )
    slots, background_states = lax.optimization_barrier((slots, background_states))
    cuts = shift_all(cut_share(background_states, share), SPACE[2])
    own_rows, cuts[1] = lax.optimization_barrier((exchange(slots), cuts[1]))
    by_slab = regroup(cuts)
    other_rows = swap_shares(own_rows)
    points_by_slab = shift_all(by_slab, SPACE[:2])

    own = own_gram(own_rows, measurement_anomaly_matrix.shape[1], groups)
    blended = patch_weights(own, other_rows)
    analysis = update_points(blended, points_by_slab, order)
    analysis = exchange(analysis.reshape(-1, own_members, share), PARTNERS + ("boot",))
    return place_pieces(analysis.reshape(device_count, groups, own_members, share), order)


def solution(mesh):
    groups, devices = mesh.shape["boot"], mesh.shape["space"]
    cut = 2 if devices % 4 == 0 else 1
    mesh = Mesh(
        mesh.devices.reshape(groups, cut, cut, devices // cut**2), ("boot",) + SPACE
    )
    in_specs = (
        P(SPACE, None),
        P(SPACE, None),
        P(SPACE),
        P(SPACE),
        P(SPACE, None),
        P(SPACE, None),
        P(("boot",) + SPACE),
    )
    out_specs = P(("boot",) + SPACE, None)
    return jax.shard_map(local, mesh=mesh, in_specs=in_specs, out_specs=out_specs, check_vma=False)
```

```python
import functools

import jax
import jax.numpy as jnp
from jax import lax
from jax.experimental import pallas as pl
from jax.experimental.pallas import tpu as pltpu
from jax.sharding import Mesh
from jax.sharding import PartitionSpec as P

NS_STEPS = 6
SPACE = ("za", "zb", "near")
PARTNERS = ("near", "zb", "za")
LANES = 128
ROWS = 8
MEBI = 1024 * 1024
F32 = jnp.float32
BF16 = jnp.bfloat16


def partner_order(sizes):
    za, zb, near = sizes
    return [(a * zb + b) * near + c for c in range(near) for b in range(zb) for a in range(za)]


def pack_kernel(groups, order, *refs):
    sources, slots_ref, fetched = refs[:6], refs[6], refs[7:13]
    block_ref, tail_ref, info_ref, sems = refs[13:]
    copies = [
        pltpu.make_async_copy(source, target, sems.at[i])
        for i, (source, target) in enumerate(zip(sources, fetched))
    ]
    for copy in copies:
        copy.start()
    for copy in copies[:-1]:
        copy.wait()
    targets_ref, local_ref, mult_ref, prec_ref, dep_ref, rows_ref = fetched
    patches, _, width = block_ref.shape
    count, members = rows_ref.shape
    share = width // members * ROWS
    patch_id = lax.broadcasted_iota(jnp.int32, (patches, count), 0)
    first = patch_id == targets_ref[0:1, :]
    second = patch_id == targets_ref[1:2, :]
    named = jnp.logical_or(first, second)
    earlier = lax.broadcasted_iota(jnp.int32, (count, count), 0) < lax.broadcasted_iota(
        jnp.int32, (count, count), 1
    )
    rank = jnp.dot(
        named.astype(F32).astype(BF16), earlier.astype(F32).astype(BF16), preferred_element_type=F32
    )
    rank = jnp.where(named, rank, -1.0)

    slots = groups * share
    slot_id = lax.broadcasted_iota(jnp.int32, (slots, count), 0) + lax.axis_index("boot") * share
    slot_id = jnp.where(slot_id < slots, slot_id, slot_id - slots).astype(F32)
    named_by = [
        jnp.where(slot_id == rank[patch : patch + 1, :], 1.0, 0.0) for patch in order
    ]
    picks = jnp.concatenate([pick[0:share, :] for pick in named_by], axis=0).astype(BF16)
    copies[-1].wait()
    picked = jnp.dot(picks, rows_ref[...], preferred_element_type=F32)
    for patch in range(patches):
        place = patch * share
        blocks = [picked[place + i : place + i + ROWS, :] for i in range(0, share, ROWS)]
        block_ref[patch] = jnp.concatenate(blocks, axis=1).astype(BF16)
    blocks_out = pltpu.make_async_copy(block_ref, slots_ref.at[:, :, 0:width], sems.at[6])
    blocks_out.start()

    mult = mult_ref[...].reshape(1, count).astype(F32)
    prec = prec_ref[...].reshape(1, count)
    weight = local_ref[...].astype(F32) / 1024.0 * (mult * prec)
    weight = weight.astype(BF16).astype(F32)
    dep = dep_ref[...].astype(F32).reshape(1, count)
    by_patch = jnp.where(first, weight[0:1, :], jnp.where(second, weight[1:2, :], 0.0))
    info_ref[...] = jnp.zeros(info_ref.shape, F32)
    info_ref[0:patches, :] = by_patch
    info_ref[patches : patches + 1, :] = dep
    info = jnp.dot(
        jnp.concatenate(named_by, axis=0).astype(BF16),
        info_ref[...].T.astype(BF16),
        preferred_element_type=F32,
    )
    lane = lax.broadcasted_iota(jnp.int32, (ROWS, LANES), 1)
    height = slots // ROWS
    for place, patch in enumerate(order):
        tail = jnp.zeros((ROWS, LANES), F32)
        for i in range(height):
            begin = place * slots + i * ROWS
            block = info[begin : begin + ROWS, :]
            tail = jnp.where(lane == i, block[:, patch : patch + 1], tail)
            tail = jnp.where(lane == height + i, block[:, patches : patches + 1], tail)
        tail_ref[place] = tail.astype(BF16)
    tails_out = pltpu.make_async_copy(tail_ref, slots_ref.at[:, :, width:], sems.at[7])
    tails_out.start()
    blocks_out.wait()
    tails_out.wait()


def pack(targets, local, mult, prec, dep, rows, order, share, groups):
    count, members = rows.shape
    patches = len(order)
    operands = (targets.T, local.T, mult, prec, dep, rows)
    width = share // ROWS * members
    return pl.pallas_call(
        functools.partial(pack_kernel, groups, order),
        out_shape=jax.ShapeDtypeStruct((patches, ROWS, width + LANES), BF16),
        in_specs=[pl.BlockSpec(memory_space=pl.ANY)] * len(operands),
        out_specs=pl.BlockSpec(memory_space=pl.ANY),
        scratch_shapes=[pltpu.VMEM(operand.shape, operand.dtype) for operand in operands]
        + [
            pltpu.VMEM((patches, ROWS, width), BF16),
            pltpu.VMEM((patches, ROWS, LANES), BF16),
            pltpu.VMEM((LANES, count), F32),
            pltpu.SemaphoreType.DMA((len(operands) + 2,)),
        ],
        compiler_params=pltpu.CompilerParams(vmem_limit_bytes=64 * MEBI),
        cost_estimate=pl.CostEstimate(
            flops=2 * patches * share * count * members,
            bytes_accessed=2 * (patches * share + count) * members,
            transcendentals=0,
        ),
        name="pack_rows",
    )(*operands)


def slot_rows(rows_ref, members):
    blocks = []
    for source in range(rows_ref.shape[0]):
        block = rows_ref[source].astype(F32)
        for begin in range(0, block.shape[1] - LANES, members):
            blocks.append(block[:, begin : begin + members])
    return jnp.concatenate(blocks, axis=0)


def slot_tails(rows_ref):
    return [
        rows_ref[source, :, rows_ref.shape[2] - LANES :].astype(F32)
        for source in range(rows_ref.shape[0])
    ]


def scaled_rows(rows, tails, position, groups):
    height = rows.shape[0] // len(tails) // ROWS
    blocks, drive = [], jnp.zeros((ROWS, rows.shape[1]), F32)
    for source, tail in enumerate(tails):
        for i in range(height):
            begin = (source * height + i) * ROWS
            column = position * height + i
            block = tail[:, column : column + 1] * rows[begin : begin + ROWS, :]
            block = block.astype(BF16).astype(F32)
            blocks.append(block)
            column += groups * height
            drive = drive + tail[:, column : column + 1] * block
    return jnp.concatenate(blocks, axis=0).astype(BF16), jnp.sum(drive, axis=0, keepdims=True)


def gram_kernel(groups, *refs):
    rows_ref, right_ref, corner_ref, drive_ref, tails_ref, ordered_ref, turned_ref = refs
    members, half = right_ref.shape
    rows = slot_rows(rows_ref, members)
    ordered_ref[...] = rows.astype(BF16)
    turned_ref[...] = rows.T.astype(BF16)
    tails = slot_tails(rows_ref)
    for source, tail in enumerate(tails):
        tails_ref[source] = tail
    scaled, drive_ref[...] = scaled_rows(rows, tails, 0, groups)
    dot = functools.partial(jnp.dot, preferred_element_type=F32)
    right_ref[...] = dot(turned_ref[...], scaled[:, half:])
    corner_ref[...] = dot(turned_ref[0:half, :], scaled[:, 0:half])


def own_gram(rows, members, groups):
    sources, height, width = rows.shape
    slots = sources * height * ((width - LANES) // members)
    return pl.pallas_call(
        functools.partial(gram_kernel, groups),
        out_shape=(
            jax.ShapeDtypeStruct((members, members // 2), F32),
            jax.ShapeDtypeStruct((members // 2, members // 2), F32),
            jax.ShapeDtypeStruct((1, members), F32),
            jax.ShapeDtypeStruct((sources, height, LANES), F32),
            jax.ShapeDtypeStruct((slots, members), BF16),
            jax.ShapeDtypeStruct((members, slots), BF16),
        ),
        compiler_params=pltpu.CompilerParams(vmem_limit_bytes=16 * MEBI),
        cost_estimate=pl.CostEstimate(
            flops=4 * members * members * slots,
            bytes_accessed=6 * slots * members,
            transcendentals=0,
        ),
        name="own_gram",
    )(rows)


def diagonal_column(value, eye):
    size = value.shape[1]
    parts = []
    for begin in range(0, size, LANES):
        block = value[:, begin : begin + LANES]
        block = block if value.shape[0] == 1 else block[begin : begin + LANES, :]
        parts.append(jnp.sum(jnp.where(eye, block, 0.0), axis=1, keepdims=True))
    return jnp.concatenate(parts, axis=0)


def symmetric_product(left_ref, right_ref):
    half = left_ref.shape[0] // 2
    dot = functools.partial(jnp.dot, preferred_element_type=F32)
    return (
        dot(left_ref[...], right_ref[:, half:]),
        dot(left_ref[0:half, :], right_ref[:, 0:half]),
    )


def put_symmetric(ref, right, corner):
    half = corner.shape[0]
    right = right.astype(BF16)
    ref[:, half:] = right
    ref[0:half, 0:half] = corner.astype(BF16)
    ref[half:, 0:half] = right[0:half, :].T


def weights_kernel(*refs):
    right_ref, corner_ref, drive_ref, tails_ref, ordered_ref, turned_ref = refs[:6]
    groups = (len(refs) - 6) // 8
    rows_refs, blended_ref = refs[6 : 5 + groups], refs[5 + groups]
    scratch = [refs[6 + groups + 7 * c : 13 + groups + 7 * c] for c in range(groups)]
    members, half = right_ref.shape
    chains = [
        (*state, both.at[0:members], both.at[members : 2 * members], z_off, w_high)
        for *state, both, z_off, w_high in scratch
    ]
    row_id = lax.broadcasted_iota(jnp.int32, (members, members), 0)
    col_id = lax.broadcasted_iota(jnp.int32, (members, members), 1)
    identity = jnp.where(row_id == col_id, 1.0, 0.0)
    eye = lax.broadcasted_iota(jnp.int32, (LANES, LANES), 0) == lax.broadcasted_iota(
        jnp.int32, (LANES, LANES), 1
    )
    dot = functools.partial(jnp.dot, preferred_element_type=F32)

    def diagonal_row(lower, corner):
        return jnp.concatenate(
            [
                jnp.sum(
                    jnp.where(eye, part[begin : begin + LANES, begin : begin + LANES], 0.0),
                    axis=0,
                    keepdims=True,
                )
                for part in (corner, lower)
                for begin in range(0, half, LANES)
            ],
            axis=1,
        )

    def split(w_high, right, corner):
        put_symmetric(w_high, right, corner)
        for first, part in ((0, corner), (half, right[half:, :])):
            for begin in range(0, half, LANES):
                block = part[begin : begin + LANES, begin : begin + LANES]
                place = slice(first + begin, first + begin + LANES)
                w_high[place, place] = jnp.where(eye, 0.0, block).astype(BF16)
        return 1.5 + diagonal_row(right[half:, :], corner)

    def advance(factor, w_high, right, corner, high):
        change_right, change_corner = symmetric_product(high, w_high)
        return (
            factor[:, half:] * right + change_right,
            factor[:, 0:half] * corner + change_corner,
        )

    tails = [[tails_ref[source] for source in range(tails_ref.shape[0])]]
    tails += [slot_tails(rows_ref) for rows_ref in rows_refs]
    rights, corners, drives = [right_ref[...]], [corner_ref[...]], [drive_ref[...]]
    rows = ordered_ref[...].astype(F32)
    for chain in range(1, groups):
        scaled, drive = scaled_rows(rows, tails[chain], groups - chain, groups)
        rights.append(dot(turned_ref[...], scaled[:, half:]))
        corners.append(dot(turned_ref[0:half, :], scaled[:, 0:half]))
        drives.append(drive)
    for turn, rows_ref in enumerate(rows_refs, 1):
        rows = slot_rows(rows_ref, members)
        turned = rows.T.astype(BF16)
        for chain in range(groups):
            scaled, drive = scaled_rows(rows, tails[chain], (turn - chain) % groups, groups)
            rights[chain] = rights[chain] + dot(turned, scaled[:, half:])
            corners[chain] = corners[chain] + dot(turned[0:half, :], scaled[:, 0:half])
            drives[chain] = drives[chain] + drive

    frobenius = []
    for chain, (y_right, y_corner, z_right, z_corner, y_high, z_high, _, w_high) in enumerate(
        chains
    ):
        right = identity[:, half:] + rights[chain] / (members - 1.0)
        corner = identity[0:half, 0:half] + corners[chain] / (members - 1.0)
        squares = right * right
        squares = 2.0 * squares[0:half, :] + squares[half:, :] + corner * corner
        squares = jnp.sum(jnp.sum(squares, axis=0, keepdims=True), axis=1, keepdims=True)
        frobenius.append(jnp.sqrt(squares))
        right, corner = right / frobenius[chain], corner / frobenius[chain]
        factor = split(w_high, -0.5 * right, -0.5 * corner)
        put_symmetric(y_high, right, corner)
        y_right[...], y_corner[...] = advance(factor, w_high, right, corner, y_high)
        z_right[...] = 0.25 * right - 0.75 * identity[:, half:]
        z_corner[...] = 0.25 * corner - 0.75 * identity[0:half, 0:half]
        put_symmetric(y_high, y_right[...], y_corner[...])
        put_symmetric(z_high, z_right[...], z_corner[...])

    def step(_, carry):
        factors = [
            split(chain[7], *symmetric_product(chain[5], chain[4])) for chain in chains
        ]
        for factor, chain, (*_, both, _, w_high) in zip(factors, chains, scratch):
            changes = dot(both[...], w_high[:, half:])
            for first, right, corner, high in (
                (0, chain[0], chain[1], chain[4]),
                (members, chain[2], chain[3], chain[5]),
            ):
                change = dot(high[0:half, :], w_high[:, 0:half])
                new_right = factor[:, half:] * right[...] + changes[first : first + members, :]
                new_corner = factor[:, 0:half] * corner[...] + change
                right[...], corner[...] = new_right, new_corner
                put_symmetric(high, new_right, new_corner)
        return carry

    lax.fori_loop(1, NS_STEPS - 1, step, 0)
    factors = []
    for y_right, y_corner, z_right, z_corner, y_high, z_high, z_off, w_high in chains:
        z_off[...] = z_high[...]
        for right, corner, off in ((y_right, y_corner, y_high), (z_right, z_corner, z_off)):
            for first, part in ((0, corner), (half, right)):
                for begin in range(0, half, LANES):
                    place = slice(first + begin, first + begin + LANES)
                    block = part[place, begin : begin + LANES]
                    off[place, place] = jnp.where(eye, 0.0, block).astype(BF16)
        y_row = diagonal_row(y_right[half:, :], y_corner[...])
        z_row = diagonal_row(z_right[half:, :], z_corner[...])
        z_column = diagonal_column(z_row, eye)
        right, corner = symmetric_product(z_off, y_high)
        right += z_column * y_right[...] + z_right[...] * y_row[:, half:]
        corner += z_column[0:half, :] * y_corner[...] + z_corner[...] * y_row[:, 0:half]
        factors.append(split(w_high, right, corner) - z_row * y_row)
    for chain, (_, _, z_right, z_corner, _, z_high, _, w_high) in enumerate(chains):
        right, corner = advance(factors[chain], w_high, z_right[...], z_corner[...], z_high)
        left = jnp.concatenate([corner, right[0:half, :].T], axis=0)
        root = jnp.concatenate([left, right], axis=1) * (-2.0 / jnp.sqrt(frobenius[chain]))
        inner = jnp.sum(root * diagonal_column(drives[chain], eye), axis=0, keepdims=True)
        mean_weight = jnp.sum(root * diagonal_column(inner, eye), axis=0, keepdims=True)
        blended_ref[chain] = (root + mean_weight / (members - 1.0)).astype(BF16)


def patch_weights(own, other_rows):
    groups, members = len(other_rows) + 1, own[0].shape[0]
    half = members // 2
    right, corner = pltpu.VMEM((members, half), F32), pltpu.VMEM((half, half), F32)
    chain = [right, corner] * 2 + [pltpu.VMEM((2 * members, members), BF16)]
    chain += [pltpu.VMEM((members, members), BF16)] * 2
    return pl.pallas_call(
        weights_kernel,
        out_shape=jax.ShapeDtypeStruct((groups, members, members), BF16),
        scratch_shapes=chain * groups,
        compiler_params=pltpu.CompilerParams(vmem_limit_bytes=(8 + 10 * groups) * MEBI),
        cost_estimate=pl.CostEstimate(
            flops=80 * groups * members * members * members,
            bytes_accessed=8 * members * members,
            transcendentals=0,
        ),
        name="patch_weights",
    )(*own, *other_rows)


def update_kernel(order, blended_ref, background_ref, analysis_ref):
    groups = blended_ref.shape[0]
    members, points = background_ref.shape
    rows = members // len(order)
    places = [order.index(holder) for holder in range(len(order))]
    tile = min(points, 256)
    for begin in range(0, points, tile):
        columns = slice(begin, begin + tile)
        background = background_ref[:, columns].astype(F32)
        background = jnp.concatenate(
            [background[place * rows : (place + 1) * rows, :] for place in places], axis=0
        )
        centre = jnp.sum(background, axis=0, keepdims=True) / members
        perturb = (background - centre).astype(BF16)
        blended = blended_ref[...].reshape(groups * members, members)
        updates = jnp.dot(blended, perturb, preferred_element_type=F32)
        for turn in range(groups):
            update = updates[turn * members : (turn + 1) * members, :]
            group = lax.rem(lax.axis_index("boot") + turn, groups)
            update = centre + update
            update = jnp.concatenate(
                [update[holder * rows : (holder + 1) * rows, :] for holder in order], axis=0
            )
            update = update.astype(BF16).reshape(len(order), rows, tile)
            analysis_ref[:, group, :, columns] = update


def update_points(blended, background, order):
    groups = blended.shape[0]
    members, points = background.shape
    return pl.pallas_call(
        functools.partial(update_kernel, order),
        out_shape=jax.ShapeDtypeStruct(
            (len(order), groups, members // len(order), points), BF16
        ),
        compiler_params=pltpu.CompilerParams(vmem_limit_bytes=16 * MEBI),
        cost_estimate=pl.CostEstimate(
            flops=2 * groups * members * members * points,
            bytes_accessed=2 * (groups + 1) * members * points,
            transcendentals=0,
        ),
        name="update_points",
    )(blended, background)


def cut_kernel(order, states_ref, cut_ref):
    patches, _, share = cut_ref.shape
    region = states_ref.shape[1] // patches
    offset = lax.axis_index("boot") * share
    for place, patch in enumerate(order):
        begin = pl.multiple_of(patch * region + offset, LANES)
        cut_ref[place] = states_ref[:, pl.ds(begin, share)]


def cut_share(states, order, share):
    own_members, patches = states.shape[0], len(order)
    return pl.pallas_call(
        functools.partial(cut_kernel, order),
        out_shape=jax.ShapeDtypeStruct((patches, own_members, share), BF16),
        compiler_params=pltpu.CompilerParams(vmem_limit_bytes=16 * MEBI),
        cost_estimate=pl.CostEstimate(
            flops=0, bytes_accessed=4 * patches * own_members * share, transcendentals=0
        ),
        name="cut_share",
    )(states)


def place_kernel(order, pieces_ref, whole_ref, held_ref, sems):
    groups, share = pieces_ref.shape[1], pieces_ref.shape[3]
    steps = sems.shape[0]
    width = held_ref.shape[1] // steps
    copies = []
    for step in range(steps):
        for patch in range(step * len(order) // steps, (step + 1) * len(order) // steps):
            for group in range(groups):
                begin = (patch * groups + group) * share
                held_ref[:, begin : begin + share] = pieces_ref[order.index(patch), group]
        columns = slice(step * width, (step + 1) * width)
        copies.append(
            pltpu.make_async_copy(held_ref.at[:, columns], whole_ref.at[:, columns], sems.at[step])
        )
        copies[step].start()
    for copy in copies:
        copy.wait()


def place_pieces(pieces, order):
    patches, groups, own_members, share = pieces.shape
    points = groups * patches * share
    return pl.pallas_call(
        functools.partial(place_kernel, order),
        out_specs=pl.BlockSpec(memory_space=pl.ANY),
        out_shape=jax.ShapeDtypeStruct((own_members, points), BF16),
        scratch_shapes=[pltpu.VMEM((own_members, points), BF16), pltpu.SemaphoreType.DMA((4,))],
        compiler_params=pltpu.CompilerParams(vmem_limit_bytes=16 * MEBI),
        cost_estimate=pl.CostEstimate(
            flops=0, bytes_accessed=4 * own_members * points, transcendentals=0
        ),
        name="place_pieces",
    )(pieces)


def exchange(blocks, axes=PARTNERS):
    return lax.all_to_all(blocks, axes, split_axis=0, concat_axis=0, tiled=True)


def swap_shares(own):
    groups = lax.axis_size("boot")
    return [
        lax.ppermute(own, "boot", [(g, (g - turn) % groups) for g in range(groups)])
        for turn in range(1, groups)
    ]


def local(
    background_states,
    measurement_anomaly_matrix,
    departure_vector,
    measurement_precision,
    measurement_region_targets,
    localization_factor_scaled,
    bootstrap_multiplicity,
):
    order = partner_order([lax.axis_size(axis) for axis in SPACE])
    device_count = len(order)
    groups = lax.axis_size("boot")
    local_rows = measurement_anomaly_matrix.shape[0]
    targets_per = measurement_region_targets.shape[1]
    slot_cap = 2 * targets_per * local_rows // device_count
    slot_share = -(-slot_cap // (ROWS * groups)) * ROWS
    own_members, points = background_states.shape
    share = points // device_count // groups

    slots = pack(
        measurement_region_targets,
        localization_factor_scaled,
        bootstrap_multiplicity,
        measurement_precision,
        departure_vector,
        measurement_anomaly_matrix,
        order,
        slot_share,
        groups,
    )
    own_points = cut_share(background_states, order, share)
    own_rows, own_points = lax.optimization_barrier((exchange(slots), own_points))
    other_rows = swap_shares(own_rows)
    own_points = exchange(own_points).reshape(-1, share)

    own = own_gram(own_rows, measurement_anomaly_matrix.shape[1], groups)
    blended = patch_weights(own, other_rows)
    analysis = update_points(blended, own_points, order)
    analysis = exchange(analysis.reshape(-1, own_members, share), PARTNERS + ("boot",))
    return place_pieces(analysis.reshape(device_count, groups, own_members, share), order)


def solution(mesh):
    groups, devices = mesh.shape["boot"], mesh.shape["space"]
    cut = 2 if devices % 4 == 0 else 1
    mesh = Mesh(
        mesh.devices.reshape(groups, cut, cut, devices // cut**2), ("boot",) + SPACE
    )
    in_specs = (
        P(SPACE, None),
        P(SPACE, None),
        P(SPACE),
        P(SPACE),
        P(SPACE, None),
        P(SPACE, None),
        P(("boot",) + SPACE),
    )
    out_specs = P(("boot",) + SPACE, None)
    return jax.shard_map(local, mesh=mesh, in_specs=in_specs, out_specs=out_specs, check_vma=False)
```

```python
import functools

import jax
import jax.numpy as jnp
from jax import lax
from jax.experimental import pallas as pl
from jax.experimental.pallas import tpu as pltpu
from jax.sharding import Mesh
from jax.sharding import PartitionSpec as P

NS_STEPS = 6
SPACE = ("za", "zb", "near")
PARTNERS = ("zb", "near", "za")
LANES = 128
ROWS = 8
MEBI = 1024 * 1024
F32 = jnp.float32
BF16 = jnp.bfloat16


def partner_order(sizes):
    za, zb, near = sizes
    return [(a * zb + b) * near + c for b in range(zb) for c in range(near) for a in range(za)]


def pack_kernel(groups, order, *refs):
    sources, slots_ref, fetched = refs[:6], refs[6], refs[7:13]
    block_ref, tail_ref, info_ref, sems = refs[13:]
    copies = [
        pltpu.make_async_copy(source, target, sems.at[i])
        for i, (source, target) in enumerate(zip(sources, fetched))
    ]
    for copy in copies:
        copy.start()
    for copy in copies[:-1]:
        copy.wait()
    targets_ref, local_ref, mult_ref, prec_ref, dep_ref, rows_ref = fetched
    patches, _, width = block_ref.shape
    count, members = rows_ref.shape
    share = width // members * ROWS
    patch_id = lax.broadcasted_iota(jnp.int32, (patches, count), 0)
    first = patch_id == targets_ref[0:1, :]
    second = patch_id == targets_ref[1:2, :]
    named = jnp.logical_or(first, second)
    earlier = lax.broadcasted_iota(jnp.int32, (count, count), 0) < lax.broadcasted_iota(
        jnp.int32, (count, count), 1
    )
    rank = jnp.dot(
        named.astype(F32).astype(BF16), earlier.astype(F32).astype(BF16), preferred_element_type=F32
    )
    rank = jnp.where(named, rank, -1.0)

    slots = groups * share
    slot_id = lax.broadcasted_iota(jnp.int32, (slots, count), 0) + lax.axis_index("boot") * share
    slot_id = jnp.where(slot_id < slots, slot_id, slot_id - slots).astype(F32)
    named_by = [
        jnp.where(slot_id == rank[patch : patch + 1, :], 1.0, 0.0) for patch in order
    ]
    picks = jnp.concatenate([pick[0:share, :] for pick in named_by], axis=0).astype(BF16)
    copies[-1].wait()
    picked = jnp.dot(picks, rows_ref[...], preferred_element_type=F32)
    for patch in range(patches):
        place = patch * share
        blocks = [picked[place + i : place + i + ROWS, :] for i in range(0, share, ROWS)]
        block_ref[patch] = jnp.concatenate(blocks, axis=1).astype(BF16)
    blocks_out = pltpu.make_async_copy(block_ref, slots_ref.at[:, :, 0:width], sems.at[6])
    blocks_out.start()

    mult = mult_ref[...].reshape(1, count).astype(F32)
    prec = prec_ref[...].reshape(1, count)
    weight = local_ref[...].astype(F32) / 1024.0 * (mult * prec)
    weight = weight.astype(BF16).astype(F32)
    dep = dep_ref[...].astype(F32).reshape(1, count)
    by_patch = jnp.where(first, weight[0:1, :], jnp.where(second, weight[1:2, :], 0.0))
    info_ref[...] = jnp.zeros(info_ref.shape, F32)
    info_ref[0:patches, :] = by_patch
    info_ref[patches : patches + 1, :] = dep
    info = jnp.dot(
        jnp.concatenate(named_by, axis=0).astype(BF16),
        info_ref[...].T.astype(BF16),
        preferred_element_type=F32,
    )
    lane = lax.broadcasted_iota(jnp.int32, (ROWS, LANES), 1)
    height = slots // ROWS
    for place, patch in enumerate(order):
        tail = jnp.zeros((ROWS, LANES), F32)
        for i in range(height):
            begin = place * slots + i * ROWS
            block = info[begin : begin + ROWS, :]
            tail = jnp.where(lane == i, block[:, patch : patch + 1], tail)
            tail = jnp.where(lane == height + i, block[:, patches : patches + 1], tail)
        tail_ref[place] = tail.astype(BF16)
    tails_out = pltpu.make_async_copy(tail_ref, slots_ref.at[:, :, width:], sems.at[7])
    tails_out.start()
    blocks_out.wait()
    tails_out.wait()


def pack(targets, local, mult, prec, dep, rows, order, share, groups):
    count, members = rows.shape
    patches = len(order)
    operands = (targets.T, local.T, mult, prec, dep, rows)
    width = share // ROWS * members
    return pl.pallas_call(
        functools.partial(pack_kernel, groups, order),
        out_shape=jax.ShapeDtypeStruct((patches, ROWS, width + LANES), BF16),
        in_specs=[pl.BlockSpec(memory_space=pl.ANY)] * len(operands),
        out_specs=pl.BlockSpec(memory_space=pl.ANY),
        scratch_shapes=[pltpu.VMEM(operand.shape, operand.dtype) for operand in operands]
        + [
            pltpu.VMEM((patches, ROWS, width), BF16),
            pltpu.VMEM((patches, ROWS, LANES), BF16),
            pltpu.VMEM((LANES, count), F32),
            pltpu.SemaphoreType.DMA((len(operands) + 2,)),
        ],
        compiler_params=pltpu.CompilerParams(vmem_limit_bytes=64 * MEBI),
        cost_estimate=pl.CostEstimate(
            flops=2 * patches * share * count * members,
            bytes_accessed=2 * (patches * share + count) * members,
            transcendentals=0,
        ),
        name="pack_rows",
    )(*operands)


def slot_rows(rows_ref, members):
    blocks = []
    for source in range(rows_ref.shape[0]):
        block = rows_ref[source].astype(F32)
        for begin in range(0, block.shape[1] - LANES, members):
            blocks.append(block[:, begin : begin + members])
    return jnp.concatenate(blocks, axis=0)


def slot_tails(rows_ref):
    return [
        rows_ref[source, :, rows_ref.shape[2] - LANES :].astype(F32)
        for source in range(rows_ref.shape[0])
    ]


def scaled_rows(rows, tails, position, groups):
    height = rows.shape[0] // len(tails) // ROWS
    blocks, drive = [], jnp.zeros((ROWS, rows.shape[1]), F32)
    for source, tail in enumerate(tails):
        for i in range(height):
            begin = (source * height + i) * ROWS
            column = position * height + i
            block = tail[:, column : column + 1] * rows[begin : begin + ROWS, :]
            block = block.astype(BF16).astype(F32)
            blocks.append(block)
            column += groups * height
            drive = drive + tail[:, column : column + 1] * block
    return jnp.concatenate(blocks, axis=0).astype(BF16), jnp.sum(drive, axis=0, keepdims=True)


def gram_kernel(groups, *refs):
    rows_ref, right_ref, corner_ref, drive_ref, tails_ref, ordered_ref, turned_ref = refs
    members, half = right_ref.shape
    rows = slot_rows(rows_ref, members)
    ordered_ref[...] = rows.astype(BF16)
    turned_ref[...] = rows.T.astype(BF16)
    tails = slot_tails(rows_ref)
    for source, tail in enumerate(tails):
        tails_ref[source] = tail
    scaled, drive_ref[...] = scaled_rows(rows, tails, 0, groups)
    dot = functools.partial(jnp.dot, preferred_element_type=F32)
    right_ref[...] = dot(turned_ref[...], scaled[:, half:])
    corner_ref[...] = dot(turned_ref[0:half, :], scaled[:, 0:half])


def own_gram(rows, members, groups):
    sources, height, width = rows.shape
    slots = sources * height * ((width - LANES) // members)
    return pl.pallas_call(
        functools.partial(gram_kernel, groups),
        out_shape=(
            jax.ShapeDtypeStruct((members, members // 2), F32),
            jax.ShapeDtypeStruct((members // 2, members // 2), F32),
            jax.ShapeDtypeStruct((1, members), F32),
            jax.ShapeDtypeStruct((sources, height, LANES), F32),
            jax.ShapeDtypeStruct((slots, members), BF16),
            jax.ShapeDtypeStruct((members, slots), BF16),
        ),
        compiler_params=pltpu.CompilerParams(vmem_limit_bytes=16 * MEBI),
        cost_estimate=pl.CostEstimate(
            flops=4 * members * members * slots,
            bytes_accessed=6 * slots * members,
            transcendentals=0,
        ),
        name="own_gram",
    )(rows)


def diagonal_column(value, eye):
    size = value.shape[1]
    parts = []
    for begin in range(0, size, LANES):
        block = value[:, begin : begin + LANES]
        block = block if value.shape[0] == 1 else block[begin : begin + LANES, :]
        parts.append(jnp.sum(jnp.where(eye, block, 0.0), axis=1, keepdims=True))
    return jnp.concatenate(parts, axis=0)


def symmetric_product(left_ref, right_ref):
    half = left_ref.shape[0] // 2
    dot = functools.partial(jnp.dot, preferred_element_type=F32)
    return (
        dot(left_ref[...], right_ref[:, half:]),
        dot(left_ref[0:half, :], right_ref[:, 0:half]),
    )


def put_symmetric(ref, right, corner):
    half = corner.shape[0]
    right = right.astype(BF16)
    ref[:, half:] = right
    ref[0:half, 0:half] = corner.astype(BF16)
    ref[half:, 0:half] = right[0:half, :].T


def weights_kernel(*refs):
    right_ref, corner_ref, drive_ref, tails_ref, ordered_ref, turned_ref = refs[:6]
    groups = (len(refs) - 6) // 8
    rows_refs, blended_ref = refs[6 : 5 + groups], refs[5 + groups]
    scratch = [refs[6 + groups + 7 * c : 13 + groups + 7 * c] for c in range(groups)]
    members, half = right_ref.shape
    chains = [
        (*state, both.at[0:members], both.at[members : 2 * members], z_off, w_high)
        for *state, both, z_off, w_high in scratch
    ]
    row_id = lax.broadcasted_iota(jnp.int32, (members, members), 0)
    col_id = lax.broadcasted_iota(jnp.int32, (members, members), 1)
    identity = jnp.where(row_id == col_id, 1.0, 0.0)
    eye = lax.broadcasted_iota(jnp.int32, (LANES, LANES), 0) == lax.broadcasted_iota(
        jnp.int32, (LANES, LANES), 1
    )
    dot = functools.partial(jnp.dot, preferred_element_type=F32)

    def diagonal_row(lower, corner):
        return jnp.concatenate(
            [
                jnp.sum(
                    jnp.where(eye, part[begin : begin + LANES, begin : begin + LANES], 0.0),
                    axis=0,
                    keepdims=True,
                )
                for part in (corner, lower)
                for begin in range(0, half, LANES)
            ],
            axis=1,
        )

    def split(w_high, right, corner):
        put_symmetric(w_high, right, corner)
        for first, part in ((0, corner), (half, right[half:, :])):
            for begin in range(0, half, LANES):
                block = part[begin : begin + LANES, begin : begin + LANES]
                place = slice(first + begin, first + begin + LANES)
                w_high[place, place] = jnp.where(eye, 0.0, block).astype(BF16)
        return 1.5 + diagonal_row(right[half:, :], corner)

    def advance(factor, w_high, right, corner, high):
        change_right, change_corner = symmetric_product(high, w_high)
        return (
            factor[:, half:] * right + change_right,
            factor[:, 0:half] * corner + change_corner,
        )

    tails = [[tails_ref[source] for source in range(tails_ref.shape[0])]]
    tails += [slot_tails(rows_ref) for rows_ref in rows_refs]
    rights, corners, drives = [right_ref[...]], [corner_ref[...]], [drive_ref[...]]
    rows = ordered_ref[...].astype(F32)
    for chain in range(1, groups):
        scaled, drive = scaled_rows(rows, tails[chain], groups - chain, groups)
        rights.append(dot(turned_ref[...], scaled[:, half:]))
        corners.append(dot(turned_ref[0:half, :], scaled[:, 0:half]))
        drives.append(drive)
    for turn, rows_ref in enumerate(rows_refs, 1):
        rows = slot_rows(rows_ref, members)
        turned = rows.T.astype(BF16)
        for chain in range(groups):
            scaled, drive = scaled_rows(rows, tails[chain], (turn - chain) % groups, groups)
            rights[chain] = rights[chain] + dot(turned, scaled[:, half:])
            corners[chain] = corners[chain] + dot(turned[0:half, :], scaled[:, 0:half])
            drives[chain] = drives[chain] + drive

    frobenius = []
    for chain, (y_right, y_corner, z_right, z_corner, y_high, z_high, _, w_high) in enumerate(
        chains
    ):
        right = identity[:, half:] + rights[chain] / (members - 1.0)
        corner = identity[0:half, 0:half] + corners[chain] / (members - 1.0)
        squares = right * right
        squares = 2.0 * squares[0:half, :] + squares[half:, :] + corner * corner
        squares = jnp.sum(jnp.sum(squares, axis=0, keepdims=True), axis=1, keepdims=True)
        frobenius.append(jnp.sqrt(squares))
        right, corner = right / frobenius[chain], corner / frobenius[chain]
        factor = split(w_high, -0.5 * right, -0.5 * corner)
        put_symmetric(y_high, right, corner)
        y_right[...], y_corner[...] = advance(factor, w_high, right, corner, y_high)
        z_right[...] = 0.25 * right - 0.75 * identity[:, half:]
        z_corner[...] = 0.25 * corner - 0.75 * identity[0:half, 0:half]
        put_symmetric(y_high, y_right[...], y_corner[...])
        put_symmetric(z_high, z_right[...], z_corner[...])

    def step(_, carry):
        factors = [
            split(chain[7], *symmetric_product(chain[5], chain[4])) for chain in chains
        ]
        for factor, chain, (*_, both, _, w_high) in zip(factors, chains, scratch):
            changes = dot(both[...], w_high[:, half:])
            for first, right, corner, high in (
                (0, chain[0], chain[1], chain[4]),
                (members, chain[2], chain[3], chain[5]),
            ):
                change = dot(high[0:half, :], w_high[:, 0:half])
                new_right = factor[:, half:] * right[...] + changes[first : first + members, :]
                new_corner = factor[:, 0:half] * corner[...] + change
                right[...], corner[...] = new_right, new_corner
                put_symmetric(high, new_right, new_corner)
        return carry

    lax.fori_loop(1, NS_STEPS - 1, step, 0)
    factors = []
    for y_right, y_corner, z_right, z_corner, y_high, z_high, z_off, w_high in chains:
        z_off[...] = z_high[...]
        for right, corner, off in ((y_right, y_corner, y_high), (z_right, z_corner, z_off)):
            for first, part in ((0, corner), (half, right)):
                for begin in range(0, half, LANES):
                    place = slice(first + begin, first + begin + LANES)
                    block = part[place, begin : begin + LANES]
                    off[place, place] = jnp.where(eye, 0.0, block).astype(BF16)
        y_row = diagonal_row(y_right[half:, :], y_corner[...])
        z_row = diagonal_row(z_right[half:, :], z_corner[...])
        z_column = diagonal_column(z_row, eye)
        right, corner = symmetric_product(z_off, y_high)
        right += z_column * y_right[...] + z_right[...] * y_row[:, half:]
        corner += z_column[0:half, :] * y_corner[...] + z_corner[...] * y_row[:, 0:half]
        factors.append(split(w_high, right, corner) - z_row * y_row)
    for chain, (_, _, z_right, z_corner, _, z_high, _, w_high) in enumerate(chains):
        right, corner = advance(factors[chain], w_high, z_right[...], z_corner[...], z_high)
        left = jnp.concatenate([corner, right[0:half, :].T], axis=0)
        root = jnp.concatenate([left, right], axis=1) * (-2.0 / jnp.sqrt(frobenius[chain]))
        inner = jnp.sum(root * diagonal_column(drives[chain], eye), axis=0, keepdims=True)
        mean_weight = jnp.sum(root * diagonal_column(inner, eye), axis=0, keepdims=True)
        blended_ref[chain] = (root + mean_weight / (members - 1.0)).astype(BF16)


def patch_weights(own, other_rows):
    groups, members = len(other_rows) + 1, own[0].shape[0]
    half = members // 2
    right, corner = pltpu.VMEM((members, half), F32), pltpu.VMEM((half, half), F32)
    chain = [right, corner] * 2 + [pltpu.VMEM((2 * members, members), BF16)]
    chain += [pltpu.VMEM((members, members), BF16)] * 2
    return pl.pallas_call(
        weights_kernel,
        out_shape=jax.ShapeDtypeStruct((groups, members, members), BF16),
        scratch_shapes=chain * groups,
        compiler_params=pltpu.CompilerParams(vmem_limit_bytes=(8 + 10 * groups) * MEBI),
        cost_estimate=pl.CostEstimate(
            flops=80 * groups * members * members * members,
            bytes_accessed=8 * members * members,
            transcendentals=0,
        ),
        name="patch_weights",
    )(*own, *other_rows)


def update_kernel(order, blended_ref, background_ref, analysis_ref):
    groups = blended_ref.shape[0]
    members, points = background_ref.shape
    rows = members // len(order)
    places = [order.index(holder) for holder in range(len(order))]
    tile = min(points, 256)
    for begin in range(0, points, tile):
        columns = slice(begin, begin + tile)
        background = background_ref[:, columns].astype(F32)
        background = jnp.concatenate(
            [background[place * rows : (place + 1) * rows, :] for place in places], axis=0
        )
        centre = jnp.sum(background, axis=0, keepdims=True) / members
        perturb = (background - centre).astype(BF16)
        blended = blended_ref[...].reshape(groups * members, members)
        updates = jnp.dot(blended, perturb, preferred_element_type=F32)
        for turn in range(groups):
            update = updates[turn * members : (turn + 1) * members, :]
            group = lax.rem(lax.axis_index("boot") + turn, groups)
            update = centre + update
            update = jnp.concatenate(
                [update[holder * rows : (holder + 1) * rows, :] for holder in order], axis=0
            )
            update = update.astype(BF16).reshape(len(order), rows, tile)
            analysis_ref[:, group, :, columns] = update


def update_points(blended, background, order):
    groups = blended.shape[0]
    members, points = background.shape
    return pl.pallas_call(
        functools.partial(update_kernel, order),
        out_shape=jax.ShapeDtypeStruct(
            (len(order), groups, members // len(order), points), BF16
        ),
        compiler_params=pltpu.CompilerParams(vmem_limit_bytes=16 * MEBI),
        cost_estimate=pl.CostEstimate(
            flops=2 * groups * members * members * points,
            bytes_accessed=2 * (groups + 1) * members * points,
            transcendentals=0,
        ),
        name="update_points",
    )(blended, background)


def cut_kernel(order, states_ref, cut_ref):
    patches, _, share = cut_ref.shape
    region = states_ref.shape[1] // patches
    offset = lax.axis_index("boot") * share
    for place, patch in enumerate(order):
        begin = pl.multiple_of(patch * region + offset, LANES)
        cut_ref[place] = states_ref[:, pl.ds(begin, share)]


def cut_share(states, order, share):
    own_members, patches = states.shape[0], len(order)
    return pl.pallas_call(
        functools.partial(cut_kernel, order),
        out_shape=jax.ShapeDtypeStruct((patches, own_members, share), BF16),
        compiler_params=pltpu.CompilerParams(vmem_limit_bytes=16 * MEBI),
        cost_estimate=pl.CostEstimate(
            flops=0, bytes_accessed=4 * patches * own_members * share, transcendentals=0
        ),
        name="cut_share",
    )(states)


def place_kernel(order, pieces_ref, whole_ref, held_ref, sems):
    groups, share = pieces_ref.shape[1], pieces_ref.shape[3]
    steps = sems.shape[0]
    width = held_ref.shape[1] // steps
    copies = []
    for step in range(steps):
        for patch in range(step * len(order) // steps, (step + 1) * len(order) // steps):
            for group in range(groups):
                begin = (patch * groups + group) * share
                held_ref[:, begin : begin + share] = pieces_ref[order.index(patch), group]
        columns = slice(step * width, (step + 1) * width)
        copies.append(
            pltpu.make_async_copy(held_ref.at[:, columns], whole_ref.at[:, columns], sems.at[step])
        )
        copies[step].start()
    for copy in copies:
        copy.wait()


def place_pieces(pieces, order):
    patches, groups, own_members, share = pieces.shape
    points = groups * patches * share
    return pl.pallas_call(
        functools.partial(place_kernel, order),
        out_specs=pl.BlockSpec(memory_space=pl.ANY),
        out_shape=jax.ShapeDtypeStruct((own_members, points), BF16),
        scratch_shapes=[pltpu.VMEM((own_members, points), BF16), pltpu.SemaphoreType.DMA((4,))],
        compiler_params=pltpu.CompilerParams(vmem_limit_bytes=16 * MEBI),
        cost_estimate=pl.CostEstimate(
            flops=0, bytes_accessed=4 * own_members * points, transcendentals=0
        ),
        name="place_pieces",
    )(pieces)


def exchange(blocks, axes=PARTNERS):
    return lax.all_to_all(blocks, axes, split_axis=0, concat_axis=0, tiled=True)


def swap_shares(own):
    groups = lax.axis_size("boot")
    return [
        lax.ppermute(own, "boot", [(g, (g - turn) % groups) for g in range(groups)])
        for turn in range(1, groups)
    ]


def local(
    background_states,
    measurement_anomaly_matrix,
    departure_vector,
    measurement_precision,
    measurement_region_targets,
    localization_factor_scaled,
    bootstrap_multiplicity,
):
    order = partner_order([lax.axis_size(axis) for axis in SPACE])
    device_count = len(order)
    groups = lax.axis_size("boot")
    local_rows = measurement_anomaly_matrix.shape[0]
    targets_per = measurement_region_targets.shape[1]
    slot_cap = 2 * targets_per * local_rows // device_count
    slot_share = -(-slot_cap // (ROWS * groups)) * ROWS
    own_members, points = background_states.shape
    share = points // device_count // groups

    slots = pack(
        measurement_region_targets,
        localization_factor_scaled,
        bootstrap_multiplicity,
        measurement_precision,
        departure_vector,
        measurement_anomaly_matrix,
        order,
        slot_share,
        groups,
    )
    own_points = cut_share(background_states, order, share)
    own_rows, own_points = lax.optimization_barrier((exchange(slots), own_points))
    other_rows = swap_shares(own_rows)
    own_points = exchange(own_points).reshape(-1, share)

    own = own_gram(own_rows, measurement_anomaly_matrix.shape[1], groups)
    blended = patch_weights(own, other_rows)
    analysis = update_points(blended, own_points, order)
    analysis = exchange(analysis.reshape(-1, own_members, share), PARTNERS + ("boot",))
    return place_pieces(analysis.reshape(device_count, groups, own_members, share), order)


def solution(mesh):
    groups, devices = mesh.shape["boot"], mesh.shape["space"]
    cut = 2 if devices % 4 == 0 else 1
    mesh = Mesh(
        mesh.devices.reshape(groups, cut, cut, devices // cut**2), ("boot",) + SPACE
    )
    in_specs = (
        P(SPACE, None),
        P(SPACE, None),
        P(SPACE),
        P(SPACE),
        P(SPACE, None),
        P(SPACE, None),
        P(("boot",) + SPACE),
    )
    out_specs = P(("boot",) + SPACE, None)
    return jax.shard_map(local, mesh=mesh, in_specs=in_specs, out_specs=out_specs, check_vma=False)
```

```python
import functools

import jax
import jax.numpy as jnp
from jax import lax
from jax.experimental import pallas as pl
from jax.experimental.pallas import tpu as pltpu
from jax.sharding import Mesh
from jax.sharding import PartitionSpec as P

NS_STEPS = 6
SPACE = ("za", "zb", "near")
PARTNERS = ("near", "zb", "za")
LANES = 128
ROWS = 8
MEBI = 1024 * 1024
F32 = jnp.float32
BF16 = jnp.bfloat16


def partner_order(sizes):
    za, zb, near = sizes
    return [(a * zb + b) * near + c for c in range(near) for b in range(zb) for a in range(za)]


def pack_kernel(groups, order, *refs):
    sources, slots_ref, fetched = refs[:6], refs[6], refs[7:13]
    block_ref, tail_ref, info_ref, sems = refs[13:]
    copies = [
        pltpu.make_async_copy(source, target, sems.at[i])
        for i, (source, target) in enumerate(zip(sources, fetched))
    ]
    for copy in copies:
        copy.start()
    for copy in copies[:-1]:
        copy.wait()
    targets_ref, local_ref, mult_ref, prec_ref, dep_ref, rows_ref = fetched
    patches, _, width = block_ref.shape
    count, members = rows_ref.shape
    share = width // members * ROWS
    patch_id = lax.broadcasted_iota(jnp.int32, (patches, count), 0)
    first = patch_id == targets_ref[0:1, :]
    second = patch_id == targets_ref[1:2, :]
    named = jnp.logical_or(first, second)
    earlier = lax.broadcasted_iota(jnp.int32, (count, count), 0) < lax.broadcasted_iota(
        jnp.int32, (count, count), 1
    )
    rank = jnp.dot(
        named.astype(F32).astype(BF16), earlier.astype(F32).astype(BF16), preferred_element_type=F32
    )
    rank = jnp.where(named, rank, -1.0)

    slots = groups * share
    slot_id = lax.broadcasted_iota(jnp.int32, (slots, count), 0) + lax.axis_index("boot") * share
    slot_id = jnp.where(slot_id < slots, slot_id, slot_id - slots).astype(F32)
    named_by = [
        jnp.where(slot_id == rank[patch : patch + 1, :], 1.0, 0.0) for patch in order
    ]
    picks = jnp.concatenate([pick[0:share, :] for pick in named_by], axis=0).astype(BF16)
    copies[-1].wait()
    picked = jnp.dot(picks, rows_ref[...], preferred_element_type=F32)
    for patch in range(patches):
        place = patch * share
        blocks = [picked[place + i : place + i + ROWS, :] for i in range(0, share, ROWS)]
        block_ref[patch] = jnp.concatenate(blocks, axis=1).astype(BF16)
    blocks_out = pltpu.make_async_copy(block_ref, slots_ref.at[:, :, 0:width], sems.at[6])
    blocks_out.start()

    mult = mult_ref[...].reshape(1, count).astype(F32)
    prec = prec_ref[...].reshape(1, count)
    weight = local_ref[...].astype(F32) / 1024.0 * (mult * prec)
    weight = weight.astype(BF16).astype(F32)
    dep = dep_ref[...].astype(F32).reshape(1, count)
    by_patch = jnp.where(first, weight[0:1, :], jnp.where(second, weight[1:2, :], 0.0))
    info_ref[...] = jnp.zeros(info_ref.shape, F32)
    info_ref[0:patches, :] = by_patch
    info_ref[patches : patches + 1, :] = dep
    info = jnp.dot(
        jnp.concatenate(named_by, axis=0).astype(BF16),
        info_ref[...].T.astype(BF16),
        preferred_element_type=F32,
    )
    lane = lax.broadcasted_iota(jnp.int32, (ROWS, LANES), 1)
    height = slots // ROWS
    for place, patch in enumerate(order):
        tail = jnp.zeros((ROWS, LANES), F32)
        for i in range(height):
            begin = place * slots + i * ROWS
            block = info[begin : begin + ROWS, :]
            tail = jnp.where(lane == i, block[:, patch : patch + 1], tail)
            tail = jnp.where(lane == height + i, block[:, patches : patches + 1], tail)
        tail_ref[place] = tail.astype(BF16)
    tails_out = pltpu.make_async_copy(tail_ref, slots_ref.at[:, :, width:], sems.at[7])
    tails_out.start()
    blocks_out.wait()
    tails_out.wait()


def pack(targets, local, mult, prec, dep, rows, order, share, groups):
    count, members = rows.shape
    patches = len(order)
    operands = (targets.T, local.T, mult, prec, dep, rows)
    width = share // ROWS * members
    return pl.pallas_call(
        functools.partial(pack_kernel, groups, order),
        out_shape=jax.ShapeDtypeStruct((patches, ROWS, width + LANES), BF16),
        in_specs=[pl.BlockSpec(memory_space=pl.ANY)] * len(operands),
        out_specs=pl.BlockSpec(memory_space=pl.ANY),
        scratch_shapes=[pltpu.VMEM(operand.shape, operand.dtype) for operand in operands]
        + [
            pltpu.VMEM((patches, ROWS, width), BF16),
            pltpu.VMEM((patches, ROWS, LANES), BF16),
            pltpu.VMEM((LANES, count), F32),
            pltpu.SemaphoreType.DMA((len(operands) + 2,)),
        ],
        compiler_params=pltpu.CompilerParams(vmem_limit_bytes=64 * MEBI),
        cost_estimate=pl.CostEstimate(
            flops=2 * patches * share * count * members,
            bytes_accessed=2 * (patches * share + count) * members,
            transcendentals=0,
        ),
        name="pack_rows",
    )(*operands)


def slot_rows(rows_ref, members):
    blocks = []
    for source in range(rows_ref.shape[0]):
        block = rows_ref[source].astype(F32)
        for begin in range(0, block.shape[1] - LANES, members):
            blocks.append(block[:, begin : begin + members])
    return jnp.concatenate(blocks, axis=0)


def slot_tails(rows_ref):
    return [
        rows_ref[source, :, rows_ref.shape[2] - LANES :].astype(F32)
        for source in range(rows_ref.shape[0])
    ]


def scaled_rows(rows, tails, position, groups):
    height = rows.shape[0] // len(tails) // ROWS
    blocks, drive = [], jnp.zeros((ROWS, rows.shape[1]), F32)
    for source, tail in enumerate(tails):
        for i in range(height):
            begin = (source * height + i) * ROWS
            column = position * height + i
            block = tail[:, column : column + 1] * rows[begin : begin + ROWS, :]
            block = block.astype(BF16).astype(F32)
            blocks.append(block)
            column += groups * height
            drive = drive + tail[:, column : column + 1] * block
    return jnp.concatenate(blocks, axis=0).astype(BF16), jnp.sum(drive, axis=0, keepdims=True)


def gram_kernel(groups, *refs):
    rows_ref, right_ref, corner_ref, drive_ref, tails_ref, ordered_ref, turned_ref = refs
    members, half = right_ref.shape
    rows = slot_rows(rows_ref, members)
    ordered_ref[...] = rows.astype(BF16)
    turned_ref[...] = rows.T.astype(BF16)
    tails = slot_tails(rows_ref)
    for source, tail in enumerate(tails):
        tails_ref[source] = tail
    scaled, drive_ref[...] = scaled_rows(rows, tails, 0, groups)
    dot = functools.partial(jnp.dot, preferred_element_type=F32)
    right_ref[...] = dot(turned_ref[...], scaled[:, half:])
    corner_ref[...] = dot(turned_ref[0:half, :], scaled[:, 0:half])


def own_gram(rows, members, groups):
    sources, height, width = rows.shape
    slots = sources * height * ((width - LANES) // members)
    return pl.pallas_call(
        functools.partial(gram_kernel, groups),
        out_shape=(
            jax.ShapeDtypeStruct((members, members // 2), F32),
            jax.ShapeDtypeStruct((members // 2, members // 2), F32),
            jax.ShapeDtypeStruct((1, members), F32),
            jax.ShapeDtypeStruct((sources, height, LANES), F32),
            jax.ShapeDtypeStruct((slots, members), BF16),
            jax.ShapeDtypeStruct((members, slots), BF16),
        ),
        compiler_params=pltpu.CompilerParams(vmem_limit_bytes=16 * MEBI),
        cost_estimate=pl.CostEstimate(
            flops=4 * members * members * slots,
            bytes_accessed=6 * slots * members,
            transcendentals=0,
        ),
        name="own_gram",
    )(rows)


def diagonal_column(value, eye):
    size = value.shape[1]
    parts = []
    for begin in range(0, size, LANES):
        block = value[:, begin : begin + LANES]
        block = block if value.shape[0] == 1 else block[begin : begin + LANES, :]
        parts.append(jnp.sum(jnp.where(eye, block, 0.0), axis=1, keepdims=True))
    return jnp.concatenate(parts, axis=0)


def symmetric_product(left_ref, right_ref):
    half = left_ref.shape[0] // 2
    dot = functools.partial(jnp.dot, preferred_element_type=F32)
    return (
        dot(left_ref[...], right_ref[:, half:]),
        dot(left_ref[0:half, :], right_ref[:, 0:half]),
    )


def put_symmetric(ref, right, corner):
    half = corner.shape[0]
    right = right.astype(BF16)
    ref[:, half:] = right
    ref[0:half, 0:half] = corner.astype(BF16)
    ref[half:, 0:half] = right[0:half, :].T


def weights_kernel(*refs):
    right_ref, corner_ref, drive_ref, tails_ref, ordered_ref, turned_ref = refs[:6]
    groups = (len(refs) - 6) // 9
    rows_refs, blended_ref = refs[6 : 5 + groups], refs[5 + groups]
    chains = [refs[6 + groups + 8 * c : 14 + groups + 8 * c] for c in range(groups)]
    members, half = right_ref.shape
    row_id = lax.broadcasted_iota(jnp.int32, (members, members), 0)
    col_id = lax.broadcasted_iota(jnp.int32, (members, members), 1)
    identity = jnp.where(row_id == col_id, 1.0, 0.0)
    eye = lax.broadcasted_iota(jnp.int32, (LANES, LANES), 0) == lax.broadcasted_iota(
        jnp.int32, (LANES, LANES), 1
    )
    dot = functools.partial(jnp.dot, preferred_element_type=F32)

    def diagonal_row(lower, corner):
        return jnp.concatenate(
            [
                jnp.sum(
                    jnp.where(eye, part[begin : begin + LANES, begin : begin + LANES], 0.0),
                    axis=0,
                    keepdims=True,
                )
                for part in (corner, lower)
                for begin in range(0, half, LANES)
            ],
            axis=1,
        )

    def split(w_high, right, corner):
        put_symmetric(w_high, right, corner)
        for first, part in ((0, corner), (half, right[half:, :])):
            for begin in range(0, half, LANES):
                block = part[begin : begin + LANES, begin : begin + LANES]
                place = slice(first + begin, first + begin + LANES)
                w_high[place, place] = jnp.where(eye, 0.0, block).astype(BF16)
        return 1.5 + diagonal_row(right[half:, :], corner)

    def advance(factor, w_high, right, corner, high):
        change_right, change_corner = symmetric_product(high, w_high)
        return (
            factor[:, half:] * right + change_right,
            factor[:, 0:half] * corner + change_corner,
        )

    tails = [[tails_ref[source] for source in range(tails_ref.shape[0])]]
    tails += [slot_tails(rows_ref) for rows_ref in rows_refs]
    rights, corners, drives = [right_ref[...]], [corner_ref[...]], [drive_ref[...]]
    rows = ordered_ref[...].astype(F32)
    for chain in range(1, groups):
        scaled, drive = scaled_rows(rows, tails[chain], groups - chain, groups)
        rights.append(dot(turned_ref[...], scaled[:, half:]))
        corners.append(dot(turned_ref[0:half, :], scaled[:, 0:half]))
        drives.append(drive)
    for turn, rows_ref in enumerate(rows_refs, 1):
        rows = slot_rows(rows_ref, members)
        turned = rows.T.astype(BF16)
        for chain in range(groups):
            scaled, drive = scaled_rows(rows, tails[chain], (turn - chain) % groups, groups)
            rights[chain] = rights[chain] + dot(turned, scaled[:, half:])
            corners[chain] = corners[chain] + dot(turned[0:half, :], scaled[:, 0:half])
            drives[chain] = drives[chain] + drive

    frobenius = []
    for chain, (y_right, y_corner, z_right, z_corner, y_high, z_high, _, w_high) in enumerate(
        chains
    ):
        right = identity[:, half:] + rights[chain] / (members - 1.0)
        corner = identity[0:half, 0:half] + corners[chain] / (members - 1.0)
        squares = right * right
        squares = 2.0 * squares[0:half, :] + squares[half:, :] + corner * corner
        squares = jnp.sum(jnp.sum(squares, axis=0, keepdims=True), axis=1, keepdims=True)
        frobenius.append(jnp.sqrt(squares))
        right, corner = right / frobenius[chain], corner / frobenius[chain]
        factor = split(w_high, -0.5 * right, -0.5 * corner)
        put_symmetric(y_high, right, corner)
        y_right[...], y_corner[...] = advance(factor, w_high, right, corner, y_high)
        z_right[...] = 0.25 * right - 0.75 * identity[:, half:]
        z_corner[...] = 0.25 * corner - 0.75 * identity[0:half, 0:half]
        put_symmetric(y_high, y_right[...], y_corner[...])
        put_symmetric(z_high, z_right[...], z_corner[...])

    def step(_, carry):
        factors = [
            split(chain[7], *symmetric_product(chain[5], chain[4])) for chain in chains
        ]
        for factor, chain in zip(factors, chains):
            for right, corner, high in (
                (chain[0], chain[1], chain[4]),
                (chain[2], chain[3], chain[5]),
            ):
                new_right, new_corner = advance(factor, chain[7], right[...], corner[...], high)
                right[...], corner[...] = new_right, new_corner
                put_symmetric(high, new_right, new_corner)
        return carry

    lax.fori_loop(1, NS_STEPS - 1, step, 0)
    factors = []
    for y_right, y_corner, z_right, z_corner, y_high, z_high, z_off, w_high in chains:
        z_off[...] = z_high[...]
        for right, corner, off in ((y_right, y_corner, y_high), (z_right, z_corner, z_off)):
            for first, part in ((0, corner), (half, right)):
                for begin in range(0, half, LANES):
                    place = slice(first + begin, first + begin + LANES)
                    block = part[place, begin : begin + LANES]
                    off[place, place] = jnp.where(eye, 0.0, block).astype(BF16)
        y_row = diagonal_row(y_right[half:, :], y_corner[...])
        z_row = diagonal_row(z_right[half:, :], z_corner[...])
        z_column = diagonal_column(z_row, eye)
        right, corner = symmetric_product(z_off, y_high)
        right += z_column * y_right[...] + z_right[...] * y_row[:, half:]
        corner += z_column[0:half, :] * y_corner[...] + z_corner[...] * y_row[:, 0:half]
        factors.append(split(w_high, right, corner) - z_row * y_row)
    for chain, (_, _, z_right, z_corner, _, z_high, _, w_high) in enumerate(chains):
        right, corner = advance(factors[chain], w_high, z_right[...], z_corner[...], z_high)
        left = jnp.concatenate([corner, right[0:half, :].T], axis=0)
        root = jnp.concatenate([left, right], axis=1) * (-2.0 / jnp.sqrt(frobenius[chain]))
        inner = jnp.sum(root * diagonal_column(drives[chain], eye), axis=0, keepdims=True)
        mean_weight = jnp.sum(root * diagonal_column(inner, eye), axis=0, keepdims=True)
        blended_ref[chain] = (root + mean_weight / (members - 1.0)).astype(BF16)


def patch_weights(own, other_rows):
    groups, members = len(other_rows) + 1, own[0].shape[0]
    half = members // 2
    right, corner = pltpu.VMEM((members, half), F32), pltpu.VMEM((half, half), F32)
    chain = [right, corner] * 2 + [pltpu.VMEM((members, members), BF16)] * 4
    return pl.pallas_call(
        weights_kernel,
        out_shape=jax.ShapeDtypeStruct((groups, members, members), BF16),
        scratch_shapes=chain * groups,
        compiler_params=pltpu.CompilerParams(vmem_limit_bytes=(8 + 10 * groups) * MEBI),
        cost_estimate=pl.CostEstimate(
            flops=80 * groups * members * members * members,
            bytes_accessed=8 * members * members,
            transcendentals=0,
        ),
        name="patch_weights",
    )(*own, *other_rows)


def update_kernel(order, blended_ref, background_ref, analysis_ref):
    groups = blended_ref.shape[0]
    members, points = background_ref.shape
    rows = members // len(order)
    places = [order.index(holder) for holder in range(len(order))]
    tile = min(points, 256)
    for begin in range(0, points, tile):
        columns = slice(begin, begin + tile)
        background = background_ref[:, columns].astype(F32)
        background = jnp.concatenate(
            [background[place * rows : (place + 1) * rows, :] for place in places], axis=0
        )
        centre = jnp.sum(background, axis=0, keepdims=True) / members
        perturb = (background - centre).astype(BF16)
        for turn in range(groups):
            update = jnp.dot(blended_ref[turn], perturb, preferred_element_type=F32)
            group = lax.rem(lax.axis_index("boot") + turn, groups)
            update = centre + update
            update = jnp.concatenate(
                [update[holder * rows : (holder + 1) * rows, :] for holder in order], axis=0
            )
            update = update.astype(BF16).reshape(len(order), rows, tile)
            analysis_ref[:, group, :, columns] = update


def update_points(blended, background, order):
    groups = blended.shape[0]
    members, points = background.shape
    return pl.pallas_call(
        functools.partial(update_kernel, order),
        out_shape=jax.ShapeDtypeStruct(
            (len(order), groups, members // len(order), points), BF16
        ),
        compiler_params=pltpu.CompilerParams(vmem_limit_bytes=16 * MEBI),
        cost_estimate=pl.CostEstimate(
            flops=2 * groups * members * members * points,
            bytes_accessed=2 * (groups + 1) * members * points,
            transcendentals=0,
        ),
        name="update_points",
    )(blended, background)


def cut_kernel(order, states_ref, cut_ref):
    patches, _, share = cut_ref.shape
    region = states_ref.shape[1] // patches
    offset = lax.axis_index("boot") * share
    for place, patch in enumerate(order):
        begin = pl.multiple_of(patch * region + offset, LANES)
        cut_ref[place] = states_ref[:, pl.ds(begin, share)]


def cut_share(states, order, share):
    own_members, patches = states.shape[0], len(order)
    return pl.pallas_call(
        functools.partial(cut_kernel, order),
        out_shape=jax.ShapeDtypeStruct((patches, own_members, share), BF16),
        compiler_params=pltpu.CompilerParams(vmem_limit_bytes=16 * MEBI),
        cost_estimate=pl.CostEstimate(
            flops=0, bytes_accessed=4 * patches * own_members * share, transcendentals=0
        ),
        name="cut_share",
    )(states)


def place_kernel(order, pieces_ref, whole_ref, held_ref, sems):
    groups, share = pieces_ref.shape[1], pieces_ref.shape[3]
    steps = sems.shape[0]
    width = held_ref.shape[1] // steps
    copies = []
    for step in range(steps):
        for patch in range(step * len(order) // steps, (step + 1) * len(order) // steps):
            for group in range(groups):
                begin = (patch * groups + group) * share
                held_ref[:, begin : begin + share] = pieces_ref[order.index(patch), group]
        columns = slice(step * width, (step + 1) * width)
        copies.append(
            pltpu.make_async_copy(held_ref.at[:, columns], whole_ref.at[:, columns], sems.at[step])
        )
        copies[step].start()
    for copy in copies:
        copy.wait()


def place_pieces(pieces, order):
    patches, groups, own_members, share = pieces.shape
    points = groups * patches * share
    return pl.pallas_call(
        functools.partial(place_kernel, order),
        out_specs=pl.BlockSpec(memory_space=pl.ANY),
        out_shape=jax.ShapeDtypeStruct((own_members, points), BF16),
        scratch_shapes=[pltpu.VMEM((own_members, points), BF16), pltpu.SemaphoreType.DMA((4,))],
        compiler_params=pltpu.CompilerParams(vmem_limit_bytes=16 * MEBI),
        cost_estimate=pl.CostEstimate(
            flops=0, bytes_accessed=4 * own_members * points, transcendentals=0
        ),
        name="place_pieces",
    )(pieces)


def exchange(blocks, axes=PARTNERS):
    return lax.all_to_all(blocks, axes, split_axis=0, concat_axis=0, tiled=True)


def swap_shares(own):
    groups = lax.axis_size("boot")
    return [
        lax.ppermute(own, "boot", [(g, (g - turn) % groups) for g in range(groups)])
        for turn in range(1, groups)
    ]


def local(
    background_states,
    measurement_anomaly_matrix,
    departure_vector,
    measurement_precision,
    measurement_region_targets,
    localization_factor_scaled,
    bootstrap_multiplicity,
):
    order = partner_order([lax.axis_size(axis) for axis in SPACE])
    device_count = len(order)
    groups = lax.axis_size("boot")
    local_rows = measurement_anomaly_matrix.shape[0]
    targets_per = measurement_region_targets.shape[1]
    slot_cap = 2 * targets_per * local_rows // device_count
    slot_share = -(-slot_cap // (ROWS * groups)) * ROWS
    own_members, points = background_states.shape
    share = points // device_count // groups

    slots = pack(
        measurement_region_targets,
        localization_factor_scaled,
        bootstrap_multiplicity,
        measurement_precision,
        departure_vector,
        measurement_anomaly_matrix,
        order,
        slot_share,
        groups,
    )
    own_points = cut_share(background_states, order, share)
    own_rows = exchange(slots)
    other_rows = swap_shares(own_rows)
    own_points = exchange(own_points).reshape(-1, share)

    own = own_gram(own_rows, measurement_anomaly_matrix.shape[1], groups)
    blended = patch_weights(own, other_rows)
    analysis = update_points(blended, own_points, order)
    analysis = exchange(analysis.reshape(-1, own_members, share), PARTNERS + ("boot",))
    return place_pieces(analysis.reshape(device_count, groups, own_members, share), order)


def solution(mesh):
    groups, devices = mesh.shape["boot"], mesh.shape["space"]
    cut = 2 if devices % 4 == 0 else 1
    mesh = Mesh(
        mesh.devices.reshape(groups, cut, cut, devices // cut**2), ("boot",) + SPACE
    )
    in_specs = (
        P(SPACE, None),
        P(SPACE, None),
        P(SPACE),
        P(SPACE),
        P(SPACE, None),
        P(SPACE, None),
        P(("boot",) + SPACE),
    )
    out_specs = P(("boot",) + SPACE, None)
    return jax.shard_map(local, mesh=mesh, in_specs=in_specs, out_specs=out_specs, check_vma=False)
```

```python
import functools

import jax
import jax.numpy as jnp
from jax import lax
from jax.experimental import pallas as pl
from jax.experimental.pallas import tpu as pltpu
from jax.sharding import Mesh
from jax.sharding import PartitionSpec as P

NS_STEPS = 6
SPACE = ("za", "zb", "near")
PARTNERS = ("near", "zb", "za")
LANES = 128
ROWS = 8
MEBI = 1024 * 1024
F32 = jnp.float32
BF16 = jnp.bfloat16


def partner_order(sizes):
    za, zb, near = sizes
    return [(a * zb + b) * near + c for c in range(near) for b in range(zb) for a in range(za)]


def pack_kernel(groups, order, *refs):
    sources, slots_ref, fetched = refs[:6], refs[6], refs[7:13]
    block_ref, tail_ref, info_ref, sems = refs[13:]
    copies = [
        pltpu.make_async_copy(source, target, sems.at[i])
        for i, (source, target) in enumerate(zip(sources, fetched))
    ]
    for copy in copies:
        copy.start()
    for copy in copies[:-1]:
        copy.wait()
    targets_ref, local_ref, mult_ref, prec_ref, dep_ref, rows_ref = fetched
    patches, _, width = block_ref.shape
    count, members = rows_ref.shape
    share = width // members * ROWS
    patch_id = lax.broadcasted_iota(jnp.int32, (patches, count), 0)
    first = patch_id == targets_ref[0:1, :]
    second = patch_id == targets_ref[1:2, :]
    named = jnp.logical_or(first, second)
    earlier = lax.broadcasted_iota(jnp.int32, (count, count), 0) < lax.broadcasted_iota(
        jnp.int32, (count, count), 1
    )
    rank = jnp.dot(
        named.astype(F32).astype(BF16), earlier.astype(F32).astype(BF16), preferred_element_type=F32
    )
    rank = jnp.where(named, rank, -1.0)

    slots = groups * share
    slot_id = lax.broadcasted_iota(jnp.int32, (slots, count), 0) + lax.axis_index("boot") * share
    slot_id = jnp.where(slot_id < slots, slot_id, slot_id - slots).astype(F32)
    named_by = [
        jnp.where(slot_id == rank[patch : patch + 1, :], 1.0, 0.0) for patch in order
    ]
    picks = jnp.concatenate([pick[0:share, :] for pick in named_by], axis=0).astype(BF16)
    copies[-1].wait()
    picked = jnp.dot(picks, rows_ref[...], preferred_element_type=F32)
    for patch in range(patches):
        place = patch * share
        blocks = [picked[place + i : place + i + ROWS, :] for i in range(0, share, ROWS)]
        block_ref[patch] = jnp.concatenate(blocks, axis=1).astype(BF16)
    blocks_out = pltpu.make_async_copy(block_ref, slots_ref.at[:, :, 0:width], sems.at[6])
    blocks_out.start()

    mult = mult_ref[...].reshape(1, count).astype(F32)
    prec = prec_ref[...].reshape(1, count)
    weight = local_ref[...].astype(F32) / 1024.0 * (mult * prec)
    weight = weight.astype(BF16).astype(F32)
    dep = dep_ref[...].astype(F32).reshape(1, count)
    by_patch = jnp.where(first, weight[0:1, :], jnp.where(second, weight[1:2, :], 0.0))
    info_ref[...] = jnp.zeros(info_ref.shape, F32)
    info_ref[0:patches, :] = by_patch
    info_ref[patches : patches + 1, :] = dep
    info = jnp.dot(
        jnp.concatenate(named_by, axis=0).astype(BF16),
        info_ref[...].T.astype(BF16),
        preferred_element_type=F32,
    )
    lane = lax.broadcasted_iota(jnp.int32, (ROWS, LANES), 1)
    height = slots // ROWS
    for place, patch in enumerate(order):
        tail = jnp.zeros((ROWS, LANES), F32)
        for i in range(height):
            begin = place * slots + i * ROWS
            block = info[begin : begin + ROWS, :]
            tail = jnp.where(lane == i, block[:, patch : patch + 1], tail)
            tail = jnp.where(lane == height + i, block[:, patches : patches + 1], tail)
        tail_ref[place] = tail.astype(BF16)
    tails_out = pltpu.make_async_copy(tail_ref, slots_ref.at[:, :, width:], sems.at[7])
    tails_out.start()
    blocks_out.wait()
    tails_out.wait()


def pack(targets, local, mult, prec, dep, rows, order, share, groups):
    count, members = rows.shape
    patches = len(order)
    operands = (targets.T, local.T, mult, prec, dep, rows)
    width = share // ROWS * members
    return pl.pallas_call(
        functools.partial(pack_kernel, groups, order),
        out_shape=jax.ShapeDtypeStruct((patches, ROWS, width + LANES), BF16),
        in_specs=[pl.BlockSpec(memory_space=pl.ANY)] * len(operands),
        out_specs=pl.BlockSpec(memory_space=pl.ANY),
        scratch_shapes=[pltpu.VMEM(operand.shape, operand.dtype) for operand in operands]
        + [
            pltpu.VMEM((patches, ROWS, width), BF16),
            pltpu.VMEM((patches, ROWS, LANES), BF16),
            pltpu.VMEM((LANES, count), F32),
            pltpu.SemaphoreType.DMA((len(operands) + 2,)),
        ],
        compiler_params=pltpu.CompilerParams(vmem_limit_bytes=64 * MEBI),
        cost_estimate=pl.CostEstimate(
            flops=2 * patches * share * count * members,
            bytes_accessed=2 * (patches * share + count) * members,
            transcendentals=0,
        ),
        name="pack_rows",
    )(*operands)


def slot_rows(rows_ref, members):
    blocks = []
    for source in range(rows_ref.shape[0]):
        block = rows_ref[source].astype(F32)
        for begin in range(0, block.shape[1] - LANES, members):
            blocks.append(block[:, begin : begin + members])
    return jnp.concatenate(blocks, axis=0)


def slot_tails(rows_ref):
    return [
        rows_ref[source, :, rows_ref.shape[2] - LANES :].astype(F32)
        for source in range(rows_ref.shape[0])
    ]


def scaled_rows(rows, tails, position, groups):
    height = rows.shape[0] // len(tails) // ROWS
    blocks, drive = [], jnp.zeros((ROWS, rows.shape[1]), F32)
    for source, tail in enumerate(tails):
        for i in range(height):
            begin = (source * height + i) * ROWS
            column = position * height + i
            block = tail[:, column : column + 1] * rows[begin : begin + ROWS, :]
            block = block.astype(BF16).astype(F32)
            blocks.append(block)
            column += groups * height
            drive = drive + tail[:, column : column + 1] * block
    return jnp.concatenate(blocks, axis=0).astype(BF16), jnp.sum(drive, axis=0, keepdims=True)


def gram_kernel(groups, *refs):
    rows_ref, right_ref, corner_ref, drive_ref, tails_ref, ordered_ref, turned_ref = refs
    members, half = right_ref.shape
    rows = slot_rows(rows_ref, members)
    ordered_ref[...] = rows.astype(BF16)
    turned_ref[...] = rows.T.astype(BF16)
    tails = slot_tails(rows_ref)
    for source, tail in enumerate(tails):
        tails_ref[source] = tail
    scaled, drive_ref[...] = scaled_rows(rows, tails, 0, groups)
    dot = functools.partial(jnp.dot, preferred_element_type=F32)
    right_ref[...] = dot(turned_ref[...], scaled[:, half:])
    corner_ref[...] = dot(turned_ref[0:half, :], scaled[:, 0:half])


def own_gram(rows, members, groups):
    sources, height, width = rows.shape
    slots = sources * height * ((width - LANES) // members)
    return pl.pallas_call(
        functools.partial(gram_kernel, groups),
        out_shape=(
            jax.ShapeDtypeStruct((members, members // 2), F32),
            jax.ShapeDtypeStruct((members // 2, members // 2), F32),
            jax.ShapeDtypeStruct((1, members), F32),
            jax.ShapeDtypeStruct((sources, height, LANES), F32),
            jax.ShapeDtypeStruct((slots, members), BF16),
            jax.ShapeDtypeStruct((members, slots), BF16),
        ),
        compiler_params=pltpu.CompilerParams(vmem_limit_bytes=16 * MEBI),
        cost_estimate=pl.CostEstimate(
            flops=4 * members * members * slots,
            bytes_accessed=6 * slots * members,
            transcendentals=0,
        ),
        name="own_gram",
    )(rows)


def diagonal_column(value, eye):
    size = value.shape[1]
    parts = []
    for begin in range(0, size, LANES):
        block = value[:, begin : begin + LANES]
        block = block if value.shape[0] == 1 else block[begin : begin + LANES, :]
        parts.append(jnp.sum(jnp.where(eye, block, 0.0), axis=1, keepdims=True))
    return jnp.concatenate(parts, axis=0)


def symmetric_product(left_ref, right_ref):
    half = left_ref.shape[0] // 2
    dot = functools.partial(jnp.dot, preferred_element_type=F32)
    return (
        dot(left_ref[...], right_ref[:, half:]),
        dot(left_ref[0:half, :], right_ref[:, 0:half]),
    )


def put_symmetric(ref, right, corner):
    half = corner.shape[0]
    right = right.astype(BF16)
    ref[:, half:] = right
    ref[0:half, 0:half] = corner.astype(BF16)
    ref[half:, 0:half] = right[0:half, :].T


def weights_kernel(*refs):
    right_ref, corner_ref, drive_ref, tails_ref, ordered_ref, turned_ref = refs[:6]
    groups = (len(refs) - 6) // 9
    rows_refs, blended_ref = refs[6 : 5 + groups], refs[5 + groups]
    chains = [refs[6 + groups + 8 * c : 14 + groups + 8 * c] for c in range(groups)]
    members, half = right_ref.shape
    row_id = lax.broadcasted_iota(jnp.int32, (members, members), 0)
    col_id = lax.broadcasted_iota(jnp.int32, (members, members), 1)
    identity = jnp.where(row_id == col_id, 1.0, 0.0)
    eye = lax.broadcasted_iota(jnp.int32, (LANES, LANES), 0) == lax.broadcasted_iota(
        jnp.int32, (LANES, LANES), 1
    )
    dot = functools.partial(jnp.dot, preferred_element_type=F32)

    def diagonal_row(lower, corner):
        return jnp.concatenate(
            [
                jnp.sum(
                    jnp.where(eye, part[begin : begin + LANES, begin : begin + LANES], 0.0),
                    axis=0,
                    keepdims=True,
                )
                for part in (corner, lower)
                for begin in range(0, half, LANES)
            ],
            axis=1,
        )

    def split(w_high, right, corner):
        put_symmetric(w_high, right, corner)
        for first, part in ((0, corner), (half, right[half:, :])):
            for begin in range(0, half, LANES):
                block = part[begin : begin + LANES, begin : begin + LANES]
                place = slice(first + begin, first + begin + LANES)
                w_high[place, place] = jnp.where(eye, 0.0, block).astype(BF16)
        return 1.5 + diagonal_row(right[half:, :], corner)

    def advance(factor, w_high, right, corner, high):
        change_right, change_corner = symmetric_product(high, w_high)
        return (
            factor[:, half:] * right + change_right,
            factor[:, 0:half] * corner + change_corner,
        )

    tails = [[tails_ref[source] for source in range(tails_ref.shape[0])]]
    tails += [slot_tails(rows_ref) for rows_ref in rows_refs]
    rights, corners, drives = [right_ref[...]], [corner_ref[...]], [drive_ref[...]]
    rows = ordered_ref[...].astype(F32)
    for chain in range(1, groups):
        scaled, drive = scaled_rows(rows, tails[chain], groups - chain, groups)
        rights.append(dot(turned_ref[...], scaled[:, half:]))
        corners.append(dot(turned_ref[0:half, :], scaled[:, 0:half]))
        drives.append(drive)
    for turn, rows_ref in enumerate(rows_refs, 1):
        rows = slot_rows(rows_ref, members)
        turned = rows.T.astype(BF16)
        for chain in range(groups):
            scaled, drive = scaled_rows(rows, tails[chain], (turn - chain) % groups, groups)
            rights[chain] = rights[chain] + dot(turned, scaled[:, half:])
            corners[chain] = corners[chain] + dot(turned[0:half, :], scaled[:, 0:half])
            drives[chain] = drives[chain] + drive

    frobenius = []
    for chain, (y_right, y_corner, z_right, z_corner, y_high, z_high, _, w_high) in enumerate(
        chains
    ):
        right = identity[:, half:] + rights[chain] / (members - 1.0)
        corner = identity[0:half, 0:half] + corners[chain] / (members - 1.0)
        squares = right * right
        squares = 2.0 * squares[0:half, :] + squares[half:, :] + corner * corner
        squares = jnp.sum(jnp.sum(squares, axis=0, keepdims=True), axis=1, keepdims=True)
        frobenius.append(jnp.sqrt(squares))
        right, corner = right / frobenius[chain], corner / frobenius[chain]
        factor = split(w_high, -0.5 * right, -0.5 * corner)
        put_symmetric(y_high, right, corner)
        y_right[...], y_corner[...] = advance(factor, w_high, right, corner, y_high)
        z_right[...] = 0.25 * right - 0.75 * identity[:, half:]
        z_corner[...] = 0.25 * corner - 0.75 * identity[0:half, 0:half]
        put_symmetric(y_high, y_right[...], y_corner[...])
        put_symmetric(z_high, z_right[...], z_corner[...])

    def step(_, carry):
        factors = [
            split(chain[7], *symmetric_product(chain[5], chain[4])) for chain in chains
        ]
        for factor, chain in zip(factors, chains):
            for right, corner, high in (
                (chain[0], chain[1], chain[4]),
                (chain[2], chain[3], chain[5]),
            ):
                new_right, new_corner = advance(factor, chain[7], right[...], corner[...], high)
                right[...], corner[...] = new_right, new_corner
                put_symmetric(high, new_right, new_corner)
        return carry

    lax.fori_loop(1, NS_STEPS - 1, step, 0)
    factors = []
    for y_right, y_corner, z_right, z_corner, y_high, z_high, z_off, w_high in chains:
        z_off[...] = z_high[...]
        for right, corner, off in ((y_right, y_corner, y_high), (z_right, z_corner, z_off)):
            for first, part in ((0, corner), (half, right)):
                for begin in range(0, half, LANES):
                    place = slice(first + begin, first + begin + LANES)
                    block = part[place, begin : begin + LANES]
                    off[place, place] = jnp.where(eye, 0.0, block).astype(BF16)
        y_row = diagonal_row(y_right[half:, :], y_corner[...])
        z_row = diagonal_row(z_right[half:, :], z_corner[...])
        z_column = diagonal_column(z_row, eye)
        right, corner = symmetric_product(z_off, y_high)
        right += z_column * y_right[...] + z_right[...] * y_row[:, half:]
        corner += z_column[0:half, :] * y_corner[...] + z_corner[...] * y_row[:, 0:half]
        factors.append(split(w_high, right, corner) - z_row * y_row)
    for chain, (_, _, z_right, z_corner, _, z_high, _, w_high) in enumerate(chains):
        right, corner = advance(factors[chain], w_high, z_right[...], z_corner[...], z_high)
        left = jnp.concatenate([corner, right[0:half, :].T], axis=0)
        root = jnp.concatenate([left, right], axis=1) * (-2.0 / jnp.sqrt(frobenius[chain]))
        inner = jnp.sum(root * diagonal_column(drives[chain], eye), axis=0, keepdims=True)
        mean_weight = jnp.sum(root * diagonal_column(inner, eye), axis=0, keepdims=True)
        blended_ref[chain] = (root + mean_weight / (members - 1.0)).astype(BF16)


def patch_weights(own, other_rows):
    groups, members = len(other_rows) + 1, own[0].shape[0]
    half = members // 2
    right, corner = pltpu.VMEM((members, half), F32), pltpu.VMEM((half, half), F32)
    chain = [right, corner] * 2 + [pltpu.VMEM((members, members), BF16)] * 4
    return pl.pallas_call(
        weights_kernel,
        out_shape=jax.ShapeDtypeStruct((groups, members, members), BF16),
        scratch_shapes=chain * groups,
        compiler_params=pltpu.CompilerParams(vmem_limit_bytes=(8 + 10 * groups) * MEBI),
        cost_estimate=pl.CostEstimate(
            flops=80 * groups * members * members * members,
            bytes_accessed=8 * members * members,
            transcendentals=0,
        ),
        name="patch_weights",
    )(*own, *other_rows)


def update_kernel(order, blended_ref, background_ref, analysis_ref):
    groups = blended_ref.shape[0]
    members, points = background_ref.shape
    rows = members // len(order)
    places = [order.index(holder) for holder in range(len(order))]
    tile = min(points, 256)
    for begin in range(0, points, tile):
        columns = slice(begin, begin + tile)
        background = background_ref[:, columns].astype(F32)
        background = jnp.concatenate(
            [background[place * rows : (place + 1) * rows, :] for place in places], axis=0
        )
        centre = jnp.sum(background, axis=0, keepdims=True) / members
        perturb = (background - centre).astype(BF16)
        blended = blended_ref[...].reshape(groups * members, members)
        updates = jnp.dot(blended, perturb, preferred_element_type=F32)
        for turn in range(groups):
            update = updates[turn * members : (turn + 1) * members, :]
            group = lax.rem(lax.axis_index("boot") + turn, groups)
            update = centre + update
            update = jnp.concatenate(
                [update[holder * rows : (holder + 1) * rows, :] for holder in order], axis=0
            )
            update = update.astype(BF16).reshape(len(order), rows, tile)
            analysis_ref[:, group, :, columns] = update


def update_points(blended, background, order):
    groups = blended.shape[0]
    members, points = background.shape
    return pl.pallas_call(
        functools.partial(update_kernel, order),
        out_shape=jax.ShapeDtypeStruct(
            (len(order), groups, members // len(order), points), BF16
        ),
        compiler_params=pltpu.CompilerParams(vmem_limit_bytes=16 * MEBI),
        cost_estimate=pl.CostEstimate(
            flops=2 * groups * members * members * points,
            bytes_accessed=2 * (groups + 1) * members * points,
            transcendentals=0,
        ),
        name="update_points",
    )(blended, background)


def cut_kernel(order, states_ref, cut_ref):
    patches, _, share = cut_ref.shape
    region = states_ref.shape[1] // patches
    offset = lax.axis_index("boot") * share
    for place, patch in enumerate(order):
        begin = pl.multiple_of(patch * region + offset, LANES)
        cut_ref[place] = states_ref[:, pl.ds(begin, share)]


def cut_share(states, order, share):
    own_members, patches = states.shape[0], len(order)
    return pl.pallas_call(
        functools.partial(cut_kernel, order),
        out_shape=jax.ShapeDtypeStruct((patches, own_members, share), BF16),
        compiler_params=pltpu.CompilerParams(vmem_limit_bytes=16 * MEBI),
        cost_estimate=pl.CostEstimate(
            flops=0, bytes_accessed=4 * patches * own_members * share, transcendentals=0
        ),
        name="cut_share",
    )(states)


def place_kernel(order, pieces_ref, whole_ref, held_ref, sems):
    groups, share = pieces_ref.shape[1], pieces_ref.shape[3]
    steps = sems.shape[0]
    width = held_ref.shape[1] // steps
    copies = []
    for step in range(steps):
        for patch in range(step * len(order) // steps, (step + 1) * len(order) // steps):
            for group in range(groups):
                begin = (patch * groups + group) * share
                held_ref[:, begin : begin + share] = pieces_ref[order.index(patch), group]
        columns = slice(step * width, (step + 1) * width)
        copies.append(
            pltpu.make_async_copy(held_ref.at[:, columns], whole_ref.at[:, columns], sems.at[step])
        )
        copies[step].start()
    for copy in copies:
        copy.wait()


def place_pieces(pieces, order):
    patches, groups, own_members, share = pieces.shape
    points = groups * patches * share
    return pl.pallas_call(
        functools.partial(place_kernel, order),
        out_specs=pl.BlockSpec(memory_space=pl.ANY),
        out_shape=jax.ShapeDtypeStruct((own_members, points), BF16),
        scratch_shapes=[pltpu.VMEM((own_members, points), BF16), pltpu.SemaphoreType.DMA((4,))],
        compiler_params=pltpu.CompilerParams(vmem_limit_bytes=16 * MEBI),
        cost_estimate=pl.CostEstimate(
            flops=0, bytes_accessed=4 * own_members * points, transcendentals=0
        ),
        name="place_pieces",
    )(pieces)


def exchange(blocks, axes=PARTNERS):
    return lax.all_to_all(blocks, axes, split_axis=0, concat_axis=0, tiled=True)


def swap_shares(own):
    groups = lax.axis_size("boot")
    return [
        lax.ppermute(own, "boot", [(g, (g - turn) % groups) for g in range(groups)])
        for turn in range(1, groups)
    ]


def local(
    background_states,
    measurement_anomaly_matrix,
    departure_vector,
    measurement_precision,
    measurement_region_targets,
    localization_factor_scaled,
    bootstrap_multiplicity,
):
    order = partner_order([lax.axis_size(axis) for axis in SPACE])
    device_count = len(order)
    groups = lax.axis_size("boot")
    local_rows = measurement_anomaly_matrix.shape[0]
    targets_per = measurement_region_targets.shape[1]
    slot_cap = 2 * targets_per * local_rows // device_count
    slot_share = -(-slot_cap // (ROWS * groups)) * ROWS
    own_members, points = background_states.shape
    share = points // device_count // groups

    slots = pack(
        measurement_region_targets,
        localization_factor_scaled,
        bootstrap_multiplicity,
        measurement_precision,
        departure_vector,
        measurement_anomaly_matrix,
        order,
        slot_share,
        groups,
    )
    own_points = cut_share(background_states, order, share)
    own_rows, own_points = lax.optimization_barrier((exchange(slots), own_points))
    other_rows = swap_shares(own_rows)
    own_points = exchange(own_points).reshape(-1, share)

    own = own_gram(own_rows, measurement_anomaly_matrix.shape[1], groups)
    blended = patch_weights(own, other_rows)
    analysis = update_points(blended, own_points, order)
    analysis = exchange(analysis.reshape(-1, own_members, share), PARTNERS + ("boot",))
    return place_pieces(analysis.reshape(device_count, groups, own_members, share), order)


def solution(mesh):
    groups, devices = mesh.shape["boot"], mesh.shape["space"]
    cut = 2 if devices % 4 == 0 else 1
    mesh = Mesh(
        mesh.devices.reshape(groups, cut, cut, devices // cut**2), ("boot",) + SPACE
    )
    in_specs = (
        P(SPACE, None),
        P(SPACE, None),
        P(SPACE),
        P(SPACE),
        P(SPACE, None),
        P(SPACE, None),
        P(("boot",) + SPACE),
    )
    out_specs = P(("boot",) + SPACE, None)
    return jax.shard_map(local, mesh=mesh, in_specs=in_specs, out_specs=out_specs, check_vma=False)
```
